32 devices in a mesh: section: 4 (over y, x), dp: 4 (over z), cores: 2 (over core).
Axes of the slice: x: 2, y: 2, z: 4, core: 2. Of those that a mesh axis runs over, the one named last changes fastest.
Arguments:
- arrivals: bfloat16 [2, 384, 2048], P(None, 'dp'), may hold values from -6 to 6
- in_flight: bfloat16 [4, 384, 2048], P('section', 'dp'), may hold values from -6 to 6
- cotangent: bfloat16 [2, 384, 2048], P(None, 'dp'), may hold values from -6 to 6
- grad_flight: bfloat16 [4, 384, 2048], P('section', 'dp'), may hold values from -6 to 6
- stashed: bfloat16 [4, 2, 384, 2048], P('section', None, 'dp'), may hold values from -6 to 6
- in_weight: bfloat16 [4, 2048, 4096], P('section', 'dp', 'cores'), may hold values from -0.125 to 0.125
- out_weight: bfloat16 [4, 1024, 2048], P('section', 'cores', 'dp'), may hold values from -0.1875 to 0.1875
- forward_blocks: int32 [4, 5], P('dp'), may hold values from 1 to 4, 12 in all within a row
- backward_blocks: int32 [4, 5], P('dp'), may hold values from 1 to 4, 12 in all within a row
- forward_marks: int32 [4, 5, 4, 4], P('dp'), may hold values 0 or 1
- backward_marks: int32 [4, 5, 4, 4], P('dp'), may hold values 0 or 1
Outputs:
- activations: bfloat16 [4, 2, 384, 2048], P('section', None, ('dp', 'cores'))
- input_grads: bfloat16 [4, 2, 384, 2048], P('section', None, ('dp', 'cores'))
- weight_grads: float32 [4, 1024, 2048], P('section', 'cores', 'dp')
The draws below stay inside these ranges and needn't reach their ends.
Inputs may be any that keep to these rules, and one draw needn't show every extreme that they name: `forward_blocks`: in each replica's row the 5 lengths add up to 12 blocks and the longest is 4. `backward_blocks`: in each replica's row the 5 lengths add up to 12 blocks and the longest is 4.
All inputs are finite; a program needn't handle non-finite values. No bound on the sum of `forward_marks` or of `backward_marks` on one device may be relied on, other than what follows from the above.
Results may differ from the reference program's by a relative error of at most 0.03.
Values may be sent and summed in bfloat16 or wider, within the bound.
No kernel may reach another device: no remote copies, remote signals or barrier semaphores. Data moves between devices by JAX's collectives and lax.ppermute only.
A program may use at most 64 MiB of HBM per device.

```python
import math
import jax
import jax.numpy as jnp
import numpy as np
from jax import lax

D = 2048
HEAD_DIM = 128
BLOCK = 24
BLOCKS = 4
TICKS = 2
LAYERS = 4
ROWS = 384
PROJ_WIDTH = 4096
ATTN_WIDTH = 1024
BATCHES = 5
TOTAL_BLOCKS = 12
N_DP = 4
N_CORES = 2


def with_ends(result, own_key, low, largest):
    extent = result.shape
    index_at = [jax.random.randint(jax.random.fold_in(own_key, axis), (), 0, extent[axis]) for axis in range(len(extent))]
    result = result.at[tuple(index_at)].set(low)
    longest = extent.index(max(extent))
    index_at[longest] = (index_at[longest] + 1) % extent[longest]
    return result.at[tuple(index_at)].set(largest)


def spiked(drawn, rng, source, target, blocks, factor):
    def block_of(dim):
        return (jnp.arange(drawn.shape[dim]) // (drawn.shape[dim] // blocks)).reshape((-1,) + (1,) * (drawn.ndim - 1 - dim))

    one_side = jax.random.permutation(rng, blocks)[block_of(target)]
    far = (block_of(target) + blocks // 2) % blocks
    return jnp.where((block_of(source) == one_side) | (block_of(source) == far), factor * drawn, drawn)


def steps_of(stream_key, shape, cuts, low, largest):
    def one(dim, blocks):
        heights = jax.random.uniform(jax.random.fold_in(jax.random.fold_in(stream_key, 6), dim), (blocks,), jnp.float32, low / len(cuts), largest / len(cuts))
        return jnp.repeat(jnp.exp(heights), shape[dim] // blocks).reshape((-1,) + (1,) * (len(shape) - dim - 1))

    factor_of = one(*cuts[0])
    for cut in cuts[1:]:
        factor_of = factor_of * one(*cut)
    return factor_of


def split_up(number_of, total, most, lean):
    portions = [(1 << 20) // math.isqrt(standing ** lean) + 1 for standing in range(2, number_of + 1)]
    spare, holding = total - most - (number_of - 1), [1] * (number_of - 1)
    while spare > 0:
        free = [i for i in range(number_of - 1) if holding[i] < most]
        pool, budget = sum([portions[i] for i in free]), spare
        for i in free:
            extra = min(most - holding[i], max(1, budget * portions[i] // pool), spare)
            holding[i] = holding[i] + extra
            spare = spare - extra
    return np.array([most] + holding)


def uneven_parts(stream_key, count, total, bound, lean):
    if count == 2:
        one = jax.random.randint(stream_key, (), max(1, total - bound), min(bound, total - 1) + 1)
        return jnp.stack([one, total - one])
    tallies = jnp.asarray(split_up(count, total, bound, lean), jnp.int32)
    couples = (count - 1) // 2
    giver, sink = tallies[1:1 + 2 * couples:2], tallies[2:2 + 2 * couples:2]
    margin = jnp.minimum(giver - 1, bound - sink)
    passed = jax.random.randint(jax.random.fold_in(stream_key, 1), (couples,), 0, 1 << 20) % (margin + 1)
    tallies = tallies.at[1:1 + 2 * couples:2].set(giver - passed).at[2:2 + 2 * couples:2].set(sink + passed)
    return tallies[jax.random.permutation(jax.random.fold_in(stream_key, 2), count)]


def scatter_about(own_key, extent, deviation, most, cuts=(), kind=jnp.bfloat16):
    level = steps_of(own_key, extent, cuts, -0.22, 0.18) if cuts else 1.0
    entries = jax.random.normal(own_key, extent, jnp.float32) * deviation * level
    return jnp.minimum(jnp.maximum(entries, -most), most).astype(kind)


def noise_with(own_key, shape, scale, limit, shards, heavy, kind=jnp.bfloat16):
    values = scale * jax.random.normal(own_key, shape, jnp.float32)
    if shards:
        values = values * steps_of(own_key, shape, shards, -0.22, 0.18)
    return jnp.clip(spiked(values, jax.random.fold_in(own_key, 3), *heavy), -limit, limit).astype(kind)


def setup_inputs(seed: int = 0) -> dict:
    splits = jax.random.split(jax.random.key(seed), 12)
    arrivals = scatter_about(splits[0], (TICKS, ROWS, D), 1.0, 6.0, ((1, 4),))
    in_flight = scatter_about(splits[1], (LAYERS, ROWS, D), 1.0, 6.0, ((0, 4), (1, 4)))
    cotangent = noise_with(splits[2], (TICKS, ROWS, D), 1.0, 6.0, ((1, 4),), (1, 2, 4, 2.0))
    grad_flight = noise_with(splits[3], (LAYERS, ROWS, D), 1.0, 6.0, ((0, 4), (1, 4)), (1, 2, 4, 2.0))
    stashed = scatter_about(splits[4], (LAYERS, TICKS, ROWS, D), 1.0, 6.0, ((0, 4), (2, 4)))
    in_weight = scatter_about(splits[5], (LAYERS, D, PROJ_WIDTH), D ** -0.5, 0.125, ((0, 4), (1, 4), (2, 2)))
    out_weight = scatter_about(splits[6], (LAYERS, ATTN_WIDTH, D), ATTN_WIDTH ** -0.5, 0.1875, ((0, 4), (1, 2), (2, 4)))
    forward_blocks = jax.vmap(lambda own: uneven_parts(own, BATCHES, TOTAL_BLOCKS, BLOCKS, 2))(jax.random.split(splits[7], N_DP)).reshape((N_DP, BATCHES)).astype(jnp.int32)
    backward_blocks = jax.vmap(lambda own: uneven_parts(own, BATCHES, TOTAL_BLOCKS, BLOCKS, 2))(jax.random.split(splits[8], N_DP)).reshape((N_DP, BATCHES)).astype(jnp.int32)
    forward_marks = with_ends((jax.random.randint(splits[9], (N_DP, BATCHES, BLOCKS, BLOCKS), 0, 2) < 1).astype(jnp.int32), jax.random.fold_in(splits[9], 1), 0, 1)
    backward_marks = with_ends((jax.random.randint(splits[10], (N_DP, BATCHES, BLOCKS, BLOCKS), 0, 2) < 1).astype(jnp.int32), jax.random.fold_in(splits[10], 1), 0, 1)
    return dict(arrivals=arrivals, in_flight=in_flight, cotangent=cotangent, grad_flight=grad_flight, stashed=stashed, in_weight=in_weight, out_weight=out_weight, forward_blocks=forward_blocks, backward_blocks=backward_blocks, forward_marks=forward_marks, backward_marks=backward_marks)


EPSILON = 1e-06

def block_keep(live_blocks, block_marks):
    length = BLOCKS * BLOCK
    places = jnp.arange(length, dtype=jnp.int32)
    owners = places // BLOCK
    onehot = (owners[:, None] == jnp.arange(BLOCKS, dtype=jnp.int32)[None, :]).astype(jnp.float32)
    spread = jnp.einsum('ia,rab,jb->rij', onehot, block_marks.astype(jnp.float32), onehot)
    allowed = (owners[:, None] == owners[None, :])[None] | (spread > 0.5)
    causal = (places[:, None] >= places[None, :])[None]
    tokens_live = live_blocks * BLOCK
    living = places[None, :] < tokens_live[:, None]
    keeping = causal & allowed & living[:, :, None] & living[:, None, :]
    return (keeping.astype(jnp.float32), 1.0 / tokens_live.astype(jnp.float32))

def norm_rows(values_f):
    return lax.rsqrt(lax.optimization_barrier(jnp.mean(values_f * values_f, axis=-1, keepdims=True)) + EPSILON)

def heads_forward(pre_act, keeping, inverse_count):
    scaling = HEAD_DIM ** (-0.5)
    active = jax.nn.silu(pre_act)
    gate_rows = active[:, :, :, 0]
    value_rows = active[:, :, :, 1].astype(jnp.bfloat16)
    query_rows = active[:, :, :, 2].astype(jnp.bfloat16)
    key_rows = active[:, :, :, 3].astype(jnp.bfloat16)
    scores = jnp.einsum('rigd,rjgd->rgij', query_rows.astype(jnp.float32), key_rows.astype(jnp.float32)) * scaling
    weights = keeping[:, None] * inverse_count[:, None, None, None]
    attention = (jax.nn.silu(scores) * weights).astype(jnp.bfloat16)
    mixed = jnp.einsum('rgij,rjgd->rigd', attention.astype(jnp.float32), value_rows.astype(jnp.float32))
    root_scale = lax.rsqrt(lax.optimization_barrier(jnp.mean(mixed * mixed, axis=-1, keepdims=True)) + EPSILON)
    normed = mixed * root_scale
    gated = (normed * gate_rows).astype(jnp.bfloat16)
    return (gated, (gate_rows, value_rows, query_rows, key_rows, scores, weights, attention, root_scale, normed))

def heads_backward(pre_act, saved, upstream):
    gate_rows, value_rows, query_rows, key_rows, scores, weights, attention, root_scale, normed = saved
    scaling = HEAD_DIM ** (-0.5)
    grad_gated = upstream.astype(jnp.float32)
    grad_normed = grad_gated * gate_rows
    grad_gate = grad_gated * normed
    grad_mixed = root_scale * (grad_normed - normed * lax.optimization_barrier(jnp.mean(grad_normed * normed, axis=-1, keepdims=True)))
    mixed_low = grad_mixed.astype(jnp.bfloat16)
    grad_attention = jnp.einsum('rigd,rjgd->rgij', mixed_low.astype(jnp.float32), value_rows.astype(jnp.float32))
    grad_value = jnp.einsum('rgij,rigd->rjgd', attention.astype(jnp.float32), mixed_low.astype(jnp.float32))
    sigmoid_s = jax.nn.sigmoid(scores)
    grad_scores = (grad_attention * weights * sigmoid_s * (1.0 + scores * (1.0 - sigmoid_s)) * scaling).astype(jnp.bfloat16)
    grad_query = jnp.einsum('rgij,rjgd->rigd', grad_scores.astype(jnp.float32), key_rows.astype(jnp.float32))
    grad_key = jnp.einsum('rgij,rigd->rjgd', grad_scores.astype(jnp.float32), query_rows.astype(jnp.float32))
    grad_active = jnp.stack([grad_gate, grad_value, grad_query, grad_key], axis=3)
    sigmoid_u = jax.nn.sigmoid(pre_act)
    return (grad_active * sigmoid_u * (1.0 + pre_act * (1.0 - sigmoid_u))).astype(jnp.bfloat16)

def section_forward(inputs, in_matrix, out_matrix, keeping, inverse_count):
    replicas, length, width = inputs.shape
    floats = inputs.astype(jnp.float32)
    normed_low = (floats * norm_rows(floats)).astype(jnp.bfloat16).reshape(replicas * length, width)
    columns = in_matrix.shape[1] // N_CORES
    slab_rows = out_matrix.shape[0] // N_CORES
    groups = slab_rows // HEAD_DIM
    summed = floats
    for core_no in range(N_CORES):
        pre_act = jnp.dot(normed_low, in_matrix[:, core_no * columns:(core_no + 1) * columns], preferred_element_type=jnp.float32)
        gated, unused = heads_forward(pre_act.reshape(replicas, length, groups, 4, HEAD_DIM), keeping, inverse_count)
        partial_sum = jnp.dot(gated.reshape(replicas * length, slab_rows), out_matrix[core_no * slab_rows:(core_no + 1) * slab_rows], preferred_element_type=jnp.float32)
        summed = summed + lax.optimization_barrier(partial_sum.astype(jnp.bfloat16)).astype(jnp.float32).reshape(replicas, length, width)
    return summed.astype(jnp.bfloat16)

def section_backward(inputs, upstream, in_matrix, out_matrix, keeping, inverse_count):
    replicas, length, width = inputs.shape
    floats = inputs.astype(jnp.float32)
    root_inputs = norm_rows(floats)
    scaled = floats * root_inputs
    normed_low = scaled.astype(jnp.bfloat16).reshape(replicas * length, width)
    flat_up = upstream.reshape(replicas * length, width)
    columns = in_matrix.shape[1] // N_CORES
    slab_rows = out_matrix.shape[0] // N_CORES
    groups = slab_rows // HEAD_DIM
    summed = upstream.astype(jnp.float32)
    products = []
    for core_no in range(N_CORES):
        in_slab = in_matrix[:, core_no * columns:(core_no + 1) * columns]
        out_slab = out_matrix[core_no * slab_rows:(core_no + 1) * slab_rows]
        pre_act = jnp.dot(normed_low, in_slab, preferred_element_type=jnp.float32).reshape(replicas, length, groups, 4, HEAD_DIM)
        gated, saved = heads_forward(pre_act, keeping, inverse_count)
        grad_gated = jnp.dot(flat_up, out_slab.T, preferred_element_type=jnp.float32).astype(jnp.bfloat16).reshape(replicas, length, groups, HEAD_DIM)
        grad_pre = heads_backward(pre_act, saved, grad_gated).reshape(replicas * length, columns)
        grad_normed = jnp.dot(grad_pre, in_slab.T, preferred_element_type=jnp.float32).reshape(replicas, length, width)
        back_part = root_inputs * (grad_normed - scaled * lax.optimization_barrier(jnp.mean(grad_normed * scaled, axis=-1, keepdims=True)))
        summed = summed + lax.optimization_barrier(back_part.astype(jnp.bfloat16)).astype(jnp.float32)
        products.append(jnp.einsum('rsf,rsd->rfd', gated.reshape(replicas, length, slab_rows).astype(jnp.float32), upstream.astype(jnp.float32)))
    return (summed.astype(jnp.bfloat16), jnp.concatenate(products, axis=1))

def reference(arrivals, in_flight, cotangent, grad_flight, stashed, in_weight, out_weight, forward_blocks, backward_blocks, forward_marks, backward_marks):
    ticks = arrivals.shape[0]
    rows = arrivals.shape[1]
    width = arrivals.shape[2]
    sections = in_flight.shape[0]
    length = BLOCKS * BLOCK
    replicas = rows // length

    def split(values):
        return values.reshape(replicas, length, width)
    outputs = [[None] * ticks for index in range(sections)]
    for section_no in range(sections):
        for tick_no in range(ticks):
            if section_no == 0:
                inputs = arrivals[tick_no]
            elif tick_no == 0:
                inputs = in_flight[section_no]
            else:
                inputs = outputs[section_no - 1][tick_no - 1]
            history = tick_no - section_no + sections - 1
            keeping, inverse_count = block_keep(forward_blocks[:, history], forward_marks[:, history])
            outputs[section_no][tick_no] = section_forward(split(inputs), in_weight[section_no], out_weight[section_no], keeping, inverse_count).reshape(rows, width)
    backs = [[None] * ticks for index in range(sections)]
    grads_list = [None] * sections
    scaling = (ticks * rows) ** (-0.5)
    for section_no in reversed(range(sections)):
        running = jnp.zeros((replicas, out_weight.shape[1], width), jnp.float32)
        for tick_no in range(ticks):
            if section_no == sections - 1:
                upstream = cotangent[tick_no]
            elif tick_no == 0:
                upstream = grad_flight[section_no]
            else:
                upstream = backs[section_no + 1][tick_no - 1]
            history = tick_no + section_no
            keeping, inverse_count = block_keep(backward_blocks[:, history], backward_marks[:, history])
            grad_in, product = section_backward(split(stashed[section_no, tick_no]), split(upstream), in_weight[section_no], out_weight[section_no], keeping, inverse_count)
            backs[section_no][tick_no] = grad_in.reshape(rows, width)
            running = running + product
        rounded = lax.optimization_barrier(running.astype(jnp.bfloat16)).astype(jnp.float32)
        grads_list[section_no] = lax.optimization_barrier(jnp.sum(rounded, axis=0)) * scaling
    activations = jnp.stack([jnp.stack(outputs[index]) for index in range(sections)])
    input_grads = jnp.stack([jnp.stack(backs[index]) for index in range(sections)])
    return (activations, input_grads, jnp.stack(grads_list))
```

```python
import jax
import jax.numpy as jnp
from jax import lax
from jax.sharding import PartitionSpec as P

HEAD_DIM = 128
BLOCK = 24
BLOCKS = 4


EPSILON = 1e-06


def block_keep(live_blocks, block_marks):
    length = BLOCKS * BLOCK
    places = jnp.arange(length, dtype=jnp.int32)
    owners = places // BLOCK
    onehot = (owners[:, None] == jnp.arange(BLOCKS, dtype=jnp.int32)[None, :]).astype(jnp.float32)
    spread = jnp.einsum("ia,rab,jb->rij", onehot, block_marks.astype(jnp.float32), onehot)
    allowed = (owners[:, None] == owners[None, :])[None] | (spread > 0.5)
    causal = (places[:, None] >= places[None, :])[None]
    tokens_live = live_blocks * BLOCK
    living = places[None, :] < tokens_live[:, None]
    keeping = causal & allowed & living[:, :, None] & living[:, None, :]
    return (keeping.astype(jnp.float32), 1.0 / tokens_live.astype(jnp.float32))


def choose_history(tables, history):
    matches = jnp.arange(tables.shape[1], dtype=jnp.int32) == history
    chosen = jnp.sum(jnp.where(matches[None, :, None], tables, 0), axis=1)
    return block_keep(chosen[:, 0], chosen[:, 1:].reshape(-1, BLOCKS, BLOCKS))


def norm_rows(values_f):
    return lax.rsqrt(jnp.mean(values_f * values_f, axis=-1, keepdims=True) + EPSILON)


def heads_forward(pre_act, keeping, inverse_count):
    scaling = HEAD_DIM ** (-0.5)
    active = jax.nn.silu(pre_act)
    gate_rows = active[:, :, :, 0]
    value_rows = active[:, :, :, 1].astype(jnp.bfloat16)
    query_rows = active[:, :, :, 2].astype(jnp.bfloat16)
    key_rows = active[:, :, :, 3].astype(jnp.bfloat16)
    scores = (
        jnp.einsum("rigd,rjgd->rgij", query_rows, key_rows, preferred_element_type=jnp.float32)
        * scaling
    )
    weights = keeping[:, None] * inverse_count[:, None, None, None]
    attention = (jax.nn.silu(scores) * weights).astype(jnp.bfloat16)
    mixed = jnp.einsum("rgij,rjgd->rigd", attention, value_rows, preferred_element_type=jnp.float32)
    root_scale = lax.rsqrt(jnp.mean(mixed * mixed, axis=-1, keepdims=True) + EPSILON)
    normed = mixed * root_scale
    gated = (normed * gate_rows).astype(jnp.bfloat16)
    return (
        gated,
        (
            gate_rows,
            value_rows,
            query_rows,
            key_rows,
            scores,
            weights,
            attention,
            root_scale,
            normed,
        ),
    )


def heads_backward(pre_act, saved, upstream):
    gate_rows, value_rows, query_rows, key_rows, scores, weights, attention, root_scale, normed = (
        saved
    )
    scaling = HEAD_DIM ** (-0.5)
    grad_gated = upstream.astype(jnp.float32)
    grad_normed = grad_gated * gate_rows
    grad_gate = grad_gated * normed
    grad_mixed = root_scale * (
        grad_normed - normed * jnp.mean(grad_normed * normed, axis=-1, keepdims=True)
    )
    mixed_low = grad_mixed.astype(jnp.bfloat16)
    grad_attention = jnp.einsum(
        "rigd,rjgd->rgij", mixed_low, value_rows, preferred_element_type=jnp.float32
    )
    grad_value = jnp.einsum(
        "rgij,rigd->rjgd", attention, mixed_low, preferred_element_type=jnp.float32
    )
    sigmoid_s = jax.nn.sigmoid(scores)
    grad_scores = (
        grad_attention * weights * sigmoid_s * (1.0 + scores * (1.0 - sigmoid_s)) * scaling
    ).astype(jnp.bfloat16)
    grad_query = jnp.einsum(
        "rgij,rjgd->rigd", grad_scores, key_rows, preferred_element_type=jnp.float32
    )
    grad_key = jnp.einsum(
        "rgij,rigd->rjgd", grad_scores, query_rows, preferred_element_type=jnp.float32
    )
    grad_active = jnp.stack([grad_gate, grad_value, grad_query, grad_key], axis=3)
    sigmoid_u = jax.nn.sigmoid(pre_act)
    return (grad_active * sigmoid_u * (1.0 + pre_act * (1.0 - sigmoid_u))).astype(jnp.bfloat16)


def after(value, *earlier):
    return lax.optimization_barrier((value,) + earlier)[0]


def per_device(
    arrivals,
    in_flight,
    cotangent,
    grad_flight,
    stashed,
    in_weight,
    out_weight,
    forward_blocks,
    backward_blocks,
    forward_marks,
    backward_marks,
):
    section_no = lax.axis_index("section")
    sections = lax.axis_size("section")
    core_no = lax.axis_index("cores")
    cores = lax.axis_size("cores")
    dp_no = lax.axis_index("dp")
    dp_size = lax.axis_size("dp")
    ticks = arrivals.shape[0]
    length = arrivals.shape[1]
    width = arrivals.shape[2]
    share = length // cores
    row_start = core_no * share
    in_shard = in_weight[0]
    out_shard = out_weight[0]
    depth = in_shard.shape[0]
    slab_rows = out_shard.shape[0]
    groups = slab_rows // HEAD_DIM
    columns = in_shard.shape[1]

    hosts = [2 * k + 1 if 4 * k < dp_size - 2 else 2 * k for k in range(dp_size // 2)]
    is_host = jnp.any(dp_no == jnp.array(hosts, jnp.int32))

    def fetch(x, j):
        return lax.ppermute(x, "dp", [(h ^ j, h) for h in hosts])

    def give_back(x):
        return lax.ppermute(x, "dp", [(h, h ^ 1) for h in hosts])

    def swap_cores(x):
        return lax.ppermute(x, "cores", [(c, c ^ 1) for c in range(cores)])

    def along_sections(x, by):
        pairs = [(i, i + by) for i in range(sections) if 0 <= i + by < sections]
        return lax.ppermute(x, "section", pairs)

    first_section = section_no == 0
    last_section = section_no == sections - 1
    own = jnp.stack(
        [
            stashed[0, 0],
            stashed[0, 1],
            jnp.where(first_section, arrivals[0], in_flight[0]),
            jnp.where(last_section, cotangent[0], grad_flight[0]),
            jnp.where(first_section, arrivals[1], cotangent[1]),
        ]
    )
    tables = jnp.concatenate(
        [
            jnp.concatenate([b[..., None], m.reshape(m.shape[:2] + (-1,))], axis=-1)
            for b, m in ((forward_blocks, forward_marks), (backward_blocks, backward_marks))
        ],
        axis=0,
    )
    order = [j for j in range(dp_size - 1, 0, -1)]
    in_parts = {0: in_shard}
    out_parts = {0: out_shard}
    for j in order:
        in_parts[j] = fetch(in_shard, j)
    both = jnp.stack([own, fetch(own, 1)], axis=1)
    tables = jnp.stack([tables, fetch(tables, 1)], axis=1)
    out_late = after(out_shard, *[in_parts[j] for j in order])
    for j in order:
        out_parts[j] = fetch(out_late, j)

    def columns_of(x, j):
        return lax.dynamic_slice_in_dim(x, (dp_no ^ j) * depth, depth, axis=x.ndim - 1)

    def project(normed):
        total = 0.0
        for j in range(dp_size):
            total = total + jnp.dot(
                columns_of(normed, j), in_parts[j], preferred_element_type=jnp.float32
            )
        return total

    def by_columns(pieces):
        whole = jnp.zeros(pieces[0].shape[:-1] + (width,), pieces[0].dtype)
        for j in range(dp_size):
            whole = lax.dynamic_update_slice_in_dim(
                whole, pieces[j], (dp_no ^ j) * depth, axis=whole.ndim - 1
            )
        return whole

    def normed_of(x):
        floats = x.astype(jnp.float32)
        root = norm_rows(floats)
        scaled = floats * root
        return scaled.reshape(-1, width), root.reshape(-1, 1)

    def rows_of(x, core):
        return lax.dynamic_slice_in_dim(x, core * share, share, axis=1)

    def reduce_over_cores(part, residual):
        theirs = swap_cores(rows_of(part, 1 - core_no))
        mine = rows_of(part, core_no)
        total = (
            rows_of(residual, core_no).astype(jnp.float32)
            + mine.astype(jnp.float32)
            + theirs.astype(jnp.float32)
        )
        return total.astype(jnp.bfloat16)

    def gather_over_cores(mine):
        theirs = swap_cores(mine)
        low = jnp.where(core_no == 0, mine, theirs)
        high = jnp.where(core_no == 0, theirs, mine)
        return jnp.concatenate([low, high], axis=1)

    def forward(x, tick_no):
        keeping, count = choose_history(tables[0], tick_no - section_no + sections - 1)
        scaled, unused = normed_of(x)
        pre = project(scaled.astype(jnp.bfloat16)).reshape(2, length, groups, 4, HEAD_DIM)
        gated, unused = heads_forward(pre, keeping, count)
        gated = gated.reshape(2 * length, slab_rows)
        part = by_columns(
            [
                jnp.dot(gated, out_parts[j], preferred_element_type=jnp.float32).astype(
                    jnp.bfloat16
                )
                for j in range(dp_size)
            ]
        )
        return reduce_over_cores(part.reshape(2, length, width), x)

    def recompute(x, tick_no):
        keeping, count = choose_history(tables[1], tick_no + section_no)
        scaled, root = normed_of(x)
        pre = project(scaled.astype(jnp.bfloat16)).reshape(2, length, groups, 4, HEAD_DIM)
        gated, saved = heads_forward(pre, keeping, count)
        return gated.reshape(2 * length, slab_rows), (pre, saved, scaled, root)

    def backward(kept, upstream):
        pre, saved, scaled, root = kept
        flat = upstream.reshape(2 * length, width)
        total = 0.0
        for j in range(dp_size):
            total = total + lax.dot_general(
                columns_of(flat, j),
                out_parts[j],
                (((1,), (1,)), ((), ())),
                preferred_element_type=jnp.float32,
            )
        grad_gated = total.astype(jnp.bfloat16).reshape(2, length, groups, HEAD_DIM)
        grad_pre = heads_backward(pre, saved, grad_gated).reshape(2 * length, columns)
        grad_normed = by_columns(
            [
                lax.dot_general(
                    grad_pre,
                    in_parts[j],
                    (((1,), (1,)), ((), ())),
                    preferred_element_type=jnp.float32,
                )
                for j in range(dp_size)
            ]
        )
        part = root * (
            grad_normed - scaled * jnp.mean(grad_normed * scaled, axis=-1, keepdims=True)
        )
        return reduce_over_cores(part.astype(jnp.bfloat16).reshape(2, length, width), upstream)

    def term(gated, upstream):
        return lax.dot_general(
            gated,
            upstream.reshape(2 * length, width),
            (((0,), (0,)), ((), ())),
            preferred_element_type=jnp.float32,
        )

    gated_0, kept_0 = recompute(both[0], 0)
    gated_1, kept_1 = recompute(both[1], 1)
    ahead_0 = forward(both[2], 0)
    back_0 = backward(kept_0, both[3])
    ahead_in = along_sections(ahead_0, 1)
    back_in = along_sections(back_0, -1)
    x_1 = jnp.where(first_section, both[4], gather_over_cores(ahead_in))
    g_1 = jnp.where(last_section, both[4], gather_over_cores(back_in))
    ahead_1 = forward(x_1, 1)
    back_1 = backward(kept_1, g_1)
    product = (term(gated_0, both[3]) + term(gated_1, g_1)).astype(jnp.bfloat16)

    scaling = (ticks * length * dp_size) ** (-0.5)
    grads = 0.0
    for k in range(len(hosts)):
        mine = jnp.where(dp_no == hosts[k], columns_of(product, 0), 0)
        grads = grads + mine.astype(jnp.float32)
    for j in range(1, dp_size):
        landed = lax.ppermute(columns_of(product, j), "dp", [(h, h ^ j) for h in hosts])
        grads = grads + landed.astype(jnp.float32)
    grads = grads * scaling

    def placed(mine):
        landed = give_back(mine[1])
        return jnp.where(is_host, mine[0], landed)

    ahead = jnp.stack([placed(ahead_0), placed(ahead_1)])
    back = jnp.stack([placed(back_0), placed(back_1)])
    return (ahead[None], back[None], grads[None])


def solution(mesh):
    in_specs = (
        P(None, "dp", None),
        P("section", "dp", None),
        P(None, "dp", None),
        P("section", "dp", None),
        P("section", None, "dp", None),
        P("section", "dp", "cores"),
        P("section", "cores", "dp"),
        P("dp", None),
        P("dp", None),
        P("dp", None, None, None),
        P("dp", None, None, None),
    )
    out_specs = (
        P("section", None, ("dp", "cores"), None),
        P("section", None, ("dp", "cores"), None),
        P("section", "cores", "dp"),
    )
    return jax.shard_map(
        per_device, mesh=mesh, in_specs=in_specs, out_specs=out_specs, check_vma=False
    )
```

```python
import functools

import jax
import jax.numpy as jnp
from jax import lax
from jax.experimental import pallas as pl
from jax.experimental.pallas import tpu as pltpu
from jax.sharding import PartitionSpec as P

HEAD_DIM = 128
BLOCK = 24
BLOCKS = 4
EPSILON = 1e-06
SCALING = HEAD_DIM ** (-0.5)
VMEM_BYTES = 50 * 1024 * 1024

F32 = jnp.float32
BF16 = jnp.bfloat16


def dot(a, b):
    return lax.dot_general(a, b, (((1,), (0,)), ((), ())), preferred_element_type=F32)


def dot_nt(a, b):
    return lax.dot_general(a, b, (((1,), (1,)), ((), ())), preferred_element_type=F32)


def dot_tn(a, b):
    return lax.dot_general(a, b, (((0,), (0,)), ((), ())), preferred_element_type=F32)


def row_root(floats):
    return lax.rsqrt(jnp.mean(floats * floats, axis=-1, keepdims=True) + EPSILON)


def sigmoid(x):
    return 1.0 / (1.0 + jnp.exp(-x))


def attend(pre, keep):
    sig = sigmoid(pre)
    active = pre * sig
    gate = active[:, :HEAD_DIM]
    vqk = active[:, HEAD_DIM:].astype(BF16)
    value = vqk[:, :HEAD_DIM]
    query = vqk[:, HEAD_DIM : 2 * HEAD_DIM]
    key = vqk[:, 2 * HEAD_DIM :]
    scores = dot_nt(query, key) * SCALING
    sig_s = sigmoid(scores)
    probs = (scores * sig_s * keep).astype(BF16)
    mixed = dot(probs, value)
    gated = (mixed * row_root(mixed) * gate).astype(BF16)
    return sig, gate, vqk, scores, sig_s, probs, mixed, gated


def project_kernel(n, places, offs, own, theirs, keep, *rest):
    weights = rest[:n]
    gated_out, gate_out, vqk_out, slope_out, mixed_out, probs_out, factor_out, normed = rest[n:]
    depth = weights[0].shape[0]
    length = own.shape[1]
    rows = 2 * length

    @pl.when(pl.program_id(0) == 0)
    def _():
        for i, place in enumerate(places):
            for r, source in enumerate((own, theirs)):
                floats = source[place].astype(F32)
                normed[pl.ds((2 * i + r) * length, length), :] = (
                    floats * row_root(floats)
                ).astype(BF16)

    pre_all = None
    for j in range(n):
        columns = pl.ds(pl.multiple_of(offs[j], depth), depth)
        term = dot(normed[:, columns], weights[j][...])
        pre_all = term if pre_all is None else pre_all + term
    for i in range(len(places)):
        pre = pre_all[i * rows : (i + 1) * rows]
        kept = keep[i]
        sig, gate, vqk, scores, sig_s, probs, mixed, gated = attend(pre, kept)
        gated_out[i] = gated
        if i > 0:
            gate_out[i - 1] = gate
            vqk_out[i - 1] = vqk
            slope_out[i - 1] = sig * (1.0 + pre * (1.0 - sig))
            mixed_out[i - 1] = mixed
            probs_out[i - 1, 0] = probs
            factor_out[i - 1, 0] = kept * sig_s * (1.0 + scores * (1.0 - sig_s)) * SCALING


def split_rows(core, part, send, keep):
    share = send.shape[1]
    cores = part.shape[0] // (2 * share)
    for r in range(2):
        base = r * cores * share
        mine = pl.multiple_of(base + core * share, share)
        other = pl.multiple_of(base + (cores - 1 - core) * share, share)
        send[r] = part[pl.ds(other, share), :]
        keep[r] = part[pl.ds(mine, share), :]


def out_kernel(n, core, offs, gated, *rest):
    weights = rest[:n]
    send, keep, part = rest[n:]
    depth = weights[0].shape[1]
    for j in range(n):
        columns = pl.ds(pl.multiple_of(offs[j], depth), depth)
        part[:, columns] = dot(gated[0], weights[j][...]).astype(BF16)
    split_rows(core[0], part, send, keep)


def assemble(core, fresh, mine, theirs, new_own, new_theirs, whole):
    share = mine.shape[1]
    length = new_own.shape[1]
    cores = length // share
    use_fresh = fresh != 0
    for r, source in enumerate((new_own, new_theirs)):
        for owner, landed in ((core, mine), (cores - 1 - core, theirs)):
            inside = pl.multiple_of(owner * share, share)
            rows = source[0, pl.ds(inside, share), :]
            at = pl.multiple_of(r * length + owner * share, share)
            whole[pl.ds(at, share), :] = jnp.where(use_fresh, rows, landed[r])


def forward_kernel(n, heads, core, offs, fresh, mine, theirs, new_own, new_theirs, keep, *rest):
    in_parts = rest[:n]
    out_parts = rest[n : 2 * n]
    send, kept, whole, normed, gated, part = rest[2 * n :]
    depth = in_parts[0].shape[0]
    head = pl.program_id(0)

    @pl.when(head == 0)
    def _():
        assemble(core[0], fresh[0], mine, theirs, new_own, new_theirs, whole)
        floats = whole[...].astype(F32)
        normed[...] = (floats * row_root(floats)).astype(BF16)

    pre = None
    for j in range(n):
        columns = pl.ds(pl.multiple_of(offs[j], depth), depth)
        term = dot(normed[:, columns], in_parts[j][...])
        pre = term if pre is None else pre + term
    gated[head] = attend(pre, keep[0])[-1]

    @pl.when(head == heads - 1)
    def _():
        for j in range(n):
            columns = pl.ds(pl.multiple_of(offs[j], depth), depth)
            total = None
            for h in range(heads):
                term = dot(gated[h], out_parts[j][pl.ds(h * HEAD_DIM, HEAD_DIM), :])
                total = term if total is None else total + term
            part[:, columns] = total.astype(BF16)
        split_rows(core[0], part, send, kept)


def backward_kernel(
    n, heads, core, offs, up_own, up_theirs, x_own, x_theirs, gate, vqk, slope, mixed, probs, factor, *rest
):
    out_parts = rest[:n]
    in_hbm = rest[n : 2 * n]
    send, keep, upstream, in_parts, grad_normed, part, sems = rest[2 * n :]
    depth = out_parts[0].shape[1]
    length = up_own.shape[1]
    wide = 4 * HEAD_DIM
    copies = [
        pltpu.make_async_copy(in_hbm[j], in_parts.at[j], sems.at[j]) for j in range(n)
    ]
    for copy in copies:
        copy.start()
    for r, source in enumerate((up_own, up_theirs)):
        upstream[pl.ds(r * length, length), :] = source[0]
    grad_gated = None
    for j in range(n):
        columns = pl.ds(pl.multiple_of(offs[j], depth), depth)
        term = dot_nt(upstream[:, columns], out_parts[j][...])
        grad_gated = term if grad_gated is None else grad_gated + term
    grad_gated = grad_gated.astype(BF16).astype(F32)
    grads_pre = []
    for h in range(heads):
        cut = slice(h * HEAD_DIM, (h + 1) * HEAD_DIM)
        up = grad_gated[:, cut]
        mixed_h = mixed[0, :, cut]
        root = row_root(mixed_h)
        normed = mixed_h * root
        grad_n = up * gate[0, :, cut]
        grad_gate = up * normed
        grad_mixed = root * (grad_n - normed * jnp.mean(grad_n * normed, axis=-1, keepdims=True))
        low = grad_mixed.astype(BF16)
        base = 3 * h * HEAD_DIM
        value = vqk[0, :, base : base + HEAD_DIM]
        query = vqk[0, :, base + HEAD_DIM : base + 2 * HEAD_DIM]
        key = vqk[0, :, base + 2 * HEAD_DIM : base + 3 * HEAD_DIM]
        grad_scores = (dot_nt(low, value) * factor[0, h]).astype(BF16)
        grad_value = dot_tn(probs[0, h], low)
        grad_query = dot(grad_scores, key)
        grad_key = dot_tn(grad_scores, query)
        grad_active = jnp.concatenate([grad_gate, grad_value, grad_query, grad_key], axis=1)
        grads_pre.append((grad_active * slope[0, :, h * wide : (h + 1) * wide]).astype(BF16))
    grad_pre = jnp.concatenate(grads_pre, axis=1)
    for j in range(n):
        columns = pl.ds(pl.multiple_of(offs[j], depth), depth)
        copies[j].wait()
        grad_normed[:, columns] = dot_nt(grad_pre, in_parts[j])
    for r, source in enumerate((x_own, x_theirs)):
        rows = pl.ds(r * length, length)
        floats = source[0].astype(F32)
        root = row_root(floats)
        scaled = floats * root
        grad_n = grad_normed[rows, :]
        part[rows, :] = (
            root * (grad_n - scaled * jnp.mean(grad_n * scaled, axis=-1, keepdims=True))
        ).astype(BF16)
    split_rows(core[0], part, send, keep)


def term_kernel(
    n, core, offs, fresh, mine, theirs, new_own, new_theirs, up_own, up_theirs, gated, *rest
):
    pieces = rest[:n]
    whole, upstream = rest[n:]
    depth = pieces[0].shape[1]
    length = up_own.shape[1]
    assemble(core[0], fresh[0], mine, theirs, new_own, new_theirs, whole)
    for r, source in enumerate((up_own, up_theirs)):
        upstream[pl.ds(r * length, length), :] = source[0]
    for j in range(n):
        columns = pl.ds(pl.multiple_of(offs[j], depth), depth)
        pieces[j][...] = (
            dot_tn(gated[1], upstream[:, columns]) + dot_tn(gated[2], whole[:, columns])
        ).astype(BF16)


def after(value, *earlier):
    return lax.optimization_barrier((value,) + earlier)[0]


def block_keep(live_blocks, block_marks):
    length = BLOCKS * BLOCK
    places = jnp.arange(length, dtype=jnp.int32)
    owners = places // BLOCK
    marked = jnp.repeat(jnp.repeat(block_marks, BLOCK, axis=-2), BLOCK, axis=-1) == 1
    allowed = (owners[:, None] == owners[None, :]) | marked
    causal = places[:, None] >= places[None, :]
    tokens = live_blocks[..., None, None] * BLOCK
    keeping = causal & allowed & (places[:, None] < tokens) & (places[None, :] < tokens)
    return jnp.where(keeping, 1.0 / jnp.maximum(tokens, 1).astype(F32), 0.0)


def per_device(
    arrivals,
    in_flight,
    cotangent,
    grad_flight,
    stashed,
    in_weight,
    out_weight,
    forward_blocks,
    backward_blocks,
    forward_marks,
    backward_marks,
):
    section_no = lax.axis_index("section")
    sections = lax.axis_size("section")
    core_no = lax.axis_index("cores")
    cores = lax.axis_size("cores")
    dp_no = lax.axis_index("dp")
    n = lax.axis_size("dp")
    ticks = arrivals.shape[0]
    length = arrivals.shape[1]
    width = arrivals.shape[2]
    rows = 2 * length
    share = length // cores
    in_shard = in_weight[0]
    out_shard = out_weight[0]
    depth = in_shard.shape[0]
    slab = out_shard.shape[0]
    heads = slab // HEAD_DIM
    wide = 4 * HEAD_DIM

    hosts = [2 * k + 1 if 4 * k < n - 2 else 2 * k for k in range(n // 2)]
    host_table = jnp.array(hosts, jnp.int32)
    is_host = dp_no == host_table[dp_no // 2]

    def from_partner(x):
        return lax.ppermute(x, "dp", [(h ^ 1, h) for h in hosts])

    def to_partner(x):
        return lax.ppermute(x, "dp", [(h, h ^ 1) for h in hosts])

    def from_host(x, m):
        return lax.ppermute(x, "dp", [(hosts[k ^ m], hosts[k]) for k in range(n // 2)])

    def swap_cores(x):
        return lax.ppermute(x, "cores", [(c, cores - 1 - c) for c in range(cores)])

    def along_sections(x, by):
        pairs = [(i, i + by) for i in range(sections) if 0 <= i + by < sections]
        return lax.ppermute(x, "section", pairs)

    first_section = section_no == 0
    last_section = section_no == sections - 1
    tables = jnp.concatenate(
        [
            jnp.concatenate([b[..., None], m.reshape(m.shape[:2] + (-1,))], axis=-1)
            for b, m in ((forward_blocks, forward_marks), (backward_blocks, backward_marks))
        ],
        axis=0,
    )
    own = jnp.stack(
        [
            jnp.where(first_section, arrivals[0], in_flight[0]),
            stashed[0, 0],
            stashed[0, 1],
            jnp.where(last_section, cotangent[0], grad_flight[0]),
            jnp.where(first_section, arrivals[1], cotangent[1]),
        ]
    )
    in_near = from_partner(in_shard)
    in_parts = [in_shard, in_near]
    in_parts += [from_host(in_shard, m) for m in range(1, n // 2)]
    near_tables = from_partner(tables)
    theirs = from_partner(after(own, near_tables))
    in_parts += [from_host(in_near, m) for m in range(1, n // 2)]
    out_own = after(out_shard, *in_parts[1 : 1 + n // 2])
    out_far = [from_host(out_own, m) for m in range(1, n // 2)]
    out_near = from_partner(after(out_shard, theirs))
    out_parts = [out_shard, out_near] + out_far
    out_parts += [from_host(out_near, m) for m in range(1, n // 2)]
    owners = [dp_no, dp_no ^ 1]
    owners += [host_table[(dp_no // 2) ^ m] for m in range(1, n // 2)]
    owners += [host_table[(dp_no // 2) ^ m] ^ 1 for m in range(1, n // 2)]
    offs = jnp.stack(owners).astype(jnp.int32) * depth
    core = jnp.reshape(core_no, (1,)).astype(jnp.int32)
    first_flag = jnp.reshape(first_section, (1,)).astype(jnp.int32)
    last_flag = jnp.reshape(last_section, (1,)).astype(jnp.int32)

    both_tables = jnp.stack([tables, near_tables], axis=1)
    ahead_at = sections - 1 - section_no
    chosen = jnp.stack(
        [
            lax.dynamic_index_in_dim(both_tables[way], at, axis=1, keepdims=False)
            for way, at in (
                (0, ahead_at),
                (1, section_no),
                (1, section_no + 1),
                (0, ahead_at + 1),
            )
        ]
    )
    kept = block_keep(chosen[..., 0], chosen[..., 1:].reshape(-1, 2, BLOCKS, BLOCKS))
    blank = jnp.zeros_like(kept[:, 0])
    keep = jnp.concatenate(
        [
            jnp.concatenate([kept[:, 0], blank], axis=2),
            jnp.concatenate([blank, kept[:, 1]], axis=2),
        ],
        axis=1,
    )

    smem = pl.BlockSpec(memory_space=pltpu.SMEM)
    params = pltpu.CompilerParams(vmem_limit_bytes=VMEM_BYTES)
    whole_of = lambda x: pl.BlockSpec(x.shape, lambda *_: (0,) * x.ndim)

    def row_of(x, i):
        return pl.BlockSpec((1,) + x.shape[1:], lambda *_: (i,) + (0,) * (x.ndim - 1))

    def struct(shape, dtype):
        return jax.ShapeDtypeStruct(shape, dtype)

    halves = [struct((2, share, width), BF16)] * 2
    half_specs = [pl.BlockSpec((2, share, width), lambda *_: (0, 0, 0))] * 2

    by_head = lambda lead, last: pl.BlockSpec(lead + (last,), lambda h: (0,) * len(lead) + (h,))
    square = pl.BlockSpec((2, 1, rows, rows), lambda h: (0, h, 0, 0))
    gated, gate, vqk, slope, mixed, probs, factor = pl.pallas_call(
        functools.partial(project_kernel, n, (0, 1, 2)),
        grid=(heads,),
        in_specs=[smem, whole_of(own), whole_of(theirs), pl.BlockSpec((3, rows, rows), lambda h: (0, 0, 0))]
        + [by_head((depth,), wide)] * n,
        out_specs=[
            by_head((3, rows), HEAD_DIM),
            by_head((2, rows), HEAD_DIM),
            by_head((2, rows), 3 * HEAD_DIM),
            by_head((2, rows), wide),
            by_head((2, rows), HEAD_DIM),
            square,
            square,
        ],
        out_shape=[
            struct((3, rows, slab), BF16),
            struct((2, rows, slab), F32),
            struct((2, rows, 3 * slab), BF16),
            struct((2, rows, 4 * slab), F32),
            struct((2, rows, slab), F32),
            struct((2, heads, rows, rows), BF16),
            struct((2, heads, rows, rows), F32),
        ],
        scratch_shapes=[pltpu.VMEM((3 * rows, width), BF16)],
        compiler_params=params,
        name="project",
    )(offs, own, theirs, keep, *in_parts)

    def backward(up_own, up_theirs, up_at, tick_no):
        saved = [gate, vqk, slope, mixed, probs, factor]
        return pl.pallas_call(
            functools.partial(backward_kernel, n, heads),
            grid=(1,),
            in_specs=[smem, smem, row_of(up_own, up_at[0]), row_of(up_theirs, up_at[1])]
            + [row_of(own, 1 + tick_no), row_of(theirs, 1 + tick_no)]
            + [row_of(x, tick_no) for x in saved]
            + [whole_of(out_shard)] * n
            + [pl.BlockSpec(memory_space=pl.ANY)] * n,
            out_specs=half_specs,
            out_shape=halves,
            scratch_shapes=[
                pltpu.VMEM((rows, width), BF16),
                pltpu.VMEM((n,) + in_shard.shape, BF16),
                pltpu.VMEM((rows, width), F32),
                pltpu.VMEM((rows, width), BF16),
                pltpu.SemaphoreType.DMA((n,)),
            ],
            compiler_params=params,
            name="backward",
        )(core, offs, up_own, up_theirs, own, theirs, *saved, *out_parts, *in_parts)

    def finish(residual, halves_of):
        send, mine = halves_of
        landed = swap_cores(send)
        return (residual.astype(F32) + mine.astype(F32) + landed.astype(F32)).astype(BF16)

    def own_rows(at):
        both = jnp.stack([own[at], theirs[at]])
        return lax.dynamic_slice_in_dim(both, core_no * share, share, axis=1)

    ahead_parts = pl.pallas_call(
        functools.partial(out_kernel, n),
        grid=(1,),
        in_specs=[smem, smem, row_of(gated, 0)] + [whole_of(out_shard)] * n,
        out_specs=half_specs,
        out_shape=halves,
        scratch_shapes=[pltpu.VMEM((rows, width), BF16)],
        compiler_params=params,
        name="out",
    )(core, offs, gated, *out_parts)
    ahead_0 = finish(own_rows(0), ahead_parts)
    ahead_in = along_sections(ahead_0, 1)
    back_0 = finish(own_rows(3), backward(own, theirs, (3, 3), 0))
    back_in = along_sections(back_0, -1)

    ahead_their = swap_cores(ahead_in)
    ahead_parts = pl.pallas_call(
        functools.partial(forward_kernel, n, heads),
        grid=(heads,),
        in_specs=[smem, smem, smem, whole_of(ahead_in), whole_of(ahead_their)]
        + [row_of(own, 4), row_of(theirs, 4), row_of(keep, 3)]
        + [by_head((depth,), wide)] * n
        + [whole_of(out_shard)] * n,
        out_specs=half_specs,
        out_shape=halves,
        scratch_shapes=[
            pltpu.VMEM((rows, width), BF16),
            pltpu.VMEM((rows, width), BF16),
            pltpu.VMEM((heads, rows, HEAD_DIM), BF16),
            pltpu.VMEM((rows, width), BF16),
        ],
        compiler_params=params,
        name="forward",
    )(core, offs, first_flag, ahead_in, ahead_their, own, theirs, keep, *in_parts, *out_parts)
    ahead_1 = finish(jnp.where(first_section, own_rows(4), ahead_in), ahead_parts)

    back_their = swap_cores(back_in)
    *pieces, up_1 = pl.pallas_call(
        functools.partial(term_kernel, n),
        grid=(1,),
        in_specs=[smem, smem, smem, whole_of(back_in), whole_of(back_their)]
        + [row_of(own, 4), row_of(theirs, 4), row_of(own, 3), row_of(theirs, 3), whole_of(gated)],
        out_specs=[pl.BlockSpec((slab, depth), lambda *_: (0, 0))] * n
        + [pl.BlockSpec((rows, width), lambda *_: (0, 0))],
        out_shape=[struct((slab, depth), BF16)] * n + [struct((rows, width), BF16)],
        scratch_shapes=[pltpu.VMEM((rows, width), BF16)],
        compiler_params=params,
        name="terms",
    )(core, offs, last_flag, back_in, back_their, own, theirs, own, theirs, gated)
    up_1 = up_1.reshape(2, length, width)
    back_1 = finish(
        jnp.where(last_section, own_rows(4), back_in), backward(up_1, up_1, (0, 1), 1)
    )

    scaling = (ticks * length * n) ** (-0.5)
    grads = jnp.where(is_host, pieces[0], 0).astype(F32)
    grads = grads + to_partner(pieces[1]).astype(F32)
    for m in range(1, n // 2):
        grads = grads + from_host(pieces[1 + m], m).astype(F32)
        beyond = pieces[n // 2 + m]
        landed = lax.ppermute(
            beyond, "dp", [(hosts[k ^ m], hosts[k] ^ 1) for k in range(n // 2)]
        )
        grads = grads + landed.astype(F32)
    grads = grads * scaling

    def placed(mine):
        return jnp.where(is_host, mine[0], to_partner(mine[1]))

    ahead = jnp.stack([placed(ahead_0), placed(ahead_1)])
    back = jnp.stack([placed(back_0), placed(back_1)])
    return (ahead[None], back[None], grads[None])


def solution(mesh):
    in_specs = (
        P(None, "dp", None),
        P("section", "dp", None),
        P(None, "dp", None),
        P("section", "dp", None),
        P("section", None, "dp", None),
        P("section", "dp", "cores"),
        P("section", "cores", "dp"),
        P("dp", None),
        P("dp", None),
        P("dp", None, None, None),
        P("dp", None, None, None),
    )
    out_specs = (
        P("section", None, ("dp", "cores"), None),
        P("section", None, ("dp", "cores"), None),
        P("section", "cores", "dp"),
    )
    return jax.shard_map(
        per_device, mesh=mesh, in_specs=in_specs, out_specs=out_specs, check_vma=False
    )
```

```python
import functools

import jax
import jax.numpy as jnp
from jax import lax
from jax.experimental import pallas as pl
from jax.experimental.pallas import tpu as pltpu
from jax.sharding import PartitionSpec as P

HEAD_DIM = 128
BLOCK = 24
BLOCKS = 4
EPSILON = 1e-06
SCALING = HEAD_DIM ** (-0.5)
VMEM_BYTES = 24 * 1024 * 1024

F32 = jnp.float32
BF16 = jnp.bfloat16


def dot(a, b):
    return lax.dot_general(a, b, (((1,), (0,)), ((), ())), preferred_element_type=F32)


def dot_nt(a, b):
    return lax.dot_general(a, b, (((1,), (1,)), ((), ())), preferred_element_type=F32)


def dot_tn(a, b):
    return lax.dot_general(a, b, (((0,), (0,)), ((), ())), preferred_element_type=F32)


def row_root(floats):
    return lax.rsqrt(jnp.mean(floats * floats, axis=-1, keepdims=True) + EPSILON)


def sigmoid(x):
    return 1.0 / (1.0 + jnp.exp(-x))


def attend(pre, keep):
    sig = sigmoid(pre)
    active = pre * sig
    gate = active[:, :HEAD_DIM]
    vqk = active[:, HEAD_DIM:].astype(BF16)
    value = vqk[:, :HEAD_DIM]
    query = vqk[:, HEAD_DIM : 2 * HEAD_DIM]
    key = vqk[:, 2 * HEAD_DIM :]
    scores = dot_nt(query, key) * SCALING
    sig_s = sigmoid(scores)
    probs = (scores * sig_s * keep).astype(BF16)
    mixed = dot(probs, value)
    gated = (mixed * row_root(mixed) * gate).astype(BF16)
    return sig, gate, vqk, scores, sig_s, probs, mixed, gated


def project_kernel(n, heads, offs, x_own, x_theirs, stash_own, stash_theirs, keep, *rest):
    weights = rest[:n]
    gated_out, gate_out, vqk_out, slope_out, mixed_out, probs_out, factor_out, normed = rest[n:]
    depth = weights[0].shape[0]
    length = x_own.shape[0]
    rows = 2 * length
    wide = 4 * HEAD_DIM
    head = pl.program_id(0)

    @pl.when(head == 0)
    def _():
        sources = [x_own, x_theirs]
        for t in range(stash_own.shape[0]):
            sources += [stash_own.at[t], stash_theirs.at[t]]
        for i, source in enumerate(sources):
            floats = source[...].astype(F32)
            normed[pl.ds(i * length, length), :] = (floats * row_root(floats)).astype(BF16)

    here = pl.ds(pl.multiple_of(head * wide, wide), wide)
    pre_all = None
    for j in range(n):
        columns = pl.ds(pl.multiple_of(offs[j], depth), depth)
        term = dot(normed[:, columns], weights[j][:, here])
        pre_all = term if pre_all is None else pre_all + term
    for i in range(1 + stash_own.shape[0]):
        pre = pre_all[i * rows : (i + 1) * rows]
        kept = keep[i]
        sig, gate, vqk, scores, sig_s, probs, mixed, gated = attend(pre, kept)
        gated_out[i] = gated
        if i > 0:
            gate_out[i - 1] = gate
            vqk_out[i - 1] = vqk
            slope_out[i - 1] = sig * (1.0 + pre * (1.0 - sig))
            mixed_out[i - 1] = mixed
            probs_out[i - 1, 0] = probs
            factor_out[i - 1, 0] = kept * sig_s * (1.0 + scores * (1.0 - sig_s)) * SCALING


def split_rows(core, part, send, keep):
    share = send.shape[1]
    cores = part.shape[0] // (2 * share)
    for r in range(2):
        base = r * cores * share
        mine = pl.multiple_of(base + core * share, share)
        other = pl.multiple_of(base + (cores - 1 - core) * share, share)
        send[r] = part[pl.ds(other, share), :]
        keep[r] = part[pl.ds(mine, share), :]


def out_kernel(n, core, offs, gated, *rest):
    weights = rest[:n]
    send, keep, part = rest[n:]
    depth = weights[0].shape[1]
    for j in range(n):
        columns = pl.ds(pl.multiple_of(offs[j], depth), depth)
        part[:, columns] = dot(gated[0], weights[j][...]).astype(BF16)
    split_rows(core[0], part, send, keep)


def assemble(core, fresh, mine, theirs, new_own, new_theirs, whole):
    share = mine.shape[1]
    length = new_own.shape[0]
    cores = length // share
    use_fresh = fresh != 0
    for r, source in enumerate((new_own, new_theirs)):
        for owner, landed in ((core, mine), (cores - 1 - core, theirs)):
            inside = pl.multiple_of(owner * share, share)
            rows = source[pl.ds(inside, share), :]
            at = pl.multiple_of(r * length + owner * share, share)
            whole[pl.ds(at, share), :] = jnp.where(use_fresh, rows, landed[r])


def forward_kernel(n, heads, core, offs, fresh, mine, theirs, new_own, new_theirs, keep, *rest):
    in_parts = rest[:n]
    out_parts = rest[n : 2 * n]
    send, kept, whole, normed, gated, part = rest[2 * n :]
    depth = in_parts[0].shape[0]
    head = pl.program_id(0)

    @pl.when(head == 0)
    def _():
        assemble(core[0], fresh[0], mine, theirs, new_own, new_theirs, whole)
        floats = whole[...].astype(F32)
        normed[...] = (floats * row_root(floats)).astype(BF16)

    wide = 4 * HEAD_DIM
    here = pl.ds(pl.multiple_of(head * wide, wide), wide)
    pre = None
    for j in range(n):
        columns = pl.ds(pl.multiple_of(offs[j], depth), depth)
        term = dot(normed[:, columns], in_parts[j][:, here])
        pre = term if pre is None else pre + term
    gated[head] = attend(pre, keep[keep.shape[0] - 1])[-1]

    @pl.when(head == heads - 1)
    def _():
        for j in range(n):
            columns = pl.ds(pl.multiple_of(offs[j], depth), depth)
            total = None
            for h in range(heads):
                term = dot(gated[h], out_parts[j][pl.ds(h * HEAD_DIM, HEAD_DIM), :])
                total = term if total is None else total + term
            part[:, columns] = total.astype(BF16)
        split_rows(core[0], part, send, kept)


def backward_kernel(
    n, heads, tick, core, offs, ups, x_own, x_theirs, gate, vqk, slope, mixed, probs, factor, *rest
):
    out_parts = rest[:n]
    in_parts = rest[n : 2 * n]
    send, keep, grad_normed, part = rest[2 * n :]
    depth = out_parts[0].shape[1]
    length = x_own.shape[1]
    wide = 4 * HEAD_DIM
    grad_gated = None
    for j in range(n):
        columns = pl.ds(pl.multiple_of(offs[j], depth), depth)
        term = dot_nt(ups[:, columns], out_parts[j][...])
        grad_gated = term if grad_gated is None else grad_gated + term
    grad_gated = grad_gated.astype(BF16).astype(F32)
    grads_pre = []
    for h in range(heads):
        cut = slice(h * HEAD_DIM, (h + 1) * HEAD_DIM)
        up = grad_gated[:, cut]
        mixed_h = mixed[tick, :, cut]
        root = row_root(mixed_h)
        normed = mixed_h * root
        grad_n = up * gate[tick, :, cut]
        grad_gate = up * normed
        grad_mixed = root * (grad_n - normed * jnp.mean(grad_n * normed, axis=-1, keepdims=True))
        low = grad_mixed.astype(BF16)
        base = 3 * h * HEAD_DIM
        value = vqk[tick, :, base : base + HEAD_DIM]
        query = vqk[tick, :, base + HEAD_DIM : base + 2 * HEAD_DIM]
        key = vqk[tick, :, base + 2 * HEAD_DIM : base + 3 * HEAD_DIM]
        grad_scores = (dot_nt(low, value) * factor[tick, h]).astype(BF16)
        grad_value = dot_tn(probs[tick, h], low)
        grad_query = dot(grad_scores, key)
        grad_key = dot_tn(grad_scores, query)
        grad_active = jnp.concatenate([grad_gate, grad_value, grad_query, grad_key], axis=1)
        grads_pre.append((grad_active * slope[tick, :, h * wide : (h + 1) * wide]).astype(BF16))
    grad_pre = jnp.concatenate(grads_pre, axis=1)
    for j in range(n):
        columns = pl.ds(pl.multiple_of(offs[j], depth), depth)
        grad_normed[:, columns] = dot_nt(grad_pre, in_parts[j][...])
    for r, source in enumerate((x_own, x_theirs)):
        rows = pl.ds(r * length, length)
        floats = source[tick].astype(F32)
        root = row_root(floats)
        scaled = floats * root
        grad_n = grad_normed[rows, :]
        part[rows, :] = (
            root * (grad_n - scaled * jnp.mean(grad_n * scaled, axis=-1, keepdims=True))
        ).astype(BF16)
    split_rows(core[0], part, send, keep)


def pack_kernel(n, offs, gated, up_own, up_theirs, whole, *packs):
    depth = packs[0].shape[1] - 2 * gated.shape[2]
    slab = gated.shape[2]
    length = up_own.shape[0]
    whole[:length, :] = up_own[...]
    whole[length:, :] = up_theirs[...]
    for j in range(1, n):
        pack = packs[j - 1]
        columns = pl.ds(pl.multiple_of(offs[j], depth), depth)
        pack[:, :slab] = gated[1]
        pack[:, slab : 2 * slab] = gated[2]
        pack[:length, 2 * slab :] = up_own[:, columns]
        pack[length:, 2 * slab :] = up_theirs[:, columns]


def gather_kernel(n, core, offs, fresh, mine, theirs, new_own, new_theirs, whole, *pieces):
    assemble(core[0], fresh[0], mine, theirs, new_own, new_theirs, whole)
    depth = pieces[0].shape[1]
    for j in range(1, n):
        columns = pl.ds(pl.multiple_of(offs[j], depth), depth)
        pieces[j - 1][...] = whole[:, columns]


def grads_kernel(n, scaling, host, offs, gated, up_0, up_1, *rest):
    packs = rest[: n - 1]
    pieces = rest[n - 1 : 2 * n - 2]
    out = rest[2 * n - 2]
    slab = gated.shape[2]
    depth = out.shape[1]
    at_host = host[0] != 0
    columns = pl.ds(pl.multiple_of(offs[0], depth), depth)

    def product(first, second, third, fourth):
        return dot_tn(first, third) + dot_tn(second, fourth)

    total = product(
        jnp.where(at_host, gated[1], packs[0][:, :slab]),
        jnp.where(at_host, gated[2], packs[0][:, slab : 2 * slab]),
        jnp.where(at_host, up_0[:, columns], packs[0][:, 2 * slab :]),
        jnp.where(at_host, up_1[:, columns], pieces[0][...]),
    )
    for m in range(1, n // 2):
        near, beyond = m, n // 2 + m - 1
        pack = jnp.where(at_host, packs[near][...], packs[beyond][...])
        piece = jnp.where(at_host, pieces[near][...], pieces[beyond][...])
        total = total + product(
            pack[:, :slab], pack[:, slab : 2 * slab], pack[:, 2 * slab :], piece
        )
    out[...] = total * scaling


def after(value, *earlier):
    return lax.optimization_barrier((value,) + earlier)[0]


def block_keep(live_blocks, block_marks):
    length = BLOCKS * BLOCK
    places = jnp.arange(length, dtype=jnp.int32)
    owners = places // BLOCK
    marked = jnp.repeat(jnp.repeat(block_marks, BLOCK, axis=-2), BLOCK, axis=-1) == 1
    allowed = (owners[:, None] == owners[None, :]) | marked
    causal = places[:, None] >= places[None, :]
    tokens = live_blocks[..., None, None] * BLOCK
    keeping = causal & allowed & (places[:, None] < tokens) & (places[None, :] < tokens)
    return jnp.where(keeping, 1.0 / jnp.maximum(tokens, 1).astype(F32), 0.0)


def per_device(
    arrivals,
    in_flight,
    cotangent,
    grad_flight,
    stashed,
    in_weight,
    out_weight,
    forward_blocks,
    backward_blocks,
    forward_marks,
    backward_marks,
):
    section_no = lax.axis_index("section")
    sections = lax.axis_size("section")
    core_no = lax.axis_index("cores")
    cores = lax.axis_size("cores")
    dp_no = lax.axis_index("dp")
    n = lax.axis_size("dp")
    ticks = arrivals.shape[0]
    length = arrivals.shape[1]
    width = arrivals.shape[2]
    rows = 2 * length
    share = length // cores
    in_shard = in_weight[0]
    out_shard = out_weight[0]
    depth = in_shard.shape[0]
    slab = out_shard.shape[0]
    heads = slab // HEAD_DIM
    wide = 4 * HEAD_DIM

    hosts = [2 * k + 1 if 4 * k < n - 2 else 2 * k for k in range(n // 2)]
    host_table = jnp.array(hosts, jnp.int32)
    is_host = dp_no == host_table[dp_no // 2]

    def from_partner(x):
        return lax.ppermute(x, "dp", [(h ^ 1, h) for h in hosts])

    def to_partner(x):
        return lax.ppermute(x, "dp", [(h, h ^ 1) for h in hosts])

    def from_host(x, m):
        return lax.ppermute(x, "dp", [(hosts[k ^ m], hosts[k]) for k in range(n // 2)])

    def to_beyond(x, m):
        return lax.ppermute(
            x, "dp", [(hosts[k ^ m], hosts[k] ^ 1) for k in range(n // 2)]
        )

    def swap_cores(x):
        return lax.ppermute(x, "cores", [(c, cores - 1 - c) for c in range(cores)])

    def along_sections(x, by):
        pairs = [(i, i + by) for i in range(sections) if 0 <= i + by < sections]
        return lax.ppermute(x, "section", pairs)

    first_section = section_no == 0
    last_section = section_no == sections - 1
    between = range(1, n // 2)

    in_near = from_partner(in_shard)
    in_far = [from_host(in_shard, m) for m in between]
    in_near, in_far, rows_in, tables_in = lax.optimization_barrier(
        (
            in_near,
            in_far,
            (arrivals, in_flight, cotangent, grad_flight, stashed),
            (forward_blocks, forward_marks, backward_blocks, backward_marks),
        )
    )
    in_parts = [in_shard, in_near] + in_far + [from_host(in_near, m) for m in between]
    arrivals, in_flight, cotangent, grad_flight, stashed = rows_in
    tables = jnp.concatenate(
        [
            jnp.concatenate([b[..., None], m.reshape(m.shape[:2] + (-1,))], axis=-1)
            for b, m in (tables_in[:2], tables_in[2:])
        ],
        axis=0,
    )
    near_tables = from_partner(tables)
    stash_own = stashed[0]
    stash_theirs = from_partner(stash_own)
    x_own = jnp.where(first_section, arrivals[0], in_flight[0])
    x_theirs = from_partner(x_own)
    up_own = jnp.where(last_section, cotangent[0], grad_flight[0])
    new_own = jnp.where(first_section, arrivals[1], cotangent[1])
    out_late, up_late, new_late, stash_theirs, x_theirs = lax.optimization_barrier(
        (out_shard, up_own, new_own, stash_theirs, x_theirs)
    )
    out_near = from_partner(out_late)
    out_far = [from_host(out_late, m) for m in between]
    up_theirs = from_partner(up_late)
    new_theirs = from_partner(new_late)
    out_parts = [out_shard, out_near] + out_far + [from_host(out_near, m) for m in between]
    owners = [dp_no, dp_no ^ 1]
    owners += [host_table[(dp_no // 2) ^ m] for m in range(1, n // 2)]
    owners += [host_table[(dp_no // 2) ^ m] ^ 1 for m in range(1, n // 2)]
    offs = jnp.stack(owners).astype(jnp.int32) * depth
    core = jnp.reshape(core_no, (1,)).astype(jnp.int32)
    first_flag = jnp.reshape(first_section, (1,)).astype(jnp.int32)
    host_flag = jnp.reshape(is_host, (1,)).astype(jnp.int32)
    last_flag = jnp.reshape(last_section, (1,)).astype(jnp.int32)

    both_tables = jnp.stack([tables, near_tables], axis=1)
    ahead_at = sections - 1 - section_no
    chosen = jnp.stack(
        [
            lax.dynamic_index_in_dim(both_tables[way], at, axis=1, keepdims=False)
            for way, at in (
                (0, ahead_at),
                (1, section_no),
                (1, section_no + 1),
                (0, ahead_at + 1),
            )
        ]
    )
    kept = block_keep(chosen[..., 0], chosen[..., 1:].reshape(-1, 2, BLOCKS, BLOCKS))
    blank = jnp.zeros_like(kept[:, 0])
    keep = jnp.concatenate(
        [
            jnp.concatenate([kept[:, 0], blank], axis=2),
            jnp.concatenate([blank, kept[:, 1]], axis=2),
        ],
        axis=1,
    )

    smem = pl.BlockSpec(memory_space=pltpu.SMEM)
    vmem = pl.BlockSpec(memory_space=pltpu.VMEM)
    params = pltpu.CompilerParams(vmem_limit_bytes=VMEM_BYTES)

    def cost(multiply_adds, bytes_accessed):
        return pl.CostEstimate(
            flops=2 * multiply_adds, bytes_accessed=bytes_accessed, transcendentals=0
        )

    def struct(shape, dtype):
        return jax.ShapeDtypeStruct(shape, dtype)

    halves = [struct((2, share, width), BF16)] * 2
    matmul = rows * width * 4 * slab
    weight_bytes = 2 * width * 5 * slab

    by_head = lambda lead, last: pl.BlockSpec(lead + (last,), lambda h: (0,) * len(lead) + (h,))
    square = pl.BlockSpec((2, 1, rows, rows), lambda h: (0, h, 0, 0))
    gated, gate, vqk, slope, mixed, probs, factor = pl.pallas_call(
        functools.partial(project_kernel, n, heads),
        grid=(heads,),
        in_specs=[smem] + [vmem] * (5 + n),
        out_specs=[
            by_head((3, rows), HEAD_DIM),
            by_head((2, rows), HEAD_DIM),
            by_head((2, rows), 3 * HEAD_DIM),
            by_head((2, rows), wide),
            by_head((2, rows), HEAD_DIM),
            square,
            square,
        ],
        out_shape=[
            struct((3, rows, slab), BF16),
            struct((2, rows, slab), F32),
            struct((2, rows, 3 * slab), BF16),
            struct((2, rows, 4 * slab), F32),
            struct((2, rows, slab), F32),
            struct((2, heads, rows, rows), BF16),
            struct((2, heads, rows, rows), F32),
        ],
        scratch_shapes=[pltpu.VMEM((3 * rows, width), BF16)],
        compiler_params=params,
        cost_estimate=cost(3 * matmul, 2 * weight_bytes),
        name="project",
    )(offs, x_own, x_theirs, stash_own, stash_theirs, keep, *in_parts)

    def backward(ups, tick_no):
        saved = [gate, vqk, slope, mixed, probs, factor]
        return pl.pallas_call(
            functools.partial(backward_kernel, n, heads, tick_no),
            in_specs=[smem] * 2 + [vmem] * (3 + len(saved) + 2 * n),
            out_specs=[vmem] * 2,
            out_shape=halves,
            scratch_shapes=[
                pltpu.VMEM((rows, width), F32),
                pltpu.VMEM((rows, width), BF16),
            ],
            compiler_params=params,
            cost_estimate=cost(2 * matmul, 2 * weight_bytes),
            name="backward",
        )(core, offs, ups, stash_own, stash_theirs, *saved, *out_parts, *in_parts)

    gated, new_theirs = lax.optimization_barrier((gated, new_theirs))

    def summed(residual, mine, landed):
        return (residual.astype(F32) + mine.astype(F32) + landed.astype(F32)).astype(BF16)

    def own_rows(mine, others):
        return lax.dynamic_slice_in_dim(jnp.stack([mine, others]), core_no * share, share, axis=1)

    up_0, *packs = pl.pallas_call(
        functools.partial(pack_kernel, n),
        in_specs=[smem] + [vmem] * 3,
        out_specs=[vmem] * n,
        out_shape=[struct((rows, width), BF16)]
        + [struct((rows, 2 * slab + depth), BF16)] * (n - 1),
        compiler_params=params,
        name="pack",
    )(offs, gated, up_own, up_theirs)
    packs, out_parts = lax.optimization_barrier((packs, out_parts))

    ahead_send, ahead_keep = pl.pallas_call(
        functools.partial(out_kernel, n),
        in_specs=[smem] * 2 + [vmem] * (1 + n),
        out_specs=[vmem] * 2,
        out_shape=halves,
        scratch_shapes=[pltpu.VMEM((rows, width), BF16)],
        compiler_params=params,
        cost_estimate=cost(matmul // 4, weight_bytes // 4),
        name="out",
    )(core, offs, gated, *out_parts)
    ahead_0 = summed(own_rows(x_own, x_theirs), ahead_keep, swap_cores(ahead_send))
    ahead_in = along_sections(ahead_0, 1)
    packs_near = [to_partner(packs[0])] + [from_host(packs[m], m) for m in between]
    back_send, back_keep = backward(after(up_0, ahead_0), 0)
    back_send, back_keep, ahead_in, packs_near = lax.optimization_barrier(
        (back_send, back_keep, ahead_in, packs_near)
    )
    back_0 = summed(own_rows(up_own, up_theirs), back_keep, swap_cores(back_send))
    back_in = along_sections(back_0, -1)

    packs_beyond = [to_beyond(packs[n // 2 + m - 1], m) for m in between]
    ahead_their = swap_cores(ahead_in)
    ahead_send, ahead_keep = pl.pallas_call(
        functools.partial(forward_kernel, n, heads),
        grid=(heads,),
        in_specs=[smem] * 3 + [vmem] * (5 + 2 * n),
        out_specs=[vmem] * 2,
        out_shape=halves,
        scratch_shapes=[
            pltpu.VMEM((rows, width), BF16),
            pltpu.VMEM((rows, width), BF16),
            pltpu.VMEM((heads, rows, HEAD_DIM), BF16),
            pltpu.VMEM((rows, width), BF16),
        ],
        compiler_params=params,
        cost_estimate=cost(2 * matmul, 2 * weight_bytes),
        name="forward",
    )(
        core, offs, first_flag, ahead_in, ahead_their, new_own, new_theirs, keep, *in_parts, *out_parts
    )
    ahead_send, ahead_keep, back_in, packs_beyond = lax.optimization_barrier(
        (ahead_send, ahead_keep, back_in, packs_beyond)
    )
    new_rows = own_rows(new_own, new_theirs)
    ahead_1 = summed(
        jnp.where(first_section, new_rows, ahead_in), ahead_keep, swap_cores(ahead_send)
    )

    back_their = swap_cores(back_in)
    up_1, *pieces = pl.pallas_call(
        functools.partial(gather_kernel, n),
        in_specs=[smem] * 3 + [vmem] * 4,
        out_specs=[vmem] * n,
        out_shape=[struct((rows, width), BF16)] + [struct((rows, depth), BF16)] * (n - 1),
        compiler_params=params,
        name="gather",
    )(core, offs, last_flag, back_in, back_their, new_own, new_theirs)
    landed = [to_partner(pieces[0])] + [from_host(pieces[m], m) for m in between]
    landed += [to_beyond(pieces[n // 2 + m - 1], m) for m in between]
    back_send, back_keep = backward(up_1, 1)
    back_send, back_keep, landed = lax.optimization_barrier((back_send, back_keep, landed))
    back_1 = summed(
        jnp.where(last_section, new_rows, back_in), back_keep, swap_cores(back_send)
    )

    grads = pl.pallas_call(
        functools.partial(grads_kernel, n, (ticks * length * n) ** (-0.5)),
        in_specs=[smem] * 2 + [vmem] * (3 + 2 * (n - 1)),
        out_specs=vmem,
        out_shape=struct((slab, depth), F32),
        compiler_params=params,
        cost_estimate=cost(matmul // 4, weight_bytes // 4),
        name="grads",
    )(
        host_flag, offs, gated, up_0, up_1, *packs_near, *packs_beyond, *landed
    )

    first_pair = to_partner(jnp.stack([ahead_0[1], back_0[1]]))
    ahead = jnp.stack(
        [
            jnp.where(is_host, ahead_0[0], first_pair[0]),
            jnp.where(is_host, ahead_1[0], to_partner(ahead_1[1])),
        ]
    )
    back = jnp.stack(
        [
            jnp.where(is_host, back_0[0], first_pair[1]),
            jnp.where(is_host, back_1[0], to_partner(back_1[1])),
        ]
    )
    return (ahead[None], back[None], grads[None])


def solution(mesh):
    in_specs = (
        P(None, "dp", None),
        P("section", "dp", None),
        P(None, "dp", None),
        P("section", "dp", None),
        P("section", None, "dp", None),
        P("section", "dp", "cores"),
        P("section", "cores", "dp"),
        P("dp", None),
        P("dp", None),
        P("dp", None, None, None),
        P("dp", None, None, None),
    )
    out_specs = (
        P("section", None, ("dp", "cores"), None),
        P("section", None, ("dp", "cores"), None),
        P("section", "cores", "dp"),
    )
    return jax.shard_map(
        per_device, mesh=mesh, in_specs=in_specs, out_specs=out_specs, check_vma=False
    )
```

```python
import functools

import jax
import jax.numpy as jnp
from jax import lax
from jax.experimental import pallas as pl
from jax.experimental.pallas import tpu as pltpu
from jax.sharding import PartitionSpec as P

HEAD_DIM = 128
BLOCK = 24
BLOCKS = 4
EPSILON = 1e-06
SCALING = HEAD_DIM ** (-0.5)
VMEM_BYTES = 50 * 1024 * 1024

F32 = jnp.float32
BF16 = jnp.bfloat16


def dot(a, b):
    return lax.dot_general(a, b, (((1,), (0,)), ((), ())), preferred_element_type=F32)


def dot_nt(a, b):
    return lax.dot_general(a, b, (((1,), (1,)), ((), ())), preferred_element_type=F32)


def dot_tn(a, b):
    return lax.dot_general(a, b, (((0,), (0,)), ((), ())), preferred_element_type=F32)


def row_root(floats):
    return lax.rsqrt(jnp.mean(floats * floats, axis=-1, keepdims=True) + EPSILON)


def sigmoid(x):
    return 1.0 / (1.0 + jnp.exp(-x))


def attend(pre, keep):
    sig = sigmoid(pre)
    active = pre * sig
    gate = active[:, :HEAD_DIM]
    vqk = active[:, HEAD_DIM:].astype(BF16)
    value = vqk[:, :HEAD_DIM]
    query = vqk[:, HEAD_DIM : 2 * HEAD_DIM]
    key = vqk[:, 2 * HEAD_DIM :]
    scores = dot_nt(query, key) * SCALING
    sig_s = sigmoid(scores)
    probs = (scores * sig_s * keep).astype(BF16)
    mixed = dot(probs, value)
    gated = (mixed * row_root(mixed) * gate).astype(BF16)
    return sig, gate, vqk, scores, sig_s, probs, mixed, gated


def project(normed, offs, weights):
    total = None
    for j, weight in enumerate(weights):
        depth = weight.shape[0]
        columns = pl.ds(pl.multiple_of(offs[j], depth), depth)
        term = dot(normed[:, columns], weight[...])
        total = term if total is None else total + term
    return total


def project_kernel(parts, offs, x_own, x_theirs, stash_own, stash_theirs, keep, *rest):
    weights = rest[:parts]
    gated_out, gate_out, vqk_out, slope_out, mixed_out, probs_out, factor_out, normed = rest[parts:]
    length = x_own.shape[0]
    rows = 2 * length

    @pl.when(pl.program_id(0) == 0)
    def _():
        sources = [x_own, x_theirs]
        for t in range(stash_own.shape[0]):
            sources += [stash_own.at[t], stash_theirs.at[t]]
        for i, source in enumerate(sources):
            floats = source[...].astype(F32)
            normed[pl.ds(i * length, length), :] = (floats * row_root(floats)).astype(BF16)

    pre_all = project(normed, offs, weights)
    for i in range(1 + stash_own.shape[0]):
        pre = pre_all[i * rows : (i + 1) * rows]
        kept = keep[i]
        sig, gate, vqk, scores, sig_s, probs, mixed, gated = attend(pre, kept)
        gated_out[i] = gated
        if i > 0:
            gate_out[i - 1] = gate
            vqk_out[i - 1] = vqk
            slope_out[i - 1] = sig * (1.0 + pre * (1.0 - sig))
            mixed_out[i - 1] = mixed
            probs_out[i - 1, 0] = probs
            factor_out[i - 1, 0] = kept * sig_s * (1.0 + scores * (1.0 - sig_s)) * SCALING


def split_rows(core, part, send, keep):
    share = send.shape[1]
    cores = part.shape[0] // (2 * share)
    for r in range(2):
        base = r * cores * share
        mine = pl.multiple_of(base + core * share, share)
        other = pl.multiple_of(base + (cores - 1 - core) * share, share)
        send[r] = part[pl.ds(other, share), :]
        keep[r] = part[pl.ds(mine, share), :]


def out_kernel(n, core, offs, gated, *rest):
    weights = rest[:n]
    send, keep, part = rest[n:]
    depth = weights[0].shape[1]
    for j in range(n):
        columns = pl.ds(pl.multiple_of(offs[j], depth), depth)
        part[:, columns] = dot(gated[0], weights[j][...]).astype(BF16)
    split_rows(core[0], part, send, keep)


def assemble(core, fresh, mine, theirs, new_own, new_theirs, whole):
    share = mine.shape[1]
    length = new_own.shape[0]
    cores = length // share
    use_fresh = fresh != 0
    for r, source in enumerate((new_own, new_theirs)):
        for owner, landed in ((core, mine), (cores - 1 - core, theirs)):
            inside = pl.multiple_of(owner * share, share)
            rows = source[pl.ds(inside, share), :]
            at = pl.multiple_of(r * length + owner * share, share)
            whole[pl.ds(at, share), :] = jnp.where(use_fresh, rows, landed[r])


def forward_kernel(parts, heads, core, in_offs, offs, fresh, mine, theirs, new_own, new_theirs, keep, *rest):
    in_parts = rest[:parts]
    out_parts = rest[parts:-6]
    send, kept, whole, normed, gated, part = rest[-6:]
    depth = out_parts[0].shape[1]
    head = pl.program_id(0)

    @pl.when(head == 0)
    def _():
        assemble(core[0], fresh[0], mine, theirs, new_own, new_theirs, whole)
        floats = whole[...].astype(F32)
        normed[...] = (floats * row_root(floats)).astype(BF16)

    gated[head] = attend(project(normed, in_offs, in_parts), keep[0])[-1]

    @pl.when(head == heads - 1)
    def _():
        for j in range(len(out_parts)):
            columns = pl.ds(pl.multiple_of(offs[j], depth), depth)
            total = None
            for h in range(heads):
                term = dot(gated[h], out_parts[j][pl.ds(h * HEAD_DIM, HEAD_DIM), :])
                total = term if total is None else total + term
            part[:, columns] = total.astype(BF16)
        split_rows(core[0], part, send, kept)


def backward_kernel(parts, n, tick, core, in_offs, offs, *rest):
    count = 9 + n + parts
    sources, rest = rest[:count], rest[count:]
    send, keep = rest[:2]
    held, (grad_normed, part, sems) = rest[2 : 2 + count], rest[2 + count :]
    ups, gate, vqk, slope, mixed, probs, factor, x_own, x_theirs = held[:9]
    out_parts, in_parts = held[9 : 9 + n], held[9 + n :]
    copies = []
    for i, (source, target) in enumerate(zip(sources, held)):
        if 1 <= i < 9:
            source = source.at[tick]
        copies.append(pltpu.make_async_copy(source, target, sems.at[i]))
    first = [0] + list(range(9, 9 + n))
    second = [1, 4, 2, 5, 6, 3]
    last = list(range(9 + n, count))
    for i in first + second + last + [7, 8]:
        copies[i].start()
    for i in first:
        copies[i].wait()
    depth = out_parts[0].shape[1]
    length = x_own.shape[0]
    wide = 4 * HEAD_DIM
    heads = out_parts[0].shape[0] // HEAD_DIM
    grad_gated = None
    for j in range(n):
        columns = pl.ds(pl.multiple_of(offs[j], depth), depth)
        term = dot_nt(ups[:, columns], out_parts[j][...])
        grad_gated = term if grad_gated is None else grad_gated + term
    grad_gated = grad_gated.astype(BF16).astype(F32)
    for i in second:
        copies[i].wait()
    grads_pre = []
    for h in range(heads):
        cut = slice(h * HEAD_DIM, (h + 1) * HEAD_DIM)
        up = grad_gated[:, cut]
        mixed_h = mixed[:, cut]
        root = row_root(mixed_h)
        normed = mixed_h * root
        grad_n = up * gate[:, cut]
        grad_gate = up * normed
        grad_mixed = root * (grad_n - normed * jnp.mean(grad_n * normed, axis=-1, keepdims=True))
        low = grad_mixed.astype(BF16)
        base = 3 * h * HEAD_DIM
        value = vqk[:, base : base + HEAD_DIM]
        query = vqk[:, base + HEAD_DIM : base + 2 * HEAD_DIM]
        key = vqk[:, base + 2 * HEAD_DIM : base + 3 * HEAD_DIM]
        grad_scores = (dot_nt(low, value) * factor[h]).astype(BF16)
        grad_value = dot_tn(probs[h], low)
        grad_query = dot(grad_scores, key)
        grad_key = dot_tn(grad_scores, query)
        grad_active = jnp.concatenate([grad_gate, grad_value, grad_query, grad_key], axis=1)
        grads_pre.append((grad_active * slope[:, h * wide : (h + 1) * wide]).astype(BF16))
    grad_pre = jnp.concatenate(grads_pre, axis=1)
    for j in range(parts):
        rows_of = in_parts[j].shape[0]
        columns = pl.ds(pl.multiple_of(in_offs[j], rows_of), rows_of)
        copies[last[j]].wait()
        grad_normed[:, columns] = dot_nt(grad_pre, in_parts[j][...])
    for i in (7, 8):
        copies[i].wait()
    for r, source in enumerate((x_own, x_theirs)):
        rows = pl.ds(r * length, length)
        floats = source[...].astype(F32)
        root = row_root(floats)
        scaled = floats * root
        grad_n = grad_normed[rows, :]
        part[rows, :] = (
            root * (grad_n - scaled * jnp.mean(grad_n * scaled, axis=-1, keepdims=True))
        ).astype(BF16)
    split_rows(core[0], part, send, keep)


def pack_kernel(n, offs, gated, up_own, up_theirs, whole, *packs):
    depth = packs[0].shape[1] - 2 * gated.shape[2]
    slab = gated.shape[2]
    length = up_own.shape[0]
    whole[:length, :] = up_own[...]
    whole[length:, :] = up_theirs[...]
    for j in range(1, n):
        pack = packs[j - 1]
        columns = pl.ds(pl.multiple_of(offs[j], depth), depth)
        pack[:, :slab] = gated[1]
        pack[:, slab : 2 * slab] = gated[2]
        pack[:length, 2 * slab :] = up_own[:, columns]
        pack[length:, 2 * slab :] = up_theirs[:, columns]


def gather_kernel(n, core, offs, fresh, mine, theirs, new_own, new_theirs, whole, *pieces):
    assemble(core[0], fresh[0], mine, theirs, new_own, new_theirs, whole)
    depth = pieces[0].shape[1]
    for j in range(1, n):
        columns = pl.ds(pl.multiple_of(offs[j], depth), depth)
        pieces[j - 1][...] = whole[:, columns]


def grads_kernel(n, scaling, host, offs, gated, up_0, up_1, *rest):
    packs = rest[: n - 1]
    pieces = rest[n - 1 : 2 * n - 2]
    out = rest[2 * n - 2]
    slab = gated.shape[2]
    depth = out.shape[1]
    at_host = host[0] != 0
    columns = pl.ds(pl.multiple_of(offs[0], depth), depth)

    def product(first, second, third, fourth):
        return dot_tn(first, third) + dot_tn(second, fourth)

    total = product(
        jnp.where(at_host, gated[1], packs[0][:, :slab]),
        jnp.where(at_host, gated[2], packs[0][:, slab : 2 * slab]),
        jnp.where(at_host, up_0[:, columns], packs[0][:, 2 * slab :]),
        jnp.where(at_host, up_1[:, columns], pieces[0][...]),
    )
    for m in range(1, n // 2):
        near, beyond = m, n // 2 + m - 1
        pack = jnp.where(at_host, packs[near][...], packs[beyond][...])
        piece = jnp.where(at_host, pieces[near][...], pieces[beyond][...])
        total = total + product(
            pack[:, :slab], pack[:, slab : 2 * slab], pack[:, 2 * slab :], piece
        )
    out[...] = total * scaling


def after(value, *earlier):
    return lax.optimization_barrier((value,) + earlier)[0]


def block_keep(live_blocks, block_marks):
    length = BLOCKS * BLOCK
    places = jnp.arange(length, dtype=jnp.int32)
    owners = places // BLOCK
    marked = jnp.repeat(jnp.repeat(block_marks, BLOCK, axis=-2), BLOCK, axis=-1) == 1
    allowed = (owners[:, None] == owners[None, :]) | marked
    causal = places[:, None] >= places[None, :]
    tokens = live_blocks[..., None, None] * BLOCK
    keeping = causal & allowed & (places[:, None] < tokens) & (places[None, :] < tokens)
    return jnp.where(keeping, 1.0 / jnp.maximum(tokens, 1).astype(F32), 0.0)


def per_device(
    arrivals,
    in_flight,
    cotangent,
    grad_flight,
    stashed,
    in_weight,
    out_weight,
    forward_blocks,
    backward_blocks,
    forward_marks,
    backward_marks,
):
    section_no = lax.axis_index("section")
    sections = lax.axis_size("section")
    core_no = lax.axis_index("cores")
    cores = lax.axis_size("cores")
    dp_no = lax.axis_index("dp")
    n = lax.axis_size("dp")
    ticks = arrivals.shape[0]
    length = arrivals.shape[1]
    width = arrivals.shape[2]
    rows = 2 * length
    share = length // cores
    in_shard = in_weight[0]
    out_shard = out_weight[0]
    depth = in_shard.shape[0]
    slab = out_shard.shape[0]
    heads = slab // HEAD_DIM
    wide = 4 * HEAD_DIM

    hosts = [2 * k + 1 if 4 * k < n - 2 else 2 * k for k in range(n // 2)]
    host_table = jnp.array(hosts, jnp.int32)
    is_host = dp_no == host_table[dp_no // 2]

    def from_partner(x):
        return lax.ppermute(x, "dp", [(h ^ 1, h) for h in hosts])

    def to_partner(x):
        return lax.ppermute(x, "dp", [(h, h ^ 1) for h in hosts])

    def from_host(x, m):
        return lax.ppermute(x, "dp", [(hosts[k ^ m], hosts[k]) for k in range(n // 2)])

    def to_beyond(x, m):
        return lax.ppermute(
            x, "dp", [(hosts[k ^ m], hosts[k] ^ 1) for k in range(n // 2)]
        )

    def swap_cores(x):
        return lax.ppermute(x, "cores", [(c, cores - 1 - c) for c in range(cores)])

    def along_sections(x, by):
        pairs = [(i, i + by) for i in range(sections) if 0 <= i + by < sections]
        return lax.ppermute(x, "section", pairs)

    first_section = section_no == 0
    last_section = section_no == sections - 1
    between = range(1, n // 2)

    pieces = max(1, min(2, depth // 256))
    piece = depth // pieces
    in_far = [from_host(in_shard, m) for m in between]
    in_near = [
        from_partner(in_shard[i * piece : (i + 1) * piece]) for i in range(pieces)
    ]
    in_pass = [from_host(in_near[0], m) for m in between]
    in_far, in_near, rows_in, tables_in = lax.optimization_barrier(
        (
            in_far,
            in_near,
            (arrivals, in_flight, cotangent, grad_flight, stashed),
            (forward_blocks, forward_marks, backward_blocks, backward_marks),
        )
    )
    in_pass += [from_host(in_near[i], m) for i in range(1, pieces) for m in between]
    in_parts = [in_shard] + in_far + in_near + in_pass
    arrivals, in_flight, cotangent, grad_flight, stashed = rows_in
    tables = jnp.concatenate(
        [
            jnp.concatenate([b[..., None], m.reshape(m.shape[:2] + (-1,))], axis=-1)
            for b, m in (tables_in[:2], tables_in[2:])
        ],
        axis=0,
    )
    near_tables = from_partner(tables)
    stash_own = stashed[0]
    stash_theirs = from_partner(stash_own)
    x_own = jnp.where(first_section, arrivals[0], in_flight[0])
    x_theirs = from_partner(x_own)
    up_own = jnp.where(last_section, cotangent[0], grad_flight[0])
    new_own = jnp.where(first_section, arrivals[1], cotangent[1])
    out_late, up_late, new_late, stash_theirs, x_theirs = lax.optimization_barrier(
        (out_shard, up_own, new_own, stash_theirs, x_theirs)
    )
    out_near = from_partner(out_late)
    out_far = [from_host(out_late, m) for m in between]
    up_theirs = from_partner(up_late)
    new_theirs = from_partner(new_late)
    out_parts = [out_shard, out_near] + out_far + [from_host(out_near, m) for m in between]
    far_hosts = [host_table[(dp_no // 2) ^ m] for m in between]
    owners = [dp_no, dp_no ^ 1] + far_hosts + [h ^ 1 for h in far_hosts]
    offs = jnp.stack(owners).astype(jnp.int32) * depth
    in_offs = [dp_no * depth] + [h * depth for h in far_hosts]
    in_offs += [(dp_no ^ 1) * depth + i * piece for i in range(pieces)]
    in_offs += [(h ^ 1) * depth + i * piece for i in range(pieces) for h in far_hosts]
    in_offs = jnp.stack(in_offs).astype(jnp.int32)
    parts = len(in_parts)
    core = jnp.reshape(core_no, (1,)).astype(jnp.int32)
    first_flag = jnp.reshape(first_section, (1,)).astype(jnp.int32)
    host_flag = jnp.reshape(is_host, (1,)).astype(jnp.int32)
    last_flag = jnp.reshape(last_section, (1,)).astype(jnp.int32)

    both_tables = jnp.stack([tables, near_tables], axis=1)
    ahead_at = sections - 1 - section_no
    chosen = jnp.stack(
        [
            lax.dynamic_index_in_dim(both_tables[way], at, axis=1, keepdims=False)
            for way, at in (
                (0, ahead_at),
                (1, section_no),
                (1, section_no + 1),
                (0, ahead_at + 1),
            )
        ]
    )
    kept = block_keep(chosen[..., 0], chosen[..., 1:].reshape(-1, 2, BLOCKS, BLOCKS))
    blank = jnp.zeros_like(kept[:, 0])
    keep = jnp.concatenate(
        [
            jnp.concatenate([kept[:, 0], blank], axis=2),
            jnp.concatenate([blank, kept[:, 1]], axis=2),
        ],
        axis=1,
    )

    smem = pl.BlockSpec(memory_space=pltpu.SMEM)
    hbm = pl.BlockSpec(memory_space=pl.ANY)

    def all_of(*arrays):
        return [pl.BlockSpec(x.shape, lambda *_, d=x.ndim: (0,) * d) for x in arrays]

    def row_of(x, i):
        return pl.BlockSpec((1,) + x.shape[1:], lambda *_: (i,) + (0,) * (x.ndim - 1))

    params = pltpu.CompilerParams(vmem_limit_bytes=VMEM_BYTES)

    def cost(multiply_adds, bytes_accessed):
        return pl.CostEstimate(
            flops=2 * multiply_adds, bytes_accessed=bytes_accessed, transcendentals=0
        )

    def struct(shape, dtype):
        return jax.ShapeDtypeStruct(shape, dtype)

    halves = [struct((2, share, width), BF16)] * 2
    matmul = rows * width * 4 * slab
    weight_bytes = 2 * width * 5 * slab

    by_head = lambda lead, last: pl.BlockSpec(lead + (last,), lambda h: (0,) * len(lead) + (h,))
    square = pl.BlockSpec((2, 1, rows, rows), lambda h: (0, h, 0, 0))
    gated, gate, vqk, slope, mixed, probs, factor = pl.pallas_call(
        functools.partial(project_kernel, parts),
        grid=(heads,),
        in_specs=[smem]
        + all_of(x_own, x_theirs, stash_own, stash_theirs, keep)
        + [by_head((x.shape[0],), wide) for x in in_parts],
        out_specs=[
            by_head((3, rows), HEAD_DIM),
            by_head((2, rows), HEAD_DIM),
            by_head((2, rows), 3 * HEAD_DIM),
            by_head((2, rows), wide),
            by_head((2, rows), HEAD_DIM),
            square,
            square,
        ],
        out_shape=[
            struct((3, rows, slab), BF16),
            struct((2, rows, slab), F32),
            struct((2, rows, 3 * slab), BF16),
            struct((2, rows, 4 * slab), F32),
            struct((2, rows, slab), F32),
            struct((2, heads, rows, rows), BF16),
            struct((2, heads, rows, rows), F32),
        ],
        scratch_shapes=[pltpu.VMEM((3 * rows, width), BF16)],
        compiler_params=params,
        cost_estimate=cost(3 * matmul, 2 * weight_bytes),
        name="project",
    )(in_offs, x_own, x_theirs, stash_own, stash_theirs, keep, *in_parts)

    def backward(ups, tick_no):
        layered = [gate, vqk, slope, mixed, probs, factor, stash_own, stash_theirs]
        plain = list(out_parts) + list(in_parts)
        return pl.pallas_call(
            functools.partial(backward_kernel, parts, n, tick_no),
            grid=(1,),
            in_specs=[smem] * 3 + [hbm] * (1 + len(layered) + len(plain)),
            out_specs=all_of(*halves),
            out_shape=halves,
            scratch_shapes=[pltpu.VMEM(ups.shape, BF16)]
            + [pltpu.VMEM(x.shape[1:], x.dtype) for x in layered]
            + [pltpu.VMEM(x.shape, x.dtype) for x in plain]
            + [
                pltpu.VMEM((rows, width), F32),
                pltpu.VMEM((rows, width), BF16),
                pltpu.SemaphoreType.DMA((1 + len(layered) + len(plain),)),
            ],
            compiler_params=params,
            cost_estimate=cost(2 * matmul, 2 * weight_bytes),
            name="backward",
        )(core, in_offs, offs, ups, *layered, *plain)

    gated, new_theirs = lax.optimization_barrier((gated, new_theirs))

    def summed(residual, mine, landed):
        return (residual.astype(F32) + mine.astype(F32) + landed.astype(F32)).astype(BF16)

    def own_rows(mine, others):
        return lax.dynamic_slice_in_dim(jnp.stack([mine, others]), core_no * share, share, axis=1)

    pack_shapes = [struct((rows, width), BF16)]
    pack_shapes += [struct((rows, 2 * slab + depth), BF16)] * (n - 1)
    up_0, *packs = pl.pallas_call(
        functools.partial(pack_kernel, n),
        grid=(1,),
        in_specs=[smem] + all_of(gated, up_own, up_theirs),
        out_specs=all_of(*pack_shapes),
        out_shape=pack_shapes,
        compiler_params=params,
        name="pack",
    )(offs, gated, up_own, up_theirs)
    packs, out_parts = lax.optimization_barrier((packs, out_parts))

    ahead_send, ahead_keep = pl.pallas_call(
        functools.partial(out_kernel, n),
        grid=(1,),
        in_specs=[smem] * 2 + [row_of(gated, 0)] + all_of(*out_parts),
        out_specs=all_of(*halves),
        out_shape=halves,
        scratch_shapes=[pltpu.VMEM((rows, width), BF16)],
        compiler_params=params,
        cost_estimate=cost(matmul // 4, weight_bytes // 4),
        name="out",
    )(core, offs, gated, *out_parts)
    ahead_0 = summed(own_rows(x_own, x_theirs), ahead_keep, swap_cores(ahead_send))
    ahead_in = along_sections(ahead_0, 1)
    packs_near = [to_partner(packs[0])] + [from_host(packs[m], m) for m in between]
    back_send, back_keep = backward(after(up_0, ahead_0), 0)
    back_send, back_keep, ahead_in, packs_near = lax.optimization_barrier(
        (back_send, back_keep, ahead_in, packs_near)
    )
    back_0 = summed(own_rows(up_own, up_theirs), back_keep, swap_cores(back_send))
    back_in = along_sections(back_0, -1)

    packs_beyond = [to_beyond(packs[n // 2 + m - 1], m) for m in between]
    ahead_their = swap_cores(ahead_in)
    ahead_send, ahead_keep = pl.pallas_call(
        functools.partial(forward_kernel, parts, heads),
        grid=(heads,),
        in_specs=[smem] * 4
        + all_of(ahead_in, ahead_their, new_own, new_theirs)
        + [row_of(keep, keep.shape[0] - 1)]
        + [by_head((x.shape[0],), wide) for x in in_parts]
        + all_of(*out_parts),
        out_specs=all_of(*halves),
        out_shape=halves,
        scratch_shapes=[
            pltpu.VMEM((rows, width), BF16),
            pltpu.VMEM((rows, width), BF16),
            pltpu.VMEM((heads, rows, HEAD_DIM), BF16),
            pltpu.VMEM((rows, width), BF16),
        ],
        compiler_params=params,
        cost_estimate=cost(2 * matmul, 2 * weight_bytes),
        name="forward",
    )(
        core,
        in_offs,
        offs,
        first_flag,
        ahead_in,
        ahead_their,
        new_own,
        new_theirs,
        keep,
        *in_parts,
        *out_parts,
    )
    ahead_send, ahead_keep, back_in, packs_beyond = lax.optimization_barrier(
        (ahead_send, ahead_keep, back_in, packs_beyond)
    )
    new_rows = own_rows(new_own, new_theirs)
    ahead_1 = summed(
        jnp.where(first_section, new_rows, ahead_in), ahead_keep, swap_cores(ahead_send)
    )

    back_their = swap_cores(back_in)
    cut_shapes = [struct((rows, width), BF16)] + [struct((rows, depth), BF16)] * (n - 1)
    up_1, *cuts = pl.pallas_call(
        functools.partial(gather_kernel, n),
        grid=(1,),
        in_specs=[smem] * 3 + all_of(back_in, back_their, new_own, new_theirs),
        out_specs=all_of(*cut_shapes),
        out_shape=cut_shapes,
        compiler_params=params,
        name="gather",
    )(core, offs, last_flag, back_in, back_their, new_own, new_theirs)
    landed = [to_partner(cuts[0])] + [from_host(cuts[m], m) for m in between]
    landed += [to_beyond(cuts[n // 2 + m - 1], m) for m in between]
    back_send, back_keep = backward(up_1, 1)
    back_send, back_keep, landed = lax.optimization_barrier((back_send, back_keep, landed))
    back_1 = summed(
        jnp.where(last_section, new_rows, back_in), back_keep, swap_cores(back_send)
    )

    grads = pl.pallas_call(
        functools.partial(grads_kernel, n, (ticks * length * n) ** (-0.5)),
        grid=(1,),
        in_specs=[smem] * 2 + all_of(gated, up_0, up_1, *packs_near, *packs_beyond, *landed),
        out_specs=pl.BlockSpec((slab, depth), lambda *_: (0, 0)),
        out_shape=struct((slab, depth), F32),
        compiler_params=params,
        cost_estimate=cost(matmul // 4, weight_bytes // 4),
        name="grads",
    )(
        host_flag, offs, gated, up_0, up_1, *packs_near, *packs_beyond, *landed
    )

    first_pair = to_partner(jnp.stack([ahead_0[1], back_0[1]]))
    ahead = jnp.stack(
        [
            jnp.where(is_host, ahead_0[0], first_pair[0]),
            jnp.where(is_host, ahead_1[0], to_partner(ahead_1[1])),
        ]
    )
    back = jnp.stack(
        [
            jnp.where(is_host, back_0[0], first_pair[1]),
            jnp.where(is_host, back_1[0], to_partner(back_1[1])),
        ]
    )
    return (ahead[None], back[None], grads[None])


def solution(mesh):
    in_specs = (
        P(None, "dp", None),
        P("section", "dp", None),
        P(None, "dp", None),
        P("section", "dp", None),
        P("section", None, "dp", None),
        P("section", "dp", "cores"),
        P("section", "cores", "dp"),
        P("dp", None),
        P("dp", None),
        P("dp", None, None, None),
        P("dp", None, None, None),
    )
    out_specs = (
        P("section", None, ("dp", "cores"), None),
        P("section", None, ("dp", "cores"), None),
        P("section", "cores", "dp"),
    )
    return jax.shard_map(
        per_device, mesh=mesh, in_specs=in_specs, out_specs=out_specs, check_vma=False
    )
```

```python
import functools

import jax
import jax.numpy as jnp
from jax import lax
from jax.experimental import pallas as pl
from jax.experimental.pallas import tpu as pltpu
from jax.sharding import PartitionSpec as P

HEAD_DIM = 128
BLOCK = 24
BLOCKS = 4
EPSILON = 1e-06
SCALING = HEAD_DIM ** (-0.5)
VMEM_BYTES = 30 * 1024 * 1024

F32 = jnp.float32
BF16 = jnp.bfloat16


def dot(a, b):
    return lax.dot_general(a, b, (((1,), (0,)), ((), ())), preferred_element_type=F32)


def dot_nt(a, b):
    return lax.dot_general(a, b, (((1,), (1,)), ((), ())), preferred_element_type=F32)


def dot_tn(a, b):
    return lax.dot_general(a, b, (((0,), (0,)), ((), ())), preferred_element_type=F32)


def row_root(floats):
    return lax.rsqrt(jnp.mean(floats * floats, axis=-1, keepdims=True) + EPSILON)


def sigmoid(x):
    return 1.0 / (1.0 + jnp.exp(-x))


def attend(pre, keep):
    sig = sigmoid(pre)
    active = pre * sig
    gate = active[:, :HEAD_DIM]
    vqk = active[:, HEAD_DIM:].astype(BF16)
    value = vqk[:, :HEAD_DIM]
    query = vqk[:, HEAD_DIM : 2 * HEAD_DIM]
    key = vqk[:, 2 * HEAD_DIM :]
    scores = dot_nt(query, key) * SCALING
    sig_s = sigmoid(scores)
    probs = (scores * sig_s * keep).astype(BF16)
    mixed = dot(probs, value)
    gated = (mixed * row_root(mixed) * gate).astype(BF16)
    return sig, gate, vqk, scores, sig_s, probs, mixed, gated


def project(normed, offs, weights):
    total = None
    for j, weight in enumerate(weights):
        depth = weight.shape[0]
        columns = pl.ds(pl.multiple_of(offs[j], depth), depth)
        term = dot(normed[:, columns], weight[...])
        total = term if total is None else total + term
    return total


def project_kernel(parts, offs, x_own, x_theirs, stash_own, stash_theirs, keep, *rest):
    weights = rest[:parts]
    gated_out, gate_out, vqk_out, slope_out, mixed_out, probs_out, factor_out, normed = rest[parts:]
    length = x_own.shape[0]
    rows = 2 * length

    @pl.when(pl.program_id(0) == 0)
    def _():
        sources = [x_own, x_theirs]
        for t in range(stash_own.shape[0]):
            sources += [stash_own.at[t], stash_theirs.at[t]]
        for i, source in enumerate(sources):
            floats = source[...].astype(F32)
            normed[pl.ds(i * length, length), :] = (floats * row_root(floats)).astype(BF16)

    pre_all = project(normed, offs, weights)
    for i in range(1 + stash_own.shape[0]):
        pre = pre_all[i * rows : (i + 1) * rows]
        kept = keep[i]
        sig, gate, vqk, scores, sig_s, probs, mixed, gated = attend(pre, kept)
        gated_out[i] = gated
        if i > 0:
            gate_out[i - 1] = gate
            vqk_out[i - 1] = vqk
            slope_out[i - 1] = sig * (1.0 + pre * (1.0 - sig))
            mixed_out[i - 1] = mixed
            probs_out[i - 1, 0] = probs
            factor_out[i - 1, 0] = kept * sig_s * (1.0 + scores * (1.0 - sig_s)) * SCALING


def split_rows(core, part, send, keep):
    share = send.shape[1]
    cores = part.shape[0] // (2 * share)
    for r in range(2):
        base = r * cores * share
        mine = pl.multiple_of(base + core * share, share)
        other = pl.multiple_of(base + (cores - 1 - core) * share, share)
        send[r] = part[pl.ds(other, share), :]
        keep[r] = part[pl.ds(mine, share), :]


def out_kernel(n, core, offs, gated, *rest):
    weights = rest[:n]
    send, keep, part = rest[n:]
    depth = weights[0].shape[1]
    for j in range(n):
        columns = pl.ds(pl.multiple_of(offs[j], depth), depth)
        part[:, columns] = dot(gated[0], weights[j][...]).astype(BF16)
    split_rows(core[0], part, send, keep)


def assemble(core, fresh, mine, theirs, new_own, new_theirs, whole):
    share = mine.shape[1]
    length = new_own.shape[0]
    cores = length // share
    use_fresh = fresh != 0
    for r, source in enumerate((new_own, new_theirs)):
        for owner, landed in ((core, mine), (cores - 1 - core, theirs)):
            inside = pl.multiple_of(owner * share, share)
            rows = source[pl.ds(inside, share), :]
            at = pl.multiple_of(r * length + owner * share, share)
            whole[pl.ds(at, share), :] = jnp.where(use_fresh, rows, landed[r])


def forward_kernel(parts, heads, core, in_offs, offs, fresh, mine, theirs, new_own, new_theirs, keep, *rest):
    in_parts = rest[:parts]
    out_parts = rest[parts:-6]
    send, kept, whole, normed, gated, part = rest[-6:]
    depth = out_parts[0].shape[1]
    head = pl.program_id(0)

    @pl.when(head == 0)
    def _():
        assemble(core[0], fresh[0], mine, theirs, new_own, new_theirs, whole)
        floats = whole[...].astype(F32)
        normed[...] = (floats * row_root(floats)).astype(BF16)

    gated[head] = attend(project(normed, in_offs, in_parts), keep[0])[-1]

    @pl.when(head == heads - 1)
    def _():
        for j in range(len(out_parts)):
            columns = pl.ds(pl.multiple_of(offs[j], depth), depth)
            total = None
            for h in range(heads):
                term = dot(gated[h], out_parts[j][pl.ds(h * HEAD_DIM, HEAD_DIM), :])
                total = term if total is None else total + term
            part[:, columns] = total.astype(BF16)
        split_rows(core[0], part, send, kept)


def backward_kernel(parts, n, tick, core, in_offs, offs, *rest):
    count = 9 + n + parts
    sources, rest = rest[:count], rest[count:]
    send, keep = rest[:2]
    held, (grad_normed, part, sems) = rest[2 : 2 + count], rest[2 + count :]
    ups, gate, vqk, slope, mixed, probs, factor, x_own, x_theirs = held[:9]
    out_parts, in_parts = held[9 : 9 + n], held[9 + n :]
    copies = []
    for i, (source, target) in enumerate(zip(sources, held)):
        if 1 <= i < 9:
            source = source.at[tick]
        copies.append(pltpu.make_async_copy(source, target, sems.at[i]))
    first = [0] + list(range(9, 9 + n))
    second = [1, 4, 2, 5, 6, 3]
    last = list(range(9 + n, count))
    for i in first + second + last + [7, 8]:
        copies[i].start()
    for i in first:
        copies[i].wait()
    depth = out_parts[0].shape[1]
    length = x_own.shape[0]
    wide = 4 * HEAD_DIM
    heads = out_parts[0].shape[0] // HEAD_DIM
    grad_gated = None
    for j in range(n):
        columns = pl.ds(pl.multiple_of(offs[j], depth), depth)
        term = dot_nt(ups[:, columns], out_parts[j][...])
        grad_gated = term if grad_gated is None else grad_gated + term
    grad_gated = grad_gated.astype(BF16).astype(F32)
    for i in second:
        copies[i].wait()
    grads_pre = []
    for h in range(heads):
        cut = slice(h * HEAD_DIM, (h + 1) * HEAD_DIM)
        up = grad_gated[:, cut]
        mixed_h = mixed[:, cut]
        root = row_root(mixed_h)
        normed = mixed_h * root
        grad_n = up * gate[:, cut]
        grad_gate = up * normed
        grad_mixed = root * (grad_n - normed * jnp.mean(grad_n * normed, axis=-1, keepdims=True))
        low = grad_mixed.astype(BF16)
        base = 3 * h * HEAD_DIM
        value = vqk[:, base : base + HEAD_DIM]
        query = vqk[:, base + HEAD_DIM : base + 2 * HEAD_DIM]
        key = vqk[:, base + 2 * HEAD_DIM : base + 3 * HEAD_DIM]
        grad_scores = (dot_nt(low, value) * factor[h]).astype(BF16)
        grad_value = dot_tn(probs[h], low)
        grad_query = dot(grad_scores, key)
        grad_key = dot_tn(grad_scores, query)
        grad_active = jnp.concatenate([grad_gate, grad_value, grad_query, grad_key], axis=1)
        grads_pre.append((grad_active * slope[:, h * wide : (h + 1) * wide]).astype(BF16))
    grad_pre = jnp.concatenate(grads_pre, axis=1)
    for j in range(parts):
        rows_of = in_parts[j].shape[0]
        columns = pl.ds(pl.multiple_of(in_offs[j], rows_of), rows_of)
        copies[last[j]].wait()
        grad_normed[:, columns] = dot_nt(grad_pre, in_parts[j][...])
    for i in (7, 8):
        copies[i].wait()
    for r, source in enumerate((x_own, x_theirs)):
        rows = pl.ds(r * length, length)
        floats = source[...].astype(F32)
        root = row_root(floats)
        scaled = floats * root
        grad_n = grad_normed[rows, :]
        part[rows, :] = (
            root * (grad_n - scaled * jnp.mean(grad_n * scaled, axis=-1, keepdims=True))
        ).astype(BF16)
    split_rows(core[0], part, send, keep)


def pack_kernel(n, offs, gated, up_own, up_theirs, whole, *packs):
    depth = packs[0].shape[1] - 2 * gated.shape[2]
    slab = gated.shape[2]
    length = up_own.shape[0]
    whole[:length, :] = up_own[...]
    whole[length:, :] = up_theirs[...]
    for j in range(1, n):
        pack = packs[j - 1]
        columns = pl.ds(pl.multiple_of(offs[j], depth), depth)
        pack[:, :slab] = gated[1]
        pack[:, slab : 2 * slab] = gated[2]
        pack[:length, 2 * slab :] = up_own[:, columns]
        pack[length:, 2 * slab :] = up_theirs[:, columns]


def settle_kernel(core, fresh, own, theirs, passed, keep, landed, earlier, total, pair):
    share = keep.shape[1]
    here = pl.ds(pl.multiple_of(core[0] * share, share), share)
    for r, source in enumerate((own, theirs)):
        residual = jnp.where(fresh[0] != 0, source[here, :], passed[r])
        total[r] = (
            residual.astype(F32) + keep[r].astype(F32) + landed[r].astype(F32)
        ).astype(BF16)
    pair[0] = earlier[1]
    pair[1] = total[1]


def gather_kernel(n, core, offs, fresh, mine, theirs, new_own, new_theirs, whole, *pieces):
    assemble(core[0], fresh[0], mine, theirs, new_own, new_theirs, whole)
    depth = pieces[0].shape[1]
    for j in range(1, n):
        columns = pl.ds(pl.multiple_of(offs[j], depth), depth)
        pieces[j - 1][...] = whole[:, columns]


def grads_kernel(n, scaling, host, offs, gated, up_0, up_1, *rest):
    packs = rest[: n - 1]
    pieces = rest[n - 1 : 2 * n - 2]
    out = rest[2 * n - 2]
    slab = gated.shape[2]
    depth = out.shape[1]
    at_host = host[0] != 0
    columns = pl.ds(pl.multiple_of(offs[0], depth), depth)

    def product(first, second, third, fourth):
        return dot_tn(first, third) + dot_tn(second, fourth)

    total = product(
        jnp.where(at_host, gated[1], packs[0][:, :slab]),
        jnp.where(at_host, gated[2], packs[0][:, slab : 2 * slab]),
        jnp.where(at_host, up_0[:, columns], packs[0][:, 2 * slab :]),
        jnp.where(at_host, up_1[:, columns], pieces[0][...]),
    )
    for m in range(1, n // 2):
        near, beyond = m, n // 2 + m - 1
        pack = jnp.where(at_host, packs[near][...], packs[beyond][...])
        piece = jnp.where(at_host, pieces[near][...], pieces[beyond][...])
        total = total + product(
            pack[:, :slab], pack[:, slab : 2 * slab], pack[:, 2 * slab :], piece
        )
    out[...] = total * scaling


def after(value, *earlier):
    return lax.optimization_barrier((value,) + earlier)[0]


def block_keep(live_blocks, block_marks):
    length = BLOCKS * BLOCK
    places = jnp.arange(length, dtype=jnp.int32)
    owners = places // BLOCK
    marked = jnp.repeat(jnp.repeat(block_marks, BLOCK, axis=-2), BLOCK, axis=-1) == 1
    allowed = (owners[:, None] == owners[None, :]) | marked
    causal = places[:, None] >= places[None, :]
    tokens = live_blocks[..., None, None] * BLOCK
    keeping = causal & allowed & (places[:, None] < tokens) & (places[None, :] < tokens)
    return jnp.where(keeping, 1.0 / jnp.maximum(tokens, 1).astype(F32), 0.0)


def per_device(
    arrivals,
    in_flight,
    cotangent,
    grad_flight,
    stashed,
    in_weight,
    out_weight,
    forward_blocks,
    backward_blocks,
    forward_marks,
    backward_marks,
):
    section_no = lax.axis_index("section")
    sections = lax.axis_size("section")
    core_no = lax.axis_index("cores")
    cores = lax.axis_size("cores")
    dp_no = lax.axis_index("dp")
    n = lax.axis_size("dp")
    ticks = arrivals.shape[0]
    length = arrivals.shape[1]
    width = arrivals.shape[2]
    rows = 2 * length
    share = length // cores
    in_shard = in_weight[0]
    out_shard = out_weight[0]
    depth = in_shard.shape[0]
    slab = out_shard.shape[0]
    heads = slab // HEAD_DIM
    wide = 4 * HEAD_DIM

    hosts = [2 * k + 1 if 4 * k < n - 2 else 2 * k for k in range(n // 2)]
    host_table = jnp.array(hosts, jnp.int32)
    is_host = dp_no == host_table[dp_no // 2]

    def from_partner(x):
        return lax.ppermute(x, "dp", [(h ^ 1, h) for h in hosts])

    def to_partner(x):
        return lax.ppermute(x, "dp", [(h, h ^ 1) for h in hosts])

    def from_host(x, m):
        return lax.ppermute(x, "dp", [(hosts[k ^ m], hosts[k]) for k in range(n // 2)])

    def to_beyond(x, m):
        return lax.ppermute(
            x, "dp", [(hosts[k ^ m], hosts[k] ^ 1) for k in range(n // 2)]
        )

    def swap_cores(x):
        return lax.ppermute(x, "cores", [(c, cores - 1 - c) for c in range(cores)])

    def along_sections(x, by):
        pairs = [(i, i + by) for i in range(sections) if 0 <= i + by < sections]
        return lax.ppermute(x, "section", pairs)

    first_section = section_no == 0
    last_section = section_no == sections - 1
    between = range(1, n // 2)

    pieces = max(1, min(2, depth // 256))
    piece = depth // pieces
    in_far = [from_host(in_shard, m) for m in between]
    in_near = [
        from_partner(in_shard[i * piece : (i + 1) * piece]) for i in range(pieces)
    ]
    out_near = from_partner(out_shard)
    in_pass = [from_host(in_near[0], m) for m in between]
    in_far, in_near, rows_in, tables_in = lax.optimization_barrier(
        (
            in_far,
            in_near,
            (arrivals, in_flight, cotangent, grad_flight, stashed),
            (forward_blocks, forward_marks, backward_blocks, backward_marks),
        )
    )
    in_pass += [from_host(in_near[i], m) for i in range(1, pieces) for m in between]
    in_parts = [in_shard] + in_far + in_near + in_pass
    arrivals, in_flight, cotangent, grad_flight, stashed = rows_in
    tables = jnp.concatenate(
        [
            jnp.concatenate([b[..., None], m.reshape(m.shape[:2] + (-1,))], axis=-1)
            for b, m in (tables_in[:2], tables_in[2:])
        ],
        axis=0,
    )
    near_tables = from_partner(tables)
    stash_own = stashed[0]
    stash_theirs = from_partner(stash_own)
    x_own = jnp.where(first_section, arrivals[0], in_flight[0])
    x_theirs = from_partner(x_own)
    up_own = jnp.where(last_section, cotangent[0], grad_flight[0])
    new_own = jnp.where(first_section, arrivals[1], cotangent[1])
    out_own, out_near, near_tables = lax.optimization_barrier((out_shard, out_near, near_tables))
    out_far = [from_host(out_own, m) for m in between]
    out_parts = [out_shard, out_near] + out_far + [from_host(out_near, m) for m in between]
    up_late, new_late, stash_theirs, x_theirs = lax.optimization_barrier(
        (up_own, new_own, stash_theirs, x_theirs)
    )
    up_theirs = from_partner(up_late)
    new_theirs = from_partner(new_late)
    far_hosts = [host_table[(dp_no // 2) ^ m] for m in between]
    owners = [dp_no, dp_no ^ 1] + far_hosts + [h ^ 1 for h in far_hosts]
    offs = jnp.stack(owners).astype(jnp.int32) * depth
    in_offs = [dp_no * depth] + [h * depth for h in far_hosts]
    in_offs += [(dp_no ^ 1) * depth + i * piece for i in range(pieces)]
    in_offs += [(h ^ 1) * depth + i * piece for i in range(pieces) for h in far_hosts]
    in_offs = jnp.stack(in_offs).astype(jnp.int32)
    parts = len(in_parts)
    core = jnp.reshape(core_no, (1,)).astype(jnp.int32)
    first_flag = jnp.reshape(first_section, (1,)).astype(jnp.int32)
    always = jnp.ones((1,), jnp.int32)
    host_flag = jnp.reshape(is_host, (1,)).astype(jnp.int32)
    last_flag = jnp.reshape(last_section, (1,)).astype(jnp.int32)

    both_tables = jnp.stack([tables, near_tables], axis=1)
    ahead_at = sections - 1 - section_no
    chosen = jnp.stack(
        [
            lax.dynamic_index_in_dim(both_tables[way], at, axis=1, keepdims=False)
            for way, at in (
                (0, ahead_at),
                (1, section_no),
                (1, section_no + 1),
                (0, ahead_at + 1),
            )
        ]
    )
    kept = block_keep(chosen[..., 0], chosen[..., 1:].reshape(-1, 2, BLOCKS, BLOCKS))
    blank = jnp.zeros_like(kept[:, 0])
    keep = jnp.concatenate(
        [
            jnp.concatenate([kept[:, 0], blank], axis=2),
            jnp.concatenate([blank, kept[:, 1]], axis=2),
        ],
        axis=1,
    )

    smem = pl.BlockSpec(memory_space=pltpu.SMEM)
    hbm = pl.BlockSpec(memory_space=pl.ANY)

    def all_of(*arrays):
        return [pl.BlockSpec(x.shape, lambda *_, d=x.ndim: (0,) * d) for x in arrays]

    def row_of(x, i):
        return pl.BlockSpec((1,) + x.shape[1:], lambda *_: (i,) + (0,) * (x.ndim - 1))

    params = pltpu.CompilerParams(vmem_limit_bytes=VMEM_BYTES)

    def cost(multiply_adds, bytes_accessed):
        return pl.CostEstimate(
            flops=2 * multiply_adds, bytes_accessed=bytes_accessed, transcendentals=0
        )

    def struct(shape, dtype):
        return jax.ShapeDtypeStruct(shape, dtype)

    halves = [struct((2, share, width), BF16)] * 2
    matmul = rows * width * 4 * slab
    weight_bytes = 2 * width * 5 * slab

    by_head = lambda lead, last: pl.BlockSpec(lead + (last,), lambda h: (0,) * len(lead) + (h,))
    square = pl.BlockSpec((2, 1, rows, rows), lambda h: (0, h, 0, 0))
    gated, gate, vqk, slope, mixed, probs, factor = pl.pallas_call(
        functools.partial(project_kernel, parts),
        grid=(heads,),
        in_specs=[smem]
        + all_of(x_own, x_theirs, stash_own, stash_theirs, keep)
        + [by_head((x.shape[0],), wide) for x in in_parts],
        out_specs=[
            by_head((3, rows), HEAD_DIM),
            by_head((2, rows), HEAD_DIM),
            by_head((2, rows), 3 * HEAD_DIM),
            by_head((2, rows), wide),
            by_head((2, rows), HEAD_DIM),
            square,
            square,
        ],
        out_shape=[
            struct((3, rows, slab), BF16),
            struct((2, rows, slab), F32),
            struct((2, rows, 3 * slab), BF16),
            struct((2, rows, 4 * slab), F32),
            struct((2, rows, slab), F32),
            struct((2, heads, rows, rows), BF16),
            struct((2, heads, rows, rows), F32),
        ],
        scratch_shapes=[pltpu.VMEM((3 * rows, width), BF16)],
        compiler_params=params,
        cost_estimate=cost(3 * matmul, 2 * weight_bytes),
        name="project",
    )(in_offs, x_own, x_theirs, stash_own, stash_theirs, keep, *in_parts)

    def backward(ups, tick_no):
        layered = [gate, vqk, slope, mixed, probs, factor, stash_own, stash_theirs]
        plain = list(out_parts) + list(in_parts)
        return pl.pallas_call(
            functools.partial(backward_kernel, parts, n, tick_no),
            grid=(1,),
            in_specs=[smem] * 3 + [hbm] * (1 + len(layered) + len(plain)),
            out_specs=all_of(*halves),
            out_shape=halves,
            scratch_shapes=[pltpu.VMEM(ups.shape, BF16)]
            + [pltpu.VMEM(x.shape[1:], x.dtype) for x in layered]
            + [pltpu.VMEM(x.shape, x.dtype) for x in plain]
            + [
                pltpu.VMEM((rows, width), F32),
                pltpu.VMEM((rows, width), BF16),
                pltpu.SemaphoreType.DMA((1 + len(layered) + len(plain),)),
            ],
            compiler_params=params,
            cost_estimate=cost(2 * matmul, 2 * weight_bytes),
            name="backward",
        )(core, in_offs, offs, ups, *layered, *plain)

    gated, new_theirs = lax.optimization_barrier((gated, new_theirs))

    def summed(residual, mine, landed):
        return (residual.astype(F32) + mine.astype(F32) + landed.astype(F32)).astype(BF16)

    def own_rows(mine, others):
        return lax.dynamic_slice_in_dim(jnp.stack([mine, others]), core_no * share, share, axis=1)

    pack_shapes = [struct((rows, width), BF16)]
    pack_shapes += [struct((rows, 2 * slab + depth), BF16)] * (n - 1)
    up_0, *packs = pl.pallas_call(
        functools.partial(pack_kernel, n),
        grid=(1,),
        in_specs=[smem] + all_of(gated, up_own, up_theirs),
        out_specs=all_of(*pack_shapes),
        out_shape=pack_shapes,
        compiler_params=params,
        name="pack",
    )(offs, gated, up_own, up_theirs)
    packs, out_parts = lax.optimization_barrier((packs, out_parts))

    ahead_send, ahead_keep = pl.pallas_call(
        functools.partial(out_kernel, n),
        grid=(1,),
        in_specs=[smem] * 2 + [row_of(gated, 0)] + all_of(*out_parts),
        out_specs=all_of(*halves),
        out_shape=halves,
        scratch_shapes=[pltpu.VMEM((rows, width), BF16)],
        compiler_params=params,
        cost_estimate=cost(matmul // 4, weight_bytes // 4),
        name="out",
    )(core, offs, gated, *out_parts)
    ahead_0 = summed(own_rows(x_own, x_theirs), ahead_keep, swap_cores(ahead_send))
    ahead_in = along_sections(ahead_0, 1)
    packs_near = [to_partner(packs[0])] + [from_host(packs[m], m) for m in between]
    back_send, back_keep = backward(after(up_0, ahead_0), 0)
    back_send, back_keep, ahead_in, packs_near = lax.optimization_barrier(
        (back_send, back_keep, ahead_in, packs_near)
    )
    back_landed = swap_cores(back_send)
    back_0, first_pair = pl.pallas_call(
        settle_kernel,
        grid=(1,),
        in_specs=[smem] * 2
        + all_of(up_own, up_theirs, back_keep, back_keep, back_landed, ahead_0),
        out_specs=all_of(*halves),
        out_shape=halves,
        compiler_params=params,
        name="settle",
    )(core, always, up_own, up_theirs, back_keep, back_keep, back_landed, ahead_0)
    back_in = along_sections(back_0, -1)
    first_pair = to_partner(first_pair)

    packs_beyond = [to_beyond(packs[n // 2 + m - 1], m) for m in between]
    ahead_their = swap_cores(ahead_in)
    ahead_send, ahead_keep = pl.pallas_call(
        functools.partial(forward_kernel, parts, heads),
        grid=(heads,),
        in_specs=[smem] * 4
        + all_of(ahead_in, ahead_their, new_own, new_theirs)
        + [row_of(keep, keep.shape[0] - 1)]
        + [by_head((x.shape[0],), wide) for x in in_parts]
        + all_of(*out_parts),
        out_specs=all_of(*halves),
        out_shape=halves,
        scratch_shapes=[
            pltpu.VMEM((rows, width), BF16),
            pltpu.VMEM((rows, width), BF16),
            pltpu.VMEM((heads, rows, HEAD_DIM), BF16),
            pltpu.VMEM((rows, width), BF16),
        ],
        compiler_params=params,
        cost_estimate=cost(2 * matmul, 2 * weight_bytes),
        name="forward",
    )(
        core,
        in_offs,
        offs,
        first_flag,
        ahead_in,
        ahead_their,
        new_own,
        new_theirs,
        keep,
        *in_parts,
        *out_parts,
    )
    ahead_send, ahead_keep, back_in, packs_beyond, first_pair = lax.optimization_barrier(
        (ahead_send, ahead_keep, back_in, packs_beyond, first_pair)
    )
    new_rows = own_rows(new_own, new_theirs)
    ahead_1 = summed(
        jnp.where(first_section, new_rows, ahead_in), ahead_keep, swap_cores(ahead_send)
    )

    back_their = swap_cores(back_in)
    cut_shapes = [struct((rows, width), BF16)] + [struct((rows, depth), BF16)] * (n - 1)
    up_1, *cuts = pl.pallas_call(
        functools.partial(gather_kernel, n),
        grid=(1,),
        in_specs=[smem] * 3 + all_of(back_in, back_their, new_own, new_theirs),
        out_specs=all_of(*cut_shapes),
        out_shape=cut_shapes,
        compiler_params=params,
        name="gather",
    )(core, offs, last_flag, back_in, back_their, new_own, new_theirs)
    landed = [to_partner(cuts[0])] + [from_host(cuts[m], m) for m in between]
    landed += [to_beyond(cuts[n // 2 + m - 1], m) for m in between]
    back_send, back_keep = backward(up_1, 1)
    ahead_given = to_partner(ahead_1[1])
    back_send, back_keep, landed, ahead_given = lax.optimization_barrier(
        (back_send, back_keep, landed, ahead_given)
    )
    back_1 = summed(
        jnp.where(last_section, new_rows, back_in), back_keep, swap_cores(back_send)
    )

    grads = pl.pallas_call(
        functools.partial(grads_kernel, n, (ticks * length * n) ** (-0.5)),
        grid=(1,),
        in_specs=[smem] * 2 + all_of(gated, up_0, up_1, *packs_near, *packs_beyond, *landed),
        out_specs=pl.BlockSpec((slab, depth), lambda *_: (0, 0)),
        out_shape=struct((slab, depth), F32),
        compiler_params=params,
        cost_estimate=cost(matmul // 4, weight_bytes // 4),
        name="grads",
    )(
        host_flag, offs, after(gated, back_1), up_0, up_1, *packs_near, *packs_beyond, *landed
    )

    ahead = jnp.stack(
        [
            jnp.where(is_host, ahead_0[0], first_pair[0]),
            jnp.where(is_host, ahead_1[0], ahead_given),
        ]
    )
    back = jnp.stack(
        [
            jnp.where(is_host, back_0[0], first_pair[1]),
            jnp.where(is_host, back_1[0], to_partner(back_1[1])),
        ]
    )
    return (ahead[None], back[None], grads[None])


def solution(mesh):
    in_specs = (
        P(None, "dp", None),
        P("section", "dp", None),
        P(None, "dp", None),
        P("section", "dp", None),
        P("section", None, "dp", None),
        P("section", "dp", "cores"),
        P("section", "cores", "dp"),
        P("dp", None),
        P("dp", None),
        P("dp", None, None, None),
        P("dp", None, None, None),
    )
    out_specs = (
        P("section", None, ("dp", "cores"), None),
        P("section", None, ("dp", "cores"), None),
        P("section", "cores", "dp"),
    )
    return jax.shard_map(
        per_device, mesh=mesh, in_specs=in_specs, out_specs=out_specs, check_vma=False
    )
```

```python
import functools

import jax
import jax.numpy as jnp
from jax import lax
from jax.experimental import pallas as pl
from jax.experimental.pallas import tpu as pltpu
from jax.sharding import PartitionSpec as P

HEAD_DIM = 128
BLOCK = 24
BLOCKS = 4
EPSILON = 1e-06
SCALING = HEAD_DIM ** (-0.5)
VMEM_BYTES = 58 * 1024 * 1024

F32 = jnp.float32
BF16 = jnp.bfloat16


def on_host(kernel):
    def guarded(host, *refs):
        pl.when(host[0] != 0)(functools.partial(kernel, *refs))

    return guarded


def dot(a, b):
    return lax.dot_general(a, b, (((1,), (0,)), ((), ())), preferred_element_type=F32)


def dot_nt(a, b):
    return lax.dot_general(a, b, (((1,), (1,)), ((), ())), preferred_element_type=F32)


def dot_tn(a, b):
    return lax.dot_general(a, b, (((0,), (0,)), ((), ())), preferred_element_type=F32)


def row_root(floats):
    return lax.rsqrt(jnp.mean(floats * floats, axis=-1, keepdims=True) + EPSILON)


def sigmoid(x):
    return 1.0 / (1.0 + jnp.exp(-x))


def attend(pre, keep):
    sig = sigmoid(pre)
    active = pre * sig
    gate = active[:, :HEAD_DIM]
    vqk = active[:, HEAD_DIM:].astype(BF16)
    value = vqk[:, :HEAD_DIM]
    query = vqk[:, HEAD_DIM : 2 * HEAD_DIM]
    key = vqk[:, 2 * HEAD_DIM :]
    scores = dot_nt(query, key) * SCALING
    sig_s = sigmoid(scores)
    probs = (scores * sig_s * keep).astype(BF16)
    mixed = dot(probs, value)
    gated = (mixed * row_root(mixed) * gate).astype(BF16)
    return sig, gate, vqk, scores, sig_s, probs, mixed, gated


def project(normed, offs, weights):
    total = None
    for j, weight in enumerate(weights):
        depth = weight.shape[0]
        columns = pl.ds(pl.multiple_of(offs[j], depth), depth)
        term = dot(normed[:, columns], weight[...])
        total = term if total is None else total + term
    return total


def project_kernel(parts, offs, x_own, x_theirs, stash_own, stash_theirs, keep, *rest):
    weights = rest[:parts]
    gated_out, gate_out, vqk_out, slope_out, mixed_out, probs_out, factor_out, normed = rest[parts:]
    length = x_own.shape[0]
    rows = 2 * length

    @pl.when(pl.program_id(0) == 0)
    def _():
        sources = [x_own, x_theirs]
        for t in range(stash_own.shape[0]):
            sources += [stash_own.at[t], stash_theirs.at[t]]
        for i, source in enumerate(sources):
            floats = source[...].astype(F32)
            normed[pl.ds(i * length, length), :] = (floats * row_root(floats)).astype(BF16)

    pre_all = project(normed, offs, weights)
    for i in range(1 + stash_own.shape[0]):
        pre = pre_all[i * rows : (i + 1) * rows]
        kept = keep[i]
        sig, gate, vqk, scores, sig_s, probs, mixed, gated = attend(pre, kept)
        gated_out[i] = gated
        if i > 0:
            gate_out[i - 1] = gate
            vqk_out[i - 1] = vqk
            slope_out[i - 1] = sig * (1.0 + pre * (1.0 - sig))
            mixed_out[i - 1] = mixed
            probs_out[i - 1, 0] = probs
            factor_out[i - 1, 0] = kept * sig_s * (1.0 + scores * (1.0 - sig_s)) * SCALING


def split_rows(core, part, send, keep):
    share = send.shape[1]
    cores = part.shape[0] // (2 * share)
    for r in range(2):
        base = r * cores * share
        mine = pl.multiple_of(base + core * share, share)
        other = pl.multiple_of(base + (cores - 1 - core) * share, share)
        send[r] = part[pl.ds(other, share), :]
        keep[r] = part[pl.ds(mine, share), :]


def out_kernel(n, core, offs, gated, *rest):
    weights = rest[:n]
    send, keep, part = rest[n:]
    depth = weights[0].shape[1]
    for j in range(n):
        columns = pl.ds(pl.multiple_of(offs[j], depth), depth)
        part[:, columns] = dot(gated[0], weights[j][...]).astype(BF16)
    split_rows(core[0], part, send, keep)


def assemble(core, fresh, mine, theirs, new_own, new_theirs, whole):
    share = mine.shape[1]
    length = new_own.shape[0]
    cores = length // share
    use_fresh = fresh != 0
    for r, source in enumerate((new_own, new_theirs)):
        for owner, landed in ((core, mine), (cores - 1 - core, theirs)):
            inside = pl.multiple_of(owner * share, share)
            rows = source[pl.ds(inside, share), :]
            at = pl.multiple_of(r * length + owner * share, share)
            whole[pl.ds(at, share), :] = jnp.where(use_fresh, rows, landed[r])


def forward_kernel(parts, heads, core, in_offs, offs, fresh, mine, theirs, new_own, new_theirs, keep, *rest):
    in_parts = rest[:parts]
    out_parts = rest[parts:-6]
    send, kept, whole, normed, gated, part = rest[-6:]
    depth = out_parts[0].shape[1]
    head = pl.program_id(0)

    @pl.when(head == 0)
    def _():
        assemble(core[0], fresh[0], mine, theirs, new_own, new_theirs, whole)
        floats = whole[...].astype(F32)
        normed[...] = (floats * row_root(floats)).astype(BF16)

    gated[head] = attend(project(normed, in_offs, in_parts), keep[0])[-1]

    @pl.when(head == heads - 1)
    def _():
        for j in range(len(out_parts)):
            columns = pl.ds(pl.multiple_of(offs[j], depth), depth)
            total = None
            for h in range(heads):
                term = dot(gated[h], out_parts[j][pl.ds(h * HEAD_DIM, HEAD_DIM), :])
                total = term if total is None else total + term
            part[:, columns] = total.astype(BF16)
        split_rows(core[0], part, send, kept)


def backward_kernel(parts, n, tick, core, in_offs, offs, *rest):
    count = 9 + n + parts
    sources, rest = rest[:count], rest[count:]
    send, keep = rest[:2]
    held, (grad_normed, part, sems) = rest[2 : 2 + count], rest[2 + count :]
    ups, gate, vqk, slope, mixed, probs, factor, x_own, x_theirs = held[:9]
    out_parts, in_parts = held[9 : 9 + n], held[9 + n :]
    copies = []
    for i, (source, target) in enumerate(zip(sources, held)):
        if 1 <= i < 9:
            source = source.at[tick]
        copies.append(pltpu.make_async_copy(source, target, sems.at[i]))
    first = [0] + list(range(9, 9 + n))
    second = [1, 4, 2, 5, 6, 3]
    last = list(range(9 + n, count))
    for i in first + second + last + [7, 8]:
        copies[i].start()
    for i in first:
        copies[i].wait()
    depth = out_parts[0].shape[1]
    length = x_own.shape[0]
    wide = 4 * HEAD_DIM
    heads = out_parts[0].shape[0] // HEAD_DIM
    grad_gated = None
    for j in range(n):
        columns = pl.ds(pl.multiple_of(offs[j], depth), depth)
        term = dot_nt(ups[:, columns], out_parts[j][...])
        grad_gated = term if grad_gated is None else grad_gated + term
    grad_gated = grad_gated.astype(BF16).astype(F32)
    for i in second:
        copies[i].wait()
    grads_pre = []
    for h in range(heads):
        cut = slice(h * HEAD_DIM, (h + 1) * HEAD_DIM)
        up = grad_gated[:, cut]
        mixed_h = mixed[:, cut]
        root = row_root(mixed_h)
        normed = mixed_h * root
        grad_n = up * gate[:, cut]
        grad_gate = up * normed
        grad_mixed = root * (grad_n - normed * jnp.mean(grad_n * normed, axis=-1, keepdims=True))
        low = grad_mixed.astype(BF16)
        base = 3 * h * HEAD_DIM
        value = vqk[:, base : base + HEAD_DIM]
        query = vqk[:, base + HEAD_DIM : base + 2 * HEAD_DIM]
        key = vqk[:, base + 2 * HEAD_DIM : base + 3 * HEAD_DIM]
        grad_scores = (dot_nt(low, value) * factor[h]).astype(BF16)
        grad_value = dot_tn(probs[h], low)
        grad_query = dot(grad_scores, key)
        grad_key = dot_tn(grad_scores, query)
        grad_active = jnp.concatenate([grad_gate, grad_value, grad_query, grad_key], axis=1)
        grads_pre.append((grad_active * slope[:, h * wide : (h + 1) * wide]).astype(BF16))
    grad_pre = jnp.concatenate(grads_pre, axis=1)
    for j in range(parts):
        rows_of = in_parts[j].shape[0]
        columns = pl.ds(pl.multiple_of(in_offs[j], rows_of), rows_of)
        copies[last[j]].wait()
        grad_normed[:, columns] = dot_nt(grad_pre, in_parts[j][...])
    for i in (7, 8):
        copies[i].wait()
    for r, source in enumerate((x_own, x_theirs)):
        rows = pl.ds(r * length, length)
        floats = source[...].astype(F32)
        root = row_root(floats)
        scaled = floats * root
        grad_n = grad_normed[rows, :]
        part[rows, :] = (
            root * (grad_n - scaled * jnp.mean(grad_n * scaled, axis=-1, keepdims=True))
        ).astype(BF16)
    split_rows(core[0], part, send, keep)


def pack_kernel(n, offs, gated, up_own, up_theirs, whole, *packs):
    depth = packs[0].shape[1] - 2 * gated.shape[2]
    slab = gated.shape[2]
    length = up_own.shape[0]
    whole[:length, :] = up_own[...]
    whole[length:, :] = up_theirs[...]
    for j in range(1, n):
        pack = packs[j - 1]
        columns = pl.ds(pl.multiple_of(offs[j], depth), depth)
        pack[:, :slab] = gated[1]
        pack[:, slab : 2 * slab] = gated[2]
        pack[:length, 2 * slab :] = up_own[:, columns]
        pack[length:, 2 * slab :] = up_theirs[:, columns]


def settle_kernel(core, fresh, own, theirs, passed, keep, landed, earlier, total, pair):
    share = keep.shape[1]
    here = pl.ds(pl.multiple_of(core[0] * share, share), share)
    for r, source in enumerate((own, theirs)):
        residual = jnp.where(fresh[0] != 0, source[here, :], passed[r])
        total[r] = (
            residual.astype(F32) + keep[r].astype(F32) + landed[r].astype(F32)
        ).astype(BF16)
    pair[0] = earlier[1]
    pair[1] = total[1]


def gather_kernel(n, core, offs, fresh, mine, theirs, new_own, new_theirs, whole, *pieces):
    assemble(core[0], fresh[0], mine, theirs, new_own, new_theirs, whole)
    depth = pieces[0].shape[1]
    for j in range(1, n):
        columns = pl.ds(pl.multiple_of(offs[j], depth), depth)
        pieces[j - 1][...] = whole[:, columns]


def grads_kernel(n, scaling, host, offs, gated, up_0, up_1, *rest):
    packs = rest[: n - 1]
    pieces = rest[n - 1 : 2 * n - 2]
    out = rest[2 * n - 2]
    slab = gated.shape[2]
    depth = out.shape[1]
    at_host = host[0] != 0
    columns = pl.ds(pl.multiple_of(offs[0], depth), depth)

    def product(first, second, third, fourth):
        return dot_tn(first, third) + dot_tn(second, fourth)

    total = product(
        jnp.where(at_host, gated[1], packs[0][:, :slab]),
        jnp.where(at_host, gated[2], packs[0][:, slab : 2 * slab]),
        jnp.where(at_host, up_0[:, columns], packs[0][:, 2 * slab :]),
        jnp.where(at_host, up_1[:, columns], pieces[0][...]),
    )
    for m in range(1, n // 2):
        near, beyond = m, n // 2 + m - 1
        pack = jnp.where(at_host, packs[near][...], packs[beyond][...])
        piece = jnp.where(at_host, pieces[near][...], pieces[beyond][...])
        total = total + product(
            pack[:, :slab], pack[:, slab : 2 * slab], pack[:, 2 * slab :], piece
        )
    out[...] = total * scaling


def after(value, *earlier):
    return lax.optimization_barrier((value,) + earlier)[0]


def block_keep(live_blocks, block_marks):
    length = BLOCKS * BLOCK
    places = jnp.arange(length, dtype=jnp.int32)
    owners = places // BLOCK
    marked = jnp.repeat(jnp.repeat(block_marks, BLOCK, axis=-2), BLOCK, axis=-1) == 1
    allowed = (owners[:, None] == owners[None, :]) | marked
    causal = places[:, None] >= places[None, :]
    tokens = live_blocks[..., None, None] * BLOCK
    keeping = causal & allowed & (places[:, None] < tokens) & (places[None, :] < tokens)
    return jnp.where(keeping, 1.0 / jnp.maximum(tokens, 1).astype(F32), 0.0)


def per_device(
    arrivals,
    in_flight,
    cotangent,
    grad_flight,
    stashed,
    in_weight,
    out_weight,
    forward_blocks,
    backward_blocks,
    forward_marks,
    backward_marks,
):
    section_no = lax.axis_index("section")
    sections = lax.axis_size("section")
    core_no = lax.axis_index("cores")
    cores = lax.axis_size("cores")
    dp_no = lax.axis_index("dp")
    n = lax.axis_size("dp")
    ticks = arrivals.shape[0]
    length = arrivals.shape[1]
    width = arrivals.shape[2]
    rows = 2 * length
    share = length // cores
    in_shard = in_weight[0]
    out_shard = out_weight[0]
    depth = in_shard.shape[0]
    slab = out_shard.shape[0]
    heads = slab // HEAD_DIM
    wide = 4 * HEAD_DIM

    hosts = [2 * k + 1 if 4 * k < n - 2 else 2 * k for k in range(n // 2)]
    host_table = jnp.array(hosts, jnp.int32)
    is_host = dp_no == host_table[dp_no // 2]

    def from_partner(x):
        return lax.ppermute(x, "dp", [(h ^ 1, h) for h in hosts])

    def to_partner(x):
        return lax.ppermute(x, "dp", [(h, h ^ 1) for h in hosts])

    def from_host(x, m):
        return lax.ppermute(x, "dp", [(hosts[k ^ m], hosts[k]) for k in range(n // 2)])

    def to_beyond(x, m):
        return lax.ppermute(
            x, "dp", [(hosts[k ^ m], hosts[k] ^ 1) for k in range(n // 2)]
        )

    def swap_cores(x):
        pairs = [(h * cores + c, (h + 1) * cores - 1 - c) for h in hosts for c in range(cores)]
        return lax.ppermute(x, ("dp", "cores"), pairs)

    def along_sections(x, by):
        pairs = [
            (i * n + h, (i + by) * n + h)
            for i in range(sections)
            if 0 <= i + by < sections
            for h in hosts
        ]
        return lax.ppermute(x, ("section", "dp"), pairs)

    first_section = section_no == 0
    last_section = section_no == sections - 1
    between = range(1, n // 2)

    pieces = max(1, min(2, depth // 256))
    piece = depth // pieces
    in_far = [from_host(in_shard, m) for m in between]
    in_near = [
        from_partner(in_shard[i * piece : (i + 1) * piece]) for i in range(pieces)
    ]
    out_near = from_partner(out_shard)
    in_pass = [from_host(in_near[0], m) for m in between]
    in_far, in_near, rows_in, tables_in = lax.optimization_barrier(
        (
            in_far,
            in_near,
            (arrivals, in_flight, cotangent, grad_flight, stashed),
            (forward_blocks, forward_marks, backward_blocks, backward_marks),
        )
    )
    in_pass += [from_host(in_near[i], m) for i in range(1, pieces) for m in between]
    in_parts = [in_shard] + in_far + in_near + in_pass
    arrivals, in_flight, cotangent, grad_flight, stashed = rows_in
    tables = jnp.concatenate(
        [
            jnp.concatenate([b[..., None], m.reshape(m.shape[:2] + (-1,))], axis=-1)
            for b, m in (tables_in[:2], tables_in[2:])
        ],
        axis=0,
    )
    near_tables = from_partner(tables)
    stash_own = stashed[0]
    stash_theirs = from_partner(stash_own)
    x_own = jnp.where(first_section, arrivals[0], in_flight[0])
    x_theirs = from_partner(x_own)
    up_own = jnp.where(last_section, cotangent[0], grad_flight[0])
    new_own = jnp.where(first_section, arrivals[1], cotangent[1])
    out_own, out_near, near_tables = lax.optimization_barrier((out_shard, out_near, near_tables))
    out_far = [from_host(out_own, m) for m in between]
    out_parts = [out_shard, out_near] + out_far + [from_host(out_near, m) for m in between]
    up_late, new_late, stash_theirs, x_theirs = lax.optimization_barrier(
        (up_own, new_own, stash_theirs, x_theirs)
    )
    up_theirs = from_partner(up_late)
    new_theirs = from_partner(new_late)
    far_hosts = [host_table[(dp_no // 2) ^ m] for m in between]
    owners = [dp_no, dp_no ^ 1] + far_hosts + [h ^ 1 for h in far_hosts]
    offs = jnp.stack(owners).astype(jnp.int32) * depth
    in_offs = [dp_no * depth] + [h * depth for h in far_hosts]
    in_offs += [(dp_no ^ 1) * depth + i * piece for i in range(pieces)]
    in_offs += [(h ^ 1) * depth + i * piece for i in range(pieces) for h in far_hosts]
    in_offs = jnp.stack(in_offs).astype(jnp.int32)
    parts = len(in_parts)
    core = jnp.reshape(core_no, (1,)).astype(jnp.int32)
    first_flag = jnp.reshape(first_section, (1,)).astype(jnp.int32)
    always = jnp.ones((1,), jnp.int32)
    host_flag = jnp.reshape(is_host, (1,)).astype(jnp.int32)
    last_flag = jnp.reshape(last_section, (1,)).astype(jnp.int32)

    both_tables = jnp.stack([tables, near_tables], axis=1)
    ahead_at = sections - 1 - section_no
    chosen = jnp.stack(
        [
            lax.dynamic_index_in_dim(both_tables[way], at, axis=1, keepdims=False)
            for way, at in (
                (0, ahead_at),
                (1, section_no),
                (1, section_no + 1),
                (0, ahead_at + 1),
            )
        ]
    )
    kept = block_keep(chosen[..., 0], chosen[..., 1:].reshape(-1, 2, BLOCKS, BLOCKS))
    blank = jnp.zeros_like(kept[:, 0])
    keep = jnp.concatenate(
        [
            jnp.concatenate([kept[:, 0], blank], axis=2),
            jnp.concatenate([blank, kept[:, 1]], axis=2),
        ],
        axis=1,
    )

    smem = pl.BlockSpec(memory_space=pltpu.SMEM)
    hbm = pl.BlockSpec(memory_space=pl.ANY)

    def all_of(*arrays):
        return [pl.BlockSpec(x.shape, lambda *_, d=x.ndim: (0,) * d) for x in arrays]

    def row_of(x, i):
        return pl.BlockSpec((1,) + x.shape[1:], lambda *_: (i,) + (0,) * (x.ndim - 1))

    params = pltpu.CompilerParams(vmem_limit_bytes=VMEM_BYTES)

    def cost(multiply_adds, bytes_accessed):
        return pl.CostEstimate(
            flops=2 * multiply_adds, bytes_accessed=bytes_accessed, transcendentals=0
        )

    def struct(shape, dtype):
        return jax.ShapeDtypeStruct(shape, dtype)

    halves = [struct((2, share, width), BF16)] * 2
    matmul = rows * width * 4 * slab
    weight_bytes = 2 * width * 5 * slab

    by_head = lambda lead, last: pl.BlockSpec(lead + (last,), lambda h: (0,) * len(lead) + (h,))
    square = pl.BlockSpec((2, 1, rows, rows), lambda h: (0, h, 0, 0))
    gated, gate, vqk, slope, mixed, probs, factor = pl.pallas_call(
        on_host(functools.partial(project_kernel, parts)),
        grid=(heads,),
        in_specs=[smem] * 2
        + all_of(x_own, x_theirs, stash_own, stash_theirs, keep)
        + [by_head((x.shape[0],), wide) for x in in_parts],
        out_specs=[
            by_head((3, rows), HEAD_DIM),
            by_head((2, rows), HEAD_DIM),
            by_head((2, rows), 3 * HEAD_DIM),
            by_head((2, rows), wide),
            by_head((2, rows), HEAD_DIM),
            square,
            square,
        ],
        out_shape=[
            struct((3, rows, slab), BF16),
            struct((2, rows, slab), F32),
            struct((2, rows, 3 * slab), BF16),
            struct((2, rows, 4 * slab), F32),
            struct((2, rows, slab), F32),
            struct((2, heads, rows, rows), BF16),
            struct((2, heads, rows, rows), F32),
        ],
        scratch_shapes=[pltpu.VMEM((3 * rows, width), BF16)],
        compiler_params=params,
        cost_estimate=cost(3 * matmul, 2 * weight_bytes),
        name="project",
    )(host_flag, in_offs, x_own, x_theirs, stash_own, stash_theirs, keep, *in_parts)

    def backward(ups, tick_no):
        layered = [gate, vqk, slope, mixed, probs, factor, stash_own, stash_theirs]
        plain = list(out_parts) + list(in_parts)
        return pl.pallas_call(
            on_host(functools.partial(backward_kernel, parts, n, tick_no)),
            grid=(1,),
            in_specs=[smem] * 4 + [hbm] * (1 + len(layered) + len(plain)),
            out_specs=all_of(*halves),
            out_shape=halves,
            scratch_shapes=[pltpu.VMEM(ups.shape, BF16)]
            + [pltpu.VMEM(x.shape[1:], x.dtype) for x in layered]
            + [pltpu.VMEM(x.shape, x.dtype) for x in plain]
            + [
                pltpu.VMEM((rows, width), F32),
                pltpu.VMEM((rows, width), BF16),
                pltpu.SemaphoreType.DMA((1 + len(layered) + len(plain),)),
            ],
            compiler_params=params,
            cost_estimate=cost(2 * matmul, 2 * weight_bytes),
            name="backward",
        )(host_flag, core, in_offs, offs, ups, *layered, *plain)

    gated, new_theirs = lax.optimization_barrier((gated, new_theirs))

    def summed(residual, mine, landed):
        return (residual.astype(F32) + mine.astype(F32) + landed.astype(F32)).astype(BF16)

    def own_rows(mine, others):
        return lax.dynamic_slice_in_dim(jnp.stack([mine, others]), core_no * share, share, axis=1)

    pack_shapes = [struct((rows, width), BF16)]
    pack_shapes += [struct((rows, 2 * slab + depth), BF16)] * (n - 1)
    up_0, *packs = pl.pallas_call(
        on_host(functools.partial(pack_kernel, n)),
        grid=(1,),
        in_specs=[smem] * 2 + all_of(gated, up_own, up_theirs),
        out_specs=all_of(*pack_shapes),
        out_shape=pack_shapes,
        compiler_params=params,
        name="pack",
    )(host_flag, offs, gated, up_own, up_theirs)
    packs, out_parts = lax.optimization_barrier((packs, out_parts))

    ahead_send, ahead_keep = pl.pallas_call(
        on_host(functools.partial(out_kernel, n)),
        grid=(1,),
        in_specs=[smem] * 3 + [row_of(gated, 0)] + all_of(*out_parts),
        out_specs=all_of(*halves),
        out_shape=halves,
        scratch_shapes=[pltpu.VMEM((rows, width), BF16)],
        compiler_params=params,
        cost_estimate=cost(matmul // 4, weight_bytes // 4),
        name="out",
    )(host_flag, core, offs, gated, *out_parts)
    ahead_0 = summed(own_rows(x_own, x_theirs), ahead_keep, swap_cores(ahead_send))
    ahead_in = along_sections(ahead_0, 1)
    packs_near = [to_partner(packs[0])] + [from_host(packs[m], m) for m in between]
    back_send, back_keep = backward(after(up_0, ahead_0), 0)
    back_send, back_keep, ahead_in, packs_near = lax.optimization_barrier(
        (back_send, back_keep, ahead_in, packs_near)
    )
    back_landed = swap_cores(back_send)
    back_0, first_pair = pl.pallas_call(
        on_host(settle_kernel),
        grid=(1,),
        in_specs=[smem] * 3
        + all_of(up_own, up_theirs, back_keep, back_keep, back_landed, ahead_0),
        out_specs=all_of(*halves),
        out_shape=halves,
        compiler_params=params,
        name="settle",
    )(host_flag, core, always, up_own, up_theirs, back_keep, back_keep, back_landed, ahead_0)
    back_in = along_sections(back_0, -1)
    first_pair = to_partner(first_pair)

    packs_beyond = [to_beyond(packs[n // 2 + m - 1], m) for m in between]
    ahead_their = swap_cores(ahead_in)
    ahead_send, ahead_keep = pl.pallas_call(
        on_host(functools.partial(forward_kernel, parts, heads)),
        grid=(heads,),
        in_specs=[smem] * 5
        + all_of(ahead_in, ahead_their, new_own, new_theirs)
        + [row_of(keep, keep.shape[0] - 1)]
        + [by_head((x.shape[0],), wide) for x in in_parts]
        + all_of(*out_parts),
        out_specs=all_of(*halves),
        out_shape=halves,
        scratch_shapes=[
            pltpu.VMEM((rows, width), BF16),
            pltpu.VMEM((rows, width), BF16),
            pltpu.VMEM((heads, rows, HEAD_DIM), BF16),
            pltpu.VMEM((rows, width), BF16),
        ],
        compiler_params=params,
        cost_estimate=cost(2 * matmul, 2 * weight_bytes),
        name="forward",
    )(host_flag, core,
        in_offs,
        offs,
        first_flag,
        ahead_in,
        ahead_their,
        new_own,
        new_theirs,
        keep,
        *in_parts,
        *out_parts,
    )
    ahead_send, ahead_keep, back_in, packs_beyond, first_pair = lax.optimization_barrier(
        (ahead_send, ahead_keep, back_in, packs_beyond, first_pair)
    )
    new_rows = own_rows(new_own, new_theirs)
    ahead_1 = summed(
        jnp.where(first_section, new_rows, ahead_in), ahead_keep, swap_cores(ahead_send)
    )

    back_their = swap_cores(back_in)
    cut_shapes = [struct((rows, width), BF16)] + [struct((rows, depth), BF16)] * (n - 1)
    up_1, *cuts = pl.pallas_call(
        on_host(functools.partial(gather_kernel, n)),
        grid=(1,),
        in_specs=[smem] * 4 + all_of(back_in, back_their, new_own, new_theirs),
        out_specs=all_of(*cut_shapes),
        out_shape=cut_shapes,
        compiler_params=params,
        name="gather",
    )(host_flag, core, offs, last_flag, back_in, back_their, new_own, new_theirs)
    landed = [to_partner(cuts[0])] + [from_host(cuts[m], m) for m in between]
    landed += [to_beyond(cuts[n // 2 + m - 1], m) for m in between]
    back_send, back_keep = backward(up_1, 1)
    ahead_given = to_partner(ahead_1[1])
    back_send, back_keep, landed, ahead_given = lax.optimization_barrier(
        (back_send, back_keep, landed, ahead_given)
    )
    back_1 = summed(
        jnp.where(last_section, new_rows, back_in), back_keep, swap_cores(back_send)
    )

    grads = pl.pallas_call(
        functools.partial(grads_kernel, n, (ticks * length * n) ** (-0.5)),
        grid=(1,),
        in_specs=[smem] * 2 + all_of(gated, up_0, up_1, *packs_near, *packs_beyond, *landed),
        out_specs=pl.BlockSpec((slab, depth), lambda *_: (0, 0)),
        out_shape=struct((slab, depth), F32),
        compiler_params=params,
        cost_estimate=cost(matmul // 4, weight_bytes // 4),
        name="grads",
    )(
        host_flag, offs, after(gated, back_1), up_0, up_1, *packs_near, *packs_beyond, *landed
    )

    ahead = jnp.stack(
        [
            jnp.where(is_host, ahead_0[0], first_pair[0]),
            jnp.where(is_host, ahead_1[0], ahead_given),
        ]
    )
    back = jnp.stack(
        [
            jnp.where(is_host, back_0[0], first_pair[1]),
            jnp.where(is_host, back_1[0], to_partner(back_1[1])),
        ]
    )
    return (ahead[None], back[None], grads[None])


def solution(mesh):
    in_specs = (
        P(None, "dp", None),
        P("section", "dp", None),
        P(None, "dp", None),
        P("section", "dp", None),
        P("section", None, "dp", None),
        P("section", "dp", "cores"),
        P("section", "cores", "dp"),
        P("dp", None),
        P("dp", None),
        P("dp", None, None, None),
        P("dp", None, None, None),
    )
    out_specs = (
        P("section", None, ("dp", "cores"), None),
        P("section", None, ("dp", "cores"), None),
        P("section", "cores", "dp"),
    )
    return jax.shard_map(
        per_device, mesh=mesh, in_specs=in_specs, out_specs=out_specs, check_vma=False
    )
```

```python
import functools

import jax
import jax.numpy as jnp
from jax import lax
from jax.experimental import pallas as pl
from jax.experimental.pallas import tpu as pltpu
from jax.sharding import PartitionSpec as P

HEAD_DIM = 128
BLOCK = 24
BLOCKS = 4
EPSILON = 1e-06
SCALING = HEAD_DIM ** (-0.5)
VMEM_BYTES = 50 * 1024 * 1024
SMALL_VMEM_BYTES = 16 * 1024 * 1024

F32 = jnp.float32
BF16 = jnp.bfloat16


def on_host(kernel):
    def guarded(host, *refs):
        pl.when(host[0] != 0)(functools.partial(kernel, *refs))

    return guarded


def dot(a, b):
    return lax.dot_general(a, b, (((1,), (0,)), ((), ())), preferred_element_type=F32)


def dot_nt(a, b):
    return lax.dot_general(a, b, (((1,), (1,)), ((), ())), preferred_element_type=F32)


def dot_tn(a, b):
    return lax.dot_general(a, b, (((0,), (0,)), ((), ())), preferred_element_type=F32)


def row_root(floats):
    return lax.rsqrt(jnp.mean(floats * floats, axis=-1, keepdims=True) + EPSILON)


def sigmoid(x):
    return 1.0 / (1.0 + jnp.exp(-x))


def attend(pre, keep):
    sig = sigmoid(pre)
    active = pre * sig
    gate = active[:, :HEAD_DIM]
    vqk = active[:, HEAD_DIM:].astype(BF16)
    value = vqk[:, :HEAD_DIM]
    query = vqk[:, HEAD_DIM : 2 * HEAD_DIM]
    key = vqk[:, 2 * HEAD_DIM :]
    scores = dot_nt(query, key) * SCALING
    sig_s = sigmoid(scores)
    probs = (scores * sig_s * keep).astype(BF16)
    mixed = dot(probs, value)
    gated = (mixed * row_root(mixed) * gate).astype(BF16)
    return sig, gate, vqk, scores, sig_s, probs, mixed, gated


def project(normed, offs, weights):
    total = None
    for j, weight in enumerate(weights):
        depth = weight.shape[0]
        columns = pl.ds(pl.multiple_of(offs[j], depth), depth)
        term = dot(normed[:, columns], weight[...])
        total = term if total is None else total + term
    return total


def project_kernel(parts, offs, x_own, x_theirs, stash_own, stash_theirs, keep, *rest):
    weights = rest[:parts]
    gated_out, gate_out, vqk_out, slope_out, mixed_out, probs_out, factor_out, normed = rest[parts:]
    length = x_own.shape[0]
    rows = 2 * length

    @pl.when(pl.program_id(0) == 0)
    def _():
        sources = [x_own, x_theirs]
        for t in range(stash_own.shape[0]):
            sources += [stash_own.at[t], stash_theirs.at[t]]
        for i, source in enumerate(sources):
            floats = source[...].astype(F32)
            normed[pl.ds(i * length, length), :] = (floats * row_root(floats)).astype(BF16)

    pre_all = project(normed, offs, weights)
    for i in range(1 + stash_own.shape[0]):
        pre = pre_all[i * rows : (i + 1) * rows]
        kept = keep[i]
        sig, gate, vqk, scores, sig_s, probs, mixed, gated = attend(pre, kept)
        gated_out[i] = gated
        if i > 0:
            gate_out[i - 1] = gate
            vqk_out[i - 1] = vqk
            slope_out[i - 1] = sig * (1.0 + pre * (1.0 - sig))
            mixed_out[i - 1] = mixed
            probs_out[i - 1, 0] = probs
            factor_out[i - 1, 0] = kept * sig_s * (1.0 + scores * (1.0 - sig_s)) * SCALING


def split_rows(core, part, send, keep):
    share = send.shape[1]
    cores = part.shape[0] // (2 * share)
    for r in range(2):
        base = r * cores * share
        mine = pl.multiple_of(base + core * share, share)
        other = pl.multiple_of(base + (cores - 1 - core) * share, share)
        send[r] = part[pl.ds(other, share), :]
        keep[r] = part[pl.ds(mine, share), :]


def out_kernel(n, core, offs, gated, *rest):
    weights = rest[:n]
    send, keep, part = rest[n:]
    depth = weights[0].shape[1]
    for j in range(n):
        columns = pl.ds(pl.multiple_of(offs[j], depth), depth)
        part[:, columns] = dot(gated[0], weights[j][...]).astype(BF16)
    split_rows(core[0], part, send, keep)


def assemble(core, fresh, mine, theirs, new_own, new_theirs, whole):
    share = mine.shape[1]
    length = new_own.shape[0]
    cores = length // share
    use_fresh = fresh != 0
    for r, source in enumerate((new_own, new_theirs)):
        for owner, landed in ((core, mine), (cores - 1 - core, theirs)):
            inside = pl.multiple_of(owner * share, share)
            rows = source[pl.ds(inside, share), :]
            at = pl.multiple_of(r * length + owner * share, share)
            whole[pl.ds(at, share), :] = jnp.where(use_fresh, rows, landed[r])


def forward_kernel(parts, heads, core, in_offs, offs, fresh, mine, theirs, new_own, new_theirs, keep, *rest):
    in_parts = rest[:parts]
    out_parts = rest[parts:-6]
    send, kept, whole, normed, gated, part = rest[-6:]
    depth = out_parts[0].shape[1]
    head = pl.program_id(0)

    @pl.when(head == 0)
    def _():
        assemble(core[0], fresh[0], mine, theirs, new_own, new_theirs, whole)
        floats = whole[...].astype(F32)
        normed[...] = (floats * row_root(floats)).astype(BF16)

    gated[head] = attend(project(normed, in_offs, in_parts), keep[0])[-1]

    @pl.when(head == heads - 1)
    def _():
        for j in range(len(out_parts)):
            columns = pl.ds(pl.multiple_of(offs[j], depth), depth)
            total = None
            for h in range(heads):
                term = dot(gated[h], out_parts[j][pl.ds(h * HEAD_DIM, HEAD_DIM), :])
                total = term if total is None else total + term
            part[:, columns] = total.astype(BF16)
        split_rows(core[0], part, send, kept)


def backward_kernel(parts, n, tick, core, in_offs, offs, *rest):
    count = 9 + n + parts
    sources, rest = rest[:count], rest[count:]
    send, keep = rest[:2]
    held, (grad_normed, part, sems) = rest[2 : 2 + count], rest[2 + count :]
    ups, gate, vqk, slope, mixed, probs, factor, x_own, x_theirs = held[:9]
    out_parts, in_parts = held[9 : 9 + n], held[9 + n :]
    copies = []
    for i, (source, target) in enumerate(zip(sources, held)):
        if 1 <= i < 9:
            source = source.at[tick]
        copies.append(pltpu.make_async_copy(source, target, sems.at[i]))
    first = [0] + list(range(9, 9 + n))
    second = [1, 4, 2, 5, 6, 3]
    last = list(range(9 + n, count))
    for i in first + second + last + [7, 8]:
        copies[i].start()
    for i in first:
        copies[i].wait()
    depth = out_parts[0].shape[1]
    length = x_own.shape[0]
    wide = 4 * HEAD_DIM
    heads = out_parts[0].shape[0] // HEAD_DIM
    grad_gated = None
    for j in range(n):
        columns = pl.ds(pl.multiple_of(offs[j], depth), depth)
        term = dot_nt(ups[:, columns], out_parts[j][...])
        grad_gated = term if grad_gated is None else grad_gated + term
    grad_gated = grad_gated.astype(BF16).astype(F32)
    for i in second:
        copies[i].wait()
    grads_pre = []
    for h in range(heads):
        cut = slice(h * HEAD_DIM, (h + 1) * HEAD_DIM)
        up = grad_gated[:, cut]
        mixed_h = mixed[:, cut]
        root = row_root(mixed_h)
        normed = mixed_h * root
        grad_n = up * gate[:, cut]
        grad_gate = up * normed
        grad_mixed = root * (grad_n - normed * jnp.mean(grad_n * normed, axis=-1, keepdims=True))
        low = grad_mixed.astype(BF16)
        base = 3 * h * HEAD_DIM
        value = vqk[:, base : base + HEAD_DIM]
        query = vqk[:, base + HEAD_DIM : base + 2 * HEAD_DIM]
        key = vqk[:, base + 2 * HEAD_DIM : base + 3 * HEAD_DIM]
        grad_scores = (dot_nt(low, value) * factor[h]).astype(BF16)
        grad_value = dot_tn(probs[h], low)
        grad_query = dot(grad_scores, key)
        grad_key = dot_tn(grad_scores, query)
        grad_active = jnp.concatenate([grad_gate, grad_value, grad_query, grad_key], axis=1)
        grads_pre.append((grad_active * slope[:, h * wide : (h + 1) * wide]).astype(BF16))
    grad_pre = jnp.concatenate(grads_pre, axis=1)
    for j in range(parts):
        rows_of = in_parts[j].shape[0]
        columns = pl.ds(pl.multiple_of(in_offs[j], rows_of), rows_of)
        copies[last[j]].wait()
        grad_normed[:, columns] = dot_nt(grad_pre, in_parts[j][...])
    for i in (7, 8):
        copies[i].wait()
    for r, source in enumerate((x_own, x_theirs)):
        rows = pl.ds(r * length, length)
        floats = source[...].astype(F32)
        root = row_root(floats)
        scaled = floats * root
        grad_n = grad_normed[rows, :]
        part[rows, :] = (
            root * (grad_n - scaled * jnp.mean(grad_n * scaled, axis=-1, keepdims=True))
        ).astype(BF16)
    split_rows(core[0], part, send, keep)


def pack_kernel(n, offs, gated, up_own, up_theirs, whole, *packs):
    depth = packs[0].shape[1] - 2 * gated.shape[2]
    slab = gated.shape[2]
    length = up_own.shape[0]
    whole[:length, :] = up_own[...]
    whole[length:, :] = up_theirs[...]
    for j in range(1, n):
        pack = packs[j - 1]
        columns = pl.ds(pl.multiple_of(offs[j], depth), depth)
        pack[:, :slab] = gated[1]
        pack[:, slab : 2 * slab] = gated[2]
        pack[:length, 2 * slab :] = up_own[:, columns]
        pack[length:, 2 * slab :] = up_theirs[:, columns]


def settle_kernel(core, fresh, own, theirs, passed, keep, landed, earlier, total, pair):
    share = keep.shape[1]
    here = pl.ds(pl.multiple_of(core[0] * share, share), share)
    for r, source in enumerate((own, theirs)):
        residual = jnp.where(fresh[0] != 0, source[here, :], passed[r])
        total[r] = (
            residual.astype(F32) + keep[r].astype(F32) + landed[r].astype(F32)
        ).astype(BF16)
    pair[0] = earlier[1]
    pair[1] = total[1]


def gather_kernel(n, core, offs, fresh, mine, theirs, new_own, new_theirs, whole, *pieces):
    assemble(core[0], fresh[0], mine, theirs, new_own, new_theirs, whole)
    depth = pieces[0].shape[1]
    for j in range(1, n):
        columns = pl.ds(pl.multiple_of(offs[j], depth), depth)
        pieces[j - 1][...] = whole[:, columns]


def grads_kernel(n, scaling, host, offs, gated, up_0, up_1, *rest):
    packs = rest[: n - 1]
    pieces = rest[n - 1 : 2 * n - 2]
    out = rest[2 * n - 2]
    slab = gated.shape[2]
    depth = out.shape[1]
    at_host = host[0] != 0
    columns = pl.ds(pl.multiple_of(offs[0], depth), depth)

    def product(first, second, third, fourth):
        return dot_tn(first, third) + dot_tn(second, fourth)

    total = product(
        jnp.where(at_host, gated[1], packs[0][:, :slab]),
        jnp.where(at_host, gated[2], packs[0][:, slab : 2 * slab]),
        jnp.where(at_host, up_0[:, columns], packs[0][:, 2 * slab :]),
        jnp.where(at_host, up_1[:, columns], pieces[0][...]),
    )
    for m in range(1, n // 2):
        near, beyond = m, n // 2 + m - 1
        pack = jnp.where(at_host, packs[near][...], packs[beyond][...])
        piece = jnp.where(at_host, pieces[near][...], pieces[beyond][...])
        total = total + product(
            pack[:, :slab], pack[:, slab : 2 * slab], pack[:, 2 * slab :], piece
        )
    out[...] = total * scaling


def after(value, *earlier):
    return lax.optimization_barrier((value,) + earlier)[0]


def block_keep(live_blocks, block_marks):
    length = BLOCKS * BLOCK
    places = jnp.arange(length, dtype=jnp.int32)
    owners = places // BLOCK
    marked = jnp.repeat(jnp.repeat(block_marks, BLOCK, axis=-2), BLOCK, axis=-1) == 1
    allowed = (owners[:, None] == owners[None, :]) | marked
    causal = places[:, None] >= places[None, :]
    tokens = live_blocks[..., None, None] * BLOCK
    keeping = causal & allowed & (places[:, None] < tokens) & (places[None, :] < tokens)
    return jnp.where(keeping, 1.0 / jnp.maximum(tokens, 1).astype(F32), 0.0)


def per_device(
    arrivals,
    in_flight,
    cotangent,
    grad_flight,
    stashed,
    in_weight,
    out_weight,
    forward_blocks,
    backward_blocks,
    forward_marks,
    backward_marks,
):
    section_no = lax.axis_index("section")
    sections = lax.axis_size("section")
    core_no = lax.axis_index("cores")
    cores = lax.axis_size("cores")
    dp_no = lax.axis_index("dp")
    n = lax.axis_size("dp")
    ticks = arrivals.shape[0]
    length = arrivals.shape[1]
    width = arrivals.shape[2]
    rows = 2 * length
    share = length // cores
    in_shard = in_weight[0]
    out_shard = out_weight[0]
    depth = in_shard.shape[0]
    slab = out_shard.shape[0]
    heads = slab // HEAD_DIM
    wide = 4 * HEAD_DIM

    hosts = [2 * k + 1 if 4 * k < n - 2 else 2 * k for k in range(n // 2)]
    host_table = jnp.array(hosts, jnp.int32)
    is_host = dp_no == host_table[dp_no // 2]

    def from_partner(x):
        return lax.ppermute(x, "dp", [(h ^ 1, h) for h in hosts])

    def to_partner(x):
        return lax.ppermute(x, "dp", [(h, h ^ 1) for h in hosts])

    def from_host(x, m):
        return lax.ppermute(x, "dp", [(hosts[k ^ m], hosts[k]) for k in range(n // 2)])

    def to_beyond(x, m):
        return lax.ppermute(
            x, "dp", [(hosts[k ^ m], hosts[k] ^ 1) for k in range(n // 2)]
        )

    def swap_cores(x):
        return lax.ppermute(x, "cores", [(c, cores - 1 - c) for c in range(cores)])

    def along_sections(x, by):
        pairs = [
            (i * n + h, (i + by) * n + h)
            for i in range(sections)
            if 0 <= i + by < sections
            for h in hosts
        ]
        return lax.ppermute(x, ("section", "dp"), pairs)

    first_section = section_no == 0
    last_section = section_no == sections - 1
    between = range(1, n // 2)

    pieces = max(1, min(2, depth // 256))
    piece = depth // pieces
    in_far = [from_host(in_shard, m) for m in between]
    in_near = [
        from_partner(in_shard[i * piece : (i + 1) * piece]) for i in range(pieces)
    ]
    out_near = from_partner(out_shard)
    in_pass = [from_host(in_near[0], m) for m in between]
    in_far, in_near, rows_in, tables_in = lax.optimization_barrier(
        (
            in_far,
            in_near,
            (arrivals, in_flight, cotangent, grad_flight, stashed),
            (forward_blocks, forward_marks, backward_blocks, backward_marks),
        )
    )
    in_pass += [from_host(in_near[i], m) for i in range(1, pieces) for m in between]
    in_parts = [in_shard] + in_far + in_near + in_pass
    arrivals, in_flight, cotangent, grad_flight, stashed = rows_in
    tables = jnp.concatenate(
        [
            jnp.concatenate([b[..., None], m.reshape(m.shape[:2] + (-1,))], axis=-1)
            for b, m in (tables_in[:2], tables_in[2:])
        ],
        axis=0,
    )
    near_tables = from_partner(tables)
    stash_own = stashed[0]
    stash_theirs = from_partner(stash_own)
    x_own = jnp.where(first_section, arrivals[0], in_flight[0])
    x_theirs = from_partner(x_own)
    up_own = jnp.where(last_section, cotangent[0], grad_flight[0])
    new_own = jnp.where(first_section, arrivals[1], cotangent[1])
    out_own, out_near, near_tables = lax.optimization_barrier((out_shard, out_near, near_tables))
    out_far = [from_host(out_own, m) for m in between]
    out_parts = [out_shard, out_near] + out_far + [from_host(out_near, m) for m in between]
    up_late, new_late, stash_theirs = lax.optimization_barrier((up_own, new_own, stash_theirs))
    up_theirs = from_partner(up_late)
    new_theirs = from_partner(new_late)
    far_hosts = [host_table[(dp_no // 2) ^ m] for m in between]
    owners = [dp_no, dp_no ^ 1] + far_hosts + [h ^ 1 for h in far_hosts]
    offs = jnp.stack(owners).astype(jnp.int32) * depth
    in_offs = [dp_no * depth] + [h * depth for h in far_hosts]
    in_offs += [(dp_no ^ 1) * depth + i * piece for i in range(pieces)]
    in_offs += [(h ^ 1) * depth + i * piece for i in range(pieces) for h in far_hosts]
    in_offs = jnp.stack(in_offs).astype(jnp.int32)
    parts = len(in_parts)
    core = jnp.reshape(core_no, (1,)).astype(jnp.int32)
    first_flag = jnp.reshape(first_section, (1,)).astype(jnp.int32)
    always = jnp.ones((1,), jnp.int32)
    host_flag = jnp.reshape(is_host, (1,)).astype(jnp.int32)
    last_flag = jnp.reshape(last_section, (1,)).astype(jnp.int32)

    both_tables = jnp.stack([tables, near_tables], axis=1)
    ahead_at = sections - 1 - section_no
    chosen = jnp.stack(
        [
            lax.dynamic_index_in_dim(both_tables[way], at, axis=1, keepdims=False)
            for way, at in (
                (0, ahead_at),
                (1, section_no),
                (1, section_no + 1),
                (0, ahead_at + 1),
            )
        ]
    )
    kept = block_keep(chosen[..., 0], chosen[..., 1:].reshape(-1, 2, BLOCKS, BLOCKS))
    blank = jnp.zeros_like(kept[:, 0])
    keep = jnp.concatenate(
        [
            jnp.concatenate([kept[:, 0], blank], axis=2),
            jnp.concatenate([blank, kept[:, 1]], axis=2),
        ],
        axis=1,
    )

    smem = pl.BlockSpec(memory_space=pltpu.SMEM)
    hbm = pl.BlockSpec(memory_space=pl.ANY)

    def all_of(*arrays):
        return [pl.BlockSpec(x.shape, lambda *_, d=x.ndim: (0,) * d) for x in arrays]

    def row_of(x, i):
        return pl.BlockSpec((1,) + x.shape[1:], lambda *_: (i,) + (0,) * (x.ndim - 1))

    params = pltpu.CompilerParams(vmem_limit_bytes=VMEM_BYTES)
    small = pltpu.CompilerParams(vmem_limit_bytes=SMALL_VMEM_BYTES)

    def cost(multiply_adds, bytes_accessed):
        return pl.CostEstimate(
            flops=2 * multiply_adds, bytes_accessed=bytes_accessed, transcendentals=0
        )

    def struct(shape, dtype):
        return jax.ShapeDtypeStruct(shape, dtype)

    halves = [struct((2, share, width), BF16)] * 2
    matmul = rows * width * 4 * slab
    weight_bytes = 2 * width * 5 * slab

    by_head = lambda lead, last: pl.BlockSpec(lead + (last,), lambda h: (0,) * len(lead) + (h,))
    square = pl.BlockSpec((2, 1, rows, rows), lambda h: (0, h, 0, 0))
    gated, gate, vqk, slope, mixed, probs, factor = pl.pallas_call(
        on_host(functools.partial(project_kernel, parts)),
        grid=(heads,),
        in_specs=[smem] * 2
        + all_of(x_own, x_theirs, stash_own, stash_theirs, keep)
        + [by_head((x.shape[0],), wide) for x in in_parts],
        out_specs=[
            by_head((3, rows), HEAD_DIM),
            by_head((2, rows), HEAD_DIM),
            by_head((2, rows), 3 * HEAD_DIM),
            by_head((2, rows), wide),
            by_head((2, rows), HEAD_DIM),
            square,
            square,
        ],
        out_shape=[
            struct((3, rows, slab), BF16),
            struct((2, rows, slab), F32),
            struct((2, rows, 3 * slab), BF16),
            struct((2, rows, 4 * slab), F32),
            struct((2, rows, slab), F32),
            struct((2, heads, rows, rows), BF16),
            struct((2, heads, rows, rows), F32),
        ],
        scratch_shapes=[pltpu.VMEM((3 * rows, width), BF16)],
        compiler_params=params,
        cost_estimate=cost(3 * matmul, 2 * weight_bytes),
        name="project",
    )(host_flag, in_offs, x_own, x_theirs, stash_own, stash_theirs, keep, *in_parts)

    def backward(ups, tick_no):
        layered = [gate, vqk, slope, mixed, probs, factor, stash_own, stash_theirs]
        plain = list(out_parts) + list(in_parts)
        return pl.pallas_call(
            on_host(functools.partial(backward_kernel, parts, n, tick_no)),
            grid=(1,),
            in_specs=[smem] * 4 + [hbm] * (1 + len(layered) + len(plain)),
            out_specs=all_of(*halves),
            out_shape=halves,
            scratch_shapes=[pltpu.VMEM(ups.shape, BF16)]
            + [pltpu.VMEM(x.shape[1:], x.dtype) for x in layered]
            + [pltpu.VMEM(x.shape, x.dtype) for x in plain]
            + [
                pltpu.VMEM((rows, width), F32),
                pltpu.VMEM((rows, width), BF16),
                pltpu.SemaphoreType.DMA((1 + len(layered) + len(plain),)),
            ],
            compiler_params=params,
            cost_estimate=cost(2 * matmul, 2 * weight_bytes),
            name="backward",
        )(host_flag, core, in_offs, offs, ups, *layered, *plain)

    gated, new_theirs = lax.optimization_barrier((gated, new_theirs))

    def summed(residual, mine, landed):
        return (residual.astype(F32) + mine.astype(F32) + landed.astype(F32)).astype(BF16)

    def own_rows(mine, others):
        return lax.dynamic_slice_in_dim(jnp.stack([mine, others]), core_no * share, share, axis=1)

    pack_shapes = [struct((rows, width), BF16)]
    pack_shapes += [struct((rows, 2 * slab + depth), BF16)] * (n - 1)
    up_0, *packs = pl.pallas_call(
        functools.partial(pack_kernel, n),
        grid=(1,),
        in_specs=[smem] * 1 + all_of(gated, up_own, up_theirs),
        out_specs=all_of(*pack_shapes),
        out_shape=pack_shapes,
        compiler_params=small,
        name="pack",
    )(offs, gated, up_own, up_theirs)
    packs, out_parts = lax.optimization_barrier((packs, out_parts))

    ahead_send, ahead_keep = pl.pallas_call(
        functools.partial(out_kernel, n),
        grid=(1,),
        in_specs=[smem] * 2 + [row_of(gated, 0)] + all_of(*out_parts),
        out_specs=all_of(*halves),
        out_shape=halves,
        scratch_shapes=[pltpu.VMEM((rows, width), BF16)],
        compiler_params=small,
        cost_estimate=cost(matmul // 4, weight_bytes // 4),
        name="out",
    )(core, offs, gated, *out_parts)
    ahead_0 = summed(own_rows(x_own, x_theirs), ahead_keep, swap_cores(ahead_send))
    ahead_in = along_sections(ahead_0, 1)
    packs_near = [to_partner(packs[0])] + [from_host(packs[m], m) for m in between]
    back_send, back_keep = backward(after(up_0, ahead_0), 0)
    back_send, back_keep, ahead_in, packs_near = lax.optimization_barrier(
        (back_send, back_keep, ahead_in, packs_near)
    )
    back_landed = swap_cores(back_send)
    back_0, first_pair = pl.pallas_call(
        settle_kernel,
        grid=(1,),
        in_specs=[smem] * 2
        + all_of(up_own, up_theirs, back_keep, back_keep, back_landed, ahead_0),
        out_specs=all_of(*halves),
        out_shape=halves,
        compiler_params=small,
        name="settle",
    )(core, always, up_own, up_theirs, back_keep, back_keep, back_landed, ahead_0)
    back_in = along_sections(back_0, -1)
    first_pair = to_partner(first_pair)

    packs_beyond = [to_beyond(packs[n // 2 + m - 1], m) for m in between]
    ahead_their = swap_cores(ahead_in)
    ahead_send, ahead_keep = pl.pallas_call(
        on_host(functools.partial(forward_kernel, parts, heads)),
        grid=(heads,),
        in_specs=[smem] * 5
        + all_of(ahead_in, ahead_their, new_own, new_theirs)
        + [row_of(keep, keep.shape[0] - 1)]
        + [by_head((x.shape[0],), wide) for x in in_parts]
        + all_of(*out_parts),
        out_specs=all_of(*halves),
        out_shape=halves,
        scratch_shapes=[
            pltpu.VMEM((rows, width), BF16),
            pltpu.VMEM((rows, width), BF16),
            pltpu.VMEM((heads, rows, HEAD_DIM), BF16),
            pltpu.VMEM((rows, width), BF16),
        ],
        compiler_params=params,
        cost_estimate=cost(2 * matmul, 2 * weight_bytes),
        name="forward",
    )(host_flag, core,
        in_offs,
        offs,
        first_flag,
        ahead_in,
        ahead_their,
        new_own,
        new_theirs,
        keep,
        *in_parts,
        *out_parts,
    )
    ahead_send, ahead_keep, back_in, packs_beyond, first_pair = lax.optimization_barrier(
        (ahead_send, ahead_keep, back_in, packs_beyond, first_pair)
    )
    new_rows = own_rows(new_own, new_theirs)
    ahead_1 = summed(
        jnp.where(first_section, new_rows, ahead_in), ahead_keep, swap_cores(ahead_send)
    )

    back_their = swap_cores(back_in)
    cut_shapes = [struct((rows, width), BF16)] + [struct((rows, depth), BF16)] * (n - 1)
    up_1, *cuts = pl.pallas_call(
        functools.partial(gather_kernel, n),
        grid=(1,),
        in_specs=[smem] * 3 + all_of(back_in, back_their, new_own, new_theirs),
        out_specs=all_of(*cut_shapes),
        out_shape=cut_shapes,
        compiler_params=small,
        name="gather",
    )(core, offs, last_flag, back_in, back_their, new_own, new_theirs)
    landed = [to_partner(cuts[0])] + [from_host(cuts[m], m) for m in between]
    landed += [to_beyond(cuts[n // 2 + m - 1], m) for m in between]
    back_send, back_keep = backward(up_1, 1)
    ahead_given = to_partner(ahead_1[1])
    back_send, back_keep, landed, ahead_given = lax.optimization_barrier(
        (back_send, back_keep, landed, ahead_given)
    )
    back_1 = summed(
        jnp.where(last_section, new_rows, back_in), back_keep, swap_cores(back_send)
    )

    grads = pl.pallas_call(
        functools.partial(grads_kernel, n, (ticks * length * n) ** (-0.5)),
        grid=(1,),
        in_specs=[smem] * 2 + all_of(gated, up_0, up_1, *packs_near, *packs_beyond, *landed),
        out_specs=pl.BlockSpec((slab, depth), lambda *_: (0, 0)),
        out_shape=struct((slab, depth), F32),
        compiler_params=small,
        cost_estimate=cost(matmul // 4, weight_bytes // 4),
        name="grads",
    )(
        host_flag, offs, after(gated, back_1), up_0, up_1, *packs_near, *packs_beyond, *landed
    )

    ahead = jnp.stack(
        [
            jnp.where(is_host, ahead_0[0], first_pair[0]),
            jnp.where(is_host, ahead_1[0], ahead_given),
        ]
    )
    back = jnp.stack(
        [
            jnp.where(is_host, back_0[0], first_pair[1]),
            jnp.where(is_host, back_1[0], to_partner(back_1[1])),
        ]
    )
    return (ahead[None], back[None], grads[None])


def solution(mesh):
    in_specs = (
        P(None, "dp", None),
        P("section", "dp", None),
        P(None, "dp", None),
        P("section", "dp", None),
        P("section", None, "dp", None),
        P("section", "dp", "cores"),
        P("section", "cores", "dp"),
        P("dp", None),
        P("dp", None),
        P("dp", None, None, None),
        P("dp", None, None, None),
    )
    out_specs = (
        P("section", None, ("dp", "cores"), None),
        P("section", None, ("dp", "cores"), None),
        P("section", "cores", "dp"),
    )
    return jax.shard_map(
        per_device, mesh=mesh, in_specs=in_specs, out_specs=out_specs, check_vma=False
    )
```

```python
import functools

import jax
import jax.numpy as jnp
from jax import lax
from jax.experimental import pallas as pl
from jax.experimental.pallas import tpu as pltpu
from jax.sharding import PartitionSpec as P

HEAD_DIM = 128
BLOCK = 24
BLOCKS = 4
EPSILON = 1e-06
SCALING = HEAD_DIM ** (-0.5)
VMEM_BYTES = 50 * 1024 * 1024
SMALL_VMEM_BYTES = 16 * 1024 * 1024

F32 = jnp.float32
BF16 = jnp.bfloat16


def on_host(kernel):
    def guarded(host, *refs):
        pl.when(host[0] != 0)(functools.partial(kernel, *refs))

    return guarded


def dot(a, b):
    return lax.dot_general(a, b, (((1,), (0,)), ((), ())), preferred_element_type=F32)


def dot_nt(a, b):
    return lax.dot_general(a, b, (((1,), (1,)), ((), ())), preferred_element_type=F32)


def dot_tn(a, b):
    return lax.dot_general(a, b, (((0,), (0,)), ((), ())), preferred_element_type=F32)


def row_root(floats):
    return lax.rsqrt(jnp.mean(floats * floats, axis=-1, keepdims=True) + EPSILON)


def sigmoid(x):
    return 1.0 / (1.0 + jnp.exp(-x))


def attend(pre, keep):
    sig = sigmoid(pre)
    active = pre * sig
    gate = active[:, :HEAD_DIM]
    vqk = active[:, HEAD_DIM:].astype(BF16)
    value = vqk[:, :HEAD_DIM]
    query = vqk[:, HEAD_DIM : 2 * HEAD_DIM]
    key = vqk[:, 2 * HEAD_DIM :]
    scores = dot_nt(query, key) * SCALING
    sig_s = sigmoid(scores)
    probs = (scores * sig_s * keep).astype(BF16)
    mixed = dot(probs, value)
    gated = (mixed * row_root(mixed) * gate).astype(BF16)
    return sig, gate, vqk, scores, sig_s, probs, mixed, gated


def project(normed, offs, weights):
    total = None
    for j, weight in enumerate(weights):
        depth = weight.shape[0]
        columns = pl.ds(pl.multiple_of(offs[j], depth), depth)
        term = dot(normed[:, columns], weight[...])
        total = term if total is None else total + term
    return total


def project_kernel(parts, offs, x_own, x_theirs, stash_own, stash_theirs, keep, *rest):
    weights = rest[:parts]
    gated_out, gate_out, vqk_out, slope_out, mixed_out, probs_out, factor_out, normed = rest[parts:]
    length = x_own.shape[0]
    rows = 2 * length

    @pl.when(pl.program_id(0) == 0)
    def _():
        sources = [x_own, x_theirs]
        for t in range(stash_own.shape[0]):
            sources += [stash_own.at[t], stash_theirs.at[t]]
        for i, source in enumerate(sources):
            floats = source[...].astype(F32)
            normed[pl.ds(i * length, length), :] = (floats * row_root(floats)).astype(BF16)

    pre_all = project(normed, offs, weights)
    for i in range(1 + stash_own.shape[0]):
        pre = pre_all[i * rows : (i + 1) * rows]
        kept = keep[i]
        sig, gate, vqk, scores, sig_s, probs, mixed, gated = attend(pre, kept)
        gated_out[i] = gated
        if i > 0:
            gate_out[i - 1] = gate
            vqk_out[i - 1] = vqk
            slope_out[i - 1] = sig * (1.0 + pre * (1.0 - sig))
            mixed_out[i - 1] = mixed
            probs_out[i - 1, 0] = probs
            factor_out[i - 1, 0] = kept * sig_s * (1.0 + scores * (1.0 - sig_s)) * SCALING


def split_rows(core, part, send, keep):
    share = send.shape[1]
    cores = part.shape[0] // (2 * share)
    for r in range(2):
        base = r * cores * share
        mine = pl.multiple_of(base + core * share, share)
        other = pl.multiple_of(base + (cores - 1 - core) * share, share)
        send[r] = part[pl.ds(other, share), :]
        keep[r] = part[pl.ds(mine, share), :]


def out_kernel(n, core, offs, gated, *rest):
    weights = rest[:n]
    send, keep, part = rest[n:]
    depth = weights[0].shape[1]
    for j in range(n):
        columns = pl.ds(pl.multiple_of(offs[j], depth), depth)
        part[:, columns] = dot(gated[0], weights[j][...]).astype(BF16)
    split_rows(core[0], part, send, keep)


def assemble(core, fresh, mine, theirs, new_own, new_theirs, whole):
    share = mine.shape[1]
    length = new_own.shape[0]
    cores = length // share
    use_fresh = fresh != 0
    for r, source in enumerate((new_own, new_theirs)):
        for owner, landed in ((core, mine), (cores - 1 - core, theirs)):
            inside = pl.multiple_of(owner * share, share)
            rows = source[pl.ds(inside, share), :]
            at = pl.multiple_of(r * length + owner * share, share)
            whole[pl.ds(at, share), :] = jnp.where(use_fresh, rows, landed[r])


def forward_kernel(parts, heads, core, in_offs, offs, fresh, mine, theirs, new_own, new_theirs, keep, *rest):
    in_parts = rest[:parts]
    out_parts = rest[parts:-6]
    send, kept, whole, normed, gated, part = rest[-6:]
    depth = out_parts[0].shape[1]
    head = pl.program_id(0)

    @pl.when(head == 0)
    def _():
        assemble(core[0], fresh[0], mine, theirs, new_own, new_theirs, whole)
        floats = whole[...].astype(F32)
        normed[...] = (floats * row_root(floats)).astype(BF16)

    gated[head] = attend(project(normed, in_offs, in_parts), keep[0])[-1]

    @pl.when(head == heads - 1)
    def _():
        for j in range(len(out_parts)):
            columns = pl.ds(pl.multiple_of(offs[j], depth), depth)
            total = None
            for h in range(heads):
                term = dot(gated[h], out_parts[j][pl.ds(h * HEAD_DIM, HEAD_DIM), :])
                total = term if total is None else total + term
            part[:, columns] = total.astype(BF16)
        split_rows(core[0], part, send, kept)


def backward_kernel(parts, n, tick, core, in_offs, offs, *rest):
    count = 9 + n + parts
    sources, rest = rest[:count], rest[count:]
    send, keep = rest[:2]
    held, (grad_normed, part, sems) = rest[2 : 2 + count], rest[2 + count :]
    ups, gate, vqk, slope, mixed, probs, factor, x_own, x_theirs = held[:9]
    out_parts, in_parts = held[9 : 9 + n], held[9 + n :]
    wide = 4 * HEAD_DIM
    heads = out_parts[0].shape[0] // HEAD_DIM
    copies = []
    for i, (source, target) in enumerate(zip(sources[: 9 + n], held[: 9 + n])):
        if 1 <= i < 9:
            source = source.at[tick]
        copies.append(pltpu.make_async_copy(source, target, sems.at[i]))
    by_head = []
    for h in range(heads):
        of_head = slice(h * wide, (h + 1) * wide)
        by_head.append(
            [
                pltpu.make_async_copy(
                    sources[9 + n + j].at[:, of_head],
                    in_parts[j].at[:, of_head],
                    sems.at[9 + n + h * parts + j],
                )
                for j in range(parts)
            ]
        )
    first = [0] + list(range(9, 9 + n))
    second = [1, 4, 2, 5, 6, 3]
    for i in first + second:
        copies[i].start()
    for of_head in by_head:
        for copy in of_head:
            copy.start()
    for i in (7, 8):
        copies[i].start()
    for i in first:
        copies[i].wait()
    depth = out_parts[0].shape[1]
    length = x_own.shape[0]
    grad_gated = None
    for j in range(n):
        columns = pl.ds(pl.multiple_of(offs[j], depth), depth)
        term = dot_nt(ups[:, columns], out_parts[j][...])
        grad_gated = term if grad_gated is None else grad_gated + term
    grad_gated = grad_gated.astype(BF16).astype(F32)
    for i in second:
        copies[i].wait()

    def through_head(h):
        cut = slice(h * HEAD_DIM, (h + 1) * HEAD_DIM)
        up = grad_gated[:, cut]
        mixed_h = mixed[:, cut]
        root = row_root(mixed_h)
        normed = mixed_h * root
        grad_n = up * gate[:, cut]
        grad_gate = up * normed
        grad_mixed = root * (grad_n - normed * jnp.mean(grad_n * normed, axis=-1, keepdims=True))
        low = grad_mixed.astype(BF16)
        base = 3 * h * HEAD_DIM
        value = vqk[:, base : base + HEAD_DIM]
        query = vqk[:, base + HEAD_DIM : base + 2 * HEAD_DIM]
        key = vqk[:, base + 2 * HEAD_DIM : base + 3 * HEAD_DIM]
        grad_scores = (dot_nt(low, value) * factor[h]).astype(BF16)
        grad_value = dot_tn(probs[h], low)
        grad_query = dot(grad_scores, key)
        grad_key = dot_tn(grad_scores, query)
        grad_active = jnp.concatenate([grad_gate, grad_value, grad_query, grad_key], axis=1)
        return (grad_active * slope[:, h * wide : (h + 1) * wide]).astype(BF16)

    grad_pre = through_head(0)
    for h in range(heads):
        for copy in by_head[h]:
            copy.wait()
        following = through_head(h + 1) if h + 1 < heads else None
        for j in range(parts):
            rows_of = in_parts[j].shape[0]
            columns = pl.ds(pl.multiple_of(in_offs[j], rows_of), rows_of)
            term = dot_nt(grad_pre, in_parts[j][:, h * wide : (h + 1) * wide])
            if h == 0:
                grad_normed[:, columns] = term
            else:
                grad_normed[:, columns] += term
        grad_pre = following
    for i in (7, 8):
        copies[i].wait()
    for r, source in enumerate((x_own, x_theirs)):
        rows = pl.ds(r * length, length)
        floats = source[...].astype(F32)
        root = row_root(floats)
        scaled = floats * root
        grad_n = grad_normed[rows, :]
        part[rows, :] = (
            root * (grad_n - scaled * jnp.mean(grad_n * scaled, axis=-1, keepdims=True))
        ).astype(BF16)
    split_rows(core[0], part, send, keep)


def pack_kernel(n, offs, gated, up_own, up_theirs, whole, *packs):
    depth = packs[0].shape[1] - 2 * gated.shape[2]
    slab = gated.shape[2]
    length = up_own.shape[0]
    whole[:length, :] = up_own[...]
    whole[length:, :] = up_theirs[...]
    for j in range(1, n):
        pack = packs[j - 1]
        columns = pl.ds(pl.multiple_of(offs[j], depth), depth)
        pack[:, :slab] = gated[1]
        pack[:, slab : 2 * slab] = gated[2]
        pack[:length, 2 * slab :] = up_own[:, columns]
        pack[length:, 2 * slab :] = up_theirs[:, columns]


def settle_kernel(core, fresh, own, theirs, passed, keep, landed, earlier, total, pair):
    share = keep.shape[1]
    here = pl.ds(pl.multiple_of(core[0] * share, share), share)
    for r, source in enumerate((own, theirs)):
        residual = jnp.where(fresh[0] != 0, source[here, :], passed[r])
        total[r] = (
            residual.astype(F32) + keep[r].astype(F32) + landed[r].astype(F32)
        ).astype(BF16)
    pair[0] = earlier[1]
    pair[1] = total[1]


def gather_kernel(n, core, offs, fresh, mine, theirs, new_own, new_theirs, whole, *pieces):
    assemble(core[0], fresh[0], mine, theirs, new_own, new_theirs, whole)
    depth = pieces[0].shape[1]
    for j in range(1, n):
        columns = pl.ds(pl.multiple_of(offs[j], depth), depth)
        pieces[j - 1][...] = whole[:, columns]


def grads_kernel(n, scaling, host, offs, gated, up_0, up_1, *rest):
    packs = rest[: n - 1]
    pieces = rest[n - 1 : 2 * n - 2]
    out = rest[2 * n - 2]
    slab = gated.shape[2]
    depth = out.shape[1]
    at_host = host[0] != 0
    columns = pl.ds(pl.multiple_of(offs[0], depth), depth)

    def product(first, second, third, fourth):
        return dot_tn(first, third) + dot_tn(second, fourth)

    total = product(
        jnp.where(at_host, gated[1], packs[0][:, :slab]),
        jnp.where(at_host, gated[2], packs[0][:, slab : 2 * slab]),
        jnp.where(at_host, up_0[:, columns], packs[0][:, 2 * slab :]),
        jnp.where(at_host, up_1[:, columns], pieces[0][...]),
    )
    for m in range(1, n // 2):
        near, beyond = m, n // 2 + m - 1
        pack = jnp.where(at_host, packs[near][...], packs[beyond][...])
        piece = jnp.where(at_host, pieces[near][...], pieces[beyond][...])
        total = total + product(
            pack[:, :slab], pack[:, slab : 2 * slab], pack[:, 2 * slab :], piece
        )
    out[...] = total * scaling


def after(value, *earlier):
    return lax.optimization_barrier((value,) + earlier)[0]


def block_keep(live_blocks, block_marks):
    length = BLOCKS * BLOCK
    places = jnp.arange(length, dtype=jnp.int32)
    owners = places // BLOCK
    marked = jnp.repeat(jnp.repeat(block_marks, BLOCK, axis=-2), BLOCK, axis=-1) == 1
    allowed = (owners[:, None] == owners[None, :]) | marked
    causal = places[:, None] >= places[None, :]
    tokens = live_blocks[..., None, None] * BLOCK
    keeping = causal & allowed & (places[:, None] < tokens) & (places[None, :] < tokens)
    return jnp.where(keeping, 1.0 / jnp.maximum(tokens, 1).astype(F32), 0.0)


def per_device(
    arrivals,
    in_flight,
    cotangent,
    grad_flight,
    stashed,
    in_weight,
    out_weight,
    forward_blocks,
    backward_blocks,
    forward_marks,
    backward_marks,
):
    section_no = lax.axis_index("section")
    sections = lax.axis_size("section")
    core_no = lax.axis_index("cores")
    cores = lax.axis_size("cores")
    dp_no = lax.axis_index("dp")
    n = lax.axis_size("dp")
    ticks = arrivals.shape[0]
    length = arrivals.shape[1]
    width = arrivals.shape[2]
    rows = 2 * length
    share = length // cores
    in_shard = in_weight[0]
    out_shard = out_weight[0]
    depth = in_shard.shape[0]
    slab = out_shard.shape[0]
    heads = slab // HEAD_DIM
    wide = 4 * HEAD_DIM

    hosts = [2 * k + 1 if 4 * k < n - 2 else 2 * k for k in range(n // 2)]
    host_table = jnp.array(hosts, jnp.int32)
    is_host = dp_no == host_table[dp_no // 2]

    def from_partner(x):
        return lax.ppermute(x, "dp", [(h ^ 1, h) for h in hosts])

    def to_partner(x):
        return lax.ppermute(x, "dp", [(h, h ^ 1) for h in hosts])

    def from_host(x, m):
        return lax.ppermute(x, "dp", [(hosts[k ^ m], hosts[k]) for k in range(n // 2)])

    def to_beyond(x, m):
        return lax.ppermute(
            x, "dp", [(hosts[k ^ m], hosts[k] ^ 1) for k in range(n // 2)]
        )

    def swap_cores(x):
        return lax.ppermute(x, "cores", [(c, cores - 1 - c) for c in range(cores)])

    def along_sections(x, by):
        pairs = [
            (i * n + h, (i + by) * n + h)
            for i in range(sections)
            if 0 <= i + by < sections
            for h in hosts
        ]
        return lax.ppermute(x, ("section", "dp"), pairs)

    first_section = section_no == 0
    last_section = section_no == sections - 1
    between = range(1, n // 2)

    pieces = max(1, min(2, depth // 256))
    piece = depth // pieces
    in_far = [from_host(in_shard, m) for m in between]
    in_near = [
        from_partner(in_shard[i * piece : (i + 1) * piece]) for i in range(pieces)
    ]
    out_near = from_partner(out_shard)
    in_pass = [from_host(in_near[0], m) for m in between]
    in_far, in_near, rows_in, tables_in = lax.optimization_barrier(
        (
            in_far,
            in_near,
            (arrivals, in_flight, cotangent, grad_flight, stashed),
            (forward_blocks, forward_marks, backward_blocks, backward_marks),
        )
    )
    in_pass += [from_host(in_near[i], m) for i in range(1, pieces) for m in between]
    in_parts = [in_shard] + in_far + in_near + in_pass
    arrivals, in_flight, cotangent, grad_flight, stashed = rows_in
    tables = jnp.concatenate(
        [
            jnp.concatenate([b[..., None], m.reshape(m.shape[:2] + (-1,))], axis=-1)
            for b, m in (tables_in[:2], tables_in[2:])
        ],
        axis=0,
    )
    near_tables = from_partner(tables)
    stash_own = stashed[0]
    stash_theirs = from_partner(stash_own)
    x_own = jnp.where(first_section, arrivals[0], in_flight[0])
    x_theirs = from_partner(x_own)
    up_own = jnp.where(last_section, cotangent[0], grad_flight[0])
    new_own = jnp.where(first_section, arrivals[1], cotangent[1])
    out_own, out_near, near_tables = lax.optimization_barrier((out_shard, out_near, near_tables))
    out_far = [from_host(out_own, m) for m in between]
    out_parts = [out_shard, out_near] + out_far + [from_host(out_near, m) for m in between]
    up_late, new_late, stash_theirs = lax.optimization_barrier((up_own, new_own, stash_theirs))
    up_theirs = from_partner(up_late)
    new_theirs = from_partner(new_late)
    far_hosts = [host_table[(dp_no // 2) ^ m] for m in between]
    owners = [dp_no, dp_no ^ 1] + far_hosts + [h ^ 1 for h in far_hosts]
    offs = jnp.stack(owners).astype(jnp.int32) * depth
    in_offs = [dp_no * depth] + [h * depth for h in far_hosts]
    in_offs += [(dp_no ^ 1) * depth + i * piece for i in range(pieces)]
    in_offs += [(h ^ 1) * depth + i * piece for i in range(pieces) for h in far_hosts]
    in_offs = jnp.stack(in_offs).astype(jnp.int32)
    parts = len(in_parts)
    core = jnp.reshape(core_no, (1,)).astype(jnp.int32)
    first_flag = jnp.reshape(first_section, (1,)).astype(jnp.int32)
    host_flag = jnp.reshape(is_host, (1,)).astype(jnp.int32)
    last_flag = jnp.reshape(last_section, (1,)).astype(jnp.int32)

    both_tables = jnp.stack([tables, near_tables], axis=1)
    ahead_at = sections - 1 - section_no
    chosen = jnp.stack(
        [
            lax.dynamic_index_in_dim(both_tables[way], at, axis=1, keepdims=False)
            for way, at in (
                (0, ahead_at),
                (1, section_no),
                (1, section_no + 1),
                (0, ahead_at + 1),
            )
        ]
    )
    kept = block_keep(chosen[..., 0], chosen[..., 1:].reshape(-1, 2, BLOCKS, BLOCKS))
    blank = jnp.zeros_like(kept[:, 0])
    keep = jnp.concatenate(
        [
            jnp.concatenate([kept[:, 0], blank], axis=2),
            jnp.concatenate([blank, kept[:, 1]], axis=2),
        ],
        axis=1,
    )

    smem = pl.BlockSpec(memory_space=pltpu.SMEM)
    hbm = pl.BlockSpec(memory_space=pl.ANY)

    def all_of(*arrays):
        return [pl.BlockSpec(x.shape, lambda *_, d=x.ndim: (0,) * d) for x in arrays]

    def row_of(x, i):
        return pl.BlockSpec((1,) + x.shape[1:], lambda *_: (i,) + (0,) * (x.ndim - 1))

    params = pltpu.CompilerParams(vmem_limit_bytes=VMEM_BYTES)
    small = pltpu.CompilerParams(vmem_limit_bytes=SMALL_VMEM_BYTES)

    def cost(multiply_adds, bytes_accessed):
        return pl.CostEstimate(
            flops=2 * multiply_adds, bytes_accessed=bytes_accessed, transcendentals=0
        )

    def struct(shape, dtype):
        return jax.ShapeDtypeStruct(shape, dtype)

    halves = [struct((2, share, width), BF16)] * 2
    matmul = rows * width * 4 * slab
    weight_bytes = 2 * width * 5 * slab

    by_head = lambda lead, last: pl.BlockSpec(lead + (last,), lambda h: (0,) * len(lead) + (h,))
    square = pl.BlockSpec((2, 1, rows, rows), lambda h: (0, h, 0, 0))
    gated, gate, vqk, slope, mixed, probs, factor = pl.pallas_call(
        on_host(functools.partial(project_kernel, parts)),
        grid=(heads,),
        in_specs=[smem] * 2
        + all_of(x_own, x_theirs, stash_own, stash_theirs, keep)
        + [by_head((x.shape[0],), wide) for x in in_parts],
        out_specs=[
            by_head((3, rows), HEAD_DIM),
            by_head((2, rows), HEAD_DIM),
            by_head((2, rows), 3 * HEAD_DIM),
            by_head((2, rows), wide),
            by_head((2, rows), HEAD_DIM),
            square,
            square,
        ],
        out_shape=[
            struct((3, rows, slab), BF16),
            struct((2, rows, slab), F32),
            struct((2, rows, 3 * slab), BF16),
            struct((2, rows, 4 * slab), F32),
            struct((2, rows, slab), F32),
            struct((2, heads, rows, rows), BF16),
            struct((2, heads, rows, rows), F32),
        ],
        scratch_shapes=[pltpu.VMEM((3 * rows, width), BF16)],
        compiler_params=params,
        cost_estimate=cost(3 * matmul, 2 * weight_bytes),
        name="project",
    )(host_flag, in_offs, x_own, x_theirs, stash_own, stash_theirs, keep, *in_parts)

    def backward(ups, tick_no):
        layered = [gate, vqk, slope, mixed, probs, factor, stash_own, stash_theirs]
        plain = list(out_parts) + list(in_parts)
        return pl.pallas_call(
            on_host(functools.partial(backward_kernel, parts, n, tick_no)),
            grid=(1,),
            in_specs=[smem] * 4 + [hbm] * (1 + len(layered) + len(plain)),
            out_specs=all_of(*halves),
            out_shape=halves,
            scratch_shapes=[pltpu.VMEM(ups.shape, BF16)]
            + [pltpu.VMEM(x.shape[1:], x.dtype) for x in layered]
            + [pltpu.VMEM(x.shape, x.dtype) for x in plain]
            + [
                pltpu.VMEM((rows, width), F32),
                pltpu.VMEM((rows, width), BF16),
                pltpu.SemaphoreType.DMA((1 + len(layered) + n + heads * parts,)),
            ],
            compiler_params=params,
            cost_estimate=cost(2 * matmul, 2 * weight_bytes),
            name="backward",
        )(host_flag, core, in_offs, offs, ups, *layered, *plain)

    gated, new_theirs = lax.optimization_barrier((gated, new_theirs))

    def summed(residual, mine, landed):
        return (residual.astype(F32) + mine.astype(F32) + landed.astype(F32)).astype(BF16)

    def own_rows(mine, others):
        return lax.dynamic_slice_in_dim(jnp.stack([mine, others]), core_no * share, share, axis=1)

    pack_shapes = [struct((rows, width), BF16)]
    pack_shapes += [struct((rows, 2 * slab + depth), BF16)] * (n - 1)
    up_0, *packs = pl.pallas_call(
        functools.partial(pack_kernel, n),
        grid=(1,),
        in_specs=[smem] * 1 + all_of(gated, up_own, up_theirs),
        out_specs=all_of(*pack_shapes),
        out_shape=pack_shapes,
        compiler_params=small,
        name="pack",
    )(offs, gated, up_own, up_theirs)
    packs, out_parts = lax.optimization_barrier((packs, out_parts))

    ahead_send, ahead_keep = pl.pallas_call(
        functools.partial(out_kernel, n),
        grid=(1,),
        in_specs=[smem] * 2 + [row_of(gated, 0)] + all_of(*out_parts),
        out_specs=all_of(*halves),
        out_shape=halves,
        scratch_shapes=[pltpu.VMEM((rows, width), BF16)],
        compiler_params=small,
        cost_estimate=cost(matmul // 4, weight_bytes // 4),
        name="out",
    )(core, offs, gated, *out_parts)
    ahead_0 = summed(own_rows(x_own, x_theirs), ahead_keep, swap_cores(ahead_send))
    ahead_in = along_sections(ahead_0, 1)
    packs_near = [to_partner(packs[0])] + [from_host(packs[m], m) for m in between]
    back_send, back_keep = backward(after(up_0, ahead_0), 0)
    ahead_given = to_partner(ahead_0[1])
    back_send, back_keep, ahead_in, packs_near, ahead_given = lax.optimization_barrier(
        (back_send, back_keep, ahead_in, packs_near, ahead_given)
    )
    back_landed = swap_cores(back_send)
    back_0 = summed(own_rows(up_own, up_theirs), back_keep, back_landed)
    back_in = along_sections(back_0, -1)

    packs_beyond = [to_beyond(packs[n // 2 + m - 1], m) for m in between]
    ahead_their = swap_cores(ahead_in)
    ahead_send, ahead_keep = pl.pallas_call(
        on_host(functools.partial(forward_kernel, parts, heads)),
        grid=(heads,),
        in_specs=[smem] * 5
        + all_of(ahead_in, ahead_their, new_own, new_theirs)
        + [row_of(keep, keep.shape[0] - 1)]
        + [by_head((x.shape[0],), wide) for x in in_parts]
        + all_of(*out_parts),
        out_specs=all_of(*halves),
        out_shape=halves,
        scratch_shapes=[
            pltpu.VMEM((rows, width), BF16),
            pltpu.VMEM((rows, width), BF16),
            pltpu.VMEM((heads, rows, HEAD_DIM), BF16),
            pltpu.VMEM((rows, width), BF16),
        ],
        compiler_params=params,
        cost_estimate=cost(2 * matmul, 2 * weight_bytes),
        name="forward",
    )(host_flag, core,
        in_offs,
        offs,
        first_flag,
        ahead_in,
        ahead_their,
        new_own,
        new_theirs,
        keep,
        *in_parts,
        *out_parts,
    )
    ahead_send, ahead_keep, back_in, packs_beyond = lax.optimization_barrier(
        (ahead_send, ahead_keep, back_in, packs_beyond)
    )
    new_rows = own_rows(new_own, new_theirs)
    ahead_landed = swap_cores(ahead_send)
    ahead_1, pair = pl.pallas_call(
        settle_kernel,
        grid=(1,),
        in_specs=[smem] * 2
        + all_of(new_own, new_theirs, ahead_in, ahead_keep, ahead_landed, back_0),
        out_specs=all_of(*halves),
        out_shape=halves,
        compiler_params=small,
        name="settle",
    )(core, first_flag, new_own, new_theirs, ahead_in, ahead_keep, ahead_landed, back_0)

    back_their = swap_cores(back_in)
    cut_shapes = [struct((rows, width), BF16)] + [struct((rows, depth), BF16)] * (n - 1)
    up_1, *cuts = pl.pallas_call(
        functools.partial(gather_kernel, n),
        grid=(1,),
        in_specs=[smem] * 3 + all_of(back_in, back_their, new_own, new_theirs),
        out_specs=all_of(*cut_shapes),
        out_shape=cut_shapes,
        compiler_params=small,
        name="gather",
    )(core, offs, last_flag, back_in, back_their, new_own, new_theirs)
    landed = [to_partner(cuts[0])] + [from_host(cuts[m], m) for m in between]
    landed += [to_beyond(cuts[n // 2 + m - 1], m) for m in between]
    back_send, back_keep = backward(up_1, 1)
    pair = to_partner(pair)
    back_send, back_keep, landed, pair = lax.optimization_barrier(
        (back_send, back_keep, landed, pair)
    )
    back_1 = summed(
        jnp.where(last_section, new_rows, back_in), back_keep, swap_cores(back_send)
    )

    grads = pl.pallas_call(
        functools.partial(grads_kernel, n, (ticks * length * n) ** (-0.5)),
        grid=(1,),
        in_specs=[smem] * 2 + all_of(gated, up_0, up_1, *packs_near, *packs_beyond, *landed),
        out_specs=pl.BlockSpec((slab, depth), lambda *_: (0, 0)),
        out_shape=struct((slab, depth), F32),
        compiler_params=small,
        cost_estimate=cost(matmul // 4, weight_bytes // 4),
        name="grads",
    )(
        host_flag, offs, after(gated, back_1), up_0, up_1, *packs_near, *packs_beyond, *landed
    )

    ahead_given, pair = lax.optimization_barrier((ahead_given, pair, back_1))[:2]
    ahead = jnp.stack(
        [
            jnp.where(is_host, ahead_0[0], ahead_given),
            jnp.where(is_host, ahead_1[0], pair[1]),
        ]
    )
    back = jnp.stack(
        [
            jnp.where(is_host, back_0[0], pair[0]),
            jnp.where(is_host, back_1[0], to_partner(back_1[1])),
        ]
    )
    return (ahead[None], back[None], grads[None])


def solution(mesh):
    in_specs = (
        P(None, "dp", None),
        P("section", "dp", None),
        P(None, "dp", None),
        P("section", "dp", None),
        P("section", None, "dp", None),
        P("section", "dp", "cores"),
        P("section", "cores", "dp"),
        P("dp", None),
        P("dp", None),
        P("dp", None, None, None),
        P("dp", None, None, None),
    )
    out_specs = (
        P("section", None, ("dp", "cores"), None),
        P("section", None, ("dp", "cores"), None),
        P("section", "cores", "dp"),
    )
    return jax.shard_map(
        per_device, mesh=mesh, in_specs=in_specs, out_specs=out_specs, check_vma=False
    )
```

```python
import functools

import jax
import jax.numpy as jnp
from jax import lax
from jax.experimental import pallas as pl
from jax.experimental.pallas import tpu as pltpu
from jax.sharding import PartitionSpec as P

HEAD_DIM = 128
BLOCK = 24
BLOCKS = 4
EPSILON = 1e-06
SCALING = HEAD_DIM ** (-0.5)
VMEM_BYTES = 50 * 1024 * 1024
SMALL_VMEM_BYTES = 16 * 1024 * 1024

F32 = jnp.float32
BF16 = jnp.bfloat16


def on_host(kernel):
    def guarded(host, *refs):
        pl.when(host[0] != 0)(functools.partial(kernel, *refs))

    return guarded


def dot(a, b):
    return lax.dot_general(a, b, (((1,), (0,)), ((), ())), preferred_element_type=F32)


def dot_nt(a, b):
    return lax.dot_general(a, b, (((1,), (1,)), ((), ())), preferred_element_type=F32)


def dot_tn(a, b):
    return lax.dot_general(a, b, (((0,), (0,)), ((), ())), preferred_element_type=F32)


def row_root(floats):
    return lax.rsqrt(jnp.mean(floats * floats, axis=-1, keepdims=True) + EPSILON)


def sigmoid(x):
    return 1.0 / (1.0 + jnp.exp(-x))


def attend(pre, keep):
    sig = sigmoid(pre)
    active = pre * sig
    gate = active[:, :HEAD_DIM]
    vqk = active[:, HEAD_DIM:].astype(BF16)
    value = vqk[:, :HEAD_DIM]
    query = vqk[:, HEAD_DIM : 2 * HEAD_DIM]
    key = vqk[:, 2 * HEAD_DIM :]
    scores = dot_nt(query, key) * SCALING
    sig_s = sigmoid(scores)
    probs = (scores * sig_s * keep).astype(BF16)
    mixed = dot(probs, value)
    gated = (mixed * row_root(mixed) * gate).astype(BF16)
    return sig, gate, vqk, scores, sig_s, probs, mixed, gated


def project(normed, offs, weights):
    total = None
    for j, weight in enumerate(weights):
        depth = weight.shape[0]
        columns = pl.ds(pl.multiple_of(offs[j], depth), depth)
        term = dot(normed[:, columns], weight[...])
        total = term if total is None else total + term
    return total


def project_kernel(parts, offs, x_own, x_theirs, stash_own, stash_theirs, keep, *rest):
    weights = rest[:parts]
    gated_out, gate_out, vqk_out, slope_out, mixed_out, probs_out, factor_out, normed = rest[parts:]
    length = x_own.shape[0]
    rows = 2 * length

    @pl.when(pl.program_id(0) == 0)
    def _():
        sources = [x_own, x_theirs]
        for t in range(stash_own.shape[0]):
            sources += [stash_own.at[t], stash_theirs.at[t]]
        for i, source in enumerate(sources):
            floats = source[...].astype(F32)
            normed[pl.ds(i * length, length), :] = (floats * row_root(floats)).astype(BF16)

    pre_all = project(normed, offs, weights)
    for i in range(1 + stash_own.shape[0]):
        pre = pre_all[i * rows : (i + 1) * rows]
        kept = keep[i]
        sig, gate, vqk, scores, sig_s, probs, mixed, gated = attend(pre, kept)
        gated_out[i] = gated
        if i > 0:
            gate_out[i - 1] = gate
            vqk_out[i - 1] = vqk
            slope_out[i - 1] = sig * (1.0 + pre * (1.0 - sig))
            mixed_out[i - 1] = mixed
            probs_out[i - 1, 0] = probs
            factor_out[i - 1, 0] = kept * sig_s * (1.0 + scores * (1.0 - sig_s)) * SCALING


def split_rows(core, part, send, keep):
    share = send.shape[1]
    cores = part.shape[0] // (2 * share)
    for r in range(2):
        base = r * cores * share
        mine = pl.multiple_of(base + core * share, share)
        other = pl.multiple_of(base + (cores - 1 - core) * share, share)
        send[r] = part[pl.ds(other, share), :]
        keep[r] = part[pl.ds(mine, share), :]


def out_kernel(n, core, offs, gated, *rest):
    weights = rest[:n]
    send, keep, part = rest[n:]
    depth = weights[0].shape[1]
    for j in range(n):
        columns = pl.ds(pl.multiple_of(offs[j], depth), depth)
        part[:, columns] = dot(gated[0], weights[j][...]).astype(BF16)
    split_rows(core[0], part, send, keep)


def assemble(core, fresh, mine, theirs, new_own, new_theirs, whole):
    share = mine.shape[1]
    length = new_own.shape[0]
    cores = length // share
    use_fresh = fresh != 0
    for r, source in enumerate((new_own, new_theirs)):
        for owner, landed in ((core, mine), (cores - 1 - core, theirs)):
            inside = pl.multiple_of(owner * share, share)
            rows = source[pl.ds(inside, share), :]
            at = pl.multiple_of(r * length + owner * share, share)
            whole[pl.ds(at, share), :] = jnp.where(use_fresh, rows, landed[r])


def forward_kernel(parts, heads, core, in_offs, offs, fresh, mine, theirs, new_own, new_theirs, keep, *rest):
    in_parts = rest[:parts]
    out_parts = rest[parts:-6]
    send, kept, whole, normed, gated, part = rest[-6:]
    depth = out_parts[0].shape[1]
    head = pl.program_id(0)

    @pl.when(head == 0)
    def _():
        assemble(core[0], fresh[0], mine, theirs, new_own, new_theirs, whole)
        floats = whole[...].astype(F32)
        normed[...] = (floats * row_root(floats)).astype(BF16)

    gated[head] = attend(project(normed, in_offs, in_parts), keep[0])[-1]

    @pl.when(head == heads - 1)
    def _():
        for j in range(len(out_parts)):
            columns = pl.ds(pl.multiple_of(offs[j], depth), depth)
            total = None
            for h in range(heads):
                term = dot(gated[h], out_parts[j][pl.ds(h * HEAD_DIM, HEAD_DIM), :])
                total = term if total is None else total + term
            part[:, columns] = total.astype(BF16)
        split_rows(core[0], part, send, kept)


def backward_kernel(parts, n, tick, core, in_offs, offs, *rest):
    count = 9 + n + parts
    sources, rest = rest[:count], rest[count:]
    send, keep = rest[:2]
    held, (grad_normed, part, sems) = rest[2 : 2 + count], rest[2 + count :]
    ups, gate, vqk, slope, mixed, probs, factor, x_own, x_theirs = held[:9]
    out_parts, in_parts = held[9 : 9 + n], held[9 + n :]
    wide = 4 * HEAD_DIM
    heads = out_parts[0].shape[0] // HEAD_DIM
    copies = []
    for i, (source, target) in enumerate(zip(sources[: 9 + n], held[: 9 + n])):
        if 1 <= i < 9:
            source = source.at[tick]
        copies.append(pltpu.make_async_copy(source, target, sems.at[i]))
    by_head = []
    for h in range(heads):
        of_head = slice(h * wide, (h + 1) * wide)
        by_head.append(
            [
                pltpu.make_async_copy(
                    sources[9 + n + j].at[:, of_head],
                    in_parts[j].at[:, of_head],
                    sems.at[9 + n + h * parts + j],
                )
                for j in range(parts)
            ]
        )
    first = [0] + list(range(9, 9 + n))
    second = [1, 4, 2, 5, 6, 3]
    for i in first + second:
        copies[i].start()
    for of_head in by_head:
        for copy in of_head:
            copy.start()
    for i in (7, 8):
        copies[i].start()
    for i in first:
        copies[i].wait()
    depth = out_parts[0].shape[1]
    length = x_own.shape[0]
    grad_gated = None
    for j in range(n):
        columns = pl.ds(pl.multiple_of(offs[j], depth), depth)
        term = dot_nt(ups[:, columns], out_parts[j][...])
        grad_gated = term if grad_gated is None else grad_gated + term
    grad_gated = grad_gated.astype(BF16).astype(F32)
    for i in second:
        copies[i].wait()

    def through_head(h):
        cut = slice(h * HEAD_DIM, (h + 1) * HEAD_DIM)
        up = grad_gated[:, cut]
        mixed_h = mixed[:, cut]
        root = row_root(mixed_h)
        normed = mixed_h * root
        grad_n = up * gate[:, cut]
        grad_gate = up * normed
        grad_mixed = root * (grad_n - normed * jnp.mean(grad_n * normed, axis=-1, keepdims=True))
        low = grad_mixed.astype(BF16)
        base = 3 * h * HEAD_DIM
        value = vqk[:, base : base + HEAD_DIM]
        query = vqk[:, base + HEAD_DIM : base + 2 * HEAD_DIM]
        key = vqk[:, base + 2 * HEAD_DIM : base + 3 * HEAD_DIM]
        grad_scores = (dot_nt(low, value) * factor[h]).astype(BF16)
        grad_value = dot_tn(probs[h], low)
        grad_query = dot(grad_scores, key)
        grad_key = dot_tn(grad_scores, query)
        grad_active = jnp.concatenate([grad_gate, grad_value, grad_query, grad_key], axis=1)
        return (grad_active * slope[:, h * wide : (h + 1) * wide]).astype(BF16)

    grad_pre = through_head(0)
    for h in range(heads):
        for copy in by_head[h]:
            copy.wait()
        following = through_head(h + 1) if h + 1 < heads else None
        for j in range(parts):
            rows_of = in_parts[j].shape[0]
            columns = pl.ds(pl.multiple_of(in_offs[j], rows_of), rows_of)
            term = dot_nt(grad_pre, in_parts[j][:, h * wide : (h + 1) * wide])
            if h == 0:
                grad_normed[:, columns] = term
            else:
                grad_normed[:, columns] += term
        grad_pre = following
    for i in (7, 8):
        copies[i].wait()
    for r, source in enumerate((x_own, x_theirs)):
        rows = pl.ds(r * length, length)
        floats = source[...].astype(F32)
        root = row_root(floats)
        scaled = floats * root
        grad_n = grad_normed[rows, :]
        part[rows, :] = (
            root * (grad_n - scaled * jnp.mean(grad_n * scaled, axis=-1, keepdims=True))
        ).astype(BF16)
    split_rows(core[0], part, send, keep)


def pack_kernel(n, offs, gated, up_own, up_theirs, whole, *packs):
    depth = packs[-1].shape[1] - 2 * gated.shape[2]
    slab = gated.shape[2]
    length = up_own.shape[0]
    whole[:length, :] = up_own[...]
    whole[length:, :] = up_theirs[...]
    for j in range(1, n):
        pack = packs[j - 1]
        columns = pl.ds(pl.multiple_of(offs[j], depth), depth)
        pack[:, :slab] = gated[1]
        pack[:, slab : 2 * slab] = gated[2]
        if j > 1:
            pack[:length, 2 * slab :] = up_own[:, columns]
            pack[length:, 2 * slab :] = up_theirs[:, columns]


def settle_kernel(core, fresh, own, theirs, passed, keep, landed, total, other):
    share = keep.shape[1]
    here = pl.ds(pl.multiple_of(core[0] * share, share), share)
    for r, source in enumerate((own, theirs)):
        residual = jnp.where(fresh[0] != 0, source[here, :], passed[r])
        total[r] = (
            residual.astype(F32) + keep[r].astype(F32) + landed[r].astype(F32)
        ).astype(BF16)
    other[...] = total[1]


def gather_kernel(n, core, offs, fresh, mine, theirs, new_own, new_theirs, whole, *pieces):
    assemble(core[0], fresh[0], mine, theirs, new_own, new_theirs, whole)
    depth = pieces[0].shape[1]
    for j in range(1, n):
        columns = pl.ds(pl.multiple_of(offs[j], depth), depth)
        pieces[j - 1][...] = whole[:, columns]


def grads_kernel(n, scaling, host, offs, gated, up_0, up_1, up_own, up_near, *rest):
    packs = rest[: n - 1]
    pieces = rest[n - 1 : 2 * n - 2]
    out = rest[2 * n - 2]
    slab = gated.shape[2]
    depth = out.shape[1]
    at_host = host[0] != 0
    columns = pl.ds(pl.multiple_of(offs[0], depth), depth)

    def product(first, second, third, fourth):
        return dot_tn(first, third) + dot_tn(second, fourth)

    up_pair = jnp.concatenate([up_near[...], up_own[:, columns]], axis=0)
    total = product(
        jnp.where(at_host, gated[1], packs[0][:, :slab]),
        jnp.where(at_host, gated[2], packs[0][:, slab : 2 * slab]),
        jnp.where(at_host, up_0[:, columns], up_pair),
        jnp.where(at_host, up_1[:, columns], pieces[0][...]),
    )
    for m in range(1, n // 2):
        near, beyond = m, n // 2 + m - 1
        pack = jnp.where(at_host, packs[near][...], packs[beyond][...])
        piece = jnp.where(at_host, pieces[near][...], pieces[beyond][...])
        total = total + product(
            pack[:, :slab], pack[:, slab : 2 * slab], pack[:, 2 * slab :], piece
        )
    out[...] = total * scaling


def after(value, *earlier):
    return lax.optimization_barrier((value,) + earlier)[0]


def block_keep(live_blocks, block_marks):
    length = BLOCKS * BLOCK
    places = jnp.arange(length, dtype=jnp.int32)
    owners = places // BLOCK
    marked = jnp.repeat(jnp.repeat(block_marks, BLOCK, axis=-2), BLOCK, axis=-1) == 1
    allowed = (owners[:, None] == owners[None, :]) | marked
    causal = places[:, None] >= places[None, :]
    tokens = live_blocks[..., None, None] * BLOCK
    keeping = causal & allowed & (places[:, None] < tokens) & (places[None, :] < tokens)
    return jnp.where(keeping, 1.0 / jnp.maximum(tokens, 1).astype(F32), 0.0)


def per_device(
    arrivals,
    in_flight,
    cotangent,
    grad_flight,
    stashed,
    in_weight,
    out_weight,
    forward_blocks,
    backward_blocks,
    forward_marks,
    backward_marks,
):
    section_no = lax.axis_index("section")
    sections = lax.axis_size("section")
    core_no = lax.axis_index("cores")
    cores = lax.axis_size("cores")
    dp_no = lax.axis_index("dp")
    n = lax.axis_size("dp")
    ticks = arrivals.shape[0]
    length = arrivals.shape[1]
    width = arrivals.shape[2]
    rows = 2 * length
    share = length // cores
    in_shard = in_weight[0]
    out_shard = out_weight[0]
    depth = in_shard.shape[0]
    slab = out_shard.shape[0]
    heads = slab // HEAD_DIM
    wide = 4 * HEAD_DIM

    hosts = [2 * k + 1 if 4 * k < n - 2 else 2 * k for k in range(n // 2)]
    host_table = jnp.array(hosts, jnp.int32)
    is_host = dp_no == host_table[dp_no // 2]

    def from_partner(x):
        return lax.ppermute(x, "dp", [(h ^ 1, h) for h in hosts])

    def to_partner(x):
        return lax.ppermute(x, "dp", [(h, h ^ 1) for h in hosts])

    def from_host(x, m):
        return lax.ppermute(x, "dp", [(hosts[k ^ m], hosts[k]) for k in range(n // 2)])

    def to_beyond(x, m):
        return lax.ppermute(
            x, "dp", [(hosts[k ^ m], hosts[k] ^ 1) for k in range(n // 2)]
        )

    def swap_cores(x):
        return lax.ppermute(x, "cores", [(c, cores - 1 - c) for c in range(cores)])

    def along_sections(x, by):
        pairs = [
            (i * n + h, (i + by) * n + h)
            for i in range(sections)
            if 0 <= i + by < sections
            for h in hosts
        ]
        return lax.ppermute(x, ("section", "dp"), pairs)

    first_section = section_no == 0
    last_section = section_no == sections - 1
    between = range(1, n // 2)

    pieces = max(1, min(2, depth // 256))
    piece = depth // pieces
    in_far = [from_host(in_shard, m) for m in between]
    in_near = [
        from_partner(in_shard[i * piece : (i + 1) * piece]) for i in range(pieces)
    ]
    out_near = from_partner(out_shard)
    in_pass = [from_host(in_near[0], m) for m in between]
    in_far, in_near, rows_in, tables_in = lax.optimization_barrier(
        (
            in_far,
            in_near,
            (arrivals, in_flight, cotangent, grad_flight, stashed),
            (forward_blocks, forward_marks, backward_blocks, backward_marks),
        )
    )
    in_pass += [from_host(in_near[i], m) for i in range(1, pieces) for m in between]
    in_parts = [in_shard] + in_far + in_near + in_pass
    arrivals, in_flight, cotangent, grad_flight, stashed = rows_in
    tables = jnp.concatenate(
        [
            jnp.concatenate([b[..., None], m.reshape(m.shape[:2] + (-1,))], axis=-1)
            for b, m in (tables_in[:2], tables_in[2:])
        ],
        axis=0,
    )
    near_tables = from_partner(tables)
    stash_own = stashed[0]
    stash_theirs = from_partner(stash_own)
    x_own = jnp.where(first_section, arrivals[0], in_flight[0])
    x_theirs = from_partner(x_own)
    up_own = jnp.where(last_section, cotangent[0], grad_flight[0])
    new_own = jnp.where(first_section, arrivals[1], cotangent[1])
    out_own, out_near, near_tables = lax.optimization_barrier((out_shard, out_near, near_tables))
    out_far = [from_host(out_own, m) for m in between]
    out_parts = [out_shard, out_near] + out_far + [from_host(out_near, m) for m in between]
    up_late, new_late, stash_theirs = lax.optimization_barrier((up_own, new_own, stash_theirs))
    up_theirs = from_partner(up_late)
    up_near = to_partner(
        lax.dynamic_slice_in_dim(up_late, (dp_no ^ 1) * depth, depth, axis=1)
    )
    new_theirs = from_partner(new_late)
    far_hosts = [host_table[(dp_no // 2) ^ m] for m in between]
    owners = [dp_no, dp_no ^ 1] + far_hosts + [h ^ 1 for h in far_hosts]
    offs = jnp.stack(owners).astype(jnp.int32) * depth
    in_offs = [dp_no * depth] + [h * depth for h in far_hosts]
    in_offs += [(dp_no ^ 1) * depth + i * piece for i in range(pieces)]
    in_offs += [(h ^ 1) * depth + i * piece for i in range(pieces) for h in far_hosts]
    in_offs = jnp.stack(in_offs).astype(jnp.int32)
    parts = len(in_parts)
    core = jnp.reshape(core_no, (1,)).astype(jnp.int32)
    first_flag = jnp.reshape(first_section, (1,)).astype(jnp.int32)
    host_flag = jnp.reshape(is_host, (1,)).astype(jnp.int32)
    last_flag = jnp.reshape(last_section, (1,)).astype(jnp.int32)

    both_tables = jnp.stack([tables, near_tables], axis=1)
    ahead_at = sections - 1 - section_no
    chosen = jnp.stack(
        [
            lax.dynamic_index_in_dim(both_tables[way], at, axis=1, keepdims=False)
            for way, at in (
                (0, ahead_at),
                (1, section_no),
                (1, section_no + 1),
                (0, ahead_at + 1),
            )
        ]
    )
    kept = block_keep(chosen[..., 0], chosen[..., 1:].reshape(-1, 2, BLOCKS, BLOCKS))
    blank = jnp.zeros_like(kept[:, 0])
    keep = jnp.concatenate(
        [
            jnp.concatenate([kept[:, 0], blank], axis=2),
            jnp.concatenate([blank, kept[:, 1]], axis=2),
        ],
        axis=1,
    )

    smem = pl.BlockSpec(memory_space=pltpu.SMEM)
    hbm = pl.BlockSpec(memory_space=pl.ANY)

    def all_of(*arrays):
        return [pl.BlockSpec(x.shape, lambda *_, d=x.ndim: (0,) * d) for x in arrays]

    def row_of(x, i):
        return pl.BlockSpec((1,) + x.shape[1:], lambda *_: (i,) + (0,) * (x.ndim - 1))

    params = pltpu.CompilerParams(vmem_limit_bytes=VMEM_BYTES)
    small = pltpu.CompilerParams(vmem_limit_bytes=SMALL_VMEM_BYTES)

    def cost(multiply_adds, bytes_accessed):
        return pl.CostEstimate(
            flops=2 * multiply_adds, bytes_accessed=bytes_accessed, transcendentals=0
        )

    def struct(shape, dtype):
        return jax.ShapeDtypeStruct(shape, dtype)

    halves = [struct((2, share, width), BF16)] * 2
    matmul = rows * width * 4 * slab
    weight_bytes = 2 * width * 5 * slab

    by_head = lambda lead, last: pl.BlockSpec(lead + (last,), lambda h: (0,) * len(lead) + (h,))
    square = pl.BlockSpec((2, 1, rows, rows), lambda h: (0, h, 0, 0))
    gated, gate, vqk, slope, mixed, probs, factor = pl.pallas_call(
        on_host(functools.partial(project_kernel, parts)),
        grid=(heads,),
        in_specs=[smem] * 2
        + all_of(x_own, x_theirs, stash_own, stash_theirs, keep)
        + [by_head((x.shape[0],), wide) for x in in_parts],
        out_specs=[
            by_head((3, rows), HEAD_DIM),
            by_head((2, rows), HEAD_DIM),
            by_head((2, rows), 3 * HEAD_DIM),
            by_head((2, rows), wide),
            by_head((2, rows), HEAD_DIM),
            square,
            square,
        ],
        out_shape=[
            struct((3, rows, slab), BF16),
            struct((2, rows, slab), F32),
            struct((2, rows, 3 * slab), BF16),
            struct((2, rows, 4 * slab), F32),
            struct((2, rows, slab), F32),
            struct((2, heads, rows, rows), BF16),
            struct((2, heads, rows, rows), F32),
        ],
        scratch_shapes=[pltpu.VMEM((3 * rows, width), BF16)],
        compiler_params=params,
        cost_estimate=cost(3 * matmul, 2 * weight_bytes),
        name="project",
    )(host_flag, in_offs, x_own, x_theirs, stash_own, stash_theirs, keep, *in_parts)

    def backward(ups, tick_no):
        layered = [gate, vqk, slope, mixed, probs, factor, stash_own, stash_theirs]
        plain = list(out_parts) + list(in_parts)
        return pl.pallas_call(
            on_host(functools.partial(backward_kernel, parts, n, tick_no)),
            grid=(1,),
            in_specs=[smem] * 4 + [hbm] * (1 + len(layered) + len(plain)),
            out_specs=all_of(*halves),
            out_shape=halves,
            scratch_shapes=[pltpu.VMEM(ups.shape, BF16)]
            + [pltpu.VMEM(x.shape[1:], x.dtype) for x in layered]
            + [pltpu.VMEM(x.shape, x.dtype) for x in plain]
            + [
                pltpu.VMEM((rows, width), F32),
                pltpu.VMEM((rows, width), BF16),
                pltpu.SemaphoreType.DMA((1 + len(layered) + n + heads * parts,)),
            ],
            compiler_params=params,
            cost_estimate=cost(2 * matmul, 2 * weight_bytes),
            name="backward",
        )(host_flag, core, in_offs, offs, ups, *layered, *plain)

    gated, new_theirs, up_near = lax.optimization_barrier((gated, new_theirs, up_near))

    def summed(residual, mine, landed):
        return (residual.astype(F32) + mine.astype(F32) + landed.astype(F32)).astype(BF16)

    def own_rows(mine, others):
        return lax.dynamic_slice_in_dim(jnp.stack([mine, others]), core_no * share, share, axis=1)

    pack_shapes = [struct((rows, width), BF16)]
    pack_shapes += [struct((rows, 2 * slab), BF16)]
    pack_shapes += [struct((rows, 2 * slab + depth), BF16)] * (n - 2)
    up_0, *packs = pl.pallas_call(
        functools.partial(pack_kernel, n),
        grid=(1,),
        in_specs=[smem] * 1 + all_of(gated, up_own, up_theirs),
        out_specs=all_of(*pack_shapes),
        out_shape=pack_shapes,
        compiler_params=small,
        name="pack",
    )(offs, gated, up_own, up_theirs)
    packs, out_parts = lax.optimization_barrier((packs, out_parts))

    ahead_send, ahead_keep = pl.pallas_call(
        functools.partial(out_kernel, n),
        grid=(1,),
        in_specs=[smem] * 2 + [row_of(gated, 0)] + all_of(*out_parts),
        out_specs=all_of(*halves),
        out_shape=halves,
        scratch_shapes=[pltpu.VMEM((rows, width), BF16)],
        compiler_params=small,
        cost_estimate=cost(matmul // 4, weight_bytes // 4),
        name="out",
    )(core, offs, gated, *out_parts)
    ahead_0 = summed(own_rows(x_own, x_theirs), ahead_keep, swap_cores(ahead_send))
    ahead_in = along_sections(ahead_0, 1)
    packs_near = [to_partner(packs[0])] + [from_host(packs[m], m) for m in between]
    back_send, back_keep = backward(after(up_0, ahead_0), 0)
    ahead_given = to_partner(ahead_0[1])
    back_send, back_keep, ahead_in, packs_near, ahead_given = lax.optimization_barrier(
        (back_send, back_keep, ahead_in, packs_near, ahead_given)
    )
    back_landed = swap_cores(back_send)
    back_0 = summed(own_rows(up_own, up_theirs), back_keep, back_landed)
    back_in = along_sections(back_0, -1)

    packs_beyond = [to_beyond(packs[n // 2 + m - 1], m) for m in between]
    ahead_their = swap_cores(ahead_in)
    ahead_send, ahead_keep = pl.pallas_call(
        on_host(functools.partial(forward_kernel, parts, heads)),
        grid=(heads,),
        in_specs=[smem] * 5
        + all_of(ahead_in, ahead_their, new_own, new_theirs)
        + [row_of(keep, keep.shape[0] - 1)]
        + [by_head((x.shape[0],), wide) for x in in_parts]
        + all_of(*out_parts),
        out_specs=all_of(*halves),
        out_shape=halves,
        scratch_shapes=[
            pltpu.VMEM((rows, width), BF16),
            pltpu.VMEM((rows, width), BF16),
            pltpu.VMEM((heads, rows, HEAD_DIM), BF16),
            pltpu.VMEM((rows, width), BF16),
        ],
        compiler_params=params,
        cost_estimate=cost(2 * matmul, 2 * weight_bytes),
        name="forward",
    )(host_flag, core,
        in_offs,
        offs,
        first_flag,
        ahead_in,
        ahead_their,
        new_own,
        new_theirs,
        keep,
        *in_parts,
        *out_parts,
    )
    new_rows = own_rows(new_own, new_theirs)
    ahead_landed = swap_cores(ahead_send)
    settled = [halves[0], struct((share, width), BF16)]
    ahead_1, ahead_other = pl.pallas_call(
        settle_kernel,
        grid=(1,),
        in_specs=[smem] * 2
        + all_of(new_own, new_theirs, ahead_in, ahead_keep, ahead_landed),
        out_specs=all_of(*settled),
        out_shape=settled,
        compiler_params=small,
        name="settle",
    )(core, first_flag, new_own, new_theirs, ahead_in, ahead_keep, ahead_landed)
    back_given = to_partner(back_0[1])
    ahead_1, ahead_other, back_in, packs_beyond, back_given = lax.optimization_barrier(
        (ahead_1, ahead_other, back_in, packs_beyond, back_given)
    )

    back_their = swap_cores(back_in)
    cut_shapes = [struct((rows, width), BF16)] + [struct((rows, depth), BF16)] * (n - 1)
    up_1, *cuts = pl.pallas_call(
        functools.partial(gather_kernel, n),
        grid=(1,),
        in_specs=[smem] * 3 + all_of(back_in, back_their, new_own, new_theirs),
        out_specs=all_of(*cut_shapes),
        out_shape=cut_shapes,
        compiler_params=small,
        name="gather",
    )(core, offs, last_flag, back_in, back_their, new_own, new_theirs)
    landed = [to_partner(cuts[0])] + [from_host(cuts[m], m) for m in between]
    landed += [to_beyond(cuts[n // 2 + m - 1], m) for m in between]
    back_send, back_keep = backward(up_1, 1)
    ahead_last = to_partner(ahead_other)
    back_send, back_keep, landed, ahead_last = lax.optimization_barrier(
        (back_send, back_keep, landed, ahead_last)
    )
    back_1 = summed(
        jnp.where(last_section, new_rows, back_in), back_keep, swap_cores(back_send)
    )

    grads = pl.pallas_call(
        functools.partial(grads_kernel, n, (ticks * length * n) ** (-0.5)),
        grid=(1,),
        in_specs=[smem] * 2 + all_of(
            gated, up_0, up_1, up_own, up_near, *packs_near, *packs_beyond, *landed
        ),
        out_specs=pl.BlockSpec((slab, depth), lambda *_: (0, 0)),
        out_shape=struct((slab, depth), F32),
        compiler_params=small,
        cost_estimate=cost(matmul // 4, weight_bytes // 4),
        name="grads",
    )(
        host_flag, offs, after(gated, back_1), up_0, up_1, up_own, up_near, *packs_near, *packs_beyond, *landed
    )

    ahead_given, back_given, ahead_last = lax.optimization_barrier(
        (ahead_given, back_given, ahead_last, back_1)
    )[:3]
    ahead = jnp.stack(
        [
            jnp.where(is_host, ahead_0[0], ahead_given),
            jnp.where(is_host, ahead_1[0], ahead_last),
        ]
    )
    back = jnp.stack(
        [
            jnp.where(is_host, back_0[0], back_given),
            jnp.where(is_host, back_1[0], to_partner(back_1[1])),
        ]
    )
    return (ahead[None], back[None], grads[None])


def solution(mesh):
    in_specs = (
        P(None, "dp", None),
        P("section", "dp", None),
        P(None, "dp", None),
        P("section", "dp", None),
        P("section", None, "dp", None),
        P("section", "dp", "cores"),
        P("section", "cores", "dp"),
        P("dp", None),
        P("dp", None),
        P("dp", None, None, None),
        P("dp", None, None, None),
    )
    out_specs = (
        P("section", None, ("dp", "cores"), None),
        P("section", None, ("dp", "cores"), None),
        P("section", "cores", "dp"),
    )
    return jax.shard_map(
        per_device, mesh=mesh, in_specs=in_specs, out_specs=out_specs, check_vma=False
    )
```

```python
import functools

import jax
import jax.numpy as jnp
from jax import lax
from jax.experimental import pallas as pl
from jax.experimental.pallas import tpu as pltpu
from jax.sharding import PartitionSpec as P

HEAD_DIM = 128
BLOCK = 24
BLOCKS = 4
EPSILON = 1e-06
SCALING = HEAD_DIM ** (-0.5)
VMEM_BYTES = 34 * 1024 * 1024
SMALL_VMEM_BYTES = 16 * 1024 * 1024

F32 = jnp.float32
BF16 = jnp.bfloat16


def on_host(kernel):
    def guarded(host, *refs):
        pl.when(host[0] != 0)(functools.partial(kernel, *refs))

    return guarded


def dot(a, b):
    return lax.dot_general(a, b, (((1,), (0,)), ((), ())), preferred_element_type=F32)


def dot_nt(a, b):
    return lax.dot_general(a, b, (((1,), (1,)), ((), ())), preferred_element_type=F32)


def dot_tn(a, b):
    return lax.dot_general(a, b, (((0,), (0,)), ((), ())), preferred_element_type=F32)


def row_root(floats):
    return lax.rsqrt(jnp.mean(floats * floats, axis=-1, keepdims=True) + EPSILON)


def sigmoid(x):
    return 1.0 / (1.0 + jnp.exp(-x))


def attend(pre, keep):
    sig = sigmoid(pre)
    active = pre * sig
    gate = active[:, :HEAD_DIM]
    vqk = active[:, HEAD_DIM:].astype(BF16)
    value = vqk[:, :HEAD_DIM]
    query = vqk[:, HEAD_DIM : 2 * HEAD_DIM]
    key = vqk[:, 2 * HEAD_DIM :]
    scores = dot_nt(query, key) * SCALING
    sig_s = sigmoid(scores)
    probs = (scores * sig_s * keep).astype(BF16)
    mixed = dot(probs, value)
    gated = (mixed * row_root(mixed) * gate).astype(BF16)
    return sig, gate, vqk, scores, sig_s, probs, mixed, gated


def project(normed, offs, weights, of_head):
    total = None
    for j, weight in enumerate(weights):
        depth = weight.shape[0]
        columns = pl.ds(pl.multiple_of(offs[j], depth), depth)
        term = dot(normed[:, columns], weight[:, of_head])
        total = term if total is None else total + term
    return total


def columns_of_head(h, size):
    return pl.ds(pl.multiple_of(h * size, size), size)


def weight_copies(sources, targets, sems, h):
    of_head = columns_of_head(h, 4 * HEAD_DIM)
    return [
        pltpu.make_async_copy(
            source.at[:, of_head], target.at[:, of_head], sems.at[h * len(sources) + j]
        )
        for j, (source, target) in enumerate(zip(sources, targets))
    ]


def project_kernel(parts, heads, offs, x_own, x_theirs, stash_own, stash_theirs, keep, *rest):
    sources, rest = rest[:parts], rest[parts:]
    gated_out, saved, rest = rest[0], rest[1:7], rest[7:]
    weights, rest = rest[:parts], rest[parts:]
    held, (normed, sems, out_sems) = rest[:6], rest[6:]
    gate_out, vqk_out, slope_out, mixed_out, probs_out, factor_out = held
    length = x_own.shape[0]
    rows = 2 * length
    head = pl.program_id(0)

    def saved_copies(h):
        copies = []
        for i, (source, target) in enumerate(zip(held, saved)):
            if i < 4:
                at = (slice(None), slice(None), columns_of_head(h, source.shape[2] // heads))
            else:
                at = (slice(None), h)
            copies.append(
                pltpu.make_async_copy(source.at[at], target.at[at], out_sems.at[h * 6 + i])
            )
        return copies

    @pl.when(head == 0)
    def _():
        for h in range(heads):
            for copy in weight_copies(sources, weights, sems, h):
                copy.start()
        blocks = [x_own, x_theirs]
        for t in range(stash_own.shape[0]):
            blocks += [stash_own.at[t], stash_theirs.at[t]]
        for i, block in enumerate(blocks):
            floats = block[...].astype(F32)
            normed[pl.ds(i * length, length), :] = (floats * row_root(floats)).astype(BF16)

    for copy in weight_copies(sources, weights, sems, head):
        copy.wait()
    pre_all = project(normed, offs, weights, columns_of_head(head, 4 * HEAD_DIM))
    for i in range(1 + stash_own.shape[0]):
        pre = pre_all[i * rows : (i + 1) * rows]
        kept = keep[i]
        sig, gate, vqk, scores, sig_s, probs, mixed, gated = attend(pre, kept)
        gated_out[i] = gated
        if i > 0:
            narrow = columns_of_head(head, HEAD_DIM)
            gate_out[i - 1, :, narrow] = gate
            vqk_out[i - 1, :, columns_of_head(head, 3 * HEAD_DIM)] = vqk
            slope_out[i - 1, :, columns_of_head(head, 4 * HEAD_DIM)] = sig * (
                1.0 + pre * (1.0 - sig)
            )
            mixed_out[i - 1, :, narrow] = mixed
            probs_out[i - 1, head] = probs
            factor_out[i - 1, head] = kept * sig_s * (1.0 + scores * (1.0 - sig_s)) * SCALING
    for copy in saved_copies(head):
        copy.start()

    @pl.when(head == heads - 1)
    def _():
        for h in range(heads):
            for copy in saved_copies(h):
                copy.wait()


def split_rows(core, part, send, keep):
    share = send.shape[1]
    cores = part.shape[0] // (2 * share)
    for r in range(2):
        base = r * cores * share
        mine = pl.multiple_of(base + core * share, share)
        other = pl.multiple_of(base + (cores - 1 - core) * share, share)
        send[r] = part[pl.ds(other, share), :]
        keep[r] = part[pl.ds(mine, share), :]


def out_kernel(n, core, offs, gated, *rest):
    weights = rest[:n]
    send, keep, part = rest[n:]
    depth = weights[0].shape[1]
    for j in range(n):
        columns = pl.ds(pl.multiple_of(offs[j], depth), depth)
        part[:, columns] = dot(gated[0], weights[j][...]).astype(BF16)
    split_rows(core[0], part, send, keep)


def assemble(core, fresh, mine, theirs, new_own, new_theirs, whole):
    share = mine.shape[1]
    length = new_own.shape[0]
    cores = length // share
    use_fresh = fresh != 0
    for r, source in enumerate((new_own, new_theirs)):
        for owner, landed in ((core, mine), (cores - 1 - core, theirs)):
            inside = pl.multiple_of(owner * share, share)
            rows = source[pl.ds(inside, share), :]
            at = pl.multiple_of(r * length + owner * share, share)
            whole[pl.ds(at, share), :] = jnp.where(use_fresh, rows, landed[r])


def forward_kernel(parts, heads, core, in_offs, offs, fresh, mine, theirs, new_own, new_theirs, keep, *rest):
    sources, rest = rest[:parts], rest[parts:]
    in_parts, rest = rest[-parts:], rest[:-parts]
    out_parts = rest[:-7]
    send, kept, whole, normed, gated, part, sems = rest[-7:]
    depth = out_parts[0].shape[1]
    head = pl.program_id(0)

    @pl.when(head == 0)
    def _():
        for h in range(heads):
            for copy in weight_copies(sources, in_parts, sems, h):
                copy.start()
        assemble(core[0], fresh[0], mine, theirs, new_own, new_theirs, whole)
        floats = whole[...].astype(F32)
        normed[...] = (floats * row_root(floats)).astype(BF16)

    for copy in weight_copies(sources, in_parts, sems, head):
        copy.wait()
    pre = project(normed, in_offs, in_parts, columns_of_head(head, 4 * HEAD_DIM))
    gated[head] = attend(pre, keep[0])[-1]

    @pl.when(head == heads - 1)
    def _():
        for j in range(len(out_parts)):
            columns = pl.ds(pl.multiple_of(offs[j], depth), depth)
            total = None
            for h in range(heads):
                term = dot(gated[h], out_parts[j][pl.ds(h * HEAD_DIM, HEAD_DIM), :])
                total = term if total is None else total + term
            part[:, columns] = total.astype(BF16)
        split_rows(core[0], part, send, kept)


def backward_kernel(parts, n, tick, core, in_offs, offs, *rest):
    count = 9 + n + parts
    sources, rest = rest[:count], rest[count:]
    send, keep = rest[:2]
    held, (grad_normed, part, sems) = rest[2 : 2 + count], rest[2 + count :]
    ups, gate, vqk, slope, mixed, probs, factor, x_own, x_theirs = held[:9]
    out_parts, in_parts = held[9 : 9 + n], held[9 + n :]
    wide = 4 * HEAD_DIM
    heads = out_parts[0].shape[0] // HEAD_DIM
    copies = []
    for i, (source, target) in enumerate(zip(sources[: 9 + n], held[: 9 + n])):
        if 1 <= i < 9:
            source = source.at[tick]
        copies.append(pltpu.make_async_copy(source, target, sems.at[i]))
    by_head = []
    for h in range(heads):
        of_head = slice(h * wide, (h + 1) * wide)
        by_head.append(
            [
                pltpu.make_async_copy(
                    sources[9 + n + j].at[:, of_head],
                    in_parts[j].at[:, of_head],
                    sems.at[9 + n + h * parts + j],
                )
                for j in range(parts)
            ]
        )
    first = [0] + list(range(9, 9 + n))
    second = [1, 4, 2, 5, 6, 3]
    for i in first + second:
        copies[i].start()
    for of_head in by_head:
        for copy in of_head:
            copy.start()
    for i in (7, 8):
        copies[i].start()
    for i in first:
        copies[i].wait()
    depth = out_parts[0].shape[1]
    length = x_own.shape[0]
    grad_gated = None
    for j in range(n):
        columns = pl.ds(pl.multiple_of(offs[j], depth), depth)
        term = dot_nt(ups[:, columns], out_parts[j][...])
        grad_gated = term if grad_gated is None else grad_gated + term
    grad_gated = grad_gated.astype(BF16).astype(F32)
    for i in second:
        copies[i].wait()

    def through_head(h):
        cut = slice(h * HEAD_DIM, (h + 1) * HEAD_DIM)
        up = grad_gated[:, cut]
        mixed_h = mixed[:, cut]
        root = row_root(mixed_h)
        normed = mixed_h * root
        grad_n = up * gate[:, cut]
        grad_gate = up * normed
        grad_mixed = root * (grad_n - normed * jnp.mean(grad_n * normed, axis=-1, keepdims=True))
        low = grad_mixed.astype(BF16)
        base = 3 * h * HEAD_DIM
        value = vqk[:, base : base + HEAD_DIM]
        query = vqk[:, base + HEAD_DIM : base + 2 * HEAD_DIM]
        key = vqk[:, base + 2 * HEAD_DIM : base + 3 * HEAD_DIM]
        grad_scores = (dot_nt(low, value) * factor[h]).astype(BF16)
        grad_value = dot_tn(probs[h], low)
        grad_query = dot(grad_scores, key)
        grad_key = dot_tn(grad_scores, query)
        grad_active = jnp.concatenate([grad_gate, grad_value, grad_query, grad_key], axis=1)
        return (grad_active * slope[:, h * wide : (h + 1) * wide]).astype(BF16)

    grad_pre = through_head(0)
    for h in range(heads):
        for copy in by_head[h]:
            copy.wait()
        following = through_head(h + 1) if h + 1 < heads else None
        for j in range(parts):
            rows_of = in_parts[j].shape[0]
            columns = pl.ds(pl.multiple_of(in_offs[j], rows_of), rows_of)
            term = dot_nt(grad_pre, in_parts[j][:, h * wide : (h + 1) * wide])
            if h == 0:
                grad_normed[:, columns] = term
            else:
                grad_normed[:, columns] += term
        grad_pre = following
    for i in (7, 8):
        copies[i].wait()
    for r, source in enumerate((x_own, x_theirs)):
        rows = pl.ds(r * length, length)
        floats = source[...].astype(F32)
        root = row_root(floats)
        scaled = floats * root
        grad_n = grad_normed[rows, :]
        part[rows, :] = (
            root * (grad_n - scaled * jnp.mean(grad_n * scaled, axis=-1, keepdims=True))
        ).astype(BF16)
    split_rows(core[0], part, send, keep)


def pack_kernel(n, offs, gated, up_own, up_theirs, whole, *packs):
    depth = packs[-1].shape[1] - 2 * gated.shape[2]
    slab = gated.shape[2]
    length = up_own.shape[0]
    whole[:length, :] = up_own[...]
    whole[length:, :] = up_theirs[...]
    for j in range(1, n):
        pack = packs[j - 1]
        columns = pl.ds(pl.multiple_of(offs[j], depth), depth)
        pack[:, :slab] = gated[1]
        pack[:, slab : 2 * slab] = gated[2]
        if j > 1:
            pack[:length, 2 * slab :] = up_own[:, columns]
            pack[length:, 2 * slab :] = up_theirs[:, columns]


def settle_kernel(core, fresh, own, theirs, passed, keep, landed, total, other):
    share = keep.shape[1]
    here = pl.ds(pl.multiple_of(core[0] * share, share), share)
    for r, source in enumerate((own, theirs)):
        residual = jnp.where(fresh[0] != 0, source[here, :], passed[r])
        total[r] = (
            residual.astype(F32) + keep[r].astype(F32) + landed[r].astype(F32)
        ).astype(BF16)
    other[...] = total[1]


def gather_kernel(n, core, offs, fresh, mine, theirs, new_own, new_theirs, whole, *pieces):
    assemble(core[0], fresh[0], mine, theirs, new_own, new_theirs, whole)
    depth = pieces[0].shape[1]
    for j in range(1, n):
        columns = pl.ds(pl.multiple_of(offs[j], depth), depth)
        pieces[j - 1][...] = whole[:, columns]


def grads_kernel(n, scaling, host, offs, gated, up_0, up_1, up_own, up_near, *rest):
    packs = rest[: n - 1]
    pieces = rest[n - 1 : 2 * n - 2]
    out = rest[2 * n - 2]
    slab = gated.shape[2]
    depth = out.shape[1]
    at_host = host[0] != 0
    columns = pl.ds(pl.multiple_of(offs[0], depth), depth)

    def product(first, second, third, fourth):
        return dot_tn(first, third) + dot_tn(second, fourth)

    up_pair = jnp.concatenate([up_near[...], up_own[:, columns]], axis=0)
    total = product(
        jnp.where(at_host, gated[1], packs[0][:, :slab]),
        jnp.where(at_host, gated[2], packs[0][:, slab : 2 * slab]),
        jnp.where(at_host, up_0[:, columns], up_pair),
        jnp.where(at_host, up_1[:, columns], pieces[0][...]),
    )
    for m in range(1, n // 2):
        near, beyond = m, n // 2 + m - 1
        pack = jnp.where(at_host, packs[near][...], packs[beyond][...])
        piece = jnp.where(at_host, pieces[near][...], pieces[beyond][...])
        total = total + product(
            pack[:, :slab], pack[:, slab : 2 * slab], pack[:, 2 * slab :], piece
        )
    out[...] = total * scaling


def in_hbm(arrays):
    return [pltpu.with_memory_space_constraint(x, pltpu.HBM) for x in arrays]


def after(value, *earlier):
    return lax.optimization_barrier((value,) + earlier)[0]


def block_keep(live_blocks, block_marks):
    length = BLOCKS * BLOCK
    places = jnp.arange(length, dtype=jnp.int32)
    owners = places // BLOCK
    marked = jnp.repeat(jnp.repeat(block_marks, BLOCK, axis=-2), BLOCK, axis=-1) == 1
    allowed = (owners[:, None] == owners[None, :]) | marked
    causal = places[:, None] >= places[None, :]
    tokens = live_blocks[..., None, None] * BLOCK
    keeping = causal & allowed & (places[:, None] < tokens) & (places[None, :] < tokens)
    return jnp.where(keeping, 1.0 / jnp.maximum(tokens, 1).astype(F32), 0.0)


def per_device(
    arrivals,
    in_flight,
    cotangent,
    grad_flight,
    stashed,
    in_weight,
    out_weight,
    forward_blocks,
    backward_blocks,
    forward_marks,
    backward_marks,
):
    section_no = lax.axis_index("section")
    sections = lax.axis_size("section")
    core_no = lax.axis_index("cores")
    cores = lax.axis_size("cores")
    dp_no = lax.axis_index("dp")
    n = lax.axis_size("dp")
    ticks = arrivals.shape[0]
    length = arrivals.shape[1]
    width = arrivals.shape[2]
    rows = 2 * length
    share = length // cores
    in_shard = in_weight[0]
    out_shard = out_weight[0]
    depth = in_shard.shape[0]
    slab = out_shard.shape[0]
    heads = slab // HEAD_DIM
    wide = 4 * HEAD_DIM

    hosts = [2 * k + 1 if 4 * k < n - 2 else 2 * k for k in range(n // 2)]
    host_table = jnp.array(hosts, jnp.int32)
    is_host = dp_no == host_table[dp_no // 2]

    def from_partner(x):
        return lax.ppermute(x, "dp", [(h ^ 1, h) for h in hosts])

    def to_partner(x):
        return lax.ppermute(x, "dp", [(h, h ^ 1) for h in hosts])

    def from_host(x, m):
        return lax.ppermute(x, "dp", [(hosts[k ^ m], hosts[k]) for k in range(n // 2)])

    def to_beyond(x, m):
        return lax.ppermute(
            x, "dp", [(hosts[k ^ m], hosts[k] ^ 1) for k in range(n // 2)]
        )

    def swap_cores(x):
        return lax.ppermute(x, "cores", [(c, cores - 1 - c) for c in range(cores)])

    def along_sections(x, by):
        pairs = [
            (i * n + h, (i + by) * n + h)
            for i in range(sections)
            if 0 <= i + by < sections
            for h in hosts
        ]
        return lax.ppermute(x, ("section", "dp"), pairs)

    first_section = section_no == 0
    last_section = section_no == sections - 1
    between = range(1, n // 2)

    pieces = max(1, min(2, depth // 256))
    piece = depth // pieces
    in_far = [from_host(in_shard, m) for m in between]
    in_near = [
        from_partner(in_shard[i * piece : (i + 1) * piece]) for i in range(pieces)
    ]
    out_near = from_partner(out_shard)
    in_pass = [from_host(in_near[0], m) for m in between]
    in_far, in_near, rows_in, tables_in = lax.optimization_barrier(
        (
            in_far,
            in_near,
            (arrivals, in_flight, cotangent, grad_flight, stashed),
            (forward_blocks, forward_marks, backward_blocks, backward_marks),
        )
    )
    in_pass += [from_host(in_near[i], m) for i in range(1, pieces) for m in between]
    in_parts = [in_shard] + in_far + in_near + in_pass
    arrivals, in_flight, cotangent, grad_flight, stashed = rows_in
    tables = jnp.concatenate(
        [
            jnp.concatenate([b[..., None], m.reshape(m.shape[:2] + (-1,))], axis=-1)
            for b, m in (tables_in[:2], tables_in[2:])
        ],
        axis=0,
    )
    near_tables = from_partner(tables)
    stash_own = stashed[0]
    stash_theirs = from_partner(stash_own)
    x_own = jnp.where(first_section, arrivals[0], in_flight[0])
    x_theirs = from_partner(x_own)
    up_own = jnp.where(last_section, cotangent[0], grad_flight[0])
    new_own = jnp.where(first_section, arrivals[1], cotangent[1])
    out_own, out_near, near_tables = lax.optimization_barrier((out_shard, out_near, near_tables))
    out_far = [from_host(out_own, m) for m in between]
    out_parts = [out_shard, out_near] + out_far + [from_host(out_near, m) for m in between]
    up_late, new_late, stash_theirs = lax.optimization_barrier((up_own, new_own, stash_theirs))
    up_theirs = from_partner(up_late)
    up_near = to_partner(
        lax.dynamic_slice_in_dim(up_late, (dp_no ^ 1) * depth, depth, axis=1)
    )
    new_theirs = from_partner(new_late)
    far_hosts = [host_table[(dp_no // 2) ^ m] for m in between]
    owners = [dp_no, dp_no ^ 1] + far_hosts + [h ^ 1 for h in far_hosts]
    offs = jnp.stack(owners).astype(jnp.int32) * depth
    in_offs = [dp_no * depth] + [h * depth for h in far_hosts]
    in_offs += [(dp_no ^ 1) * depth + i * piece for i in range(pieces)]
    in_offs += [(h ^ 1) * depth + i * piece for i in range(pieces) for h in far_hosts]
    in_offs = jnp.stack(in_offs).astype(jnp.int32)
    parts = len(in_parts)
    core = jnp.reshape(core_no, (1,)).astype(jnp.int32)
    first_flag = jnp.reshape(first_section, (1,)).astype(jnp.int32)
    host_flag = jnp.reshape(is_host, (1,)).astype(jnp.int32)
    last_flag = jnp.reshape(last_section, (1,)).astype(jnp.int32)

    both_tables = jnp.stack([tables, near_tables], axis=1)
    ahead_at = sections - 1 - section_no
    chosen = jnp.stack(
        [
            lax.dynamic_index_in_dim(both_tables[way], at, axis=1, keepdims=False)
            for way, at in (
                (0, ahead_at),
                (1, section_no),
                (1, section_no + 1),
                (0, ahead_at + 1),
            )
        ]
    )
    kept = block_keep(chosen[..., 0], chosen[..., 1:].reshape(-1, 2, BLOCKS, BLOCKS))
    blank = jnp.zeros_like(kept[:, 0])
    keep = jnp.concatenate(
        [
            jnp.concatenate([kept[:, 0], blank], axis=2),
            jnp.concatenate([blank, kept[:, 1]], axis=2),
        ],
        axis=1,
    )

    smem = pl.BlockSpec(memory_space=pltpu.SMEM)
    hbm = pl.BlockSpec(memory_space=pltpu.HBM)

    def all_of(*arrays):
        return [pl.BlockSpec(x.shape, lambda *_, d=x.ndim: (0,) * d) for x in arrays]

    def row_of(x, i):
        return pl.BlockSpec((1,) + x.shape[1:], lambda *_: (i,) + (0,) * (x.ndim - 1))

    params = pltpu.CompilerParams(vmem_limit_bytes=VMEM_BYTES)
    small = pltpu.CompilerParams(vmem_limit_bytes=SMALL_VMEM_BYTES)

    def cost(multiply_adds, bytes_accessed):
        return pl.CostEstimate(
            flops=2 * multiply_adds, bytes_accessed=bytes_accessed, transcendentals=0
        )

    def struct(shape, dtype):
        return jax.ShapeDtypeStruct(shape, dtype)

    halves = [struct((2, share, width), BF16)] * 2
    matmul = rows * width * 4 * slab
    weight_bytes = 2 * width * 5 * slab

    by_head = lambda lead, last: pl.BlockSpec(lead + (last,), lambda h: (0,) * len(lead) + (h,))
    saved_shapes = [
        struct((2, rows, slab), F32),
        struct((2, rows, 3 * slab), BF16),
        struct((2, rows, 4 * slab), F32),
        struct((2, rows, slab), F32),
        struct((2, heads, rows, rows), BF16),
        struct((2, heads, rows, rows), F32),
    ]
    weight_scratch = [pltpu.VMEM(x.shape, BF16) for x in in_parts]
    gated, gate, vqk, slope, mixed, probs, factor = pl.pallas_call(
        on_host(functools.partial(project_kernel, parts, heads)),
        grid=(heads,),
        in_specs=[smem] * 2
        + all_of(x_own, x_theirs, stash_own, stash_theirs, keep)
        + [hbm] * parts,
        out_specs=[by_head((3, rows), HEAD_DIM)] + [hbm] * 6,
        out_shape=[struct((3, rows, slab), BF16)]
        + [pltpu.HBM(x.shape, x.dtype) for x in saved_shapes],
        scratch_shapes=weight_scratch
        + [pltpu.VMEM(x.shape, x.dtype) for x in saved_shapes]
        + [
            pltpu.VMEM((3 * rows, width), BF16),
            pltpu.SemaphoreType.DMA((heads * parts,)),
            pltpu.SemaphoreType.DMA((heads * 6,)),
        ],
        compiler_params=params,
        cost_estimate=cost(3 * matmul, 2 * weight_bytes),
        name="project",
    )(host_flag, in_offs, x_own, x_theirs, stash_own, stash_theirs, keep, *in_hbm(in_parts))

    def backward(ups, tick_no):
        layered = [gate, vqk, slope, mixed, probs, factor, stash_own, stash_theirs]
        plain = list(out_parts) + list(in_parts)
        return pl.pallas_call(
            on_host(functools.partial(backward_kernel, parts, n, tick_no)),
            grid=(1,),
            in_specs=[smem] * 4 + [hbm] * (1 + len(layered) + len(plain)),
            out_specs=all_of(*halves),
            out_shape=halves,
            scratch_shapes=[pltpu.VMEM(ups.shape, BF16)]
            + [pltpu.VMEM(x.shape[1:], x.dtype) for x in layered]
            + [pltpu.VMEM(x.shape, x.dtype) for x in plain]
            + [
                pltpu.VMEM((rows, width), F32),
                pltpu.VMEM((rows, width), BF16),
                pltpu.SemaphoreType.DMA((1 + len(layered) + n + heads * parts,)),
            ],
            compiler_params=params,
            cost_estimate=cost(2 * matmul, 2 * weight_bytes),
            name="backward",
        )(host_flag, core, in_offs, offs, ups, *in_hbm(layered), *out_parts, *in_hbm(in_parts))

    gated, new_theirs, up_near = lax.optimization_barrier((gated, new_theirs, up_near))

    def summed(residual, mine, landed):
        return (residual.astype(F32) + mine.astype(F32) + landed.astype(F32)).astype(BF16)

    def own_rows(mine, others):
        return lax.dynamic_slice_in_dim(jnp.stack([mine, others]), core_no * share, share, axis=1)

    pack_shapes = [struct((rows, width), BF16)]
    pack_shapes += [struct((rows, 2 * slab), BF16)]
    pack_shapes += [struct((rows, 2 * slab + depth), BF16)] * (n - 2)
    up_0, *packs = pl.pallas_call(
        functools.partial(pack_kernel, n),
        grid=(1,),
        in_specs=[smem] * 1 + all_of(gated, up_own, up_theirs),
        out_specs=all_of(*pack_shapes),
        out_shape=pack_shapes,
        compiler_params=small,
        name="pack",
    )(offs, gated, up_own, up_theirs)
    packs, out_parts = lax.optimization_barrier((packs, out_parts))

    ahead_send, ahead_keep = pl.pallas_call(
        functools.partial(out_kernel, n),
        grid=(1,),
        in_specs=[smem] * 2 + [row_of(gated, 0)] + all_of(*out_parts),
        out_specs=all_of(*halves),
        out_shape=halves,
        scratch_shapes=[pltpu.VMEM((rows, width), BF16)],
        compiler_params=small,
        cost_estimate=cost(matmul // 4, weight_bytes // 4),
        name="out",
    )(core, offs, gated, *out_parts)
    ahead_0 = summed(own_rows(x_own, x_theirs), ahead_keep, swap_cores(ahead_send))
    ahead_in = along_sections(ahead_0, 1)
    packs_near = [to_partner(packs[0])] + [from_host(packs[m], m) for m in between]
    back_send, back_keep = backward(after(up_0, ahead_0), 0)
    ahead_given = to_partner(ahead_0[1])
    back_send, back_keep, ahead_in, packs_near, ahead_given = lax.optimization_barrier(
        (back_send, back_keep, ahead_in, packs_near, ahead_given)
    )
    back_landed = swap_cores(back_send)
    back_0 = summed(own_rows(up_own, up_theirs), back_keep, back_landed)
    back_in = along_sections(back_0, -1)

    packs_beyond = [to_beyond(packs[n // 2 + m - 1], m) for m in between]
    ahead_their = swap_cores(ahead_in)
    ahead_send, ahead_keep = pl.pallas_call(
        on_host(functools.partial(forward_kernel, parts, heads)),
        grid=(heads,),
        in_specs=[smem] * 5
        + all_of(ahead_in, ahead_their, new_own, new_theirs)
        + [row_of(keep, keep.shape[0] - 1)]
        + [hbm] * parts
        + all_of(*out_parts),
        out_specs=all_of(*halves),
        out_shape=halves,
        scratch_shapes=[
            pltpu.VMEM((rows, width), BF16),
            pltpu.VMEM((rows, width), BF16),
            pltpu.VMEM((heads, rows, HEAD_DIM), BF16),
            pltpu.VMEM((rows, width), BF16),
            pltpu.SemaphoreType.DMA((heads * parts,)),
        ]
        + weight_scratch,
        compiler_params=params,
        cost_estimate=cost(2 * matmul, 2 * weight_bytes),
        name="forward",
    )(host_flag, core,
        in_offs,
        offs,
        first_flag,
        ahead_in,
        ahead_their,
        new_own,
        new_theirs,
        keep,
        *in_hbm(in_parts),
        *out_parts,
    )
    new_rows = own_rows(new_own, new_theirs)
    ahead_landed = swap_cores(ahead_send)
    settled = [halves[0], struct((share, width), BF16)]
    ahead_1, ahead_other = pl.pallas_call(
        settle_kernel,
        grid=(1,),
        in_specs=[smem] * 2
        + all_of(new_own, new_theirs, ahead_in, ahead_keep, ahead_landed),
        out_specs=all_of(*settled),
        out_shape=settled,
        compiler_params=small,
        name="settle",
    )(core, first_flag, new_own, new_theirs, ahead_in, ahead_keep, ahead_landed)
    back_given = to_partner(back_0[1])
    ahead_1, ahead_other, back_in, packs_beyond, back_given = lax.optimization_barrier(
        (ahead_1, ahead_other, back_in, packs_beyond, back_given)
    )

    back_their = swap_cores(back_in)
    cut_shapes = [struct((rows, width), BF16)] + [struct((rows, depth), BF16)] * (n - 1)
    up_1, *cuts = pl.pallas_call(
        functools.partial(gather_kernel, n),
        grid=(1,),
        in_specs=[smem] * 3 + all_of(back_in, back_their, new_own, new_theirs),
        out_specs=all_of(*cut_shapes),
        out_shape=cut_shapes,
        compiler_params=small,
        name="gather",
    )(core, offs, last_flag, back_in, back_their, new_own, new_theirs)
    landed = [to_partner(cuts[0])] + [from_host(cuts[m], m) for m in between]
    landed += [to_beyond(cuts[n // 2 + m - 1], m) for m in between]
    back_send, back_keep = backward(up_1, 1)
    ahead_last = to_partner(ahead_other)
    back_send, back_keep, landed, ahead_last = lax.optimization_barrier(
        (back_send, back_keep, landed, ahead_last)
    )
    back_1 = summed(
        jnp.where(last_section, new_rows, back_in), back_keep, swap_cores(back_send)
    )

    grads = pl.pallas_call(
        functools.partial(grads_kernel, n, (ticks * length * n) ** (-0.5)),
        grid=(1,),
        in_specs=[smem] * 2 + all_of(
            gated, up_0, up_1, up_own, up_near, *packs_near, *packs_beyond, *landed
        ),
        out_specs=pl.BlockSpec((slab, depth), lambda *_: (0, 0)),
        out_shape=struct((slab, depth), F32),
        compiler_params=small,
        cost_estimate=cost(matmul // 4, weight_bytes // 4),
        name="grads",
    )(
        host_flag, offs, after(gated, back_1), up_0, up_1, up_own, up_near, *packs_near, *packs_beyond, *landed
    )

    ahead_given, back_given, ahead_last = lax.optimization_barrier(
        (ahead_given, back_given, ahead_last, back_1)
    )[:3]
    ahead = jnp.stack(
        [
            jnp.where(is_host, ahead_0[0], ahead_given),
            jnp.where(is_host, ahead_1[0], ahead_last),
        ]
    )
    back = jnp.stack(
        [
            jnp.where(is_host, back_0[0], back_given),
            jnp.where(is_host, back_1[0], to_partner(back_1[1])),
        ]
    )
    return (ahead[None], back[None], grads[None])


def solution(mesh):
    in_specs = (
        P(None, "dp", None),
        P("section", "dp", None),
        P(None, "dp", None),
        P("section", "dp", None),
        P("section", None, "dp", None),
        P("section", "dp", "cores"),
        P("section", "cores", "dp"),
        P("dp", None),
        P("dp", None),
        P("dp", None, None, None),
        P("dp", None, None, None),
    )
    out_specs = (
        P("section", None, ("dp", "cores"), None),
        P("section", None, ("dp", "cores"), None),
        P("section", "cores", "dp"),
    )
    return jax.shard_map(
        per_device, mesh=mesh, in_specs=in_specs, out_specs=out_specs, check_vma=False
    )
```

```python
import functools

import jax
import jax.numpy as jnp
from jax import lax
from jax.experimental import pallas as pl
from jax.experimental.pallas import tpu as pltpu
from jax.sharding import PartitionSpec as P

HEAD_DIM = 128
BLOCK = 24
BLOCKS = 4
EPSILON = 1e-06
SCALING = HEAD_DIM ** (-0.5)
VMEM_BYTES = 34 * 1024 * 1024
SMALL_VMEM_BYTES = 16 * 1024 * 1024

F32 = jnp.float32
BF16 = jnp.bfloat16


def on_host(kernel):
    def guarded(host, *refs):
        pl.when(host[0] != 0)(functools.partial(kernel, *refs))

    return guarded


def dot(a, b):
    return lax.dot_general(a, b, (((1,), (0,)), ((), ())), preferred_element_type=F32)


def dot_nt(a, b):
    return lax.dot_general(a, b, (((1,), (1,)), ((), ())), preferred_element_type=F32)


def dot_tn(a, b):
    return lax.dot_general(a, b, (((0,), (0,)), ((), ())), preferred_element_type=F32)


def row_root(floats):
    return lax.rsqrt(jnp.mean(floats * floats, axis=-1, keepdims=True) + EPSILON)


def sigmoid(x):
    return 1.0 / (1.0 + jnp.exp(-x))


def attend(pre, keep):
    sig = sigmoid(pre)
    active = pre * sig
    gate = active[:, :HEAD_DIM]
    vqk = active[:, HEAD_DIM:].astype(BF16)
    value = vqk[:, :HEAD_DIM]
    query = vqk[:, HEAD_DIM : 2 * HEAD_DIM]
    key = vqk[:, 2 * HEAD_DIM :]
    scores = dot_nt(query, key) * SCALING
    sig_s = sigmoid(scores)
    probs = (scores * sig_s * keep).astype(BF16)
    mixed = dot(probs, value)
    gated = (mixed * row_root(mixed) * gate).astype(BF16)
    return sig, gate, vqk, scores, sig_s, probs, mixed, gated


def project(normed, offs, weights, of_head):
    total = None
    for j, weight in enumerate(weights):
        depth = weight.shape[0]
        columns = pl.ds(pl.multiple_of(offs[j], depth), depth)
        term = dot(normed[:, columns], weight[:, of_head])
        total = term if total is None else total + term
    return total


def columns_of_head(h, size):
    return pl.ds(pl.multiple_of(h * size, size), size)


def weight_copies(sources, targets, sems, h):
    of_head = columns_of_head(h, 4 * HEAD_DIM)
    return [
        pltpu.make_async_copy(
            source.at[:, of_head], target.at[:, of_head], sems.at[h * len(sources) + j]
        )
        for j, (source, target) in enumerate(zip(sources, targets))
    ]


def project_kernel(parts, heads, offs, x_own, x_theirs, stash_own, stash_theirs, keep, *rest):
    sources, rest = rest[:parts], rest[parts:]
    gated_out, saved, rest = rest[0], rest[1:7], rest[7:]
    weights, rest = rest[:parts], rest[parts:]
    held, (normed, sems, out_sems) = rest[:6], rest[6:]
    gate_out, vqk_out, slope_out, mixed_out, probs_out, factor_out = held
    length = x_own.shape[0]
    rows = 2 * length
    head = pl.program_id(0)

    def saved_copies(h):
        copies = []
        for i, (source, target) in enumerate(zip(held, saved)):
            if i < 4:
                at = (slice(None), slice(None), columns_of_head(h, source.shape[2] // heads))
            else:
                at = (slice(None), h)
            copies.append(
                pltpu.make_async_copy(source.at[at], target.at[at], out_sems.at[h * 6 + i])
            )
        return copies

    @pl.when(head == 0)
    def _():
        for h in range(heads):
            for copy in weight_copies(sources, weights, sems, h):
                copy.start()
        blocks = [x_own, x_theirs]
        for t in range(stash_own.shape[0]):
            blocks += [stash_own.at[t], stash_theirs.at[t]]
        for i, block in enumerate(blocks):
            floats = block[...].astype(F32)
            normed[pl.ds(i * length, length), :] = (floats * row_root(floats)).astype(BF16)

    for copy in weight_copies(sources, weights, sems, head):
        copy.wait()
    pre_all = project(normed, offs, weights, columns_of_head(head, 4 * HEAD_DIM))
    for i in range(1 + stash_own.shape[0]):
        pre = pre_all[i * rows : (i + 1) * rows]
        kept = keep[i]
        sig, gate, vqk, scores, sig_s, probs, mixed, gated = attend(pre, kept)
        gated_out[i] = gated
        if i > 0:
            narrow = columns_of_head(head, HEAD_DIM)
            gate_out[i - 1, :, narrow] = gate
            vqk_out[i - 1, :, columns_of_head(head, 3 * HEAD_DIM)] = vqk
            slope_out[i - 1, :, columns_of_head(head, 4 * HEAD_DIM)] = sig * (
                1.0 + pre * (1.0 - sig)
            )
            mixed_out[i - 1, :, narrow] = mixed
            probs_out[i - 1, head] = probs
            factor_out[i - 1, head] = kept * sig_s * (1.0 + scores * (1.0 - sig_s)) * SCALING
    for copy in saved_copies(head):
        copy.start()

    @pl.when(head == heads - 1)
    def _():
        for h in range(heads):
            for copy in saved_copies(h):
                copy.wait()


def split_rows(core, part, send, keep):
    share = send.shape[1]
    cores = part.shape[0] // (2 * share)
    for r in range(2):
        base = r * cores * share
        mine = pl.multiple_of(base + core * share, share)
        other = pl.multiple_of(base + (cores - 1 - core) * share, share)
        send[r] = part[pl.ds(other, share), :]
        keep[r] = part[pl.ds(mine, share), :]


def out_kernel(n, core, offs, gated, *rest):
    weights = rest[:n]
    send, keep, part = rest[n:]
    depth = weights[0].shape[1]
    for j in range(n):
        columns = pl.ds(pl.multiple_of(offs[j], depth), depth)
        part[:, columns] = dot(gated[0], weights[j][...]).astype(BF16)
    split_rows(core[0], part, send, keep)


def assemble(core, fresh, mine, theirs, new_own, new_theirs, whole):
    share = mine.shape[1]
    length = new_own.shape[0]
    cores = length // share
    use_fresh = fresh != 0
    for r, source in enumerate((new_own, new_theirs)):
        for owner, landed in ((core, mine), (cores - 1 - core, theirs)):
            inside = pl.multiple_of(owner * share, share)
            rows = source[pl.ds(inside, share), :]
            at = pl.multiple_of(r * length + owner * share, share)
            whole[pl.ds(at, share), :] = jnp.where(use_fresh, rows, landed[r])


def forward_kernel(parts, heads, core, in_offs, offs, fresh, mine, theirs, new_own, new_theirs, keep, *rest):
    sources, rest = rest[:parts], rest[parts:]
    in_parts, rest = rest[-parts:], rest[:-parts]
    out_parts = rest[:-7]
    send, kept, whole, normed, gated, part, sems = rest[-7:]
    depth = out_parts[0].shape[1]
    head = pl.program_id(0)

    @pl.when(head == 0)
    def _():
        for h in range(heads):
            for copy in weight_copies(sources, in_parts, sems, h):
                copy.start()
        assemble(core[0], fresh[0], mine, theirs, new_own, new_theirs, whole)
        floats = whole[...].astype(F32)
        normed[...] = (floats * row_root(floats)).astype(BF16)

    for copy in weight_copies(sources, in_parts, sems, head):
        copy.wait()
    pre = project(normed, in_offs, in_parts, columns_of_head(head, 4 * HEAD_DIM))
    gated[head] = attend(pre, keep[0])[-1]

    @pl.when(head == heads - 1)
    def _():
        for j in range(len(out_parts)):
            columns = pl.ds(pl.multiple_of(offs[j], depth), depth)
            total = None
            for h in range(heads):
                term = dot(gated[h], out_parts[j][pl.ds(h * HEAD_DIM, HEAD_DIM), :])
                total = term if total is None else total + term
            part[:, columns] = total.astype(BF16)
        split_rows(core[0], part, send, kept)


def backward_kernel(parts, n, tick, core, in_offs, offs, *rest):
    count = 9 + n + parts
    sources, rest = rest[:count], rest[count:]
    send, keep = rest[:2]
    held, (grad_normed, part, sems) = rest[2 : 2 + count], rest[2 + count :]
    ups, gate, vqk, slope, mixed, probs, factor, x_own, x_theirs = held[:9]
    out_parts, in_parts = held[9 : 9 + n], held[9 + n :]
    wide = 4 * HEAD_DIM
    heads = out_parts[0].shape[0] // HEAD_DIM
    copies = []
    for i, (source, target) in enumerate(zip(sources[: 9 + n], held[: 9 + n])):
        if 1 <= i < 9:
            source = source.at[tick]
        copies.append(pltpu.make_async_copy(source, target, sems.at[i]))
    by_head = []
    for h in range(heads):
        of_head = slice(h * wide, (h + 1) * wide)
        by_head.append(
            [
                pltpu.make_async_copy(
                    sources[9 + n + j].at[:, of_head],
                    in_parts[j].at[:, of_head],
                    sems.at[9 + n + h * parts + j],
                )
                for j in range(parts)
            ]
        )
    first = [0] + list(range(9, 9 + n))
    second = [1, 4, 2, 5, 6, 3]
    for i in first + second:
        copies[i].start()
    for of_head in by_head:
        for copy in of_head:
            copy.start()
    for i in (7, 8):
        copies[i].start()
    for i in first:
        copies[i].wait()
    depth = out_parts[0].shape[1]
    length = x_own.shape[0]
    grad_gated = None
    for j in range(n):
        columns = pl.ds(pl.multiple_of(offs[j], depth), depth)
        term = dot_nt(ups[:, columns], out_parts[j][...])
        grad_gated = term if grad_gated is None else grad_gated + term
    grad_gated = grad_gated.astype(BF16).astype(F32)
    for i in second:
        copies[i].wait()

    def through_head(h):
        cut = slice(h * HEAD_DIM, (h + 1) * HEAD_DIM)
        up = grad_gated[:, cut]
        mixed_h = mixed[:, cut]
        root = row_root(mixed_h)
        normed = mixed_h * root
        grad_n = up * gate[:, cut]
        grad_gate = up * normed
        grad_mixed = root * (grad_n - normed * jnp.mean(grad_n * normed, axis=-1, keepdims=True))
        low = grad_mixed.astype(BF16)
        base = 3 * h * HEAD_DIM
        value = vqk[:, base : base + HEAD_DIM]
        query = vqk[:, base + HEAD_DIM : base + 2 * HEAD_DIM]
        key = vqk[:, base + 2 * HEAD_DIM : base + 3 * HEAD_DIM]
        grad_scores = (dot_nt(low, value) * factor[h]).astype(BF16)
        grad_value = dot_tn(probs[h], low)
        grad_query = dot(grad_scores, key)
        grad_key = dot_tn(grad_scores, query)
        grad_active = jnp.concatenate([grad_gate, grad_value, grad_query, grad_key], axis=1)
        return (grad_active * slope[:, h * wide : (h + 1) * wide]).astype(BF16)

    grad_pre = through_head(0)
    for h in range(heads):
        for copy in by_head[h]:
            copy.wait()
        following = through_head(h + 1) if h + 1 < heads else None
        for j in range(parts):
            rows_of = in_parts[j].shape[0]
            columns = pl.ds(pl.multiple_of(in_offs[j], rows_of), rows_of)
            term = dot_nt(grad_pre, in_parts[j][:, h * wide : (h + 1) * wide])
            if h == 0:
                grad_normed[:, columns] = term
            else:
                grad_normed[:, columns] += term
        grad_pre = following
    for i in (7, 8):
        copies[i].wait()
    for r, source in enumerate((x_own, x_theirs)):
        rows = pl.ds(r * length, length)
        floats = source[...].astype(F32)
        root = row_root(floats)
        scaled = floats * root
        grad_n = grad_normed[rows, :]
        part[rows, :] = (
            root * (grad_n - scaled * jnp.mean(grad_n * scaled, axis=-1, keepdims=True))
        ).astype(BF16)
    split_rows(core[0], part, send, keep)


def pack_kernel(n, offs, gated, up_own, up_theirs, whole, *packs):
    depth = packs[0].shape[1] - 2 * gated.shape[2]
    slab = gated.shape[2]
    length = up_own.shape[0]
    whole[:length, :] = up_own[...]
    whole[length:, :] = up_theirs[...]
    for j in range(2, n):
        pack = packs[j - 2]
        columns = pl.ds(pl.multiple_of(offs[j], depth), depth)
        pack[:, :slab] = gated[1]
        pack[:, slab : 2 * slab] = gated[2]
        pack[:length, 2 * slab :] = up_own[:, columns]
        pack[length:, 2 * slab :] = up_theirs[:, columns]


def fold(rows, target, start):
    share, width = rows.shape
    blocks = target.shape[0] // share
    size = width // blocks
    for k in range(blocks):
        target[k * share : (k + 1) * share, start:] = rows[:, k * size : (k + 1) * size]


def unfold(folded, share):
    return jnp.concatenate(
        [folded[i : i + share] for i in range(0, folded.shape[0], share)], axis=1
    )


def first_kernel(core, own, theirs, keep, landed, gated, total, pack):
    share = keep.shape[1]
    slab = gated.shape[2]
    here = pl.ds(pl.multiple_of(core[0] * share, share), share)
    for r, source in enumerate((own, theirs)):
        total[r] = (
            source[here, :].astype(F32) + keep[r].astype(F32) + landed[r].astype(F32)
        ).astype(BF16)
    pack[:, :slab] = gated[1]
    pack[:, slab : 2 * slab] = gated[2]
    fold(total[1], pack, 2 * slab)


def settle_kernel(core, fresh, own, theirs, passed, keep, landed, total, other):
    share = keep.shape[1]
    here = pl.ds(pl.multiple_of(core[0] * share, share), share)
    for r, source in enumerate((own, theirs)):
        residual = jnp.where(fresh[0] != 0, source[here, :], passed[r])
        total[r] = (
            residual.astype(F32) + keep[r].astype(F32) + landed[r].astype(F32)
        ).astype(BF16)
    other[...] = total[1]


def gather_kernel(
    n, core, offs, fresh, mine, theirs, new_own, new_theirs, other, whole, *pieces
):
    assemble(core[0], fresh[0], mine, theirs, new_own, new_theirs, whole)
    depth = pieces[-1].shape[1]
    for j in range(1, n):
        columns = pl.ds(pl.multiple_of(offs[j], depth), depth)
        pieces[j - 1][:, :depth] = whole[:, columns]
    fold(other[...], pieces[0], depth)


def grads_kernel(n, scaling, host, offs, gated, up_0, up_1, up_own, up_near, *rest):
    packs = rest[: n - 1]
    pieces = rest[n - 1 : 2 * n - 2]
    out = rest[2 * n - 2]
    slab = gated.shape[2]
    depth = out.shape[1]
    at_host = host[0] != 0
    columns = pl.ds(pl.multiple_of(offs[0], depth), depth)

    def product(first, second, third, fourth):
        return dot_tn(first, third) + dot_tn(second, fourth)

    up_pair = jnp.concatenate([up_near[...], up_own[:, columns]], axis=0)
    total = product(
        jnp.where(at_host, gated[1], packs[0][:, :slab]),
        jnp.where(at_host, gated[2], packs[0][:, slab : 2 * slab]),
        jnp.where(at_host, up_0[:, columns], up_pair),
        jnp.where(at_host, up_1[:, columns], pieces[0][:, :depth]),
    )
    for m in range(1, n // 2):
        near, beyond = m, n // 2 + m - 1
        pack = jnp.where(at_host, packs[near][...], packs[beyond][...])
        piece = jnp.where(at_host, pieces[near][...], pieces[beyond][...])
        total = total + product(
            pack[:, :slab], pack[:, slab : 2 * slab], pack[:, 2 * slab :], piece
        )
    out[...] = total * scaling


def in_hbm(arrays):
    return [pltpu.with_memory_space_constraint(x, pltpu.HBM) for x in arrays]


def after(value, *earlier):
    return lax.optimization_barrier((value,) + earlier)[0]


def block_keep(live_blocks, block_marks):
    length = BLOCKS * BLOCK
    places = jnp.arange(length, dtype=jnp.int32)
    owners = places // BLOCK
    marked = jnp.repeat(jnp.repeat(block_marks, BLOCK, axis=-2), BLOCK, axis=-1) == 1
    allowed = (owners[:, None] == owners[None, :]) | marked
    causal = places[:, None] >= places[None, :]
    tokens = live_blocks[..., None, None] * BLOCK
    keeping = causal & allowed & (places[:, None] < tokens) & (places[None, :] < tokens)
    return jnp.where(keeping, 1.0 / jnp.maximum(tokens, 1).astype(F32), 0.0)


def per_device(
    arrivals,
    in_flight,
    cotangent,
    grad_flight,
    stashed,
    in_weight,
    out_weight,
    forward_blocks,
    backward_blocks,
    forward_marks,
    backward_marks,
):
    section_no = lax.axis_index("section")
    sections = lax.axis_size("section")
    core_no = lax.axis_index("cores")
    cores = lax.axis_size("cores")
    dp_no = lax.axis_index("dp")
    n = lax.axis_size("dp")
    ticks = arrivals.shape[0]
    length = arrivals.shape[1]
    width = arrivals.shape[2]
    rows = 2 * length
    share = length // cores
    in_shard = in_weight[0]
    out_shard = out_weight[0]
    depth = in_shard.shape[0]
    slab = out_shard.shape[0]
    heads = slab // HEAD_DIM
    wide = 4 * HEAD_DIM

    hosts = [2 * k + 1 if 4 * k < n - 2 else 2 * k for k in range(n // 2)]
    host_table = jnp.array(hosts, jnp.int32)
    is_host = dp_no == host_table[dp_no // 2]

    def from_partner(x):
        return lax.ppermute(x, "dp", [(h ^ 1, h) for h in hosts])

    def to_partner(x):
        return lax.ppermute(x, "dp", [(h, h ^ 1) for h in hosts])

    def from_host(x, m):
        return lax.ppermute(x, "dp", [(hosts[k ^ m], hosts[k]) for k in range(n // 2)])

    def to_beyond(x, m):
        return lax.ppermute(
            x, "dp", [(hosts[k ^ m], hosts[k] ^ 1) for k in range(n // 2)]
        )

    def swap_cores(x):
        return lax.ppermute(x, "cores", [(c, cores - 1 - c) for c in range(cores)])

    def along_sections(x, by):
        pairs = [
            (i * n + h, (i + by) * n + h)
            for i in range(sections)
            if 0 <= i + by < sections
            for h in hosts
        ]
        return lax.ppermute(x, ("section", "dp"), pairs)

    first_section = section_no == 0
    last_section = section_no == sections - 1
    between = range(1, n // 2)

    pieces = max(1, min(2, depth // 256))
    piece = depth // pieces
    in_far = [from_host(in_shard, m) for m in between]
    in_near = [
        from_partner(in_shard[i * piece : (i + 1) * piece]) for i in range(pieces)
    ]
    out_near = from_partner(out_shard)
    in_pass = [from_host(in_near[0], m) for m in between]
    in_far, in_near, rows_in, tables_in = lax.optimization_barrier(
        (
            in_far,
            in_near,
            (arrivals, in_flight, cotangent, grad_flight, stashed),
            (forward_blocks, forward_marks, backward_blocks, backward_marks),
        )
    )
    in_pass += [from_host(in_near[i], m) for i in range(1, pieces) for m in between]
    in_parts = [in_shard] + in_far + in_near + in_pass
    arrivals, in_flight, cotangent, grad_flight, stashed = rows_in
    tables = jnp.concatenate(
        [
            jnp.concatenate([b[..., None], m.reshape(m.shape[:2] + (-1,))], axis=-1)
            for b, m in (tables_in[:2], tables_in[2:])
        ],
        axis=0,
    )
    near_tables = from_partner(tables)
    stash_own = stashed[0]
    stash_theirs = from_partner(stash_own)
    x_own = jnp.where(first_section, arrivals[0], in_flight[0])
    x_theirs = from_partner(x_own)
    up_own = jnp.where(last_section, cotangent[0], grad_flight[0])
    new_own = jnp.where(first_section, arrivals[1], cotangent[1])
    out_own, out_near, near_tables = lax.optimization_barrier((out_shard, out_near, near_tables))
    out_far = [from_host(out_own, m) for m in between]
    out_parts = [out_shard, out_near] + out_far + [from_host(out_near, m) for m in between]
    up_late, new_late, stash_theirs = lax.optimization_barrier((up_own, new_own, stash_theirs))
    up_theirs = from_partner(up_late)
    up_near = to_partner(
        lax.dynamic_slice_in_dim(up_late, (dp_no ^ 1) * depth, depth, axis=1)
    )
    new_theirs = from_partner(new_late)
    far_hosts = [host_table[(dp_no // 2) ^ m] for m in between]
    owners = [dp_no, dp_no ^ 1] + far_hosts + [h ^ 1 for h in far_hosts]
    offs = jnp.stack(owners).astype(jnp.int32) * depth
    in_offs = [dp_no * depth] + [h * depth for h in far_hosts]
    in_offs += [(dp_no ^ 1) * depth + i * piece for i in range(pieces)]
    in_offs += [(h ^ 1) * depth + i * piece for i in range(pieces) for h in far_hosts]
    in_offs = jnp.stack(in_offs).astype(jnp.int32)
    parts = len(in_parts)
    core = jnp.reshape(core_no, (1,)).astype(jnp.int32)
    first_flag = jnp.reshape(first_section, (1,)).astype(jnp.int32)
    host_flag = jnp.reshape(is_host, (1,)).astype(jnp.int32)
    last_flag = jnp.reshape(last_section, (1,)).astype(jnp.int32)

    both_tables = jnp.stack([tables, near_tables], axis=1)
    ahead_at = sections - 1 - section_no
    chosen = jnp.stack(
        [
            lax.dynamic_index_in_dim(both_tables[way], at, axis=1, keepdims=False)
            for way, at in (
                (0, ahead_at),
                (1, section_no),
                (1, section_no + 1),
                (0, ahead_at + 1),
            )
        ]
    )
    kept = block_keep(chosen[..., 0], chosen[..., 1:].reshape(-1, 2, BLOCKS, BLOCKS))
    blank = jnp.zeros_like(kept[:, 0])
    keep = jnp.concatenate(
        [
            jnp.concatenate([kept[:, 0], blank], axis=2),
            jnp.concatenate([blank, kept[:, 1]], axis=2),
        ],
        axis=1,
    )

    smem = pl.BlockSpec(memory_space=pltpu.SMEM)
    hbm = pl.BlockSpec(memory_space=pltpu.HBM)

    def all_of(*arrays):
        return [pl.BlockSpec(x.shape, lambda *_, d=x.ndim: (0,) * d) for x in arrays]

    def row_of(x, i):
        return pl.BlockSpec((1,) + x.shape[1:], lambda *_: (i,) + (0,) * (x.ndim - 1))

    params = pltpu.CompilerParams(vmem_limit_bytes=VMEM_BYTES)
    small = pltpu.CompilerParams(vmem_limit_bytes=SMALL_VMEM_BYTES)

    def cost(multiply_adds, bytes_accessed):
        return pl.CostEstimate(
            flops=2 * multiply_adds, bytes_accessed=bytes_accessed, transcendentals=0
        )

    def struct(shape, dtype):
        return jax.ShapeDtypeStruct(shape, dtype)

    halves = [struct((2, share, width), BF16)] * 2
    matmul = rows * width * 4 * slab
    weight_bytes = 2 * width * 5 * slab

    by_head = lambda lead, last: pl.BlockSpec(lead + (last,), lambda h: (0,) * len(lead) + (h,))
    saved_shapes = [
        struct((2, rows, slab), F32),
        struct((2, rows, 3 * slab), BF16),
        struct((2, rows, 4 * slab), F32),
        struct((2, rows, slab), F32),
        struct((2, heads, rows, rows), BF16),
        struct((2, heads, rows, rows), F32),
    ]
    weight_scratch = [pltpu.VMEM(x.shape, BF16) for x in in_parts]
    gated, gate, vqk, slope, mixed, probs, factor = pl.pallas_call(
        on_host(functools.partial(project_kernel, parts, heads)),
        grid=(heads,),
        in_specs=[smem] * 2
        + all_of(x_own, x_theirs, stash_own, stash_theirs, keep)
        + [hbm] * parts,
        out_specs=[by_head((3, rows), HEAD_DIM)] + [hbm] * 6,
        out_shape=[struct((3, rows, slab), BF16)]
        + [pltpu.HBM(x.shape, x.dtype) for x in saved_shapes],
        scratch_shapes=weight_scratch
        + [pltpu.VMEM(x.shape, x.dtype) for x in saved_shapes]
        + [
            pltpu.VMEM((3 * rows, width), BF16),
            pltpu.SemaphoreType.DMA((heads * parts,)),
            pltpu.SemaphoreType.DMA((heads * 6,)),
        ],
        compiler_params=params,
        cost_estimate=cost(3 * matmul, 2 * weight_bytes),
        name="project",
    )(host_flag, in_offs, x_own, x_theirs, stash_own, stash_theirs, keep, *in_hbm(in_parts))

    def backward(ups, tick_no):
        layered = [gate, vqk, slope, mixed, probs, factor, stash_own, stash_theirs]
        plain = list(out_parts) + list(in_parts)
        return pl.pallas_call(
            on_host(functools.partial(backward_kernel, parts, n, tick_no)),
            grid=(1,),
            in_specs=[smem] * 4 + [hbm] * (1 + len(layered) + len(plain)),
            out_specs=all_of(*halves),
            out_shape=halves,
            scratch_shapes=[pltpu.VMEM(ups.shape, BF16)]
            + [pltpu.VMEM(x.shape[1:], x.dtype) for x in layered]
            + [pltpu.VMEM(x.shape, x.dtype) for x in plain]
            + [
                pltpu.VMEM((rows, width), F32),
                pltpu.VMEM((rows, width), BF16),
                pltpu.SemaphoreType.DMA((1 + len(layered) + n + heads * parts,)),
            ],
            compiler_params=params,
            cost_estimate=cost(2 * matmul, 2 * weight_bytes),
            name="backward",
        )(host_flag, core, in_offs, offs, ups, *in_hbm(layered), *out_parts, *in_hbm(in_parts))

    gated, new_theirs, up_near = lax.optimization_barrier((gated, new_theirs, up_near))

    def summed(residual, mine, landed):
        return (residual.astype(F32) + mine.astype(F32) + landed.astype(F32)).astype(BF16)

    def own_rows(mine, others):
        return lax.dynamic_slice_in_dim(jnp.stack([mine, others]), core_no * share, share, axis=1)

    pack_shapes = [struct((rows, width), BF16)]
    pack_shapes += [struct((rows, 2 * slab + depth), BF16)] * (n - 2)
    folded = share * width // rows
    up_0, *packs = pl.pallas_call(
        functools.partial(pack_kernel, n),
        grid=(1,),
        in_specs=[smem] * 1 + all_of(gated, up_own, up_theirs),
        out_specs=all_of(*pack_shapes),
        out_shape=pack_shapes,
        compiler_params=small,
        name="pack",
    )(offs, gated, up_own, up_theirs)
    packs, out_parts = lax.optimization_barrier((packs, out_parts))

    ahead_send, ahead_keep = pl.pallas_call(
        functools.partial(out_kernel, n),
        grid=(1,),
        in_specs=[smem] * 2 + [row_of(gated, 0)] + all_of(*out_parts),
        out_specs=all_of(*halves),
        out_shape=halves,
        scratch_shapes=[pltpu.VMEM((rows, width), BF16)],
        compiler_params=small,
        cost_estimate=cost(matmul // 4, weight_bytes // 4),
        name="out",
    )(core, offs, gated, *out_parts)
    ahead_landed = swap_cores(ahead_send)
    first_shapes = [halves[0], struct((rows, 2 * slab + folded), BF16)]
    ahead_0, partner_pack = pl.pallas_call(
        first_kernel,
        grid=(1,),
        in_specs=[smem] + all_of(x_own, x_theirs, ahead_keep, ahead_landed, gated),
        out_specs=all_of(*first_shapes),
        out_shape=first_shapes,
        compiler_params=small,
        name="first",
    )(core, x_own, x_theirs, ahead_keep, ahead_landed, gated)
    ahead_in = along_sections(ahead_0, 1)
    packs_near = [to_partner(partner_pack)] + [from_host(packs[m - 1], m) for m in between]
    back_send, back_keep = backward(after(up_0, ahead_0), 0)
    back_send, back_keep, ahead_in, packs_near = lax.optimization_barrier(
        (back_send, back_keep, ahead_in, packs_near)
    )
    back_landed = swap_cores(back_send)
    back_0 = summed(own_rows(up_own, up_theirs), back_keep, back_landed)
    back_in = along_sections(back_0, -1)

    packs_beyond = [to_beyond(packs[n // 2 + m - 2], m) for m in between]
    ahead_their = swap_cores(ahead_in)
    ahead_send, ahead_keep = pl.pallas_call(
        on_host(functools.partial(forward_kernel, parts, heads)),
        grid=(heads,),
        in_specs=[smem] * 5
        + all_of(ahead_in, ahead_their, new_own, new_theirs)
        + [row_of(keep, keep.shape[0] - 1)]
        + [hbm] * parts
        + all_of(*out_parts),
        out_specs=all_of(*halves),
        out_shape=halves,
        scratch_shapes=[
            pltpu.VMEM((rows, width), BF16),
            pltpu.VMEM((rows, width), BF16),
            pltpu.VMEM((heads, rows, HEAD_DIM), BF16),
            pltpu.VMEM((rows, width), BF16),
            pltpu.SemaphoreType.DMA((heads * parts,)),
        ]
        + weight_scratch,
        compiler_params=params,
        cost_estimate=cost(2 * matmul, 2 * weight_bytes),
        name="forward",
    )(host_flag, core,
        in_offs,
        offs,
        first_flag,
        ahead_in,
        ahead_their,
        new_own,
        new_theirs,
        keep,
        *in_hbm(in_parts),
        *out_parts,
    )
    new_rows = own_rows(new_own, new_theirs)
    ahead_landed = swap_cores(ahead_send)
    settled = [halves[0], struct((share, width), BF16)]
    ahead_1, ahead_other = pl.pallas_call(
        settle_kernel,
        grid=(1,),
        in_specs=[smem] * 2
        + all_of(new_own, new_theirs, ahead_in, ahead_keep, ahead_landed),
        out_specs=all_of(*settled),
        out_shape=settled,
        compiler_params=small,
        name="settle",
    )(core, first_flag, new_own, new_theirs, ahead_in, ahead_keep, ahead_landed)
    back_given = to_partner(back_0[1])
    ahead_1, ahead_other, back_in, packs_beyond, back_given = lax.optimization_barrier(
        (ahead_1, ahead_other, back_in, packs_beyond, back_given)
    )

    back_their = swap_cores(back_in)
    cut_shapes = [struct((rows, width), BF16), struct((rows, depth + folded), BF16)]
    cut_shapes += [struct((rows, depth), BF16)] * (n - 2)
    up_1, *cuts = pl.pallas_call(
        functools.partial(gather_kernel, n),
        grid=(1,),
        in_specs=[smem] * 3 + all_of(back_in, back_their, new_own, new_theirs, ahead_other),
        out_specs=all_of(*cut_shapes),
        out_shape=cut_shapes,
        compiler_params=small,
        name="gather",
    )(core, offs, last_flag, back_in, back_their, new_own, new_theirs, ahead_other)
    landed = [to_partner(cuts[0])] + [from_host(cuts[m], m) for m in between]
    landed += [to_beyond(cuts[n // 2 + m - 1], m) for m in between]
    back_send, back_keep = backward(up_1, 1)
    back_send, back_keep, landed = lax.optimization_barrier((back_send, back_keep, landed))
    back_1 = summed(
        jnp.where(last_section, new_rows, back_in), back_keep, swap_cores(back_send)
    )

    grads = pl.pallas_call(
        functools.partial(grads_kernel, n, (ticks * length * n) ** (-0.5)),
        grid=(1,),
        in_specs=[smem] * 2 + all_of(
            gated, up_0, up_1, up_own, up_near, *packs_near, *packs_beyond, *landed
        ),
        out_specs=pl.BlockSpec((slab, depth), lambda *_: (0, 0)),
        out_shape=struct((slab, depth), F32),
        compiler_params=small,
        cost_estimate=cost(matmul // 4, weight_bytes // 4),
        name="grads",
    )(
        host_flag, offs, after(gated, back_1), up_0, up_1, up_own, up_near, *packs_near, *packs_beyond, *landed
    )

    first_pack, last_cut, back_given = lax.optimization_barrier(
        (packs_near[0], landed[0], back_given, grads)
    )[:3]
    ahead = jnp.stack(
        [
            jnp.where(is_host, ahead_0[0], unfold(first_pack[:, 2 * slab :], share)),
            jnp.where(is_host, ahead_1[0], unfold(last_cut[:, depth:], share)),
        ]
    )
    back = jnp.stack(
        [
            jnp.where(is_host, back_0[0], back_given),
            jnp.where(is_host, back_1[0], to_partner(back_1[1])),
        ]
    )
    return (ahead[None], back[None], grads[None])


def solution(mesh):
    in_specs = (
        P(None, "dp", None),
        P("section", "dp", None),
        P(None, "dp", None),
        P("section", "dp", None),
        P("section", None, "dp", None),
        P("section", "dp", "cores"),
        P("section", "cores", "dp"),
        P("dp", None),
        P("dp", None),
        P("dp", None, None, None),
        P("dp", None, None, None),
    )
    out_specs = (
        P("section", None, ("dp", "cores"), None),
        P("section", None, ("dp", "cores"), None),
        P("section", "cores", "dp"),
    )
    return jax.shard_map(
        per_device, mesh=mesh, in_specs=in_specs, out_specs=out_specs, check_vma=False
    )
```

```python
import functools

import jax
import jax.numpy as jnp
from jax import lax
from jax.experimental import pallas as pl
from jax.experimental.pallas import tpu as pltpu
from jax.sharding import PartitionSpec as P

HEAD_DIM = 128
BLOCK = 24
BLOCKS = 4
EPSILON = 1e-06
SCALING = HEAD_DIM ** (-0.5)
VMEM_BYTES = 34 * 1024 * 1024
SMALL_VMEM_BYTES = 16 * 1024 * 1024

F32 = jnp.float32
BF16 = jnp.bfloat16


def on_host(kernel):
    def guarded(host, *refs):
        pl.when(host[0] != 0)(functools.partial(kernel, *refs))

    return guarded


def dot(a, b):
    return lax.dot_general(a, b, (((1,), (0,)), ((), ())), preferred_element_type=F32)


def dot_nt(a, b):
    return lax.dot_general(a, b, (((1,), (1,)), ((), ())), preferred_element_type=F32)


def dot_tn(a, b):
    return lax.dot_general(a, b, (((0,), (0,)), ((), ())), preferred_element_type=F32)


def row_root(floats):
    return lax.rsqrt(jnp.mean(floats * floats, axis=-1, keepdims=True) + EPSILON)


def sigmoid(x):
    return 1.0 / (1.0 + jnp.exp(-x))


def attend(pre, keep):
    sig = sigmoid(pre)
    active = pre * sig
    gate = active[:, :HEAD_DIM]
    vqk = active[:, HEAD_DIM:].astype(BF16)
    value = vqk[:, :HEAD_DIM]
    query = vqk[:, HEAD_DIM : 2 * HEAD_DIM]
    key = vqk[:, 2 * HEAD_DIM :]
    scores = dot_nt(query, key) * SCALING
    sig_s = sigmoid(scores)
    probs = (scores * sig_s * keep).astype(BF16)
    mixed = dot(probs, value)
    gated = (mixed * row_root(mixed) * gate).astype(BF16)
    return sig, gate, vqk, scores, sig_s, probs, mixed, gated


def project(normed, offs, weights, of_head):
    total = None
    for j, weight in enumerate(weights):
        depth = weight.shape[0]
        columns = pl.ds(pl.multiple_of(offs[j], depth), depth)
        term = dot(normed[:, columns], weight[:, of_head])
        total = term if total is None else total + term
    return total


def columns_of_head(h, size):
    return pl.ds(pl.multiple_of(h * size, size), size)


def weight_copies(sources, targets, sems, h):
    of_head = columns_of_head(h, 4 * HEAD_DIM)
    return [
        pltpu.make_async_copy(
            source.at[:, of_head], target.at[:, of_head], sems.at[h * len(sources) + j]
        )
        for j, (source, target) in enumerate(zip(sources, targets))
    ]


def project_kernel(parts, heads, offs, x_own, x_theirs, stash_own, stash_theirs, keep, *rest):
    sources, rest = rest[:parts], rest[parts:]
    gated_out, saved, rest = rest[0], rest[1:7], rest[7:]
    weights, rest = rest[:parts], rest[parts:]
    held, (normed, sems, out_sems) = rest[:6], rest[6:]
    gate_out, vqk_out, slope_out, mixed_out, probs_out, factor_out = held
    length = x_own.shape[0]
    rows = 2 * length
    head = pl.program_id(0)

    def saved_copies(h):
        copies = []
        for i, (source, target) in enumerate(zip(held, saved)):
            if i < 4:
                at = (slice(None), slice(None), columns_of_head(h, source.shape[2] // heads))
            else:
                at = (slice(None), h)
            copies.append(
                pltpu.make_async_copy(source.at[at], target.at[at], out_sems.at[h * 6 + i])
            )
        return copies

    @pl.when(head == 0)
    def _():
        for h in range(heads):
            for copy in weight_copies(sources, weights, sems, h):
                copy.start()
        blocks = [x_own, x_theirs]
        for t in range(stash_own.shape[0]):
            blocks += [stash_own.at[t], stash_theirs.at[t]]
        for i, block in enumerate(blocks):
            floats = block[...].astype(F32)
            normed[pl.ds(i * length, length), :] = (floats * row_root(floats)).astype(BF16)

    for copy in weight_copies(sources, weights, sems, head):
        copy.wait()
    pre_all = project(normed, offs, weights, columns_of_head(head, 4 * HEAD_DIM))
    for i in range(1 + stash_own.shape[0]):
        pre = pre_all[i * rows : (i + 1) * rows]
        kept = keep[i]
        sig, gate, vqk, scores, sig_s, probs, mixed, gated = attend(pre, kept)
        gated_out[i] = gated
        if i > 0:
            narrow = columns_of_head(head, HEAD_DIM)
            gate_out[i - 1, :, narrow] = gate
            vqk_out[i - 1, :, columns_of_head(head, 3 * HEAD_DIM)] = vqk
            slope_out[i - 1, :, columns_of_head(head, 4 * HEAD_DIM)] = sig * (
                1.0 + pre * (1.0 - sig)
            )
            mixed_out[i - 1, :, narrow] = mixed
            probs_out[i - 1, head] = probs
            factor_out[i - 1, head] = kept * sig_s * (1.0 + scores * (1.0 - sig_s)) * SCALING
    for copy in saved_copies(head):
        copy.start()

    @pl.when(head == heads - 1)
    def _():
        for h in range(heads):
            for copy in saved_copies(h):
                copy.wait()


def split_rows(core, part, send, keep):
    share = send.shape[1]
    cores = part.shape[0] // (2 * share)
    for r in range(2):
        base = r * cores * share
        mine = pl.multiple_of(base + core * share, share)
        other = pl.multiple_of(base + (cores - 1 - core) * share, share)
        send[r] = part[pl.ds(other, share), :]
        keep[r] = part[pl.ds(mine, share), :]


def out_kernel(n, core, offs, gated, *rest):
    weights = rest[:n]
    send, keep, part = rest[n:]
    depth = weights[0].shape[1]
    for j in range(n):
        columns = pl.ds(pl.multiple_of(offs[j], depth), depth)
        part[:, columns] = dot(gated[0], weights[j][...]).astype(BF16)
    split_rows(core[0], part, send, keep)


def assemble(core, fresh, mine, theirs, new_own, new_theirs, whole):
    share = mine.shape[1]
    length = new_own.shape[0]
    cores = length // share
    use_fresh = fresh != 0
    for r, source in enumerate((new_own, new_theirs)):
        for owner, landed in ((core, mine), (cores - 1 - core, theirs)):
            inside = pl.multiple_of(owner * share, share)
            rows = source[pl.ds(inside, share), :]
            at = pl.multiple_of(r * length + owner * share, share)
            whole[pl.ds(at, share), :] = jnp.where(use_fresh, rows, landed[r])


def forward_kernel(parts, heads, core, in_offs, offs, fresh, mine, theirs, new_own, new_theirs, keep, *rest):
    sources, rest = rest[:parts], rest[parts:]
    in_parts, rest = rest[-parts:], rest[:-parts]
    out_parts = rest[:-7]
    send, kept, whole, normed, gated, part, sems = rest[-7:]
    depth = out_parts[0].shape[1]
    head = pl.program_id(0)

    @pl.when(head == 0)
    def _():
        for h in range(heads):
            for copy in weight_copies(sources, in_parts, sems, h):
                copy.start()
        assemble(core[0], fresh[0], mine, theirs, new_own, new_theirs, whole)
        floats = whole[...].astype(F32)
        normed[...] = (floats * row_root(floats)).astype(BF16)

    for copy in weight_copies(sources, in_parts, sems, head):
        copy.wait()
    pre = project(normed, in_offs, in_parts, columns_of_head(head, 4 * HEAD_DIM))
    gated[head] = attend(pre, keep[0])[-1]

    @pl.when(head == heads - 1)
    def _():
        for j in range(len(out_parts)):
            columns = pl.ds(pl.multiple_of(offs[j], depth), depth)
            total = None
            for h in range(heads):
                term = dot(gated[h], out_parts[j][pl.ds(h * HEAD_DIM, HEAD_DIM), :])
                total = term if total is None else total + term
            part[:, columns] = total.astype(BF16)
        split_rows(core[0], part, send, kept)


def backward_kernel(parts, n, tick, split, core, in_offs, offs, *rest):
    count = 8 + n + parts
    up_sources, rest = rest[: 1 + split], rest[1 + split :]
    sources, rest = (None,) + rest[:count], rest[count:]
    send, keep = rest[:2]
    held, (grad_normed, part, up_sems, sems) = rest[2 : 3 + count], rest[3 + count :]
    ups, gate, vqk, slope, mixed, probs, factor, x_own, x_theirs = held[:9]
    out_parts, in_parts = held[9 : 9 + n], held[9 + n :]
    wide = 4 * HEAD_DIM
    heads = out_parts[0].shape[0] // HEAD_DIM
    copies = []
    for i, (source, target) in enumerate(zip(sources[: 9 + n], held[: 9 + n])):
        if i == 0:
            continue
        if i < 9:
            source = source.at[tick]
        copies.append(pltpu.make_async_copy(source, target, sems.at[i]))
    up_copies = []
    if split:
        share = up_sources[0].shape[1]
        cores = ups.shape[0] // (2 * share)
        for half, owner in enumerate((core[0], cores - 1 - core[0])):
            for r in range(2):
                at = pl.multiple_of((r * cores + owner) * share, share)
                up_copies.append(
                    pltpu.make_async_copy(
                        up_sources[half].at[r],
                        ups.at[pl.ds(at, share), :],
                        up_sems.at[2 * half + r],
                    )
                )
    else:
        up_copies.append(pltpu.make_async_copy(up_sources[0], ups, up_sems.at[0]))
    copies = [None] + copies
    by_head = []
    for h in range(heads):
        of_head = slice(h * wide, (h + 1) * wide)
        by_head.append(
            [
                pltpu.make_async_copy(
                    sources[9 + n + j].at[:, of_head],
                    in_parts[j].at[:, of_head],
                    sems.at[9 + n + h * parts + j],
                )
                for j in range(parts)
            ]
        )
    first = list(range(9, 9 + n))
    second = [1, 4, 2, 5, 6, 3]
    for copy in up_copies:
        copy.start()
    for i in first + second:
        copies[i].start()
    for of_head in by_head:
        for copy in of_head:
            copy.start()
    for i in (7, 8):
        copies[i].start()
    for copy in up_copies:
        copy.wait()
    for i in first:
        copies[i].wait()
    depth = out_parts[0].shape[1]
    length = x_own.shape[0]
    grad_gated = None
    for j in range(n):
        columns = pl.ds(pl.multiple_of(offs[j], depth), depth)
        term = dot_nt(ups[:, columns], out_parts[j][...])
        grad_gated = term if grad_gated is None else grad_gated + term
    grad_gated = grad_gated.astype(BF16).astype(F32)
    for i in second:
        copies[i].wait()

    def through_head(h):
        cut = slice(h * HEAD_DIM, (h + 1) * HEAD_DIM)
        up = grad_gated[:, cut]
        mixed_h = mixed[:, cut]
        root = row_root(mixed_h)
        normed = mixed_h * root
        grad_n = up * gate[:, cut]
        grad_gate = up * normed
        grad_mixed = root * (grad_n - normed * jnp.mean(grad_n * normed, axis=-1, keepdims=True))
        low = grad_mixed.astype(BF16)
        base = 3 * h * HEAD_DIM
        value = vqk[:, base : base + HEAD_DIM]
        query = vqk[:, base + HEAD_DIM : base + 2 * HEAD_DIM]
        key = vqk[:, base + 2 * HEAD_DIM : base + 3 * HEAD_DIM]
        grad_scores = (dot_nt(low, value) * factor[h]).astype(BF16)
        grad_value = dot_tn(probs[h], low)
        grad_query = dot(grad_scores, key)
        grad_key = dot_tn(grad_scores, query)
        grad_active = jnp.concatenate([grad_gate, grad_value, grad_query, grad_key], axis=1)
        return (grad_active * slope[:, h * wide : (h + 1) * wide]).astype(BF16)

    grad_pre = through_head(0)
    for h in range(heads):
        for copy in by_head[h]:
            copy.wait()
        following = through_head(h + 1) if h + 1 < heads else None
        for j in range(parts):
            rows_of = in_parts[j].shape[0]
            columns = pl.ds(pl.multiple_of(in_offs[j], rows_of), rows_of)
            term = dot_nt(grad_pre, in_parts[j][:, h * wide : (h + 1) * wide])
            if h == 0:
                grad_normed[:, columns] = term
            else:
                grad_normed[:, columns] += term
        grad_pre = following
    for i in (7, 8):
        copies[i].wait()
    for r, source in enumerate((x_own, x_theirs)):
        rows = pl.ds(r * length, length)
        floats = source[...].astype(F32)
        root = row_root(floats)
        scaled = floats * root
        grad_n = grad_normed[rows, :]
        part[rows, :] = (
            root * (grad_n - scaled * jnp.mean(grad_n * scaled, axis=-1, keepdims=True))
        ).astype(BF16)
    split_rows(core[0], part, send, keep)


def pack_kernel(n, offs, gated, up_own, up_theirs, whole, *packs):
    depth = packs[0].shape[1] - 2 * gated.shape[2]
    slab = gated.shape[2]
    length = up_own.shape[0]
    whole[:length, :] = up_own[...]
    whole[length:, :] = up_theirs[...]
    for j in range(2, n):
        pack = packs[j - 2]
        columns = pl.ds(pl.multiple_of(offs[j], depth), depth)
        pack[:, :slab] = gated[1]
        pack[:, slab : 2 * slab] = gated[2]
        pack[:length, 2 * slab :] = up_own[:, columns]
        pack[length:, 2 * slab :] = up_theirs[:, columns]


def fold(rows, target, start):
    share, width = rows.shape
    blocks = target.shape[0] // share
    size = width // blocks
    for k in range(blocks):
        target[k * share : (k + 1) * share, start : start + size] = rows[
            :, k * size : (k + 1) * size
        ]


def unfold(folded, share):
    return jnp.concatenate(
        [folded[i : i + share] for i in range(0, folded.shape[0], share)], axis=1
    )


def first_kernel(core, own, theirs, keep, landed, gated, total, pack):
    share = keep.shape[1]
    slab = gated.shape[2]
    here = pl.ds(pl.multiple_of(core[0] * share, share), share)
    for r, source in enumerate((own, theirs)):
        total[r] = (
            source[here, :].astype(F32) + keep[r].astype(F32) + landed[r].astype(F32)
        ).astype(BF16)
    pack[:, :slab] = gated[1]
    pack[:, slab : 2 * slab] = gated[2]
    fold(total[1], pack, 2 * slab)


def last_kernel(
    core, fresh, new_own, new_theirs, passed, keep, landed, up, up_keep, up_landed, ahead, back, pair
):
    share = keep.shape[1]
    here = pl.ds(pl.multiple_of(core[0] * share, share), share)
    for r, source in enumerate((new_own, new_theirs)):
        residual = jnp.where(fresh[0] != 0, source[here, :], passed[r])
        ahead[r] = (
            residual.astype(F32) + keep[r].astype(F32) + landed[r].astype(F32)
        ).astype(BF16)
        back[r] = (
            up[r].astype(F32) + up_keep[r].astype(F32) + up_landed[r].astype(F32)
        ).astype(BF16)
    pair[0] = ahead[1]
    pair[1] = back[1]


def cut_kernel(n, core, offs, fresh, landed, new_own, new_theirs, back, mine, *pieces):
    share = landed.shape[1]
    depth = pieces[-1].shape[1]
    here = pl.ds(pl.multiple_of(core[0] * share, share), share)
    for r, source in enumerate((new_own, new_theirs)):
        mine[r] = jnp.where(fresh[0] != 0, source[here, :], landed[r])
        for j in range(1, n):
            columns = pl.ds(pl.multiple_of(offs[j], depth), depth)
            pieces[j - 1][r * share : (r + 1) * share, :depth] = mine[r, :, columns]
    fold(back[1], pieces[0], depth)


def grads_kernel(
    n, scaling, host, core, offs, gated, up_0, up_own, up_near, mine, theirs, halves, other, *rest
):
    packs = rest[: n - 1]
    out, whole = rest[n - 1 :]
    slab = gated.shape[2]
    depth = out.shape[1]
    share = mine.shape[1]
    cores = whole.shape[0] // (2 * share)
    at_host = host[0] != 0
    columns = pl.ds(pl.multiple_of(offs[0], depth), depth)

    def product(first, second, third, upstream):
        for half, owner in enumerate((core[0], cores - 1 - core[0])):
            for r in range(2):
                at = pl.multiple_of((r * cores + owner) * share, share)
                whole[pl.ds(at, share), :] = upstream(half, r)
        return dot_tn(first, third) + dot_tn(second, whole[...])

    up_pair = jnp.concatenate([up_near[...], up_own[:, columns]], axis=0)
    total = product(
        jnp.where(at_host, gated[1], packs[0][:, :slab]),
        jnp.where(at_host, gated[2], packs[0][:, slab : 2 * slab]),
        jnp.where(at_host, up_0[:, columns], up_pair),
        lambda half, r: jnp.where(
            at_host,
            (mine, theirs)[half][r, :, columns],
            (halves, other)[half][0, r * share : (r + 1) * share, :],
        ),
    )
    for m in range(1, n // 2):
        near, beyond = m, n // 2 + m - 1
        pack = jnp.where(at_host, packs[near][...], packs[beyond][...])
        total = total + product(
            pack[:, :slab],
            pack[:, slab : 2 * slab],
            pack[:, 2 * slab :],
            lambda half, r: (halves, other)[half][m, r * share : (r + 1) * share, :],
        )
    out[...] = total * scaling


def in_hbm(arrays):
    return [pltpu.with_memory_space_constraint(x, pltpu.HBM) for x in arrays]


def after(value, *earlier):
    return lax.optimization_barrier((value,) + earlier)[0]


def block_keep(live_blocks, block_marks):
    length = BLOCKS * BLOCK
    places = jnp.arange(length, dtype=jnp.int32)
    owners = places // BLOCK
    marked = jnp.repeat(jnp.repeat(block_marks, BLOCK, axis=-2), BLOCK, axis=-1) == 1
    allowed = (owners[:, None] == owners[None, :]) | marked
    causal = places[:, None] >= places[None, :]
    tokens = live_blocks[..., None, None] * BLOCK
    keeping = causal & allowed & (places[:, None] < tokens) & (places[None, :] < tokens)
    return jnp.where(keeping, 1.0 / jnp.maximum(tokens, 1).astype(F32), 0.0)


def per_device(
    arrivals,
    in_flight,
    cotangent,
    grad_flight,
    stashed,
    in_weight,
    out_weight,
    forward_blocks,
    backward_blocks,
    forward_marks,
    backward_marks,
):
    section_no = lax.axis_index("section")
    sections = lax.axis_size("section")
    core_no = lax.axis_index("cores")
    cores = lax.axis_size("cores")
    dp_no = lax.axis_index("dp")
    n = lax.axis_size("dp")
    ticks = arrivals.shape[0]
    length = arrivals.shape[1]
    width = arrivals.shape[2]
    rows = 2 * length
    share = length // cores
    in_shard = in_weight[0]
    out_shard = out_weight[0]
    depth = in_shard.shape[0]
    slab = out_shard.shape[0]
    heads = slab // HEAD_DIM
    wide = 4 * HEAD_DIM

    hosts = [2 * k + 1 if 4 * k < n - 2 else 2 * k for k in range(n // 2)]
    host_table = jnp.array(hosts, jnp.int32)
    is_host = dp_no == host_table[dp_no // 2]

    def from_partner(x):
        return lax.ppermute(x, "dp", [(h ^ 1, h) for h in hosts])

    def to_partner(x):
        return lax.ppermute(x, "dp", [(h, h ^ 1) for h in hosts])

    def from_host(x, m):
        return lax.ppermute(x, "dp", [(hosts[k ^ m], hosts[k]) for k in range(n // 2)])

    def to_beyond(x, m):
        return lax.ppermute(
            x, "dp", [(hosts[k ^ m], hosts[k] ^ 1) for k in range(n // 2)]
        )

    def swap_cores(x):
        return lax.ppermute(x, "cores", [(c, cores - 1 - c) for c in range(cores)])

    def along_sections(x, by):
        pairs = [
            (i * n + h, (i + by) * n + h)
            for i in range(sections)
            if 0 <= i + by < sections
            for h in hosts
        ]
        return lax.ppermute(x, ("section", "dp"), pairs)

    first_section = section_no == 0
    last_section = section_no == sections - 1
    between = range(1, n // 2)

    pieces = max(1, min(2, depth // 256))
    piece = depth // pieces
    in_far = [from_host(in_shard, m) for m in between]
    in_near = [
        from_partner(in_shard[i * piece : (i + 1) * piece]) for i in range(pieces)
    ]
    out_near = from_partner(out_shard)
    in_pass = [from_host(in_near[0], m) for m in between]
    in_far, in_near, rows_in, tables_in = lax.optimization_barrier(
        (
            in_far,
            in_near,
            (arrivals, in_flight, cotangent, grad_flight, stashed),
            (forward_blocks, forward_marks, backward_blocks, backward_marks),
        )
    )
    in_pass += [from_host(in_near[i], m) for i in range(1, pieces) for m in between]
    in_parts = [in_shard] + in_far + in_near + in_pass
    arrivals, in_flight, cotangent, grad_flight, stashed = rows_in
    tables = jnp.concatenate(
        [
            jnp.concatenate([b[..., None], m.reshape(m.shape[:2] + (-1,))], axis=-1)
            for b, m in (tables_in[:2], tables_in[2:])
        ],
        axis=0,
    )
    near_tables = from_partner(tables)
    stash_own = stashed[0]
    stash_theirs = from_partner(stash_own)
    x_own = jnp.where(first_section, arrivals[0], in_flight[0])
    x_theirs = from_partner(x_own)
    up_own = jnp.where(last_section, cotangent[0], grad_flight[0])
    new_own = jnp.where(first_section, arrivals[1], cotangent[1])
    out_own, out_near, near_tables = lax.optimization_barrier((out_shard, out_near, near_tables))
    out_far = [from_host(out_own, m) for m in between]
    out_parts = [out_shard, out_near] + out_far + [from_host(out_near, m) for m in between]
    up_late, new_late, stash_theirs = lax.optimization_barrier((up_own, new_own, stash_theirs))
    up_theirs = from_partner(up_late)
    up_near = to_partner(
        lax.dynamic_slice_in_dim(up_late, (dp_no ^ 1) * depth, depth, axis=1)
    )
    new_theirs = from_partner(new_late)
    far_hosts = [host_table[(dp_no // 2) ^ m] for m in between]
    owners = [dp_no, dp_no ^ 1] + far_hosts + [h ^ 1 for h in far_hosts]
    offs = jnp.stack(owners).astype(jnp.int32) * depth
    in_offs = [dp_no * depth] + [h * depth for h in far_hosts]
    in_offs += [(dp_no ^ 1) * depth + i * piece for i in range(pieces)]
    in_offs += [(h ^ 1) * depth + i * piece for i in range(pieces) for h in far_hosts]
    in_offs = jnp.stack(in_offs).astype(jnp.int32)
    parts = len(in_parts)
    core = jnp.reshape(core_no, (1,)).astype(jnp.int32)
    first_flag = jnp.reshape(first_section, (1,)).astype(jnp.int32)
    host_flag = jnp.reshape(is_host, (1,)).astype(jnp.int32)
    last_flag = jnp.reshape(last_section, (1,)).astype(jnp.int32)

    both_tables = jnp.stack([tables, near_tables], axis=1)
    ahead_at = sections - 1 - section_no
    chosen = jnp.stack(
        [
            lax.dynamic_index_in_dim(both_tables[way], at, axis=1, keepdims=False)
            for way, at in (
                (0, ahead_at),
                (1, section_no),
                (1, section_no + 1),
                (0, ahead_at + 1),
            )
        ]
    )
    kept = block_keep(chosen[..., 0], chosen[..., 1:].reshape(-1, 2, BLOCKS, BLOCKS))
    blank = jnp.zeros_like(kept[:, 0])
    keep = jnp.concatenate(
        [
            jnp.concatenate([kept[:, 0], blank], axis=2),
            jnp.concatenate([blank, kept[:, 1]], axis=2),
        ],
        axis=1,
    )

    smem = pl.BlockSpec(memory_space=pltpu.SMEM)
    hbm = pl.BlockSpec(memory_space=pltpu.HBM)

    def all_of(*arrays):
        return [pl.BlockSpec(x.shape, lambda *_, d=x.ndim: (0,) * d) for x in arrays]

    def row_of(x, i):
        return pl.BlockSpec((1,) + x.shape[1:], lambda *_: (i,) + (0,) * (x.ndim - 1))

    params = pltpu.CompilerParams(vmem_limit_bytes=VMEM_BYTES)
    small = pltpu.CompilerParams(vmem_limit_bytes=SMALL_VMEM_BYTES)

    def cost(multiply_adds, bytes_accessed):
        return pl.CostEstimate(
            flops=2 * multiply_adds, bytes_accessed=bytes_accessed, transcendentals=0
        )

    def struct(shape, dtype):
        return jax.ShapeDtypeStruct(shape, dtype)

    halves = [struct((2, share, width), BF16)] * 2
    matmul = rows * width * 4 * slab
    weight_bytes = 2 * width * 5 * slab

    by_head = lambda lead, last: pl.BlockSpec(lead + (last,), lambda h: (0,) * len(lead) + (h,))
    saved_shapes = [
        struct((2, rows, slab), F32),
        struct((2, rows, 3 * slab), BF16),
        struct((2, rows, 4 * slab), F32),
        struct((2, rows, slab), F32),
        struct((2, heads, rows, rows), BF16),
        struct((2, heads, rows, rows), F32),
    ]
    weight_scratch = [pltpu.VMEM(x.shape, BF16) for x in in_parts]
    gated, gate, vqk, slope, mixed, probs, factor = pl.pallas_call(
        on_host(functools.partial(project_kernel, parts, heads)),
        grid=(heads,),
        in_specs=[smem] * 2
        + all_of(x_own, x_theirs, stash_own, stash_theirs, keep)
        + [hbm] * parts,
        out_specs=[by_head((3, rows), HEAD_DIM)] + [hbm] * 6,
        out_shape=[struct((3, rows, slab), BF16)]
        + [pltpu.HBM(x.shape, x.dtype) for x in saved_shapes],
        scratch_shapes=weight_scratch
        + [pltpu.VMEM(x.shape, x.dtype) for x in saved_shapes]
        + [
            pltpu.VMEM((3 * rows, width), BF16),
            pltpu.SemaphoreType.DMA((heads * parts,)),
            pltpu.SemaphoreType.DMA((heads * 6,)),
        ],
        compiler_params=params,
        cost_estimate=cost(3 * matmul, 2 * weight_bytes),
        name="project",
    )(host_flag, in_offs, x_own, x_theirs, stash_own, stash_theirs, keep, *in_hbm(in_parts))

    def backward(ups, tick_no):
        split = len(ups) - 1
        layered = [gate, vqk, slope, mixed, probs, factor, stash_own, stash_theirs]
        plain = list(out_parts) + list(in_parts)
        return pl.pallas_call(
            on_host(functools.partial(backward_kernel, parts, n, tick_no, split)),
            grid=(1,),
            in_specs=[smem] * 4 + [hbm] * (len(ups) + len(layered) + len(plain)),
            out_specs=all_of(*halves),
            out_shape=halves,
            scratch_shapes=[pltpu.VMEM((rows, width), BF16)]
            + [pltpu.VMEM(x.shape[1:], x.dtype) for x in layered]
            + [pltpu.VMEM(x.shape, x.dtype) for x in plain]
            + [
                pltpu.VMEM((rows, width), F32),
                pltpu.VMEM((rows, width), BF16),
                pltpu.SemaphoreType.DMA((4,)),
                pltpu.SemaphoreType.DMA((1 + len(layered) + n + heads * parts,)),
            ],
            compiler_params=params,
            cost_estimate=cost(2 * matmul, 2 * weight_bytes),
            name="backward",
        )(host_flag, core, in_offs, offs, *ups, *in_hbm(layered), *out_parts, *in_hbm(in_parts))

    gated, new_theirs, up_near = lax.optimization_barrier((gated, new_theirs, up_near))

    def summed(residual, mine, landed):
        return (residual.astype(F32) + mine.astype(F32) + landed.astype(F32)).astype(BF16)

    def own_rows(mine, others):
        return lax.dynamic_slice_in_dim(jnp.stack([mine, others]), core_no * share, share, axis=1)

    pack_shapes = [struct((rows, width), BF16)]
    pack_shapes += [struct((rows, 2 * slab + depth), BF16)] * (n - 2)
    folded = share * width // rows
    up_0, *packs = pl.pallas_call(
        functools.partial(pack_kernel, n),
        grid=(1,),
        in_specs=[smem] * 1 + all_of(gated, up_own, up_theirs),
        out_specs=all_of(*pack_shapes),
        out_shape=pack_shapes,
        compiler_params=small,
        name="pack",
    )(offs, gated, up_own, up_theirs)
    packs, out_parts = lax.optimization_barrier((packs, out_parts))

    ahead_send, ahead_keep = pl.pallas_call(
        functools.partial(out_kernel, n),
        grid=(1,),
        in_specs=[smem] * 2 + [row_of(gated, 0)] + all_of(*out_parts),
        out_specs=all_of(*halves),
        out_shape=halves,
        scratch_shapes=[pltpu.VMEM((rows, width), BF16)],
        compiler_params=small,
        cost_estimate=cost(matmul // 4, weight_bytes // 4),
        name="out",
    )(core, offs, gated, *out_parts)
    ahead_landed = swap_cores(ahead_send)
    first_shapes = [halves[0], struct((rows, 2 * slab + folded), BF16)]
    ahead_0, partner_pack = pl.pallas_call(
        first_kernel,
        grid=(1,),
        in_specs=[smem] + all_of(x_own, x_theirs, ahead_keep, ahead_landed, gated),
        out_specs=all_of(*first_shapes),
        out_shape=first_shapes,
        compiler_params=small,
        name="first",
    )(core, x_own, x_theirs, ahead_keep, ahead_landed, gated)
    ahead_in = along_sections(ahead_0, 1)
    packs_near = [to_partner(partner_pack)] + [from_host(packs[m - 1], m) for m in between]
    back_send, back_keep = backward([after(up_0, ahead_0)], 0)
    back_send, back_keep, ahead_in, packs_near = lax.optimization_barrier(
        (back_send, back_keep, ahead_in, packs_near)
    )
    back_landed = swap_cores(back_send)
    back_0 = summed(own_rows(up_own, up_theirs), back_keep, back_landed)
    back_in = along_sections(back_0, -1)

    packs_beyond = [to_beyond(packs[n // 2 + m - 2], m) for m in between]
    ahead_their = swap_cores(ahead_in)
    ahead_send, ahead_keep = pl.pallas_call(
        on_host(functools.partial(forward_kernel, parts, heads)),
        grid=(heads,),
        in_specs=[smem] * 5
        + all_of(ahead_in, ahead_their, new_own, new_theirs)
        + [row_of(keep, keep.shape[0] - 1)]
        + [hbm] * parts
        + all_of(*out_parts),
        out_specs=all_of(*halves),
        out_shape=halves,
        scratch_shapes=[
            pltpu.VMEM((rows, width), BF16),
            pltpu.VMEM((rows, width), BF16),
            pltpu.VMEM((heads, rows, HEAD_DIM), BF16),
            pltpu.VMEM((rows, width), BF16),
            pltpu.SemaphoreType.DMA((heads * parts,)),
        ]
        + weight_scratch,
        compiler_params=params,
        cost_estimate=cost(2 * matmul, 2 * weight_bytes),
        name="forward",
    )(host_flag, core,
        in_offs,
        offs,
        first_flag,
        ahead_in,
        ahead_their,
        new_own,
        new_theirs,
        keep,
        *in_hbm(in_parts),
        *out_parts,
    )
    ahead_send, ahead_keep, back_in, packs_beyond = lax.optimization_barrier(
        (ahead_send, ahead_keep, back_in, packs_beyond)
    )
    ahead_landed = swap_cores(ahead_send)

    cut_shapes = [halves[0], struct((2 * share, depth + width // 2), BF16)]
    cut_shapes += [struct((2 * share, depth), BF16)] * (n - 2)
    up_mine, *cuts = pl.pallas_call(
        functools.partial(cut_kernel, n),
        grid=(1,),
        in_specs=[smem] * 3 + all_of(back_in, new_own, new_theirs, back_0),
        out_specs=all_of(*cut_shapes),
        out_shape=cut_shapes,
        compiler_params=small,
        name="cut",
    )(core, offs, last_flag, back_in, new_own, new_theirs, back_0)
    up_their = swap_cores(up_mine)
    landed = [to_partner(cuts[0])] + [from_host(cuts[m], m) for m in between]
    landed += [to_beyond(cuts[n // 2 + m - 1], m) for m in between]
    back_send, back_keep = backward([up_mine, up_their], 1)
    back_send, back_keep, landed = lax.optimization_barrier((back_send, back_keep, landed))
    last_inputs = [new_own, new_theirs, ahead_in, ahead_keep, ahead_landed]
    last_inputs += [up_mine, back_keep, swap_cores(back_send)]
    last_shapes = [halves[0]] * 3
    ahead_1, back_1, pair = pl.pallas_call(
        last_kernel,
        grid=(1,),
        in_specs=[smem] * 2 + all_of(*last_inputs),
        out_specs=all_of(*last_shapes),
        out_shape=last_shapes,
        compiler_params=small,
        name="last",
    )(core, first_flag, *last_inputs)
    pair = to_partner(pair)

    landed_halves = jnp.stack(
        [landed[0][:, :depth]]
        + [jnp.where(is_host, landed[m], landed[n // 2 + m - 1]) for m in between]
    )
    landed_other = swap_cores(landed_halves)
    grad_inputs = [gated, up_0, up_own, up_near, up_mine, up_their, landed_halves, landed_other]
    grad_inputs += packs_near + packs_beyond
    grad_inputs[0] = after(gated, back_1)
    grads = pl.pallas_call(
        functools.partial(grads_kernel, n, (ticks * length * n) ** (-0.5)),
        grid=(1,),
        in_specs=[smem] * 3 + all_of(*grad_inputs),
        out_specs=pl.BlockSpec((slab, depth), lambda *_: (0, 0)),
        out_shape=struct((slab, depth), F32),
        scratch_shapes=[pltpu.VMEM((rows, depth), BF16)],
        compiler_params=small,
        cost_estimate=cost(matmul // 4, weight_bytes // 4),
        name="grads",
    )(host_flag, core, offs, *grad_inputs)

    first_pack, last_cut = lax.optimization_barrier((packs_near[0], landed[0], back_1))[:2]
    ahead = jnp.stack(
        [
            jnp.where(is_host, ahead_0[0], unfold(first_pack[:, 2 * slab :], share)),
            jnp.where(is_host, ahead_1[0], pair[0]),
        ]
    )
    back = jnp.stack(
        [
            jnp.where(is_host, back_0[0], unfold(last_cut[:, depth:], share)),
            jnp.where(is_host, back_1[0], pair[1]),
        ]
    )
    return (ahead[None], back[None], grads[None])


def solution(mesh):
    in_specs = (
        P(None, "dp", None),
        P("section", "dp", None),
        P(None, "dp", None),
        P("section", "dp", None),
        P("section", None, "dp", None),
        P("section", "dp", "cores"),
        P("section", "cores", "dp"),
        P("dp", None),
        P("dp", None),
        P("dp", None, None, None),
        P("dp", None, None, None),
    )
    out_specs = (
        P("section", None, ("dp", "cores"), None),
        P("section", None, ("dp", "cores"), None),
        P("section", "cores", "dp"),
    )
    return jax.shard_map(
        per_device, mesh=mesh, in_specs=in_specs, out_specs=out_specs, check_vma=False
    )
```

```python
import functools

import jax
import jax.numpy as jnp
from jax import lax
from jax.experimental import pallas as pl
from jax.experimental.pallas import tpu as pltpu
from jax.sharding import PartitionSpec as P

HEAD_DIM = 128
BLOCK = 24
BLOCKS = 4
EPSILON = 1e-06
SCALING = HEAD_DIM ** (-0.5)
VMEM_BYTES = 34 * 1024 * 1024
SMALL_VMEM_BYTES = 16 * 1024 * 1024

F32 = jnp.float32
BF16 = jnp.bfloat16


def on_host(kernel):
    def guarded(host, *refs):
        pl.when(host[0] != 0)(functools.partial(kernel, *refs))

    return guarded


def dot(a, b):
    return lax.dot_general(a, b, (((1,), (0,)), ((), ())), preferred_element_type=F32)


def dot_nt(a, b):
    return lax.dot_general(a, b, (((1,), (1,)), ((), ())), preferred_element_type=F32)


def dot_tn(a, b):
    return lax.dot_general(a, b, (((0,), (0,)), ((), ())), preferred_element_type=F32)


def row_root(floats):
    return lax.rsqrt(jnp.mean(floats * floats, axis=-1, keepdims=True) + EPSILON)


def sigmoid(x):
    return 1.0 / (1.0 + jnp.exp(-x))


def attend(pre, keep):
    sig = sigmoid(pre)
    active = pre * sig
    gate = active[:, :HEAD_DIM]
    vqk = active[:, HEAD_DIM:].astype(BF16)
    value = vqk[:, :HEAD_DIM]
    query = vqk[:, HEAD_DIM : 2 * HEAD_DIM]
    key = vqk[:, 2 * HEAD_DIM :]
    scores = dot_nt(query, key) * SCALING
    sig_s = sigmoid(scores)
    probs = (scores * sig_s * keep).astype(BF16)
    mixed = dot(probs, value)
    gated = (mixed * row_root(mixed) * gate).astype(BF16)
    return sig, gate, vqk, scores, sig_s, probs, mixed, gated


def project(normed, offs, weights, of_head):
    total = None
    for j, weight in enumerate(weights):
        depth = weight.shape[0]
        columns = pl.ds(pl.multiple_of(offs[j], depth), depth)
        term = dot(normed[:, columns], weight[:, of_head])
        total = term if total is None else total + term
    return total


def columns_of_head(h, size):
    return pl.ds(pl.multiple_of(h * size, size), size)


def weight_copies(sources, targets, sems, h):
    of_head = columns_of_head(h, 4 * HEAD_DIM)
    return [
        pltpu.make_async_copy(
            source.at[:, of_head], target.at[:, of_head], sems.at[h * len(sources) + j]
        )
        for j, (source, target) in enumerate(zip(sources, targets))
    ]


def project_kernel(parts, heads, offs, x_own, x_theirs, stash_own, stash_theirs, keep, *rest):
    sources, rest = rest[:parts], rest[parts:]
    gated_out, saved, rest = rest[0], rest[1:7], rest[7:]
    weights, rest = rest[:parts], rest[parts:]
    held, (normed, sems, out_sems) = rest[:6], rest[6:]
    gate_out, vqk_out, slope_out, mixed_out, probs_out, factor_out = held
    length = x_own.shape[0]
    rows = 2 * length
    head = pl.program_id(0)

    def saved_copies(h):
        copies = []
        for i, (source, target) in enumerate(zip(held, saved)):
            if i < 4:
                at = (slice(None), slice(None), columns_of_head(h, source.shape[2] // heads))
            else:
                at = (slice(None), h)
            copies.append(
                pltpu.make_async_copy(source.at[at], target.at[at], out_sems.at[h * 6 + i])
            )
        return copies

    @pl.when(head == 0)
    def _():
        for h in range(heads):
            for copy in weight_copies(sources, weights, sems, h):
                copy.start()
        blocks = [x_own, x_theirs]
        for t in range(stash_own.shape[0]):
            blocks += [stash_own.at[t], stash_theirs.at[t]]
        for i, block in enumerate(blocks):
            floats = block[...].astype(F32)
            normed[pl.ds(i * length, length), :] = (floats * row_root(floats)).astype(BF16)

    for copy in weight_copies(sources, weights, sems, head):
        copy.wait()
    pre_all = project(normed, offs, weights, columns_of_head(head, 4 * HEAD_DIM))
    for i in range(1 + stash_own.shape[0]):
        pre = pre_all[i * rows : (i + 1) * rows]
        kept = keep[i]
        sig, gate, vqk, scores, sig_s, probs, mixed, gated = attend(pre, kept)
        gated_out[i] = gated
        if i > 0:
            narrow = columns_of_head(head, HEAD_DIM)
            gate_out[i - 1, :, narrow] = gate
            vqk_out[i - 1, :, columns_of_head(head, 3 * HEAD_DIM)] = vqk
            slope_out[i - 1, :, columns_of_head(head, 4 * HEAD_DIM)] = sig * (
                1.0 + pre * (1.0 - sig)
            )
            mixed_out[i - 1, :, narrow] = mixed
            probs_out[i - 1, head] = probs
            factor_out[i - 1, head] = kept * sig_s * (1.0 + scores * (1.0 - sig_s)) * SCALING
    for copy in saved_copies(head):
        copy.start()

    @pl.when(head == heads - 1)
    def _():
        for h in range(heads):
            for copy in saved_copies(h):
                copy.wait()


def split_rows(core, part, send, keep):
    share = send.shape[1]
    cores = part.shape[0] // (2 * share)
    for r in range(2):
        base = r * cores * share
        mine = pl.multiple_of(base + core * share, share)
        other = pl.multiple_of(base + (cores - 1 - core) * share, share)
        send[r] = part[pl.ds(other, share), :]
        keep[r] = part[pl.ds(mine, share), :]


def out_kernel(n, core, offs, gated, *rest):
    weights = rest[:n]
    send, keep, part = rest[n:]
    depth = weights[0].shape[1]
    for j in range(n):
        columns = pl.ds(pl.multiple_of(offs[j], depth), depth)
        part[:, columns] = dot(gated[0], weights[j][...]).astype(BF16)
    split_rows(core[0], part, send, keep)


def assemble(core, fresh, mine, theirs, new_own, new_theirs, whole):
    share = mine.shape[1]
    length = new_own.shape[0]
    cores = length // share
    use_fresh = fresh != 0
    for r, source in enumerate((new_own, new_theirs)):
        for owner, landed in ((core, mine), (cores - 1 - core, theirs)):
            inside = pl.multiple_of(owner * share, share)
            rows = source[pl.ds(inside, share), :]
            at = pl.multiple_of(r * length + owner * share, share)
            whole[pl.ds(at, share), :] = jnp.where(use_fresh, rows, landed[r])


def forward_kernel(parts, heads, core, in_offs, offs, fresh, mine, theirs, new_own, new_theirs, keep, *rest):
    sources, rest = rest[:parts], rest[parts:]
    in_parts, rest = rest[-parts:], rest[:-parts]
    out_parts = rest[:-7]
    send, kept, whole, normed, gated, part, sems = rest[-7:]
    depth = out_parts[0].shape[1]
    head = pl.program_id(0)

    @pl.when(head == 0)
    def _():
        for h in range(heads):
            for copy in weight_copies(sources, in_parts, sems, h):
                copy.start()
        assemble(core[0], fresh[0], mine, theirs, new_own, new_theirs, whole)
        floats = whole[...].astype(F32)
        normed[...] = (floats * row_root(floats)).astype(BF16)

    for copy in weight_copies(sources, in_parts, sems, head):
        copy.wait()
    pre = project(normed, in_offs, in_parts, columns_of_head(head, 4 * HEAD_DIM))
    gated[head] = attend(pre, keep[0])[-1]

    @pl.when(head == heads - 1)
    def _():
        for j in range(len(out_parts)):
            columns = pl.ds(pl.multiple_of(offs[j], depth), depth)
            total = None
            for h in range(heads):
                term = dot(gated[h], out_parts[j][pl.ds(h * HEAD_DIM, HEAD_DIM), :])
                total = term if total is None else total + term
            part[:, columns] = total.astype(BF16)
        split_rows(core[0], part, send, kept)


def backward_kernel(parts, n, tick, split, core, in_offs, offs, *rest):
    count = 8 + n + parts
    up_sources, rest = rest[: 1 + split], rest[1 + split :]
    sources, rest = (None,) + rest[:count], rest[count:]
    send, keep = rest[:2]
    held, (grad_normed, part, up_sems, sems) = rest[2 : 3 + count], rest[3 + count :]
    ups, gate, vqk, slope, mixed, probs, factor, x_own, x_theirs = held[:9]
    out_parts, in_parts = held[9 : 9 + n], held[9 + n :]
    wide = 4 * HEAD_DIM
    heads = out_parts[0].shape[0] // HEAD_DIM
    copies = []
    for i, (source, target) in enumerate(zip(sources[: 9 + n], held[: 9 + n])):
        if i == 0:
            continue
        if i < 9:
            source = source.at[tick]
        copies.append(pltpu.make_async_copy(source, target, sems.at[i]))
    up_copies = []
    if split:
        share = up_sources[0].shape[1]
        cores = ups.shape[0] // (2 * share)
        for half, owner in enumerate((core[0], cores - 1 - core[0])):
            for r in range(2):
                at = pl.multiple_of((r * cores + owner) * share, share)
                up_copies.append(
                    pltpu.make_async_copy(
                        up_sources[half].at[r],
                        ups.at[pl.ds(at, share), :],
                        up_sems.at[2 * half + r],
                    )
                )
    else:
        up_copies.append(pltpu.make_async_copy(up_sources[0], ups, up_sems.at[0]))
    copies = [None] + copies
    by_head = []
    for h in range(heads):
        of_head = slice(h * wide, (h + 1) * wide)
        by_head.append(
            [
                pltpu.make_async_copy(
                    sources[9 + n + j].at[:, of_head],
                    in_parts[j].at[:, of_head],
                    sems.at[9 + n + h * parts + j],
                )
                for j in range(parts)
            ]
        )
    first = list(range(9, 9 + n))
    second = [1, 4, 2, 5, 6, 3]
    for copy in up_copies:
        copy.start()
    for i in first + second:
        copies[i].start()
    for of_head in by_head:
        for copy in of_head:
            copy.start()
    for i in (7, 8):
        copies[i].start()
    for copy in up_copies:
        copy.wait()
    depth = out_parts[0].shape[1]
    length = x_own.shape[0]
    grad_gated = None
    for j in range(n):
        columns = pl.ds(pl.multiple_of(offs[j], depth), depth)
        copies[first[j]].wait()
        term = dot_nt(ups[:, columns], out_parts[j][...])
        grad_gated = term if grad_gated is None else grad_gated + term
    grad_gated = grad_gated.astype(BF16).astype(F32)
    for i in second:
        copies[i].wait()

    def through_head(h):
        cut = slice(h * HEAD_DIM, (h + 1) * HEAD_DIM)
        up = grad_gated[:, cut]
        mixed_h = mixed[:, cut]
        root = row_root(mixed_h)
        normed = mixed_h * root
        grad_n = up * gate[:, cut]
        grad_gate = up * normed
        grad_mixed = root * (grad_n - normed * jnp.mean(grad_n * normed, axis=-1, keepdims=True))
        low = grad_mixed.astype(BF16)
        base = 3 * h * HEAD_DIM
        value = vqk[:, base : base + HEAD_DIM]
        query = vqk[:, base + HEAD_DIM : base + 2 * HEAD_DIM]
        key = vqk[:, base + 2 * HEAD_DIM : base + 3 * HEAD_DIM]
        grad_scores = (dot_nt(low, value) * factor[h]).astype(BF16)
        grad_value = dot_tn(probs[h], low)
        grad_query = dot(grad_scores, key)
        grad_key = dot_tn(grad_scores, query)
        grad_active = jnp.concatenate([grad_gate, grad_value, grad_query, grad_key], axis=1)
        return (grad_active * slope[:, h * wide : (h + 1) * wide]).astype(BF16)

    grad_pre = through_head(0)
    for h in range(heads):
        for copy in by_head[h]:
            copy.wait()
        following = through_head(h + 1) if h + 1 < heads else None
        for j in range(parts):
            rows_of = in_parts[j].shape[0]
            columns = pl.ds(pl.multiple_of(in_offs[j], rows_of), rows_of)
            term = dot_nt(grad_pre, in_parts[j][:, h * wide : (h + 1) * wide])
            if h == 0:
                grad_normed[:, columns] = term
            else:
                grad_normed[:, columns] += term
        grad_pre = following
    for i in (7, 8):
        copies[i].wait()
    for r, source in enumerate((x_own, x_theirs)):
        rows = pl.ds(r * length, length)
        floats = source[...].astype(F32)
        root = row_root(floats)
        scaled = floats * root
        grad_n = grad_normed[rows, :]
        part[rows, :] = (
            root * (grad_n - scaled * jnp.mean(grad_n * scaled, axis=-1, keepdims=True))
        ).astype(BF16)
    split_rows(core[0], part, send, keep)


def pack_kernel(n, offs, gated, up_own, up_theirs, whole, *packs):
    depth = packs[0].shape[1] - 2 * gated.shape[2]
    slab = gated.shape[2]
    length = up_own.shape[0]
    whole[:length, :] = up_own[...]
    whole[length:, :] = up_theirs[...]
    for j in range(2, n):
        pack = packs[j - 2]
        columns = pl.ds(pl.multiple_of(offs[j], depth), depth)
        pack[:, :slab] = gated[1]
        pack[:, slab : 2 * slab] = gated[2]
        pack[:length, 2 * slab :] = up_own[:, columns]
        pack[length:, 2 * slab :] = up_theirs[:, columns]


def fold(rows, target, start):
    share, width = rows.shape
    blocks = target.shape[0] // share
    size = width // blocks
    for k in range(blocks):
        target[k * share : (k + 1) * share, start : start + size] = rows[
            :, k * size : (k + 1) * size
        ]


def unfold(folded, start, target):
    share, width = target.shape
    blocks = folded.shape[0] // share
    size = width // blocks
    for k in range(blocks):
        target[:, k * size : (k + 1) * size] = folded[
            k * share : (k + 1) * share, start : start + size
        ]


def finish_kernel(slab, host, ahead_0, ahead_1, back_0, pack, message, ahead, back):
    width = back.shape[1]
    depth = message.shape[1] - width

    @pl.when(host[0] != 0)
    def _():
        ahead[0] = ahead_0[0]
        ahead[1] = ahead_1[0]
        back[...] = back_0[0]

    @pl.when(host[0] == 0)
    def _():
        unfold(pack, 2 * slab, ahead.at[0])
        unfold(message, depth + width // 2, ahead.at[1])
        unfold(message, depth, back)


def first_kernel(core, own, theirs, keep, landed, gated, total, pack):
    share = keep.shape[1]
    slab = gated.shape[2]
    here = pl.ds(pl.multiple_of(core[0] * share, share), share)
    for r, source in enumerate((own, theirs)):
        total[r] = (
            source[here, :].astype(F32) + keep[r].astype(F32) + landed[r].astype(F32)
        ).astype(BF16)
    pack[:, :slab] = gated[1]
    pack[:, slab : 2 * slab] = gated[2]
    fold(total[1], pack, 2 * slab)


def message_kernel(
    core, offs, fresh, new_own, new_theirs, passed, keep, landed, up, back, ahead, message
):
    share = keep.shape[1]
    depth = message.shape[1] - up.shape[2]
    here = pl.ds(pl.multiple_of(core[0] * share, share), share)
    columns = pl.ds(pl.multiple_of(offs[1], depth), depth)
    for r, source in enumerate((new_own, new_theirs)):
        residual = jnp.where(fresh[0] != 0, source[here, :], passed[r])
        ahead[r] = (
            residual.astype(F32) + keep[r].astype(F32) + landed[r].astype(F32)
        ).astype(BF16)
        message[r * share : (r + 1) * share, :depth] = up[r, :, columns]
    fold(back[1], message, depth)
    fold(ahead[1], message, depth + up.shape[2] // 2)


def last_kernel(up, keep, landed, back, other):
    for r in range(2):
        back[r] = (
            up[r].astype(F32) + keep[r].astype(F32) + landed[r].astype(F32)
        ).astype(BF16)
    other[...] = back[1]


def cut_kernel(n, core, offs, fresh, landed, new_own, new_theirs, mine, *pieces):
    share = landed.shape[1]
    depth = pieces[-1].shape[1]
    here = pl.ds(pl.multiple_of(core[0] * share, share), share)
    for r, source in enumerate((new_own, new_theirs)):
        mine[r] = jnp.where(fresh[0] != 0, source[here, :], landed[r])
        for j in range(2, n):
            columns = pl.ds(pl.multiple_of(offs[j], depth), depth)
            pieces[j - 2][r * share : (r + 1) * share, :] = mine[r, :, columns]


def grads_kernel(
    n, scaling, host, core, offs, gated, up_0, up_own, up_near, mine, theirs, halves, other, *rest
):
    packs = rest[: n - 1]
    out, whole = rest[n - 1 :]
    slab = gated.shape[2]
    depth = out.shape[1]
    share = mine.shape[1]
    cores = whole.shape[0] // (2 * share)
    at_host = host[0] != 0
    columns = pl.ds(pl.multiple_of(offs[0], depth), depth)

    def product(first, second, third, upstream):
        for half, owner in enumerate((core[0], cores - 1 - core[0])):
            for r in range(2):
                at = pl.multiple_of((r * cores + owner) * share, share)
                whole[pl.ds(at, share), :] = upstream(half, r)
        return dot_tn(first, third) + dot_tn(second, whole[...])

    up_pair = jnp.concatenate([up_near[...], up_own[:, columns]], axis=0)
    total = product(
        jnp.where(at_host, gated[1], packs[0][:, :slab]),
        jnp.where(at_host, gated[2], packs[0][:, slab : 2 * slab]),
        jnp.where(at_host, up_0[:, columns], up_pair),
        lambda half, r: jnp.where(
            at_host,
            (mine, theirs)[half][r, :, columns],
            (halves, other)[half][0, r * share : (r + 1) * share, :],
        ),
    )
    for m in range(1, n // 2):
        near, beyond = m, n // 2 + m - 1
        pack = jnp.where(at_host, packs[near][...], packs[beyond][...])
        total = total + product(
            pack[:, :slab],
            pack[:, slab : 2 * slab],
            pack[:, 2 * slab :],
            lambda half, r: (halves, other)[half][m, r * share : (r + 1) * share, :],
        )
    out[...] = total * scaling


def in_hbm(arrays):
    return [pltpu.with_memory_space_constraint(x, pltpu.HBM) for x in arrays]


def after(value, *earlier):
    return lax.optimization_barrier((value,) + earlier)[0]


def block_keep(live_blocks, block_marks):
    length = BLOCKS * BLOCK
    places = jnp.arange(length, dtype=jnp.int32)
    owners = places // BLOCK
    marked = jnp.repeat(jnp.repeat(block_marks, BLOCK, axis=-2), BLOCK, axis=-1) == 1
    allowed = (owners[:, None] == owners[None, :]) | marked
    causal = places[:, None] >= places[None, :]
    tokens = live_blocks[..., None, None] * BLOCK
    keeping = causal & allowed & (places[:, None] < tokens) & (places[None, :] < tokens)
    return jnp.where(keeping, 1.0 / jnp.maximum(tokens, 1).astype(F32), 0.0)


def per_device(
    arrivals,
    in_flight,
    cotangent,
    grad_flight,
    stashed,
    in_weight,
    out_weight,
    forward_blocks,
    backward_blocks,
    forward_marks,
    backward_marks,
):
    section_no = lax.axis_index("section")
    sections = lax.axis_size("section")
    core_no = lax.axis_index("cores")
    cores = lax.axis_size("cores")
    dp_no = lax.axis_index("dp")
    n = lax.axis_size("dp")
    ticks = arrivals.shape[0]
    length = arrivals.shape[1]
    width = arrivals.shape[2]
    rows = 2 * length
    share = length // cores
    in_shard = in_weight[0]
    out_shard = out_weight[0]
    depth = in_shard.shape[0]
    slab = out_shard.shape[0]
    heads = slab // HEAD_DIM
    wide = 4 * HEAD_DIM

    hosts = [2 * k + 1 if 4 * k < n - 2 else 2 * k for k in range(n // 2)]
    host_table = jnp.array(hosts, jnp.int32)
    is_host = dp_no == host_table[dp_no // 2]

    def from_partner(x):
        return lax.ppermute(x, "dp", [(h ^ 1, h) for h in hosts])

    def to_partner(x):
        return lax.ppermute(x, "dp", [(h, h ^ 1) for h in hosts])

    def from_host(x, m):
        return lax.ppermute(x, "dp", [(hosts[k ^ m], hosts[k]) for k in range(n // 2)])

    def to_beyond(x, m):
        return lax.ppermute(
            x, "dp", [(hosts[k ^ m], hosts[k] ^ 1) for k in range(n // 2)]
        )

    def swap_cores(x):
        return lax.ppermute(x, "cores", [(c, cores - 1 - c) for c in range(cores)])

    def along_sections(x, by):
        pairs = [
            (i * n + h, (i + by) * n + h)
            for i in range(sections)
            if 0 <= i + by < sections
            for h in hosts
        ]
        return lax.ppermute(x, ("section", "dp"), pairs)

    first_section = section_no == 0
    last_section = section_no == sections - 1
    between = range(1, n // 2)

    pieces = max(1, min(2, depth // 256))
    piece = depth // pieces
    in_far = [from_host(in_shard, m) for m in between]
    in_near = [
        from_partner(in_shard[i * piece : (i + 1) * piece]) for i in range(pieces)
    ]
    out_near = from_partner(out_shard)
    in_pass = [from_host(in_near[0], m) for m in between]
    in_far, in_near, rows_in, tables_in = lax.optimization_barrier(
        (
            in_far,
            in_near,
            (arrivals, in_flight, cotangent, grad_flight, stashed),
            (forward_blocks, forward_marks, backward_blocks, backward_marks),
        )
    )
    in_pass += [from_host(in_near[i], m) for i in range(1, pieces) for m in between]
    in_parts = [in_shard] + in_far + in_near + in_pass
    arrivals, in_flight, cotangent, grad_flight, stashed = rows_in
    tables = jnp.concatenate(
        [
            jnp.concatenate([b[..., None], m.reshape(m.shape[:2] + (-1,))], axis=-1)
            for b, m in (tables_in[:2], tables_in[2:])
        ],
        axis=0,
    )
    near_tables = from_partner(tables)
    stash_own = stashed[0]
    stash_theirs = from_partner(stash_own)
    x_own = jnp.where(first_section, arrivals[0], in_flight[0])
    x_theirs = from_partner(x_own)
    up_own = jnp.where(last_section, cotangent[0], grad_flight[0])
    new_own = jnp.where(first_section, arrivals[1], cotangent[1])
    out_own, out_near, near_tables = lax.optimization_barrier((out_shard, out_near, near_tables))
    out_far = [from_host(out_own, m) for m in between]
    out_parts = [out_shard, out_near] + out_far + [from_host(out_near, m) for m in between]
    up_late, new_late, stash_theirs = lax.optimization_barrier((up_own, new_own, stash_theirs))
    up_theirs = from_partner(up_late)
    up_near = to_partner(
        lax.dynamic_slice_in_dim(up_late, (dp_no ^ 1) * depth, depth, axis=1)
    )
    new_theirs = from_partner(new_late)
    far_hosts = [host_table[(dp_no // 2) ^ m] for m in between]
    owners = [dp_no, dp_no ^ 1] + far_hosts + [h ^ 1 for h in far_hosts]
    offs = jnp.stack(owners).astype(jnp.int32) * depth
    in_offs = [dp_no * depth] + [h * depth for h in far_hosts]
    in_offs += [(dp_no ^ 1) * depth + i * piece for i in range(pieces)]
    in_offs += [(h ^ 1) * depth + i * piece for i in range(pieces) for h in far_hosts]
    in_offs = jnp.stack(in_offs).astype(jnp.int32)
    parts = len(in_parts)
    core = jnp.reshape(core_no, (1,)).astype(jnp.int32)
    first_flag = jnp.reshape(first_section, (1,)).astype(jnp.int32)
    host_flag = jnp.reshape(is_host, (1,)).astype(jnp.int32)
    last_flag = jnp.reshape(last_section, (1,)).astype(jnp.int32)

    both_tables = jnp.stack([tables, near_tables], axis=1)
    ahead_at = sections - 1 - section_no
    chosen = jnp.stack(
        [
            lax.dynamic_index_in_dim(both_tables[way], at, axis=1, keepdims=False)
            for way, at in (
                (0, ahead_at),
                (1, section_no),
                (1, section_no + 1),
                (0, ahead_at + 1),
            )
        ]
    )
    kept = block_keep(chosen[..., 0], chosen[..., 1:].reshape(-1, 2, BLOCKS, BLOCKS))
    blank = jnp.zeros_like(kept[:, 0])
    keep = jnp.concatenate(
        [
            jnp.concatenate([kept[:, 0], blank], axis=2),
            jnp.concatenate([blank, kept[:, 1]], axis=2),
        ],
        axis=1,
    )

    smem = pl.BlockSpec(memory_space=pltpu.SMEM)
    hbm = pl.BlockSpec(memory_space=pltpu.HBM)

    def all_of(*arrays):
        return [pl.BlockSpec(x.shape, lambda *_, d=x.ndim: (0,) * d) for x in arrays]

    def row_of(x, i):
        return pl.BlockSpec((1,) + x.shape[1:], lambda *_: (i,) + (0,) * (x.ndim - 1))

    params = pltpu.CompilerParams(vmem_limit_bytes=VMEM_BYTES)
    small = pltpu.CompilerParams(vmem_limit_bytes=SMALL_VMEM_BYTES)

    def cost(multiply_adds, bytes_accessed):
        return pl.CostEstimate(
            flops=2 * multiply_adds, bytes_accessed=bytes_accessed, transcendentals=0
        )

    def struct(shape, dtype):
        return jax.ShapeDtypeStruct(shape, dtype)

    halves = [struct((2, share, width), BF16)] * 2
    matmul = rows * width * 4 * slab
    weight_bytes = 2 * width * 5 * slab

    by_head = lambda lead, last: pl.BlockSpec(lead + (last,), lambda h: (0,) * len(lead) + (h,))
    saved_shapes = [
        struct((2, rows, slab), F32),
        struct((2, rows, 3 * slab), BF16),
        struct((2, rows, 4 * slab), F32),
        struct((2, rows, slab), F32),
        struct((2, heads, rows, rows), BF16),
        struct((2, heads, rows, rows), F32),
    ]
    weight_scratch = [pltpu.VMEM(x.shape, BF16) for x in in_parts]
    gated, gate, vqk, slope, mixed, probs, factor = pl.pallas_call(
        on_host(functools.partial(project_kernel, parts, heads)),
        grid=(heads,),
        in_specs=[smem] * 2
        + all_of(x_own, x_theirs, stash_own, stash_theirs, keep)
        + [hbm] * parts,
        out_specs=[by_head((3, rows), HEAD_DIM)] + [hbm] * 6,
        out_shape=[struct((3, rows, slab), BF16)]
        + [pltpu.HBM(x.shape, x.dtype) for x in saved_shapes],
        scratch_shapes=weight_scratch
        + [pltpu.VMEM(x.shape, x.dtype) for x in saved_shapes]
        + [
            pltpu.VMEM((3 * rows, width), BF16),
            pltpu.SemaphoreType.DMA((heads * parts,)),
            pltpu.SemaphoreType.DMA((heads * 6,)),
        ],
        compiler_params=params,
        cost_estimate=cost(3 * matmul, 2 * weight_bytes),
        name="project",
    )(host_flag, in_offs, x_own, x_theirs, stash_own, stash_theirs, keep, *in_hbm(in_parts))

    def backward(ups, tick_no):
        split = len(ups) - 1
        layered = [gate, vqk, slope, mixed, probs, factor, stash_own, stash_theirs]
        plain = list(out_parts) + list(in_parts)
        return pl.pallas_call(
            on_host(functools.partial(backward_kernel, parts, n, tick_no, split)),
            grid=(1,),
            in_specs=[smem] * 4 + [hbm] * (len(ups) + len(layered) + len(plain)),
            out_specs=all_of(*halves),
            out_shape=halves,
            scratch_shapes=[pltpu.VMEM((rows, width), BF16)]
            + [pltpu.VMEM(x.shape[1:], x.dtype) for x in layered]
            + [pltpu.VMEM(x.shape, x.dtype) for x in plain]
            + [
                pltpu.VMEM((rows, width), F32),
                pltpu.VMEM((rows, width), BF16),
                pltpu.SemaphoreType.DMA((4,)),
                pltpu.SemaphoreType.DMA((1 + len(layered) + n + heads * parts,)),
            ],
            compiler_params=params,
            cost_estimate=cost(2 * matmul, 2 * weight_bytes),
            name="backward",
        )(host_flag, core, in_offs, offs, *ups, *in_hbm(layered), *out_parts, *in_hbm(in_parts))

    gated, new_theirs, up_near = lax.optimization_barrier((gated, new_theirs, up_near))

    def summed(residual, mine, landed):
        return (residual.astype(F32) + mine.astype(F32) + landed.astype(F32)).astype(BF16)

    def own_rows(mine, others):
        return lax.dynamic_slice_in_dim(jnp.stack([mine, others]), core_no * share, share, axis=1)

    pack_shapes = [struct((rows, width), BF16)]
    pack_shapes += [struct((rows, 2 * slab + depth), BF16)] * (n - 2)
    folded = share * width // rows
    up_0, *packs = pl.pallas_call(
        functools.partial(pack_kernel, n),
        grid=(1,),
        in_specs=[smem] * 1 + all_of(gated, up_own, up_theirs),
        out_specs=all_of(*pack_shapes),
        out_shape=pack_shapes,
        compiler_params=small,
        name="pack",
    )(offs, gated, up_own, up_theirs)
    packs, out_parts = lax.optimization_barrier((packs, out_parts))

    ahead_send, ahead_keep = pl.pallas_call(
        functools.partial(out_kernel, n),
        grid=(1,),
        in_specs=[smem] * 2 + [row_of(gated, 0)] + all_of(*out_parts),
        out_specs=all_of(*halves),
        out_shape=halves,
        scratch_shapes=[pltpu.VMEM((rows, width), BF16)],
        compiler_params=small,
        cost_estimate=cost(matmul // 4, weight_bytes // 4),
        name="out",
    )(core, offs, gated, *out_parts)
    ahead_landed = swap_cores(ahead_send)
    first_shapes = [halves[0], struct((rows, 2 * slab + folded), BF16)]
    ahead_0, partner_pack = pl.pallas_call(
        first_kernel,
        grid=(1,),
        in_specs=[smem] + all_of(x_own, x_theirs, ahead_keep, ahead_landed, gated),
        out_specs=all_of(*first_shapes),
        out_shape=first_shapes,
        compiler_params=small,
        name="first",
    )(core, x_own, x_theirs, ahead_keep, ahead_landed, gated)
    ahead_in = along_sections(ahead_0, 1)
    packs_near = [to_partner(partner_pack)] + [from_host(packs[m - 1], m) for m in between]
    back_send, back_keep = backward([after(up_0, ahead_0)], 0)
    back_send, back_keep, ahead_in, packs_near = lax.optimization_barrier(
        (back_send, back_keep, ahead_in, packs_near)
    )
    back_landed = swap_cores(back_send)
    back_0 = summed(own_rows(up_own, up_theirs), back_keep, back_landed)
    back_in = along_sections(back_0, -1)

    packs_beyond = [to_beyond(packs[n // 2 + m - 2], m) for m in between]
    ahead_their = swap_cores(ahead_in)
    ahead_send, ahead_keep = pl.pallas_call(
        on_host(functools.partial(forward_kernel, parts, heads)),
        grid=(heads,),
        in_specs=[smem] * 5
        + all_of(ahead_in, ahead_their, new_own, new_theirs)
        + [row_of(keep, keep.shape[0] - 1)]
        + [hbm] * parts
        + all_of(*out_parts),
        out_specs=all_of(*halves),
        out_shape=halves,
        scratch_shapes=[
            pltpu.VMEM((rows, width), BF16),
            pltpu.VMEM((rows, width), BF16),
            pltpu.VMEM((heads, rows, HEAD_DIM), BF16),
            pltpu.VMEM((rows, width), BF16),
            pltpu.SemaphoreType.DMA((heads * parts,)),
        ]
        + weight_scratch,
        compiler_params=params,
        cost_estimate=cost(2 * matmul, 2 * weight_bytes),
        name="forward",
    )(host_flag, core,
        in_offs,
        offs,
        first_flag,
        ahead_in,
        ahead_their,
        new_own,
        new_theirs,
        keep,
        *in_hbm(in_parts),
        *out_parts,
    )
    ahead_send, ahead_keep, back_in, packs_beyond = lax.optimization_barrier(
        (ahead_send, ahead_keep, back_in, packs_beyond)
    )
    ahead_landed = swap_cores(ahead_send)

    cut_shapes = [halves[0]] + [struct((2 * share, depth), BF16)] * (n - 2)
    up_mine, *cuts = pl.pallas_call(
        functools.partial(cut_kernel, n),
        grid=(1,),
        in_specs=[smem] * 3 + all_of(back_in, new_own, new_theirs),
        out_specs=all_of(*cut_shapes),
        out_shape=cut_shapes,
        compiler_params=small,
        name="cut",
    )(core, offs, last_flag, back_in, new_own, new_theirs)
    up_their = swap_cores(up_mine)
    landed = [from_host(cuts[m - 1], m) for m in between]
    landed += [to_beyond(cuts[n // 2 + m - 2], m) for m in between]
    message_inputs = [new_own, new_theirs, ahead_in, ahead_keep, ahead_landed, up_mine, back_0]
    message_shapes = [halves[0], struct((2 * share, depth + width), BF16)]
    ahead_1, message = pl.pallas_call(
        message_kernel,
        grid=(1,),
        in_specs=[smem] * 3 + all_of(*message_inputs),
        out_specs=all_of(*message_shapes),
        out_shape=message_shapes,
        compiler_params=small,
        name="message",
    )(core, offs, first_flag, *message_inputs)
    landed = [to_partner(message)] + landed
    back_send, back_keep = backward([up_mine, up_their], 1)
    back_send, back_keep, landed = lax.optimization_barrier((back_send, back_keep, landed))
    last_inputs = [up_mine, back_keep, swap_cores(back_send)]
    last_shapes = [halves[0], struct((share, width), BF16)]
    back_1, back_other = pl.pallas_call(
        last_kernel,
        grid=(1,),
        in_specs=all_of(*last_inputs),
        out_specs=all_of(*last_shapes),
        out_shape=last_shapes,
        compiler_params=small,
        name="last",
    )(*last_inputs)
    back_last = to_partner(back_other)

    landed_halves = jnp.stack(
        [landed[0][:, :depth]]
        + [jnp.where(is_host, landed[m], landed[n // 2 + m - 1]) for m in between]
    )
    landed_other = swap_cores(landed_halves)
    grad_inputs = [gated, up_0, up_own, up_near, up_mine, up_their, landed_halves, landed_other]
    grad_inputs += packs_near + packs_beyond
    grad_inputs[0] = after(gated, back_1)
    grads = pl.pallas_call(
        functools.partial(grads_kernel, n, (ticks * length * n) ** (-0.5)),
        grid=(1,),
        in_specs=[smem] * 3 + all_of(*grad_inputs),
        out_specs=pl.BlockSpec((slab, depth), lambda *_: (0, 0)),
        out_shape=struct((slab, depth), F32),
        scratch_shapes=[pltpu.VMEM((rows, depth), BF16)],
        compiler_params=small,
        cost_estimate=cost(matmul // 4, weight_bytes // 4),
        name="grads",
    )(host_flag, core, offs, *grad_inputs)

    first_pack, last_cut = lax.optimization_barrier((packs_near[0], landed[0], back_1))[:2]
    finish_inputs = [ahead_0, ahead_1, back_0, first_pack, last_cut]
    finish_shapes = [struct((ticks, share, width), BF16), struct((share, width), BF16)]
    ahead, back_first = pl.pallas_call(
        functools.partial(finish_kernel, slab),
        grid=(1,),
        in_specs=[smem] + all_of(*finish_inputs),
        out_specs=all_of(*finish_shapes),
        out_shape=finish_shapes,
        compiler_params=small,
        name="finish",
    )(host_flag, *finish_inputs)
    back = jnp.stack([back_first, jnp.where(is_host, back_1[0], back_last)])
    return (ahead[None], back[None], grads[None])


def solution(mesh):
    in_specs = (
        P(None, "dp", None),
        P("section", "dp", None),
        P(None, "dp", None),
        P("section", "dp", None),
        P("section", None, "dp", None),
        P("section", "dp", "cores"),
        P("section", "cores", "dp"),
        P("dp", None),
        P("dp", None),
        P("dp", None, None, None),
        P("dp", None, None, None),
    )
    out_specs = (
        P("section", None, ("dp", "cores"), None),
        P("section", None, ("dp", "cores"), None),
        P("section", "cores", "dp"),
    )
    return jax.shard_map(
        per_device, mesh=mesh, in_specs=in_specs, out_specs=out_specs, check_vma=False
    )
```

```python
import functools

import jax
import jax.numpy as jnp
from jax import lax
from jax.experimental import pallas as pl
from jax.experimental.pallas import tpu as pltpu
from jax.sharding import PartitionSpec as P

HEAD_DIM = 128
BLOCK = 24
BLOCKS = 4
EPSILON = 1e-06
SCALING = HEAD_DIM ** (-0.5)
VMEM_BYTES = 34 * 1024 * 1024
SMALL_VMEM_BYTES = 16 * 1024 * 1024

F32 = jnp.float32
BF16 = jnp.bfloat16


def on_host(kernel):
    def guarded(host, *refs):
        pl.when(host[0] != 0)(functools.partial(kernel, *refs))

    return guarded


def dot(a, b):
    return lax.dot_general(a, b, (((1,), (0,)), ((), ())), preferred_element_type=F32)


def dot_nt(a, b):
    return lax.dot_general(a, b, (((1,), (1,)), ((), ())), preferred_element_type=F32)


def dot_tn(a, b):
    return lax.dot_general(a, b, (((0,), (0,)), ((), ())), preferred_element_type=F32)


def row_root(floats):
    return lax.rsqrt(jnp.mean(floats * floats, axis=-1, keepdims=True) + EPSILON)


def sigmoid(x):
    return 1.0 / (1.0 + jnp.exp(-x))


def attend(pre, keep):
    sig = sigmoid(pre)
    active = pre * sig
    gate = active[:, :HEAD_DIM]
    vqk = active[:, HEAD_DIM:].astype(BF16)
    value = vqk[:, :HEAD_DIM]
    query = vqk[:, HEAD_DIM : 2 * HEAD_DIM]
    key = vqk[:, 2 * HEAD_DIM :]
    scores = dot_nt(query, key) * SCALING
    sig_s = sigmoid(scores)
    probs = (scores * sig_s * keep).astype(BF16)
    mixed = dot(probs, value)
    gated = (mixed * row_root(mixed) * gate).astype(BF16)
    return sig, gate, vqk, scores, sig_s, probs, mixed, gated


def project(normed, offs, weights, of_head):
    total = None
    for j, weight in enumerate(weights):
        depth = weight.shape[0]
        columns = pl.ds(pl.multiple_of(offs[j], depth), depth)
        term = dot(normed[:, columns], weight[:, of_head])
        total = term if total is None else total + term
    return total


def columns_of_head(h, size):
    return pl.ds(pl.multiple_of(h * size, size), size)


def weight_copies(sources, targets, sems, h):
    of_head = columns_of_head(h, 4 * HEAD_DIM)
    return [
        pltpu.make_async_copy(
            source.at[:, of_head], target.at[:, of_head], sems.at[h * len(sources) + j]
        )
        for j, (source, target) in enumerate(zip(sources, targets))
    ]


def project_kernel(parts, heads, offs, x_own, x_theirs, stash_own, stash_theirs, keep, *rest):
    sources, rest = rest[:parts], rest[parts:]
    gated_out, saved, rest = rest[0], rest[1:7], rest[7:]
    weights, rest = rest[:parts], rest[parts:]
    held, (normed, sems, out_sems) = rest[:6], rest[6:]
    gate_out, vqk_out, slope_out, mixed_out, probs_out, factor_out = held
    length = x_own.shape[0]
    rows = 2 * length
    head = pl.program_id(0)

    def saved_copies(h):
        copies = []
        for i, (source, target) in enumerate(zip(held, saved)):
            if i < 4:
                at = (slice(None), slice(None), columns_of_head(h, source.shape[2] // heads))
            else:
                at = (slice(None), h)
            copies.append(
                pltpu.make_async_copy(source.at[at], target.at[at], out_sems.at[h * 6 + i])
            )
        return copies

    @pl.when(head == 0)
    def _():
        for h in range(heads):
            for copy in weight_copies(sources, weights, sems, h):
                copy.start()
        blocks = [x_own, x_theirs]
        for t in range(stash_own.shape[0]):
            blocks += [stash_own.at[t], stash_theirs.at[t]]
        for i, block in enumerate(blocks):
            floats = block[...].astype(F32)
            normed[pl.ds(i * length, length), :] = (floats * row_root(floats)).astype(BF16)

    for copy in weight_copies(sources, weights, sems, head):
        copy.wait()
    pre_all = project(normed, offs, weights, columns_of_head(head, 4 * HEAD_DIM))
    for i in range(1 + stash_own.shape[0]):
        pre = pre_all[i * rows : (i + 1) * rows]
        kept = keep[i]
        sig, gate, vqk, scores, sig_s, probs, mixed, gated = attend(pre, kept)
        gated_out[i] = gated
        if i > 0:
            narrow = columns_of_head(head, HEAD_DIM)
            gate_out[i - 1, :, narrow] = gate
            vqk_out[i - 1, :, columns_of_head(head, 3 * HEAD_DIM)] = vqk
            slope_out[i - 1, :, columns_of_head(head, 4 * HEAD_DIM)] = sig * (
                1.0 + pre * (1.0 - sig)
            )
            mixed_out[i - 1, :, narrow] = mixed
            probs_out[i - 1, head] = probs
            factor_out[i - 1, head] = kept * sig_s * (1.0 + scores * (1.0 - sig_s)) * SCALING
    for copy in saved_copies(head):
        copy.start()

    @pl.when(head == heads - 1)
    def _():
        for h in range(heads):
            for copy in saved_copies(h):
                copy.wait()


def split_rows(core, part, send, keep):
    share = send.shape[1]
    cores = part.shape[0] // (2 * share)
    for r in range(2):
        base = r * cores * share
        mine = pl.multiple_of(base + core * share, share)
        other = pl.multiple_of(base + (cores - 1 - core) * share, share)
        send[r] = part[pl.ds(other, share), :]
        keep[r] = part[pl.ds(mine, share), :]


def out_kernel(n, core, offs, gated, *rest):
    weights = rest[:n]
    send, keep, part = rest[n:]
    depth = weights[0].shape[1]
    for j in range(n):
        columns = pl.ds(pl.multiple_of(offs[j], depth), depth)
        part[:, columns] = dot(gated[0], weights[j][...]).astype(BF16)
    split_rows(core[0], part, send, keep)


def assemble(core, fresh, mine, theirs, new_own, new_theirs, whole):
    share = mine.shape[1]
    length = new_own.shape[0]
    cores = length // share
    use_fresh = fresh != 0
    for r, source in enumerate((new_own, new_theirs)):
        for owner, landed in ((core, mine), (cores - 1 - core, theirs)):
            inside = pl.multiple_of(owner * share, share)
            rows = source[pl.ds(inside, share), :]
            at = pl.multiple_of(r * length + owner * share, share)
            whole[pl.ds(at, share), :] = jnp.where(use_fresh, rows, landed[r])


def forward_kernel(parts, heads, core, in_offs, offs, fresh, mine, theirs, new_own, new_theirs, keep, *rest):
    sources, rest = rest[:parts], rest[parts:]
    in_parts, rest = rest[-parts:], rest[:-parts]
    out_parts = rest[:-7]
    send, kept, whole, normed, gated, part, sems = rest[-7:]
    depth = out_parts[0].shape[1]
    head = pl.program_id(0)

    @pl.when(head == 0)
    def _():
        for h in range(heads):
            for copy in weight_copies(sources, in_parts, sems, h):
                copy.start()
        assemble(core[0], fresh[0], mine, theirs, new_own, new_theirs, whole)
        floats = whole[...].astype(F32)
        normed[...] = (floats * row_root(floats)).astype(BF16)

    for copy in weight_copies(sources, in_parts, sems, head):
        copy.wait()
    pre = project(normed, in_offs, in_parts, columns_of_head(head, 4 * HEAD_DIM))
    gated[head] = attend(pre, keep[0])[-1]

    @pl.when(head == heads - 1)
    def _():
        for j in range(len(out_parts)):
            columns = pl.ds(pl.multiple_of(offs[j], depth), depth)
            total = None
            for h in range(heads):
                term = dot(gated[h], out_parts[j][pl.ds(h * HEAD_DIM, HEAD_DIM), :])
                total = term if total is None else total + term
            part[:, columns] = total.astype(BF16)
        split_rows(core[0], part, send, kept)


def backward_kernel(parts, n, tick, split, core, in_offs, offs, *rest):
    count = 8 + n + parts
    up_sources, rest = rest[: 1 + split], rest[1 + split :]
    sources, rest = (None,) + rest[:count], rest[count:]
    send, keep = rest[:2]
    held, (grad_normed, part, up_sems, sems) = rest[2 : 3 + count], rest[3 + count :]
    ups, gate, vqk, slope, mixed, probs, factor, x_own, x_theirs = held[:9]
    out_parts, in_parts = held[9 : 9 + n], held[9 + n :]
    wide = 4 * HEAD_DIM
    heads = out_parts[0].shape[0] // HEAD_DIM
    copies = []
    for i, (source, target) in enumerate(zip(sources[: 9 + n], held[: 9 + n])):
        if i == 0:
            continue
        if i < 9:
            source = source.at[tick]
        copies.append(pltpu.make_async_copy(source, target, sems.at[i]))
    up_copies = []
    if split:
        share = up_sources[0].shape[1]
        cores = ups.shape[0] // (2 * share)
        for half, owner in enumerate((core[0], cores - 1 - core[0])):
            for r in range(2):
                at = pl.multiple_of((r * cores + owner) * share, share)
                up_copies.append(
                    pltpu.make_async_copy(
                        up_sources[half].at[r],
                        ups.at[pl.ds(at, share), :],
                        up_sems.at[2 * half + r],
                    )
                )
    else:
        up_copies.append(pltpu.make_async_copy(up_sources[0], ups, up_sems.at[0]))
    copies = [None] + copies
    by_head = []
    for h in range(heads):
        of_head = slice(h * wide, (h + 1) * wide)
        by_head.append(
            [
                pltpu.make_async_copy(
                    sources[9 + n + j].at[:, of_head],
                    in_parts[j].at[:, of_head],
                    sems.at[9 + n + h * parts + j],
                )
                for j in range(parts)
            ]
        )
    first = list(range(9, 9 + n))
    second = [1, 4, 2, 5, 6, 3]
    for copy in up_copies:
        copy.start()
    for i in first + second:
        copies[i].start()
    for of_head in by_head:
        for copy in of_head:
            copy.start()
    for i in (7, 8):
        copies[i].start()
    for copy in up_copies:
        copy.wait()
    depth = out_parts[0].shape[1]
    length = x_own.shape[0]
    grad_gated = None
    for j in range(n):
        columns = pl.ds(pl.multiple_of(offs[j], depth), depth)
        copies[first[j]].wait()
        term = dot_nt(ups[:, columns], out_parts[j][...])
        grad_gated = term if grad_gated is None else grad_gated + term
    grad_gated = grad_gated.astype(BF16).astype(F32)
    for i in second:
        copies[i].wait()

    def through_head(h):
        cut = slice(h * HEAD_DIM, (h + 1) * HEAD_DIM)
        up = grad_gated[:, cut]
        mixed_h = mixed[:, cut]
        root = row_root(mixed_h)
        normed = mixed_h * root
        grad_n = up * gate[:, cut]
        grad_gate = up * normed
        grad_mixed = root * (grad_n - normed * jnp.mean(grad_n * normed, axis=-1, keepdims=True))
        low = grad_mixed.astype(BF16)
        base = 3 * h * HEAD_DIM
        value = vqk[:, base : base + HEAD_DIM]
        query = vqk[:, base + HEAD_DIM : base + 2 * HEAD_DIM]
        key = vqk[:, base + 2 * HEAD_DIM : base + 3 * HEAD_DIM]
        grad_scores = (dot_nt(low, value) * factor[h]).astype(BF16)
        grad_value = dot_tn(probs[h], low)
        grad_query = dot(grad_scores, key)
        grad_key = dot_tn(grad_scores, query)
        grad_active = jnp.concatenate([grad_gate, grad_value, grad_query, grad_key], axis=1)
        return (grad_active * slope[:, h * wide : (h + 1) * wide]).astype(BF16)

    grad_pre = through_head(0)
    for h in range(heads):
        for copy in by_head[h]:
            copy.wait()
        following = through_head(h + 1) if h + 1 < heads else None
        for j in range(parts):
            rows_of = in_parts[j].shape[0]
            columns = pl.ds(pl.multiple_of(in_offs[j], rows_of), rows_of)
            term = dot_nt(grad_pre, in_parts[j][:, h * wide : (h + 1) * wide])
            if h == 0:
                grad_normed[:, columns] = term
            else:
                grad_normed[:, columns] += term
        grad_pre = following
    for i in (7, 8):
        copies[i].wait()
    for r, source in enumerate((x_own, x_theirs)):
        rows = pl.ds(r * length, length)
        floats = source[...].astype(F32)
        root = row_root(floats)
        scaled = floats * root
        grad_n = grad_normed[rows, :]
        part[rows, :] = (
            root * (grad_n - scaled * jnp.mean(grad_n * scaled, axis=-1, keepdims=True))
        ).astype(BF16)
    split_rows(core[0], part, send, keep)


def pack_kernel(n, offs, gated, up_own, up_theirs, whole, *packs):
    depth = packs[0].shape[1] - 2 * gated.shape[2]
    slab = gated.shape[2]
    length = up_own.shape[0]
    whole[:length, :] = up_own[...]
    whole[length:, :] = up_theirs[...]
    for j in range(2, n):
        pack = packs[j - 2]
        columns = pl.ds(pl.multiple_of(offs[j], depth), depth)
        pack[:, :slab] = gated[1]
        pack[:, slab : 2 * slab] = gated[2]
        pack[:length, 2 * slab :] = up_own[:, columns]
        pack[length:, 2 * slab :] = up_theirs[:, columns]


def fold(rows, target, start):
    share, width = rows.shape
    blocks = target.shape[0] // share
    size = width // blocks
    for k in range(blocks):
        target[k * share : (k + 1) * share, start : start + size] = rows[
            :, k * size : (k + 1) * size
        ]


def unfold(folded, start, target):
    share, width = target.shape
    blocks = folded.shape[0] // share
    size = width // blocks
    for k in range(blocks):
        target[:, k * size : (k + 1) * size] = folded[
            k * share : (k + 1) * share, start : start + size
        ]


def finish_kernel(slab, host, ahead_0, ahead_1, back_0, pack, message, ahead, back):
    width = back.shape[1]
    depth = message.shape[1] - width

    @pl.when(host[0] != 0)
    def _():
        ahead[0] = ahead_0[0]
        ahead[1] = ahead_1[0]
        back[...] = back_0[0]

    @pl.when(host[0] == 0)
    def _():
        unfold(pack, 2 * slab, ahead.at[0])
        unfold(message, depth + width // 2, ahead.at[1])
        unfold(message, depth, back)


def settle_kernel(core, own, theirs, keep, landed, total):
    share = keep.shape[1]
    here = pl.ds(pl.multiple_of(core[0] * share, share), share)
    for r, source in enumerate((own, theirs)):
        total[r] = (
            source[here, :].astype(F32) + keep[r].astype(F32) + landed[r].astype(F32)
        ).astype(BF16)


def first_kernel(core, own, theirs, keep, landed, gated, total, pack):
    slab = gated.shape[2]
    settle_kernel(core, own, theirs, keep, landed, total)
    pack[:, :slab] = gated[1]
    pack[:, slab : 2 * slab] = gated[2]
    fold(total[1], pack, 2 * slab)


def message_kernel(
    core, offs, fresh, new_own, new_theirs, passed, keep, landed, up, back, ahead, message
):
    share = keep.shape[1]
    depth = message.shape[1] - up.shape[2]
    here = pl.ds(pl.multiple_of(core[0] * share, share), share)
    columns = pl.ds(pl.multiple_of(offs[1], depth), depth)
    for r, source in enumerate((new_own, new_theirs)):
        residual = jnp.where(fresh[0] != 0, source[here, :], passed[r])
        ahead[r] = (
            residual.astype(F32) + keep[r].astype(F32) + landed[r].astype(F32)
        ).astype(BF16)
        message[r * share : (r + 1) * share, :depth] = up[r, :, columns]
    fold(back[1], message, depth)
    fold(ahead[1], message, depth + up.shape[2] // 2)


def last_kernel(up, keep, landed, back, other):
    for r in range(2):
        back[r] = (
            up[r].astype(F32) + keep[r].astype(F32) + landed[r].astype(F32)
        ).astype(BF16)
    other[...] = back[1]


def cut_kernel(n, core, offs, fresh, landed, new_own, new_theirs, mine, *pieces):
    share = landed.shape[1]
    depth = pieces[-1].shape[1]
    here = pl.ds(pl.multiple_of(core[0] * share, share), share)
    for r, source in enumerate((new_own, new_theirs)):
        mine[r] = jnp.where(fresh[0] != 0, source[here, :], landed[r])
        for j in range(2, n):
            columns = pl.ds(pl.multiple_of(offs[j], depth), depth)
            pieces[j - 2][r * share : (r + 1) * share, :] = mine[r, :, columns]


def grads_kernel(
    n, scaling, host, core, offs, gated, up_0, up_own, up_near, mine, theirs, halves, other, *rest
):
    packs = rest[: n - 1]
    out, whole = rest[n - 1 :]
    slab = gated.shape[2]
    depth = out.shape[1]
    share = mine.shape[1]
    cores = whole.shape[0] // (2 * share)
    at_host = host[0] != 0
    columns = pl.ds(pl.multiple_of(offs[0], depth), depth)

    def product(first, second, third, upstream):
        for half, owner in enumerate((core[0], cores - 1 - core[0])):
            for r in range(2):
                at = pl.multiple_of((r * cores + owner) * share, share)
                whole[pl.ds(at, share), :] = upstream(half, r)
        return dot_tn(first, third) + dot_tn(second, whole[...])

    up_pair = jnp.concatenate([up_near[...], up_own[:, columns]], axis=0)
    total = product(
        jnp.where(at_host, gated[1], packs[0][:, :slab]),
        jnp.where(at_host, gated[2], packs[0][:, slab : 2 * slab]),
        jnp.where(at_host, up_0[:, columns], up_pair),
        lambda half, r: jnp.where(
            at_host,
            (mine, theirs)[half][r, :, columns],
            (halves, other)[half][0, r * share : (r + 1) * share, :],
        ),
    )
    for m in range(1, n // 2):
        near, beyond = m, n // 2 + m - 1
        pack = jnp.where(at_host, packs[near][...], packs[beyond][...])
        total = total + product(
            pack[:, :slab],
            pack[:, slab : 2 * slab],
            pack[:, 2 * slab :],
            lambda half, r: (halves, other)[half][m, r * share : (r + 1) * share, :],
        )
    out[...] = total * scaling


def in_hbm(arrays):
    return [pltpu.with_memory_space_constraint(x, pltpu.HBM) for x in arrays]


def after(value, *earlier):
    return lax.optimization_barrier((value,) + earlier)[0]


def block_keep(live_blocks, block_marks):
    length = BLOCKS * BLOCK
    places = jnp.arange(length, dtype=jnp.int32)
    owners = places // BLOCK
    marked = jnp.repeat(jnp.repeat(block_marks, BLOCK, axis=-2), BLOCK, axis=-1) == 1
    allowed = (owners[:, None] == owners[None, :]) | marked
    causal = places[:, None] >= places[None, :]
    tokens = live_blocks[..., None, None] * BLOCK
    keeping = causal & allowed & (places[:, None] < tokens) & (places[None, :] < tokens)
    return jnp.where(keeping, 1.0 / jnp.maximum(tokens, 1).astype(F32), 0.0)


def per_device(
    arrivals,
    in_flight,
    cotangent,
    grad_flight,
    stashed,
    in_weight,
    out_weight,
    forward_blocks,
    backward_blocks,
    forward_marks,
    backward_marks,
):
    section_no = lax.axis_index("section")
    sections = lax.axis_size("section")
    core_no = lax.axis_index("cores")
    cores = lax.axis_size("cores")
    dp_no = lax.axis_index("dp")
    n = lax.axis_size("dp")
    ticks = arrivals.shape[0]
    length = arrivals.shape[1]
    width = arrivals.shape[2]
    rows = 2 * length
    share = length // cores
    in_shard = in_weight[0]
    out_shard = out_weight[0]
    depth = in_shard.shape[0]
    slab = out_shard.shape[0]
    heads = slab // HEAD_DIM
    wide = 4 * HEAD_DIM

    hosts = [2 * k + 1 if 4 * k < n - 2 else 2 * k for k in range(n // 2)]
    host_table = jnp.array(hosts, jnp.int32)
    is_host = dp_no == host_table[dp_no // 2]

    def from_partner(x):
        return lax.ppermute(x, "dp", [(h ^ 1, h) for h in hosts])

    def to_partner(x):
        return lax.ppermute(x, "dp", [(h, h ^ 1) for h in hosts])

    def from_host(x, m):
        return lax.ppermute(x, "dp", [(hosts[k ^ m], hosts[k]) for k in range(n // 2)])

    def to_beyond(x, m):
        return lax.ppermute(
            x, "dp", [(hosts[k ^ m], hosts[k] ^ 1) for k in range(n // 2)]
        )

    def swap_cores(x):
        return lax.ppermute(x, "cores", [(c, cores - 1 - c) for c in range(cores)])

    def along_sections(x, by):
        pairs = [
            (i * n + h, (i + by) * n + h)
            for i in range(sections)
            if 0 <= i + by < sections
            for h in hosts
        ]
        return lax.ppermute(x, ("section", "dp"), pairs)

    first_section = section_no == 0
    last_section = section_no == sections - 1
    between = range(1, n // 2)

    pieces = max(1, min(2, depth // 256))
    piece = depth // pieces
    in_far = [from_host(in_shard, m) for m in between]
    in_near = [
        from_partner(in_shard[i * piece : (i + 1) * piece]) for i in range(pieces)
    ]
    out_near = from_partner(out_shard)
    in_pass = [from_host(in_near[0], m) for m in between]
    in_far, in_near, rows_in, tables_in = lax.optimization_barrier(
        (
            in_far,
            in_near,
            (arrivals, in_flight, cotangent, grad_flight, stashed),
            (forward_blocks, forward_marks, backward_blocks, backward_marks),
        )
    )
    in_pass += [from_host(in_near[i], m) for i in range(1, pieces) for m in between]
    in_parts = [in_shard] + in_far + in_near + in_pass
    arrivals, in_flight, cotangent, grad_flight, stashed = rows_in
    tables = jnp.concatenate(
        [
            jnp.concatenate([b[..., None], m.reshape(m.shape[:2] + (-1,))], axis=-1)
            for b, m in (tables_in[:2], tables_in[2:])
        ],
        axis=0,
    )
    near_tables = from_partner(tables)
    stash_own = stashed[0]
    stash_theirs = from_partner(stash_own)
    x_own = jnp.where(first_section, arrivals[0], in_flight[0])
    x_theirs = from_partner(x_own)
    up_own = jnp.where(last_section, cotangent[0], grad_flight[0])
    new_own = jnp.where(first_section, arrivals[1], cotangent[1])
    out_own, out_near, near_tables = lax.optimization_barrier((out_shard, out_near, near_tables))
    out_far = [from_host(out_own, m) for m in between]
    out_parts = [out_shard, out_near] + out_far + [from_host(out_near, m) for m in between]
    up_late, new_late, stash_theirs = lax.optimization_barrier((up_own, new_own, stash_theirs))
    up_theirs = from_partner(up_late)
    up_near = to_partner(
        lax.dynamic_slice_in_dim(up_late, (dp_no ^ 1) * depth, depth, axis=1)
    )
    new_theirs = from_partner(new_late)
    far_hosts = [host_table[(dp_no // 2) ^ m] for m in between]
    owners = [dp_no, dp_no ^ 1] + far_hosts + [h ^ 1 for h in far_hosts]
    offs = jnp.stack(owners).astype(jnp.int32) * depth
    in_offs = [dp_no * depth] + [h * depth for h in far_hosts]
    in_offs += [(dp_no ^ 1) * depth + i * piece for i in range(pieces)]
    in_offs += [(h ^ 1) * depth + i * piece for i in range(pieces) for h in far_hosts]
    in_offs = jnp.stack(in_offs).astype(jnp.int32)
    parts = len(in_parts)
    core = jnp.reshape(core_no, (1,)).astype(jnp.int32)
    first_flag = jnp.reshape(first_section, (1,)).astype(jnp.int32)
    host_flag = jnp.reshape(is_host, (1,)).astype(jnp.int32)
    last_flag = jnp.reshape(last_section, (1,)).astype(jnp.int32)

    both_tables = jnp.stack([tables, near_tables], axis=1)
    ahead_at = sections - 1 - section_no
    chosen = jnp.stack(
        [
            lax.dynamic_index_in_dim(both_tables[way], at, axis=1, keepdims=False)
            for way, at in (
                (0, ahead_at),
                (1, section_no),
                (1, section_no + 1),
                (0, ahead_at + 1),
            )
        ]
    )
    kept = block_keep(chosen[..., 0], chosen[..., 1:].reshape(-1, 2, BLOCKS, BLOCKS))
    blank = jnp.zeros_like(kept[:, 0])
    keep = jnp.concatenate(
        [
            jnp.concatenate([kept[:, 0], blank], axis=2),
            jnp.concatenate([blank, kept[:, 1]], axis=2),
        ],
        axis=1,
    )

    smem = pl.BlockSpec(memory_space=pltpu.SMEM)
    hbm = pl.BlockSpec(memory_space=pltpu.HBM)

    def all_of(*arrays):
        return [pl.BlockSpec(x.shape, lambda *_, d=x.ndim: (0,) * d) for x in arrays]

    def row_of(x, i):
        return pl.BlockSpec((1,) + x.shape[1:], lambda *_: (i,) + (0,) * (x.ndim - 1))

    params = pltpu.CompilerParams(vmem_limit_bytes=VMEM_BYTES)
    small = pltpu.CompilerParams(vmem_limit_bytes=SMALL_VMEM_BYTES)

    def cost(multiply_adds, bytes_accessed):
        return pl.CostEstimate(
            flops=2 * multiply_adds, bytes_accessed=bytes_accessed, transcendentals=0
        )

    def struct(shape, dtype):
        return jax.ShapeDtypeStruct(shape, dtype)

    halves = [struct((2, share, width), BF16)] * 2
    kept_halves = [halves[0], pltpu.HBM(halves[0].shape, BF16)]
    matmul = rows * width * 4 * slab
    weight_bytes = 2 * width * 5 * slab

    by_head = lambda lead, last: pl.BlockSpec(lead + (last,), lambda h: (0,) * len(lead) + (h,))
    saved_shapes = [
        struct((2, rows, slab), F32),
        struct((2, rows, 3 * slab), BF16),
        struct((2, rows, 4 * slab), F32),
        struct((2, rows, slab), F32),
        struct((2, heads, rows, rows), BF16),
        struct((2, heads, rows, rows), F32),
    ]
    weight_scratch = [pltpu.VMEM(x.shape, BF16) for x in in_parts]
    gated, gate, vqk, slope, mixed, probs, factor = pl.pallas_call(
        on_host(functools.partial(project_kernel, parts, heads)),
        grid=(heads,),
        in_specs=[smem] * 2
        + all_of(x_own, x_theirs, stash_own, stash_theirs, keep)
        + [hbm] * parts,
        out_specs=[by_head((3, rows), HEAD_DIM)] + [hbm] * 6,
        out_shape=[struct((3, rows, slab), BF16)]
        + [pltpu.HBM(x.shape, x.dtype) for x in saved_shapes],
        scratch_shapes=weight_scratch
        + [pltpu.VMEM(x.shape, x.dtype) for x in saved_shapes]
        + [
            pltpu.VMEM((3 * rows, width), BF16),
            pltpu.SemaphoreType.DMA((heads * parts,)),
            pltpu.SemaphoreType.DMA((heads * 6,)),
        ],
        compiler_params=params,
        cost_estimate=cost(3 * matmul, 2 * weight_bytes),
        name="project",
    )(host_flag, in_offs, x_own, x_theirs, stash_own, stash_theirs, keep, *in_hbm(in_parts))

    def backward(ups, tick_no):
        split = len(ups) - 1
        layered = [gate, vqk, slope, mixed, probs, factor, stash_own, stash_theirs]
        plain = list(out_parts) + list(in_parts)
        return pl.pallas_call(
            on_host(functools.partial(backward_kernel, parts, n, tick_no, split)),
            grid=(1,),
            in_specs=[smem] * 4 + [hbm] * (len(ups) + len(layered) + len(plain)),
            out_specs=all_of(*halves),
            out_shape=kept_halves,
            scratch_shapes=[pltpu.VMEM((rows, width), BF16)]
            + [pltpu.VMEM(x.shape[1:], x.dtype) for x in layered]
            + [pltpu.VMEM(x.shape, x.dtype) for x in plain]
            + [
                pltpu.VMEM((rows, width), F32),
                pltpu.VMEM((rows, width), BF16),
                pltpu.SemaphoreType.DMA((4,)),
                pltpu.SemaphoreType.DMA((1 + len(layered) + n + heads * parts,)),
            ],
            compiler_params=params,
            cost_estimate=cost(2 * matmul, 2 * weight_bytes),
            name="backward",
        )(host_flag, core, in_offs, offs, *ups, *in_hbm(layered), *out_parts, *in_hbm(in_parts))

    gated, new_theirs, up_near = lax.optimization_barrier((gated, new_theirs, up_near))

    pack_shapes = [struct((rows, width), BF16)]
    pack_shapes += [struct((rows, 2 * slab + depth), BF16)] * (n - 2)
    folded = share * width // rows
    up_0, *packs = pl.pallas_call(
        functools.partial(pack_kernel, n),
        grid=(1,),
        in_specs=[smem] * 1 + all_of(gated, up_own, up_theirs),
        out_specs=all_of(*pack_shapes),
        out_shape=[pltpu.HBM(pack_shapes[0].shape, BF16)] + pack_shapes[1:],
        compiler_params=small,
        name="pack",
    )(offs, gated, up_own, up_theirs)
    packs, out_parts = lax.optimization_barrier((packs, out_parts))

    ahead_send, ahead_keep = pl.pallas_call(
        functools.partial(out_kernel, n),
        grid=(1,),
        in_specs=[smem] * 2 + [row_of(gated, 0)] + all_of(*out_parts),
        out_specs=all_of(*halves),
        out_shape=halves,
        scratch_shapes=[pltpu.VMEM((rows, width), BF16)],
        compiler_params=small,
        cost_estimate=cost(matmul // 4, weight_bytes // 4),
        name="out",
    )(core, offs, gated, *out_parts)
    ahead_landed = swap_cores(ahead_send)
    first_shapes = [halves[0], struct((rows, 2 * slab + folded), BF16)]
    ahead_0, partner_pack = pl.pallas_call(
        first_kernel,
        grid=(1,),
        in_specs=[smem] + all_of(x_own, x_theirs, ahead_keep, ahead_landed, gated),
        out_specs=all_of(*first_shapes),
        out_shape=first_shapes,
        compiler_params=small,
        name="first",
    )(core, *in_hbm([x_own, x_theirs]), ahead_keep, ahead_landed, gated)
    ahead_in = along_sections(ahead_0, 1)
    packs_near = [to_partner(partner_pack)] + [from_host(packs[m - 1], m) for m in between]
    back_send, back_keep = backward(in_hbm([after(up_0, ahead_0)]), 0)
    back_send, back_keep, ahead_in, packs_near = lax.optimization_barrier(
        (back_send, back_keep, ahead_in, packs_near)
    )
    back_landed = swap_cores(back_send)
    back_0 = pl.pallas_call(
        settle_kernel,
        grid=(1,),
        in_specs=[smem] + all_of(up_own, up_theirs, back_keep, back_landed),
        out_specs=all_of(halves[0])[0],
        out_shape=halves[0],
        compiler_params=small,
        name="settle",
    )(core, *in_hbm([up_own, up_theirs, back_keep]), back_landed)
    back_in = along_sections(back_0, -1)

    packs_beyond = [to_beyond(packs[n // 2 + m - 2], m) for m in between]
    ahead_their = swap_cores(ahead_in)
    ahead_send, ahead_keep = pl.pallas_call(
        on_host(functools.partial(forward_kernel, parts, heads)),
        grid=(heads,),
        in_specs=[smem] * 5
        + all_of(ahead_in, ahead_their, new_own, new_theirs)
        + [row_of(keep, keep.shape[0] - 1)]
        + [hbm] * parts
        + all_of(*out_parts),
        out_specs=all_of(*halves),
        out_shape=kept_halves,
        scratch_shapes=[
            pltpu.VMEM((rows, width), BF16),
            pltpu.VMEM((rows, width), BF16),
            pltpu.VMEM((heads, rows, HEAD_DIM), BF16),
            pltpu.VMEM((rows, width), BF16),
            pltpu.SemaphoreType.DMA((heads * parts,)),
        ]
        + weight_scratch,
        compiler_params=params,
        cost_estimate=cost(2 * matmul, 2 * weight_bytes),
        name="forward",
    )(host_flag, core,
        in_offs,
        offs,
        first_flag,
        *in_hbm([ahead_in]),
        ahead_their,
        *in_hbm([new_own, new_theirs, keep]),
        *in_hbm(in_parts),
        *out_parts,
    )
    ahead_send, ahead_keep, back_in, packs_beyond = lax.optimization_barrier(
        (ahead_send, ahead_keep, back_in, packs_beyond)
    )
    ahead_landed = swap_cores(ahead_send)

    cut_shapes = [halves[0]] + [struct((2 * share, depth), BF16)] * (n - 2)
    up_mine, *cuts = pl.pallas_call(
        functools.partial(cut_kernel, n),
        grid=(1,),
        in_specs=[smem] * 3 + all_of(back_in, new_own, new_theirs),
        out_specs=all_of(*cut_shapes),
        out_shape=cut_shapes,
        compiler_params=small,
        name="cut",
    )(core, offs, last_flag, back_in, *in_hbm([new_own, new_theirs]))
    up_their = swap_cores(up_mine)
    landed = [from_host(cuts[m - 1], m) for m in between]
    landed += [to_beyond(cuts[n // 2 + m - 2], m) for m in between]
    message_inputs = [new_own, new_theirs, ahead_in, ahead_keep, ahead_landed, up_mine, back_0]
    message_shapes = [halves[0], struct((2 * share, depth + width), BF16)]
    ahead_1, message = pl.pallas_call(
        message_kernel,
        grid=(1,),
        in_specs=[smem] * 3 + all_of(*message_inputs),
        out_specs=all_of(*message_shapes),
        out_shape=message_shapes,
        compiler_params=small,
        name="message",
    )(core, offs, first_flag, *in_hbm(message_inputs[:4]), *message_inputs[4:6], *in_hbm([back_0]))
    landed = [to_partner(message)] + landed
    back_send, back_keep = backward([up_mine, up_their], 1)
    back_send, back_keep, landed = lax.optimization_barrier((back_send, back_keep, landed))
    last_inputs = [up_mine, *in_hbm([back_keep]), swap_cores(back_send)]
    last_shapes = [halves[0], struct((share, width), BF16)]
    back_1, back_other = pl.pallas_call(
        last_kernel,
        grid=(1,),
        in_specs=all_of(*last_inputs),
        out_specs=all_of(*last_shapes),
        out_shape=last_shapes,
        compiler_params=small,
        name="last",
    )(*last_inputs)
    back_last = to_partner(back_other)

    landed_halves = jnp.stack(
        [landed[0][:, :depth]]
        + [jnp.where(is_host, landed[m], landed[n // 2 + m - 1]) for m in between]
    )
    landed_other = swap_cores(landed_halves)
    grad_inputs = [gated, up_0, up_own, up_near, up_mine, up_their, landed_halves, landed_other]
    grad_inputs += packs_near + packs_beyond
    grad_inputs[0] = after(gated, back_1)
    grad_inputs[8:] = in_hbm(grad_inputs[8:])
    grads = pl.pallas_call(
        functools.partial(grads_kernel, n, (ticks * length * n) ** (-0.5)),
        grid=(1,),
        in_specs=[smem] * 3 + all_of(*grad_inputs),
        out_specs=pl.BlockSpec((slab, depth), lambda *_: (0, 0)),
        out_shape=struct((slab, depth), F32),
        scratch_shapes=[pltpu.VMEM((rows, depth), BF16)],
        compiler_params=small,
        cost_estimate=cost(matmul // 4, weight_bytes // 4),
        name="grads",
    )(host_flag, core, offs, *grad_inputs)

    first_pack, last_cut = lax.optimization_barrier((packs_near[0], landed[0], back_1))[:2]
    finish_inputs = [ahead_0, ahead_1, back_0, first_pack, last_cut]
    finish_shapes = [struct((ticks, share, width), BF16), struct((share, width), BF16)]
    ahead, back_first = pl.pallas_call(
        functools.partial(finish_kernel, slab),
        grid=(1,),
        in_specs=[smem] + all_of(*finish_inputs),
        out_specs=all_of(*finish_shapes),
        out_shape=finish_shapes,
        compiler_params=small,
        name="finish",
    )(host_flag, *finish_inputs)
    back = jnp.stack([back_first, jnp.where(is_host, back_1[0], back_last)])
    return (ahead[None], back[None], grads[None])


def solution(mesh):
    in_specs = (
        P(None, "dp", None),
        P("section", "dp", None),
        P(None, "dp", None),
        P("section", "dp", None),
        P("section", None, "dp", None),
        P("section", "dp", "cores"),
        P("section", "cores", "dp"),
        P("dp", None),
        P("dp", None),
        P("dp", None, None, None),
        P("dp", None, None, None),
    )
    out_specs = (
        P("section", None, ("dp", "cores"), None),
        P("section", None, ("dp", "cores"), None),
        P("section", "cores", "dp"),
    )
    return jax.shard_map(
        per_device, mesh=mesh, in_specs=in_specs, out_specs=out_specs, check_vma=False
    )
```

```python
import functools

import jax
import jax.numpy as jnp
from jax import lax
from jax.experimental import pallas as pl
from jax.experimental.pallas import tpu as pltpu
from jax.sharding import PartitionSpec as P

HEAD_DIM = 128
BLOCK = 24
BLOCKS = 4
EPSILON = 1e-06
SCALING = HEAD_DIM ** (-0.5)
VMEM_BYTES = 34 * 1024 * 1024
SMALL_VMEM_BYTES = 16 * 1024 * 1024

F32 = jnp.float32
BF16 = jnp.bfloat16


def on_host(kernel):
    def guarded(host, *refs):
        pl.when(host[0] != 0)(functools.partial(kernel, *refs))

    return guarded


def dot(a, b):
    return lax.dot_general(a, b, (((1,), (0,)), ((), ())), preferred_element_type=F32)


def dot_nt(a, b):
    return lax.dot_general(a, b, (((1,), (1,)), ((), ())), preferred_element_type=F32)


def dot_tn(a, b):
    return lax.dot_general(a, b, (((0,), (0,)), ((), ())), preferred_element_type=F32)


def row_root(floats):
    return lax.rsqrt(jnp.mean(floats * floats, axis=-1, keepdims=True) + EPSILON)


def sigmoid(x):
    return 1.0 / (1.0 + jnp.exp(-x))


def attend(pre, keep):
    sig = sigmoid(pre)
    active = pre * sig
    gate = active[:, :HEAD_DIM]
    vqk = active[:, HEAD_DIM:].astype(BF16)
    value = vqk[:, :HEAD_DIM]
    query = vqk[:, HEAD_DIM : 2 * HEAD_DIM]
    key = vqk[:, 2 * HEAD_DIM :]
    scores = dot_nt(query, key) * SCALING
    sig_s = sigmoid(scores)
    probs = (scores * sig_s * keep).astype(BF16)
    mixed = dot(probs, value)
    gated = (mixed * row_root(mixed) * gate).astype(BF16)
    return sig, gate, vqk, scores, sig_s, probs, mixed, gated


def project(normed, offs, weights, of_head):
    total = None
    for j, weight in enumerate(weights):
        depth = weight.shape[0]
        columns = pl.ds(pl.multiple_of(offs[j], depth), depth)
        term = dot(normed[:, columns], weight[:, of_head])
        total = term if total is None else total + term
    return total


def columns_of_head(h, size):
    return pl.ds(pl.multiple_of(h * size, size), size)


def weight_copies(sources, targets, sems, h):
    of_head = columns_of_head(h, 4 * HEAD_DIM)
    return [
        pltpu.make_async_copy(
            source.at[:, of_head], target.at[:, of_head], sems.at[h * len(sources) + j]
        )
        for j, (source, target) in enumerate(zip(sources, targets))
    ]


def project_kernel(parts, heads, offs, x_own, x_theirs, stash_own, stash_theirs, keep, *rest):
    sources, rest = rest[:parts], rest[parts:]
    gated_out, saved, rest = rest[0], rest[1:7], rest[7:]
    weights, rest = rest[:parts], rest[parts:]
    held, (normed, sems, out_sems) = rest[:6], rest[6:]
    gate_out, vqk_out, slope_out, mixed_out, probs_out, factor_out = held
    length = x_own.shape[0]
    rows = 2 * length
    head = pl.program_id(0)

    def saved_copies(h):
        copies = []
        for i, (source, target) in enumerate(zip(held, saved)):
            if i < 4:
                at = (slice(None), slice(None), columns_of_head(h, source.shape[2] // heads))
            else:
                at = (slice(None), h)
            copies.append(
                pltpu.make_async_copy(source.at[at], target.at[at], out_sems.at[h * 6 + i])
            )
        return copies

    @pl.when(head == 0)
    def _():
        for h in range(heads):
            for copy in weight_copies(sources, weights, sems, h):
                copy.start()
        blocks = [x_own, x_theirs]
        for t in range(stash_own.shape[0]):
            blocks += [stash_own.at[t], stash_theirs.at[t]]
        for i, block in enumerate(blocks):
            floats = block[...].astype(F32)
            normed[pl.ds(i * length, length), :] = (floats * row_root(floats)).astype(BF16)

    for copy in weight_copies(sources, weights, sems, head):
        copy.wait()
    pre_all = project(normed, offs, weights, columns_of_head(head, 4 * HEAD_DIM))
    for i in range(1 + stash_own.shape[0]):
        pre = pre_all[i * rows : (i + 1) * rows]
        kept = keep[i]
        sig, gate, vqk, scores, sig_s, probs, mixed, gated = attend(pre, kept)
        gated_out[i] = gated
        if i > 0:
            narrow = columns_of_head(head, HEAD_DIM)
            gate_out[i - 1, :, narrow] = gate
            vqk_out[i - 1, :, columns_of_head(head, 3 * HEAD_DIM)] = vqk
            slope_out[i - 1, :, columns_of_head(head, 4 * HEAD_DIM)] = sig * (
                1.0 + pre * (1.0 - sig)
            )
            mixed_out[i - 1, :, narrow] = mixed
            probs_out[i - 1, head] = probs
            factor_out[i - 1, head] = kept * sig_s * (1.0 + scores * (1.0 - sig_s)) * SCALING
    for copy in saved_copies(head):
        copy.start()

    @pl.when(head == heads - 1)
    def _():
        for h in range(heads):
            for copy in saved_copies(h):
                copy.wait()


def split_rows(core, part, send, keep):
    share = send.shape[1]
    cores = part.shape[0] // (2 * share)
    for r in range(2):
        base = r * cores * share
        mine = pl.multiple_of(base + core * share, share)
        other = pl.multiple_of(base + (cores - 1 - core) * share, share)
        send[r] = part[pl.ds(other, share), :]
        keep[r] = part[pl.ds(mine, share), :]


def out_kernel(n, core, offs, gated, *rest):
    weights = rest[:n]
    send, keep, part = rest[n:]
    depth = weights[0].shape[1]
    for j in range(n):
        columns = pl.ds(pl.multiple_of(offs[j], depth), depth)
        part[:, columns] = dot(gated[0], weights[j][...]).astype(BF16)
    split_rows(core[0], part, send, keep)


def assemble(core, fresh, mine, theirs, new_own, new_theirs, whole):
    share = mine.shape[1]
    length = new_own.shape[0]
    cores = length // share
    use_fresh = fresh != 0
    for r, source in enumerate((new_own, new_theirs)):
        for owner, landed in ((core, mine), (cores - 1 - core, theirs)):
            inside = pl.multiple_of(owner * share, share)
            rows = source[pl.ds(inside, share), :]
            at = pl.multiple_of(r * length + owner * share, share)
            whole[pl.ds(at, share), :] = jnp.where(use_fresh, rows, landed[r])


def forward_kernel(parts, heads, core, in_offs, offs, fresh, mine, theirs, new_own, new_theirs, keep, *rest):
    sources, rest = rest[:parts], rest[parts:]
    in_parts, rest = rest[-parts:], rest[:-parts]
    out_parts = rest[:-7]
    send, kept, whole, normed, gated, part, sems = rest[-7:]
    depth = out_parts[0].shape[1]
    head = pl.program_id(0)

    @pl.when(head == 0)
    def _():
        for h in range(heads):
            for copy in weight_copies(sources, in_parts, sems, h):
                copy.start()
        assemble(core[0], fresh[0], mine, theirs, new_own, new_theirs, whole)
        floats = whole[...].astype(F32)
        normed[...] = (floats * row_root(floats)).astype(BF16)

    for copy in weight_copies(sources, in_parts, sems, head):
        copy.wait()
    pre = project(normed, in_offs, in_parts, columns_of_head(head, 4 * HEAD_DIM))
    gated[head] = attend(pre, keep[0])[-1]

    @pl.when(head == heads - 1)
    def _():
        for j in range(len(out_parts)):
            columns = pl.ds(pl.multiple_of(offs[j], depth), depth)
            total = None
            for h in range(heads):
                term = dot(gated[h], out_parts[j][pl.ds(h * HEAD_DIM, HEAD_DIM), :])
                total = term if total is None else total + term
            part[:, columns] = total.astype(BF16)
        split_rows(core[0], part, send, kept)


def backward_kernel(parts, n, tick, split, core, in_offs, offs, *rest):
    count = 8 + n + parts
    up_sources, rest = rest[: 1 + split], rest[1 + split :]
    sources, rest = (None,) + rest[:count], rest[count:]
    send, keep = rest[:2]
    held, (grad_normed, part, up_sems, sems) = rest[2 : 3 + count], rest[3 + count :]
    ups, gate, vqk, slope, mixed, probs, factor, x_own, x_theirs = held[:9]
    out_parts, in_parts = held[9 : 9 + n], held[9 + n :]
    wide = 4 * HEAD_DIM
    heads = out_parts[0].shape[0] // HEAD_DIM
    copies = []
    for i, (source, target) in enumerate(zip(sources[: 9 + n], held[: 9 + n])):
        if i == 0:
            continue
        if i < 9:
            source = source.at[tick]
        copies.append(pltpu.make_async_copy(source, target, sems.at[i]))
    up_copies = []
    if split:
        share = up_sources[0].shape[1]
        cores = ups.shape[0] // (2 * share)
        for half, owner in enumerate((core[0], cores - 1 - core[0])):
            for r in range(2):
                at = pl.multiple_of((r * cores + owner) * share, share)
                up_copies.append(
                    pltpu.make_async_copy(
                        up_sources[half].at[r],
                        ups.at[pl.ds(at, share), :],
                        up_sems.at[2 * half + r],
                    )
                )
    else:
        up_copies.append(pltpu.make_async_copy(up_sources[0], ups, up_sems.at[0]))
    copies = [None] + copies
    by_head = []
    for h in range(heads):
        of_head = slice(h * wide, (h + 1) * wide)
        by_head.append(
            [
                pltpu.make_async_copy(
                    sources[9 + n + j].at[:, of_head],
                    in_parts[j].at[:, of_head],
                    sems.at[9 + n + h * parts + j],
                )
                for j in range(parts)
            ]
        )
    first = list(range(9, 9 + n))
    second = [1, 4, 2, 5, 6, 3]
    for copy in up_copies:
        copy.start()
    for i in first + second:
        copies[i].start()
    for copy in up_copies:
        copy.wait()
    for i in first:
        copies[i].wait()
    for of_head in by_head:
        for copy in of_head:
            copy.start()
    for i in (7, 8):
        copies[i].start()
    depth = out_parts[0].shape[1]
    length = x_own.shape[0]
    grad_gated = None
    for j in range(n):
        columns = pl.ds(pl.multiple_of(offs[j], depth), depth)
        term = dot_nt(ups[:, columns], out_parts[j][...])
        grad_gated = term if grad_gated is None else grad_gated + term
    grad_gated = grad_gated.astype(BF16).astype(F32)
    for i in second:
        copies[i].wait()

    def through_head(h):
        cut = slice(h * HEAD_DIM, (h + 1) * HEAD_DIM)
        up = grad_gated[:, cut]
        mixed_h = mixed[:, cut]
        root = row_root(mixed_h)
        normed = mixed_h * root
        grad_n = up * gate[:, cut]
        grad_gate = up * normed
        grad_mixed = root * (grad_n - normed * jnp.mean(grad_n * normed, axis=-1, keepdims=True))
        low = grad_mixed.astype(BF16)
        base = 3 * h * HEAD_DIM
        value = vqk[:, base : base + HEAD_DIM]
        query = vqk[:, base + HEAD_DIM : base + 2 * HEAD_DIM]
        key = vqk[:, base + 2 * HEAD_DIM : base + 3 * HEAD_DIM]
        grad_scores = (dot_nt(low, value) * factor[h]).astype(BF16)
        grad_value = dot_tn(probs[h], low)
        grad_query = dot(grad_scores, key)
        grad_key = dot_tn(grad_scores, query)
        grad_active = jnp.concatenate([grad_gate, grad_value, grad_query, grad_key], axis=1)
        return (grad_active * slope[:, h * wide : (h + 1) * wide]).astype(BF16)

    grad_pre = through_head(0)
    for h in range(heads):
        for copy in by_head[h]:
            copy.wait()
        following = through_head(h + 1) if h + 1 < heads else None
        for j in range(parts):
            rows_of = in_parts[j].shape[0]
            columns = pl.ds(pl.multiple_of(in_offs[j], rows_of), rows_of)
            term = dot_nt(grad_pre, in_parts[j][:, h * wide : (h + 1) * wide])
            if h == 0:
                grad_normed[:, columns] = term
            else:
                grad_normed[:, columns] += term
        grad_pre = following
    for i in (7, 8):
        copies[i].wait()
    for r, source in enumerate((x_own, x_theirs)):
        rows = pl.ds(r * length, length)
        floats = source[...].astype(F32)
        root = row_root(floats)
        scaled = floats * root
        grad_n = grad_normed[rows, :]
        part[rows, :] = (
            root * (grad_n - scaled * jnp.mean(grad_n * scaled, axis=-1, keepdims=True))
        ).astype(BF16)
    split_rows(core[0], part, send, keep)


def pack_kernel(n, offs, gated, up_own, up_theirs, whole, *packs):
    depth = packs[0].shape[1] - 2 * gated.shape[2]
    slab = gated.shape[2]
    length = up_own.shape[0]
    whole[:length, :] = up_own[...]
    whole[length:, :] = up_theirs[...]
    for j in range(2, n):
        pack = packs[j - 2]
        columns = pl.ds(pl.multiple_of(offs[j], depth), depth)
        pack[:, :slab] = gated[1]
        pack[:, slab : 2 * slab] = gated[2]
        pack[:length, 2 * slab :] = up_own[:, columns]
        pack[length:, 2 * slab :] = up_theirs[:, columns]


def fold(rows, target, start):
    share, width = rows.shape
    blocks = target.shape[0] // share
    size = width // blocks
    for k in range(blocks):
        target[k * share : (k + 1) * share, start : start + size] = rows[
            :, k * size : (k + 1) * size
        ]


def unfold(folded, start, target):
    share, width = target.shape
    blocks = folded.shape[0] // share
    size = width // blocks
    for k in range(blocks):
        target[:, k * size : (k + 1) * size] = folded[
            k * share : (k + 1) * share, start : start + size
        ]


def finish_kernel(slab, host, ahead_0, ahead_1, back_0, pack, message, ahead, back):
    width = back.shape[1]
    depth = message.shape[1] - width

    @pl.when(host[0] != 0)
    def _():
        ahead[0] = ahead_0[0]
        ahead[1] = ahead_1[0]
        back[...] = back_0[0]

    @pl.when(host[0] == 0)
    def _():
        unfold(pack, 2 * slab, ahead.at[0])
        unfold(message, depth + width // 2, ahead.at[1])
        unfold(message, depth, back)


def settle_kernel(core, own, theirs, keep, landed, total):
    share = keep.shape[1]
    here = pl.ds(pl.multiple_of(core[0] * share, share), share)
    for r, source in enumerate((own, theirs)):
        total[r] = (
            source[here, :].astype(F32) + keep[r].astype(F32) + landed[r].astype(F32)
        ).astype(BF16)


def first_kernel(core, own, theirs, keep, landed, gated, total, pack):
    slab = gated.shape[2]
    settle_kernel(core, own, theirs, keep, landed, total)
    pack[:, :slab] = gated[1]
    pack[:, slab : 2 * slab] = gated[2]
    fold(total[1], pack, 2 * slab)


def message_kernel(
    core, offs, fresh, new_own, new_theirs, passed, keep, landed, up, back, ahead, message
):
    share = keep.shape[1]
    depth = message.shape[1] - up.shape[2]
    here = pl.ds(pl.multiple_of(core[0] * share, share), share)
    columns = pl.ds(pl.multiple_of(offs[1], depth), depth)
    for r, source in enumerate((new_own, new_theirs)):
        residual = jnp.where(fresh[0] != 0, source[here, :], passed[r])
        ahead[r] = (
            residual.astype(F32) + keep[r].astype(F32) + landed[r].astype(F32)
        ).astype(BF16)
        message[r * share : (r + 1) * share, :depth] = up[r, :, columns]
    fold(back[1], message, depth)
    fold(ahead[1], message, depth + up.shape[2] // 2)


def last_kernel(up, keep, landed, back, other):
    for r in range(2):
        back[r] = (
            up[r].astype(F32) + keep[r].astype(F32) + landed[r].astype(F32)
        ).astype(BF16)
    other[...] = back[1]


def cut_kernel(n, core, offs, fresh, landed, new_own, new_theirs, mine, *pieces):
    share = landed.shape[1]
    depth = pieces[-1].shape[1]
    here = pl.ds(pl.multiple_of(core[0] * share, share), share)
    for r, source in enumerate((new_own, new_theirs)):
        mine[r] = jnp.where(fresh[0] != 0, source[here, :], landed[r])
        for j in range(2, n):
            columns = pl.ds(pl.multiple_of(offs[j], depth), depth)
            pieces[j - 2][r * share : (r + 1) * share, :] = mine[r, :, columns]


def grads_kernel(
    n, scaling, host, core, offs, gated, up_0, up_own, up_near, mine, theirs, halves, other, *rest
):
    packs = rest[: n - 1]
    out, whole = rest[n - 1 :]
    slab = gated.shape[2]
    depth = out.shape[1]
    share = mine.shape[1]
    cores = whole.shape[0] // (2 * share)
    at_host = host[0] != 0
    columns = pl.ds(pl.multiple_of(offs[0], depth), depth)

    def product(first, second, third, upstream):
        for half, owner in enumerate((core[0], cores - 1 - core[0])):
            for r in range(2):
                at = pl.multiple_of((r * cores + owner) * share, share)
                whole[pl.ds(at, share), :] = upstream(half, r)
        return dot_tn(first, third) + dot_tn(second, whole[...])

    up_pair = jnp.concatenate([up_near[...], up_own[:, columns]], axis=0)
    total = product(
        jnp.where(at_host, gated[1], packs[0][:, :slab]),
        jnp.where(at_host, gated[2], packs[0][:, slab : 2 * slab]),
        jnp.where(at_host, up_0[:, columns], up_pair),
        lambda half, r: jnp.where(
            at_host,
            (mine, theirs)[half][r, :, columns],
            (halves, other)[half][0, r * share : (r + 1) * share, :],
        ),
    )
    for m in range(1, n // 2):
        near, beyond = m, n // 2 + m - 1
        pack = jnp.where(at_host, packs[near][...], packs[beyond][...])
        total = total + product(
            pack[:, :slab],
            pack[:, slab : 2 * slab],
            pack[:, 2 * slab :],
            lambda half, r: (halves, other)[half][m, r * share : (r + 1) * share, :],
        )
    out[...] = total * scaling


def in_hbm(arrays):
    return [pltpu.with_memory_space_constraint(x, pltpu.HBM) for x in arrays]


def after(value, *earlier):
    return lax.optimization_barrier((value,) + earlier)[0]


def block_keep(live_blocks, block_marks):
    length = BLOCKS * BLOCK
    places = jnp.arange(length, dtype=jnp.int32)
    owners = places // BLOCK
    marked = jnp.repeat(jnp.repeat(block_marks, BLOCK, axis=-2), BLOCK, axis=-1) == 1
    allowed = (owners[:, None] == owners[None, :]) | marked
    causal = places[:, None] >= places[None, :]
    tokens = live_blocks[..., None, None] * BLOCK
    keeping = causal & allowed & (places[:, None] < tokens) & (places[None, :] < tokens)
    return jnp.where(keeping, 1.0 / jnp.maximum(tokens, 1).astype(F32), 0.0)


def per_device(
    arrivals,
    in_flight,
    cotangent,
    grad_flight,
    stashed,
    in_weight,
    out_weight,
    forward_blocks,
    backward_blocks,
    forward_marks,
    backward_marks,
):
    section_no = lax.axis_index("section")
    sections = lax.axis_size("section")
    core_no = lax.axis_index("cores")
    cores = lax.axis_size("cores")
    dp_no = lax.axis_index("dp")
    n = lax.axis_size("dp")
    ticks = arrivals.shape[0]
    length = arrivals.shape[1]
    width = arrivals.shape[2]
    rows = 2 * length
    share = length // cores
    in_shard = in_weight[0]
    out_shard = out_weight[0]
    depth = in_shard.shape[0]
    slab = out_shard.shape[0]
    heads = slab // HEAD_DIM
    wide = 4 * HEAD_DIM

    hosts = [2 * k + 1 if 4 * k < n - 2 else 2 * k for k in range(n // 2)]
    host_table = jnp.array(hosts, jnp.int32)
    is_host = dp_no == host_table[dp_no // 2]

    def from_partner(x):
        return lax.ppermute(x, "dp", [(h ^ 1, h) for h in hosts])

    def to_partner(x):
        return lax.ppermute(x, "dp", [(h, h ^ 1) for h in hosts])

    def from_host(x, m):
        return lax.ppermute(x, "dp", [(hosts[k ^ m], hosts[k]) for k in range(n // 2)])

    def to_beyond(x, m):
        return lax.ppermute(
            x, "dp", [(hosts[k ^ m], hosts[k] ^ 1) for k in range(n // 2)]
        )

    def swap_cores(x):
        return lax.ppermute(x, "cores", [(c, cores - 1 - c) for c in range(cores)])

    def along_sections(x, by):
        pairs = [
            (i * n + h, (i + by) * n + h)
            for i in range(sections)
            if 0 <= i + by < sections
            for h in hosts
        ]
        return lax.ppermute(x, ("section", "dp"), pairs)

    first_section = section_no == 0
    last_section = section_no == sections - 1
    between = range(1, n // 2)

    pieces = max(1, min(2, depth // 256))
    piece = depth // pieces
    in_far = [from_host(in_shard, m) for m in between]
    in_near = [
        from_partner(in_shard[i * piece : (i + 1) * piece]) for i in range(pieces)
    ]
    out_near = from_partner(out_shard)
    in_pass = [from_host(in_near[0], m) for m in between]
    in_far, in_near, rows_in, tables_in = lax.optimization_barrier(
        (
            in_far,
            in_near,
            (arrivals, in_flight, cotangent, grad_flight, stashed),
            (forward_blocks, forward_marks, backward_blocks, backward_marks),
        )
    )
    in_pass += [from_host(in_near[i], m) for i in range(1, pieces) for m in between]
    in_parts = [in_shard] + in_far + in_near + in_pass
    arrivals, in_flight, cotangent, grad_flight, stashed = rows_in
    tables = jnp.concatenate(
        [
            jnp.concatenate([b[..., None], m.reshape(m.shape[:2] + (-1,))], axis=-1)
            for b, m in (tables_in[:2], tables_in[2:])
        ],
        axis=0,
    )
    near_tables = from_partner(tables)
    stash_own = stashed[0]
    stash_theirs = from_partner(stash_own)
    x_own = jnp.where(first_section, arrivals[0], in_flight[0])
    x_theirs = from_partner(x_own)
    up_own = jnp.where(last_section, cotangent[0], grad_flight[0])
    new_own = jnp.where(first_section, arrivals[1], cotangent[1])
    out_own, out_near, near_tables = lax.optimization_barrier((out_shard, out_near, near_tables))
    out_far = [from_host(out_own, m) for m in between]
    out_parts = [out_shard, out_near] + out_far + [from_host(out_near, m) for m in between]
    up_late, new_late, stash_theirs = lax.optimization_barrier((up_own, new_own, stash_theirs))
    up_theirs = from_partner(up_late)
    up_near = to_partner(
        lax.dynamic_slice_in_dim(up_late, (dp_no ^ 1) * depth, depth, axis=1)
    )
    new_theirs = from_partner(new_late)
    far_hosts = [host_table[(dp_no // 2) ^ m] for m in between]
    owners = [dp_no, dp_no ^ 1] + far_hosts + [h ^ 1 for h in far_hosts]
    offs = jnp.stack(owners).astype(jnp.int32) * depth
    in_offs = [dp_no * depth] + [h * depth for h in far_hosts]
    in_offs += [(dp_no ^ 1) * depth + i * piece for i in range(pieces)]
    in_offs += [(h ^ 1) * depth + i * piece for i in range(pieces) for h in far_hosts]
    in_offs = jnp.stack(in_offs).astype(jnp.int32)
    parts = len(in_parts)
    core = jnp.reshape(core_no, (1,)).astype(jnp.int32)
    first_flag = jnp.reshape(first_section, (1,)).astype(jnp.int32)
    host_flag = jnp.reshape(is_host, (1,)).astype(jnp.int32)
    last_flag = jnp.reshape(last_section, (1,)).astype(jnp.int32)

    both_tables = jnp.stack([tables, near_tables], axis=1)
    ahead_at = sections - 1 - section_no
    chosen = jnp.stack(
        [
            lax.dynamic_index_in_dim(both_tables[way], at, axis=1, keepdims=False)
            for way, at in (
                (0, ahead_at),
                (1, section_no),
                (1, section_no + 1),
                (0, ahead_at + 1),
            )
        ]
    )
    kept = block_keep(chosen[..., 0], chosen[..., 1:].reshape(-1, 2, BLOCKS, BLOCKS))
    blank = jnp.zeros_like(kept[:, 0])
    keep = jnp.concatenate(
        [
            jnp.concatenate([kept[:, 0], blank], axis=2),
            jnp.concatenate([blank, kept[:, 1]], axis=2),
        ],
        axis=1,
    )

    smem = pl.BlockSpec(memory_space=pltpu.SMEM)
    hbm = pl.BlockSpec(memory_space=pltpu.HBM)

    def all_of(*arrays):
        return [pl.BlockSpec(x.shape, lambda *_, d=x.ndim: (0,) * d) for x in arrays]

    def row_of(x, i):
        return pl.BlockSpec((1,) + x.shape[1:], lambda *_: (i,) + (0,) * (x.ndim - 1))

    params = pltpu.CompilerParams(vmem_limit_bytes=VMEM_BYTES)
    small = pltpu.CompilerParams(vmem_limit_bytes=SMALL_VMEM_BYTES)

    def cost(multiply_adds, bytes_accessed):
        return pl.CostEstimate(
            flops=2 * multiply_adds, bytes_accessed=bytes_accessed, transcendentals=0
        )

    def struct(shape, dtype):
        return jax.ShapeDtypeStruct(shape, dtype)

    halves = [struct((2, share, width), BF16)] * 2
    kept_halves = [halves[0], pltpu.HBM(halves[0].shape, BF16)]
    matmul = rows * width * 4 * slab
    weight_bytes = 2 * width * 5 * slab

    by_head = lambda lead, last: pl.BlockSpec(lead + (last,), lambda h: (0,) * len(lead) + (h,))
    saved_shapes = [
        struct((2, rows, slab), F32),
        struct((2, rows, 3 * slab), BF16),
        struct((2, rows, 4 * slab), F32),
        struct((2, rows, slab), F32),
        struct((2, heads, rows, rows), BF16),
        struct((2, heads, rows, rows), F32),
    ]
    weight_scratch = [pltpu.VMEM(x.shape, BF16) for x in in_parts]
    gated, gate, vqk, slope, mixed, probs, factor = pl.pallas_call(
        on_host(functools.partial(project_kernel, parts, heads)),
        grid=(heads,),
        in_specs=[smem] * 2
        + all_of(x_own, x_theirs, stash_own, stash_theirs, keep)
        + [hbm] * parts,
        out_specs=[by_head((3, rows), HEAD_DIM)] + [hbm] * 6,
        out_shape=[struct((3, rows, slab), BF16)]
        + [pltpu.HBM(x.shape, x.dtype) for x in saved_shapes],
        scratch_shapes=weight_scratch
        + [pltpu.VMEM(x.shape, x.dtype) for x in saved_shapes]
        + [
            pltpu.VMEM((3 * rows, width), BF16),
            pltpu.SemaphoreType.DMA((heads * parts,)),
            pltpu.SemaphoreType.DMA((heads * 6,)),
        ],
        compiler_params=params,
        cost_estimate=cost(3 * matmul, 2 * weight_bytes),
        name="project",
    )(host_flag, in_offs, x_own, x_theirs, stash_own, stash_theirs, keep, *in_hbm(in_parts))

    def backward(ups, tick_no):
        split = len(ups) - 1
        layered = [gate, vqk, slope, mixed, probs, factor, stash_own, stash_theirs]
        plain = list(out_parts) + list(in_parts)
        return pl.pallas_call(
            on_host(functools.partial(backward_kernel, parts, n, tick_no, split)),
            grid=(1,),
            in_specs=[smem] * 4 + [hbm] * (len(ups) + len(layered) + len(plain)),
            out_specs=all_of(*halves),
            out_shape=kept_halves,
            scratch_shapes=[pltpu.VMEM((rows, width), BF16)]
            + [pltpu.VMEM(x.shape[1:], x.dtype) for x in layered]
            + [pltpu.VMEM(x.shape, x.dtype) for x in plain]
            + [
                pltpu.VMEM((rows, width), F32),
                pltpu.VMEM((rows, width), BF16),
                pltpu.SemaphoreType.DMA((4,)),
                pltpu.SemaphoreType.DMA((1 + len(layered) + n + heads * parts,)),
            ],
            compiler_params=params,
            cost_estimate=cost(2 * matmul, 2 * weight_bytes),
            name="backward",
        )(host_flag, core, in_offs, offs, *ups, *in_hbm(layered), *out_parts, *in_hbm(in_parts))

    gated, new_theirs, up_near = lax.optimization_barrier((gated, new_theirs, up_near))

    pack_shapes = [struct((rows, width), BF16)]
    pack_shapes += [struct((rows, 2 * slab + depth), BF16)] * (n - 2)
    folded = share * width // rows
    up_0, *packs = pl.pallas_call(
        functools.partial(pack_kernel, n),
        grid=(1,),
        in_specs=[smem] * 1 + all_of(gated, up_own, up_theirs),
        out_specs=all_of(*pack_shapes),
        out_shape=[pltpu.HBM(pack_shapes[0].shape, BF16)] + pack_shapes[1:],
        compiler_params=small,
        name="pack",
    )(offs, gated, up_own, up_theirs)
    packs, out_parts = lax.optimization_barrier((packs, out_parts))

    ahead_send, ahead_keep = pl.pallas_call(
        functools.partial(out_kernel, n),
        grid=(1,),
        in_specs=[smem] * 2 + [row_of(gated, 0)] + all_of(*out_parts),
        out_specs=all_of(*halves),
        out_shape=halves,
        scratch_shapes=[pltpu.VMEM((rows, width), BF16)],
        compiler_params=small,
        cost_estimate=cost(matmul // 4, weight_bytes // 4),
        name="out",
    )(core, offs, gated, *out_parts)
    ahead_landed = swap_cores(ahead_send)
    first_shapes = [halves[0], struct((rows, 2 * slab + folded), BF16)]
    ahead_0, partner_pack = pl.pallas_call(
        first_kernel,
        grid=(1,),
        in_specs=[smem] + all_of(x_own, x_theirs, ahead_keep, ahead_landed, gated),
        out_specs=all_of(*first_shapes),
        out_shape=first_shapes,
        compiler_params=small,
        name="first",
    )(core, *in_hbm([x_own, x_theirs]), ahead_keep, ahead_landed, gated)
    ahead_in = along_sections(ahead_0, 1)
    packs_near = [to_partner(partner_pack)] + [from_host(packs[m - 1], m) for m in between]
    back_send, back_keep = backward(in_hbm([after(up_0, ahead_0)]), 0)
    back_send, back_keep, ahead_in, packs_near = lax.optimization_barrier(
        (back_send, back_keep, ahead_in, packs_near)
    )
    back_landed = swap_cores(back_send)
    back_0 = pl.pallas_call(
        settle_kernel,
        grid=(1,),
        in_specs=[smem] + all_of(up_own, up_theirs, back_keep, back_landed),
        out_specs=all_of(halves[0])[0],
        out_shape=halves[0],
        compiler_params=small,
        name="settle",
    )(core, *in_hbm([up_own, up_theirs, back_keep]), back_landed)
    back_in = along_sections(back_0, -1)

    packs_beyond = [to_beyond(after(packs[n // 2 + m - 2], back_0), m) for m in between]
    ahead_their = swap_cores(ahead_in)
    ahead_send, ahead_keep = pl.pallas_call(
        on_host(functools.partial(forward_kernel, parts, heads)),
        grid=(heads,),
        in_specs=[smem] * 5
        + all_of(ahead_in, ahead_their, new_own, new_theirs)
        + [row_of(keep, keep.shape[0] - 1)]
        + [hbm] * parts
        + all_of(*out_parts),
        out_specs=all_of(*halves),
        out_shape=kept_halves,
        scratch_shapes=[
            pltpu.VMEM((rows, width), BF16),
            pltpu.VMEM((rows, width), BF16),
            pltpu.VMEM((heads, rows, HEAD_DIM), BF16),
            pltpu.VMEM((rows, width), BF16),
            pltpu.SemaphoreType.DMA((heads * parts,)),
        ]
        + weight_scratch,
        compiler_params=params,
        cost_estimate=cost(2 * matmul, 2 * weight_bytes),
        name="forward",
    )(host_flag, core,
        in_offs,
        offs,
        first_flag,
        *in_hbm([ahead_in]),
        ahead_their,
        *in_hbm([new_own, new_theirs, keep]),
        *in_hbm(in_parts),
        *out_parts,
    )
    ahead_send, ahead_keep, back_in, packs_beyond = lax.optimization_barrier(
        (ahead_send, ahead_keep, back_in, packs_beyond)
    )
    ahead_landed = swap_cores(ahead_send)

    cut_shapes = [halves[0]] + [struct((2 * share, depth), BF16)] * (n - 2)
    up_mine, *cuts = pl.pallas_call(
        functools.partial(cut_kernel, n),
        grid=(1,),
        in_specs=[smem] * 3 + all_of(back_in, new_own, new_theirs),
        out_specs=all_of(*cut_shapes),
        out_shape=cut_shapes,
        compiler_params=small,
        name="cut",
    )(core, offs, last_flag, back_in, *in_hbm([new_own, new_theirs]))
    up_their = swap_cores(up_mine)
    landed = [from_host(cuts[m - 1], m) for m in between]
    landed += [to_beyond(cuts[n // 2 + m - 2], m) for m in between]
    message_inputs = [new_own, new_theirs, ahead_in, ahead_keep, ahead_landed, up_mine, back_0]
    message_shapes = [halves[0], struct((2 * share, depth + width), BF16)]
    ahead_1, message = pl.pallas_call(
        message_kernel,
        grid=(1,),
        in_specs=[smem] * 3 + all_of(*message_inputs),
        out_specs=all_of(*message_shapes),
        out_shape=message_shapes,
        compiler_params=small,
        name="message",
    )(core, offs, first_flag, *in_hbm(message_inputs[:4]), *message_inputs[4:6], *in_hbm([back_0]))
    landed = landed + [to_partner(message)]
    back_send, back_keep = backward([up_mine, up_their], 1)
    back_send, back_keep, landed = lax.optimization_barrier((back_send, back_keep, landed))
    landed = landed[-1:] + landed[:-1]
    last_inputs = [up_mine, *in_hbm([back_keep]), swap_cores(back_send)]
    last_shapes = [halves[0], struct((share, width), BF16)]
    back_1, back_other = pl.pallas_call(
        last_kernel,
        grid=(1,),
        in_specs=all_of(*last_inputs),
        out_specs=all_of(*last_shapes),
        out_shape=last_shapes,
        compiler_params=small,
        name="last",
    )(*last_inputs)
    back_last = to_partner(back_other)

    landed_halves = jnp.stack(
        [landed[0][:, :depth]]
        + [jnp.where(is_host, landed[m], landed[n // 2 + m - 1]) for m in between]
    )
    landed_other = swap_cores(landed_halves)
    grad_inputs = [gated, up_0, up_own, up_near, up_mine, up_their, landed_halves, landed_other]
    grad_inputs += packs_near + packs_beyond
    grad_inputs[0] = after(gated, back_1)
    grad_inputs[8:] = in_hbm(grad_inputs[8:])
    grads = pl.pallas_call(
        functools.partial(grads_kernel, n, (ticks * length * n) ** (-0.5)),
        grid=(1,),
        in_specs=[smem] * 3 + all_of(*grad_inputs),
        out_specs=pl.BlockSpec((slab, depth), lambda *_: (0, 0)),
        out_shape=struct((slab, depth), F32),
        scratch_shapes=[pltpu.VMEM((rows, depth), BF16)],
        compiler_params=small,
        cost_estimate=cost(matmul // 4, weight_bytes // 4),
        name="grads",
    )(host_flag, core, offs, *grad_inputs)

    first_pack, last_cut = lax.optimization_barrier((packs_near[0], landed[0], back_1))[:2]
    finish_inputs = [ahead_0, ahead_1, back_0, first_pack, last_cut]
    finish_shapes = [struct((ticks, share, width), BF16), struct((share, width), BF16)]
    ahead, back_first = pl.pallas_call(
        functools.partial(finish_kernel, slab),
        grid=(1,),
        in_specs=[smem] + all_of(*finish_inputs),
        out_specs=all_of(*finish_shapes),
        out_shape=finish_shapes,
        compiler_params=small,
        name="finish",
    )(host_flag, *finish_inputs)
    back = jnp.stack([back_first, jnp.where(is_host, back_1[0], back_last)])
    return (ahead[None], back[None], grads[None])


def solution(mesh):
    in_specs = (
        P(None, "dp", None),
        P("section", "dp", None),
        P(None, "dp", None),
        P("section", "dp", None),
        P("section", None, "dp", None),
        P("section", "dp", "cores"),
        P("section", "cores", "dp"),
        P("dp", None),
        P("dp", None),
        P("dp", None, None, None),
        P("dp", None, None, None),
    )
    out_specs = (
        P("section", None, ("dp", "cores"), None),
        P("section", None, ("dp", "cores"), None),
        P("section", "cores", "dp"),
    )
    return jax.shard_map(
        per_device, mesh=mesh, in_specs=in_specs, out_specs=out_specs, check_vma=False
    )
```

```python
import functools

import jax
import jax.numpy as jnp
from jax import lax
from jax.experimental import pallas as pl
from jax.experimental.pallas import tpu as pltpu
from jax.sharding import PartitionSpec as P

HEAD_DIM = 128
BLOCK = 24
BLOCKS = 4
EPSILON = 1e-06
SCALING = HEAD_DIM ** (-0.5)
VMEM_BYTES = 34 * 1024 * 1024
SMALL_VMEM_BYTES = 16 * 1024 * 1024

F32 = jnp.float32
BF16 = jnp.bfloat16


def on_host(kernel):
    def guarded(host, *refs):
        pl.when(host[0] != 0)(functools.partial(kernel, *refs))

    return guarded


def dot(a, b):
    return lax.dot_general(a, b, (((1,), (0,)), ((), ())), preferred_element_type=F32)


def dot_nt(a, b):
    return lax.dot_general(a, b, (((1,), (1,)), ((), ())), preferred_element_type=F32)


def dot_tn(a, b):
    return lax.dot_general(a, b, (((0,), (0,)), ((), ())), preferred_element_type=F32)


def row_root(floats):
    return lax.rsqrt(jnp.mean(floats * floats, axis=-1, keepdims=True) + EPSILON)


def sigmoid(x):
    return 1.0 / (1.0 + jnp.exp(-x))


def attend(pre, keep):
    sig = sigmoid(pre)
    active = pre * sig
    gate = active[:, :HEAD_DIM]
    vqk = active[:, HEAD_DIM:].astype(BF16)
    value = vqk[:, :HEAD_DIM]
    query = vqk[:, HEAD_DIM : 2 * HEAD_DIM]
    key = vqk[:, 2 * HEAD_DIM :]
    scores = dot_nt(query, key) * SCALING
    sig_s = sigmoid(scores)
    probs = (scores * sig_s * keep).astype(BF16)
    mixed = dot(probs, value)
    gated = (mixed * row_root(mixed) * gate).astype(BF16)
    return sig, gate, vqk, scores, sig_s, probs, mixed, gated


def project(normed, offs, weights, of_head):
    total = None
    for j, weight in enumerate(weights):
        depth = weight.shape[0]
        columns = pl.ds(pl.multiple_of(offs[j], depth), depth)
        term = dot(normed[:, columns], weight[:, of_head])
        total = term if total is None else total + term
    return total


def columns_of_head(h, size):
    return pl.ds(pl.multiple_of(h * size, size), size)


def weight_copies(sources, targets, sems, h):
    of_head = columns_of_head(h, 4 * HEAD_DIM)
    return [
        pltpu.make_async_copy(
            source.at[:, of_head], target.at[:, of_head], sems.at[h * len(sources) + j]
        )
        for j, (source, target) in enumerate(zip(sources, targets))
    ]


def project_kernel(parts, heads, offs, x_own, x_theirs, stash_own, stash_theirs, keep, *rest):
    sources, rest = rest[:parts], rest[parts:]
    gated_out, saved, rest = rest[0], rest[1:7], rest[7:]
    weights, rest = rest[:parts], rest[parts:]
    held, (normed, sems, out_sems) = rest[:6], rest[6:]
    gate_out, vqk_out, slope_out, mixed_out, probs_out, factor_out = held
    length = x_own.shape[0]
    rows = 2 * length
    head = pl.program_id(0)

    def saved_copies(h):
        copies = []
        for i, (source, target) in enumerate(zip(held, saved)):
            if i < 4:
                at = (slice(None), slice(None), columns_of_head(h, source.shape[2] // heads))
            else:
                at = (slice(None), h)
            copies.append(
                pltpu.make_async_copy(source.at[at], target.at[at], out_sems.at[h * 6 + i])
            )
        return copies

    @pl.when(head == 0)
    def _():
        for h in range(heads):
            for copy in weight_copies(sources, weights, sems, h):
                copy.start()
        blocks = [x_own, x_theirs]
        for t in range(stash_own.shape[0]):
            blocks += [stash_own.at[t], stash_theirs.at[t]]
        for i, block in enumerate(blocks):
            floats = block[...].astype(F32)
            normed[pl.ds(i * length, length), :] = (floats * row_root(floats)).astype(BF16)

    for copy in weight_copies(sources, weights, sems, head):
        copy.wait()
    pre_all = project(normed, offs, weights, columns_of_head(head, 4 * HEAD_DIM))
    for i in range(1 + stash_own.shape[0]):
        pre = pre_all[i * rows : (i + 1) * rows]
        kept = keep[i]
        sig, gate, vqk, scores, sig_s, probs, mixed, gated = attend(pre, kept)
        gated_out[i] = gated
        if i > 0:
            narrow = columns_of_head(head, HEAD_DIM)
            gate_out[i - 1, :, narrow] = gate
            vqk_out[i - 1, :, columns_of_head(head, 3 * HEAD_DIM)] = vqk
            slope_out[i - 1, :, columns_of_head(head, 4 * HEAD_DIM)] = sig * (
                1.0 + pre * (1.0 - sig)
            )
            mixed_out[i - 1, :, narrow] = mixed
            probs_out[i - 1, head] = probs
            factor_out[i - 1, head] = kept * sig_s * (1.0 + scores * (1.0 - sig_s)) * SCALING
    for copy in saved_copies(head):
        copy.start()

    @pl.when(head == heads - 1)
    def _():
        for h in range(heads):
            for copy in saved_copies(h):
                copy.wait()


def split_rows(core, part, send, keep):
    share = send.shape[1]
    cores = part.shape[0] // (2 * share)
    for r in range(2):
        base = r * cores * share
        mine = pl.multiple_of(base + core * share, share)
        other = pl.multiple_of(base + (cores - 1 - core) * share, share)
        send[r] = part[pl.ds(other, share), :]
        keep[r] = part[pl.ds(mine, share), :]


def out_kernel(n, core, offs, gated, *rest):
    weights = rest[:n]
    send, keep, part = rest[n:]
    depth = weights[0].shape[1]
    for j in range(n):
        columns = pl.ds(pl.multiple_of(offs[j], depth), depth)
        part[:, columns] = dot(gated[0], weights[j][...]).astype(BF16)
    split_rows(core[0], part, send, keep)


def assemble(core, fresh, mine, theirs, new_own, new_theirs, whole):
    share = mine.shape[1]
    length = new_own.shape[0]
    cores = length // share
    use_fresh = fresh != 0
    for r, source in enumerate((new_own, new_theirs)):
        for owner, landed in ((core, mine), (cores - 1 - core, theirs)):
            inside = pl.multiple_of(owner * share, share)
            rows = source[pl.ds(inside, share), :]
            at = pl.multiple_of(r * length + owner * share, share)
            whole[pl.ds(at, share), :] = jnp.where(use_fresh, rows, landed[r])


def forward_kernel(parts, heads, core, in_offs, offs, fresh, mine, theirs, new_own, new_theirs, keep, *rest):
    sources, rest = rest[:parts], rest[parts:]
    in_parts, rest = rest[-parts:], rest[:-parts]
    out_parts = rest[:-7]
    send, kept, whole, normed, gated, part, sems = rest[-7:]
    depth = out_parts[0].shape[1]
    head = pl.program_id(0)

    @pl.when(head == 0)
    def _():
        for h in range(heads):
            for copy in weight_copies(sources, in_parts, sems, h):
                copy.start()
        assemble(core[0], fresh[0], mine, theirs, new_own, new_theirs, whole)
        floats = whole[...].astype(F32)
        normed[...] = (floats * row_root(floats)).astype(BF16)

    for copy in weight_copies(sources, in_parts, sems, head):
        copy.wait()
    pre = project(normed, in_offs, in_parts, columns_of_head(head, 4 * HEAD_DIM))
    gated[head] = attend(pre, keep[0])[-1]

    @pl.when(head == heads - 1)
    def _():
        for j in range(len(out_parts)):
            columns = pl.ds(pl.multiple_of(offs[j], depth), depth)
            total = None
            for h in range(heads):
                term = dot(gated[h], out_parts[j][pl.ds(h * HEAD_DIM, HEAD_DIM), :])
                total = term if total is None else total + term
            part[:, columns] = total.astype(BF16)
        split_rows(core[0], part, send, kept)


def backward_kernel(parts, n, tick, split, core, in_offs, offs, *rest):
    count = 8 + n + parts
    up_sources, rest = rest[: 1 + split], rest[1 + split :]
    sources, rest = (None,) + rest[:count], rest[count:]
    send, keep = rest[:2]
    held, (grad_normed, part, up_sem, sems) = rest[2 : 3 + count], rest[3 + count :]
    ups, gate, vqk, slope, mixed, probs, factor, x_own, x_theirs = held[:9]
    out_parts, in_parts = held[9 : 9 + n], held[9 + n :]
    wide = 4 * HEAD_DIM
    heads = out_parts[0].shape[0] // HEAD_DIM
    copies = []
    for i, (source, target) in enumerate(zip(sources[: 9 + n], held[: 9 + n])):
        if i == 0:
            continue
        if i < 9:
            source = source.at[tick]
        copies.append(pltpu.make_async_copy(source, target, sems.at[i]))
    up_copies = []
    if not split:
        up_copies.append(pltpu.make_async_copy(up_sources[0], ups, up_sem))
    copies = [None] + copies
    by_head = []
    for h in range(heads):
        of_head = slice(h * wide, (h + 1) * wide)
        by_head.append(
            [
                pltpu.make_async_copy(
                    sources[9 + n + j].at[:, of_head],
                    in_parts[j].at[:, of_head],
                    sems.at[9 + n + h * parts + j],
                )
                for j in range(parts)
            ]
        )
    first = list(range(9, 9 + n))
    second = [1, 4, 2, 5, 6, 3]
    for copy in up_copies:
        copy.start()
    for i in first + second:
        copies[i].start()
    for of_head in by_head:
        for copy in of_head:
            copy.start()
    for i in (7, 8):
        copies[i].start()
    if split:
        share = up_sources[0].shape[1]
        cores = ups.shape[0] // (2 * share)
        for half, owner in enumerate((core[0], cores - 1 - core[0])):
            for r in range(2):
                at = pl.multiple_of((r * cores + owner) * share, share)
                ups[pl.ds(at, share), :] = up_sources[half][r]
    for copy in up_copies:
        copy.wait()
    depth = out_parts[0].shape[1]
    length = x_own.shape[0]
    grad_gated = None
    for j in range(n):
        columns = pl.ds(pl.multiple_of(offs[j], depth), depth)
        copies[first[j]].wait()
        term = dot_nt(ups[:, columns], out_parts[j][...])
        grad_gated = term if grad_gated is None else grad_gated + term
    grad_gated = grad_gated.astype(BF16).astype(F32)
    for i in second:
        copies[i].wait()

    def through_head(h):
        cut = slice(h * HEAD_DIM, (h + 1) * HEAD_DIM)
        up = grad_gated[:, cut]
        mixed_h = mixed[:, cut]
        root = row_root(mixed_h)
        normed = mixed_h * root
        grad_n = up * gate[:, cut]
        grad_gate = up * normed
        grad_mixed = root * (grad_n - normed * jnp.mean(grad_n * normed, axis=-1, keepdims=True))
        low = grad_mixed.astype(BF16)
        base = 3 * h * HEAD_DIM
        value = vqk[:, base : base + HEAD_DIM]
        query = vqk[:, base + HEAD_DIM : base + 2 * HEAD_DIM]
        key = vqk[:, base + 2 * HEAD_DIM : base + 3 * HEAD_DIM]
        grad_scores = (dot_nt(low, value) * factor[h]).astype(BF16)
        grad_value = dot_tn(probs[h], low)
        grad_query = dot(grad_scores, key)
        grad_key = dot_tn(grad_scores, query)
        grad_active = jnp.concatenate([grad_gate, grad_value, grad_query, grad_key], axis=1)
        return (grad_active * slope[:, h * wide : (h + 1) * wide]).astype(BF16)

    grad_pre = through_head(0)
    for h in range(heads):
        for copy in by_head[h]:
            copy.wait()
        following = through_head(h + 1) if h + 1 < heads else None
        for j in range(parts):
            rows_of = in_parts[j].shape[0]
            columns = pl.ds(pl.multiple_of(in_offs[j], rows_of), rows_of)
            term = dot_nt(grad_pre, in_parts[j][:, h * wide : (h + 1) * wide])
            if h == 0:
                grad_normed[:, columns] = term
            else:
                grad_normed[:, columns] += term
        grad_pre = following
    for i in (7, 8):
        copies[i].wait()
    for r, source in enumerate((x_own, x_theirs)):
        rows = pl.ds(r * length, length)
        floats = source[...].astype(F32)
        root = row_root(floats)
        scaled = floats * root
        grad_n = grad_normed[rows, :]
        part[rows, :] = (
            root * (grad_n - scaled * jnp.mean(grad_n * scaled, axis=-1, keepdims=True))
        ).astype(BF16)
    split_rows(core[0], part, send, keep)


def pack_kernel(n, offs, gated, up_own, up_theirs, whole, *packs):
    depth = packs[0].shape[1] - 2 * gated.shape[2]
    slab = gated.shape[2]
    length = up_own.shape[0]
    whole[:length, :] = up_own[...]
    whole[length:, :] = up_theirs[...]
    for j in range(2, n):
        pack = packs[j - 2]
        columns = pl.ds(pl.multiple_of(offs[j], depth), depth)
        pack[:, :slab] = gated[1]
        pack[:, slab : 2 * slab] = gated[2]
        pack[:length, 2 * slab :] = up_own[:, columns]
        pack[length:, 2 * slab :] = up_theirs[:, columns]


def fold(rows, target, start):
    share, width = rows.shape
    blocks = target.shape[0] // share
    size = width // blocks
    for k in range(blocks):
        target[k * share : (k + 1) * share, start : start + size] = rows[
            :, k * size : (k + 1) * size
        ]


def unfold(folded, start, target):
    share, width = target.shape
    blocks = folded.shape[0] // share
    size = width // blocks
    for k in range(blocks):
        target[:, k * size : (k + 1) * size] = folded[
            k * share : (k + 1) * share, start : start + size
        ]


def finish_kernel(slab, host, ahead_0, ahead_1, back_0, pack, message, ahead, back):
    width = back.shape[1]
    depth = message.shape[1] - width

    @pl.when(host[0] != 0)
    def _():
        ahead[0] = ahead_0[0]
        ahead[1] = ahead_1[0]
        back[...] = back_0[0]

    @pl.when(host[0] == 0)
    def _():
        unfold(pack, 2 * slab, ahead.at[0])
        unfold(message, depth + width // 2, ahead.at[1])
        unfold(message, depth, back)


def settle_kernel(core, own, theirs, keep, landed, total):
    share = keep.shape[1]
    here = pl.ds(pl.multiple_of(core[0] * share, share), share)
    for r, source in enumerate((own, theirs)):
        total[r] = (
            source[here, :].astype(F32) + keep[r].astype(F32) + landed[r].astype(F32)
        ).astype(BF16)


def first_kernel(core, own, theirs, keep, landed, gated, total, pack):
    slab = gated.shape[2]
    settle_kernel(core, own, theirs, keep, landed, total)
    pack[:, :slab] = gated[1]
    pack[:, slab : 2 * slab] = gated[2]
    fold(total[1], pack, 2 * slab)


def message_kernel(
    core, offs, fresh, new_own, new_theirs, passed, keep, landed, up, back, ahead, message
):
    share = keep.shape[1]
    depth = message.shape[1] - up.shape[2]
    here = pl.ds(pl.multiple_of(core[0] * share, share), share)
    columns = pl.ds(pl.multiple_of(offs[1], depth), depth)
    for r, source in enumerate((new_own, new_theirs)):
        residual = jnp.where(fresh[0] != 0, source[here, :], passed[r])
        ahead[r] = (
            residual.astype(F32) + keep[r].astype(F32) + landed[r].astype(F32)
        ).astype(BF16)
        message[r * share : (r + 1) * share, :depth] = up[r, :, columns]
    fold(back[1], message, depth)
    fold(ahead[1], message, depth + up.shape[2] // 2)


def last_kernel(up, keep, landed, back, other):
    for r in range(2):
        back[r] = (
            up[r].astype(F32) + keep[r].astype(F32) + landed[r].astype(F32)
        ).astype(BF16)
    other[...] = back[1]


def cut_kernel(n, core, offs, fresh, landed, new_own, new_theirs, mine, *pieces):
    share = landed.shape[1]
    depth = pieces[-1].shape[1]
    here = pl.ds(pl.multiple_of(core[0] * share, share), share)
    for r, source in enumerate((new_own, new_theirs)):
        mine[r] = jnp.where(fresh[0] != 0, source[here, :], landed[r])
        for j in range(2, n):
            columns = pl.ds(pl.multiple_of(offs[j], depth), depth)
            pieces[j - 2][r * share : (r + 1) * share, :] = mine[r, :, columns]


def grads_kernel(
    n, scaling, host, core, offs, gated, up_0, up_own, up_near, mine, theirs, halves, other, *rest
):
    packs = rest[: n - 1]
    out, whole = rest[n - 1 :]
    slab = gated.shape[2]
    depth = out.shape[1]
    share = mine.shape[1]
    cores = whole.shape[0] // (2 * share)
    at_host = host[0] != 0
    columns = pl.ds(pl.multiple_of(offs[0], depth), depth)

    def product(first, second, third, upstream):
        for half, owner in enumerate((core[0], cores - 1 - core[0])):
            for r in range(2):
                at = pl.multiple_of((r * cores + owner) * share, share)
                whole[pl.ds(at, share), :] = upstream(half, r)
        return dot_tn(first, third) + dot_tn(second, whole[...])

    up_pair = jnp.concatenate([up_near[...], up_own[:, columns]], axis=0)
    total = product(
        jnp.where(at_host, gated[1], packs[0][:, :slab]),
        jnp.where(at_host, gated[2], packs[0][:, slab : 2 * slab]),
        jnp.where(at_host, up_0[:, columns], up_pair),
        lambda half, r: jnp.where(
            at_host,
            (mine, theirs)[half][r, :, columns],
            (halves, other)[half][0, r * share : (r + 1) * share, :],
        ),
    )
    for m in range(1, n // 2):
        near, beyond = m, n // 2 + m - 1
        pack = jnp.where(at_host, packs[near][...], packs[beyond][...])
        total = total + product(
            pack[:, :slab],
            pack[:, slab : 2 * slab],
            pack[:, 2 * slab :],
            lambda half, r: (halves, other)[half][m, r * share : (r + 1) * share, :],
        )
    out[...] = total * scaling


def in_hbm(arrays):
    return [pltpu.with_memory_space_constraint(x, pltpu.HBM) for x in arrays]


def after(value, *earlier):
    return lax.optimization_barrier((value,) + earlier)[0]


def block_keep(live_blocks, block_marks):
    length = BLOCKS * BLOCK
    places = jnp.arange(length, dtype=jnp.int32)
    owners = places // BLOCK
    marked = jnp.repeat(jnp.repeat(block_marks, BLOCK, axis=-2), BLOCK, axis=-1) == 1
    allowed = (owners[:, None] == owners[None, :]) | marked
    causal = places[:, None] >= places[None, :]
    tokens = live_blocks[..., None, None] * BLOCK
    keeping = causal & allowed & (places[:, None] < tokens) & (places[None, :] < tokens)
    return jnp.where(keeping, 1.0 / jnp.maximum(tokens, 1).astype(F32), 0.0)


def per_device(
    arrivals,
    in_flight,
    cotangent,
    grad_flight,
    stashed,
    in_weight,
    out_weight,
    forward_blocks,
    backward_blocks,
    forward_marks,
    backward_marks,
):
    section_no = lax.axis_index("section")
    sections = lax.axis_size("section")
    core_no = lax.axis_index("cores")
    cores = lax.axis_size("cores")
    dp_no = lax.axis_index("dp")
    n = lax.axis_size("dp")
    ticks = arrivals.shape[0]
    length = arrivals.shape[1]
    width = arrivals.shape[2]
    rows = 2 * length
    share = length // cores
    in_shard = in_weight[0]
    out_shard = out_weight[0]
    depth = in_shard.shape[0]
    slab = out_shard.shape[0]
    heads = slab // HEAD_DIM
    wide = 4 * HEAD_DIM

    hosts = [2 * k + 1 if 4 * k < n - 2 else 2 * k for k in range(n // 2)]
    host_table = jnp.array(hosts, jnp.int32)
    is_host = dp_no == host_table[dp_no // 2]

    def from_partner(x):
        return lax.ppermute(x, "dp", [(h ^ 1, h) for h in hosts])

    def to_partner(x):
        return lax.ppermute(x, "dp", [(h, h ^ 1) for h in hosts])

    def from_host(x, m):
        return lax.ppermute(x, "dp", [(hosts[k ^ m], hosts[k]) for k in range(n // 2)])

    def to_beyond(x, m):
        return lax.ppermute(
            x, "dp", [(hosts[k ^ m], hosts[k] ^ 1) for k in range(n // 2)]
        )

    def swap_cores(x):
        return lax.ppermute(x, "cores", [(c, cores - 1 - c) for c in range(cores)])

    def along_sections(x, by):
        pairs = [
            (i * n + h, (i + by) * n + h)
            for i in range(sections)
            if 0 <= i + by < sections
            for h in hosts
        ]
        return lax.ppermute(x, ("section", "dp"), pairs)

    first_section = section_no == 0
    last_section = section_no == sections - 1
    between = range(1, n // 2)

    pieces = max(1, min(2, depth // 256))
    piece = depth // pieces
    in_far = [from_host(in_shard, m) for m in between]
    in_near = [
        from_partner(in_shard[i * piece : (i + 1) * piece]) for i in range(pieces)
    ]
    out_near = from_partner(out_shard)
    in_pass = [from_host(in_near[0], m) for m in between]
    in_far, in_near, rows_in, tables_in = lax.optimization_barrier(
        (
            in_far,
            in_near,
            (arrivals, in_flight, cotangent, grad_flight, stashed),
            (forward_blocks, forward_marks, backward_blocks, backward_marks),
        )
    )
    in_pass += [from_host(in_near[i], m) for i in range(1, pieces) for m in between]
    in_parts = [in_shard] + in_far + in_near + in_pass
    arrivals, in_flight, cotangent, grad_flight, stashed = rows_in
    tables = jnp.concatenate(
        [
            jnp.concatenate([b[..., None], m.reshape(m.shape[:2] + (-1,))], axis=-1)
            for b, m in (tables_in[:2], tables_in[2:])
        ],
        axis=0,
    )
    near_tables = from_partner(tables)
    stash_own = stashed[0]
    stash_theirs = from_partner(stash_own)
    x_own = jnp.where(first_section, arrivals[0], in_flight[0])
    x_theirs = from_partner(x_own)
    up_own = jnp.where(last_section, cotangent[0], grad_flight[0])
    new_own = jnp.where(first_section, arrivals[1], cotangent[1])
    out_own, out_near, near_tables = lax.optimization_barrier((out_shard, out_near, near_tables))
    out_far = [from_host(out_own, m) for m in between]
    out_parts = [out_shard, out_near] + out_far + [from_host(out_near, m) for m in between]
    up_late, new_late, stash_theirs = lax.optimization_barrier((up_own, new_own, stash_theirs))
    up_theirs = from_partner(up_late)
    up_near = to_partner(
        lax.dynamic_slice_in_dim(up_late, (dp_no ^ 1) * depth, depth, axis=1)
    )
    new_theirs = from_partner(new_late)
    far_hosts = [host_table[(dp_no // 2) ^ m] for m in between]
    owners = [dp_no, dp_no ^ 1] + far_hosts + [h ^ 1 for h in far_hosts]
    offs = jnp.stack(owners).astype(jnp.int32) * depth
    in_offs = [dp_no * depth] + [h * depth for h in far_hosts]
    in_offs += [(dp_no ^ 1) * depth + i * piece for i in range(pieces)]
    in_offs += [(h ^ 1) * depth + i * piece for i in range(pieces) for h in far_hosts]
    in_offs = jnp.stack(in_offs).astype(jnp.int32)
    parts = len(in_parts)
    core = jnp.reshape(core_no, (1,)).astype(jnp.int32)
    first_flag = jnp.reshape(first_section, (1,)).astype(jnp.int32)
    host_flag = jnp.reshape(is_host, (1,)).astype(jnp.int32)
    last_flag = jnp.reshape(last_section, (1,)).astype(jnp.int32)

    both_tables = jnp.stack([tables, near_tables], axis=1)
    ahead_at = sections - 1 - section_no
    chosen = jnp.stack(
        [
            lax.dynamic_index_in_dim(both_tables[way], at, axis=1, keepdims=False)
            for way, at in (
                (0, ahead_at),
                (1, section_no),
                (1, section_no + 1),
                (0, ahead_at + 1),
            )
        ]
    )
    kept = block_keep(chosen[..., 0], chosen[..., 1:].reshape(-1, 2, BLOCKS, BLOCKS))
    blank = jnp.zeros_like(kept[:, 0])
    keep = jnp.concatenate(
        [
            jnp.concatenate([kept[:, 0], blank], axis=2),
            jnp.concatenate([blank, kept[:, 1]], axis=2),
        ],
        axis=1,
    )

    smem = pl.BlockSpec(memory_space=pltpu.SMEM)
    hbm = pl.BlockSpec(memory_space=pltpu.HBM)
    vmem = pl.BlockSpec(memory_space=pltpu.VMEM)

    def all_of(*arrays):
        return [pl.BlockSpec(x.shape, lambda *_, d=x.ndim: (0,) * d) for x in arrays]

    def row_of(x, i):
        return pl.BlockSpec((1,) + x.shape[1:], lambda *_: (i,) + (0,) * (x.ndim - 1))

    params = pltpu.CompilerParams(vmem_limit_bytes=VMEM_BYTES)
    small = pltpu.CompilerParams(vmem_limit_bytes=SMALL_VMEM_BYTES)

    def cost(multiply_adds, bytes_accessed):
        return pl.CostEstimate(
            flops=2 * multiply_adds, bytes_accessed=bytes_accessed, transcendentals=0
        )

    def struct(shape, dtype):
        return jax.ShapeDtypeStruct(shape, dtype)

    halves = [struct((2, share, width), BF16)] * 2
    kept_halves = [halves[0], pltpu.HBM(halves[0].shape, BF16)]
    matmul = rows * width * 4 * slab
    weight_bytes = 2 * width * 5 * slab

    by_head = lambda lead, last: pl.BlockSpec(lead + (last,), lambda h: (0,) * len(lead) + (h,))
    saved_shapes = [
        struct((2, rows, slab), F32),
        struct((2, rows, 3 * slab), BF16),
        struct((2, rows, 4 * slab), F32),
        struct((2, rows, slab), F32),
        struct((2, heads, rows, rows), BF16),
        struct((2, heads, rows, rows), F32),
    ]
    weight_scratch = [pltpu.VMEM(x.shape, BF16) for x in in_parts]
    gated, gate, vqk, slope, mixed, probs, factor = pl.pallas_call(
        on_host(functools.partial(project_kernel, parts, heads)),
        grid=(heads,),
        in_specs=[smem] * 2
        + all_of(x_own, x_theirs, stash_own, stash_theirs, keep)
        + [hbm] * parts,
        out_specs=[by_head((3, rows), HEAD_DIM)] + [hbm] * 6,
        out_shape=[struct((3, rows, slab), BF16)]
        + [pltpu.HBM(x.shape, x.dtype) for x in saved_shapes],
        scratch_shapes=weight_scratch
        + [pltpu.VMEM(x.shape, x.dtype) for x in saved_shapes]
        + [
            pltpu.VMEM((3 * rows, width), BF16),
            pltpu.SemaphoreType.DMA((heads * parts,)),
            pltpu.SemaphoreType.DMA((heads * 6,)),
        ],
        compiler_params=params,
        cost_estimate=cost(3 * matmul, 2 * weight_bytes),
        name="project",
    )(host_flag, in_offs, x_own, x_theirs, stash_own, stash_theirs, keep, *in_hbm(in_parts))

    def backward(ups, tick_no):
        split = len(ups) - 1
        layered = [gate, vqk, slope, mixed, probs, factor, stash_own, stash_theirs]
        plain = list(out_parts) + list(in_parts)
        return pl.pallas_call(
            on_host(functools.partial(backward_kernel, parts, n, tick_no, split)),
            grid=(1,),
            in_specs=[smem] * 4
            + [vmem if split else hbm] * len(ups)
            + [hbm] * (len(layered) + len(plain)),
            out_specs=all_of(*halves),
            out_shape=kept_halves,
            scratch_shapes=[pltpu.VMEM((rows, width), BF16)]
            + [pltpu.VMEM(x.shape[1:], x.dtype) for x in layered]
            + [pltpu.VMEM(x.shape, x.dtype) for x in plain]
            + [
                pltpu.VMEM((rows, width), F32),
                pltpu.VMEM((rows, width), BF16),
                pltpu.SemaphoreType.DMA,
                pltpu.SemaphoreType.DMA((1 + len(layered) + n + heads * parts,)),
            ],
            compiler_params=params,
            cost_estimate=cost((16 if split else 2) * matmul, 2 * weight_bytes),
            name="backward",
        )(host_flag, core, in_offs, offs, *ups, *in_hbm(layered), *out_parts, *in_hbm(in_parts))

    gated, new_theirs, up_near = lax.optimization_barrier((gated, new_theirs, up_near))

    pack_shapes = [struct((rows, width), BF16)]
    pack_shapes += [struct((rows, 2 * slab + depth), BF16)] * (n - 2)
    folded = share * width // rows
    up_0, *packs = pl.pallas_call(
        functools.partial(pack_kernel, n),
        grid=(1,),
        in_specs=[smem] * 1 + all_of(gated, up_own, up_theirs),
        out_specs=all_of(*pack_shapes),
        out_shape=[pltpu.HBM(pack_shapes[0].shape, BF16)] + pack_shapes[1:],
        compiler_params=small,
        name="pack",
    )(offs, gated, up_own, up_theirs)
    packs, out_parts = lax.optimization_barrier((packs, out_parts))

    ahead_send, ahead_keep = pl.pallas_call(
        functools.partial(out_kernel, n),
        grid=(1,),
        in_specs=[smem] * 2 + [row_of(gated, 0)] + all_of(*out_parts),
        out_specs=all_of(*halves),
        out_shape=halves,
        scratch_shapes=[pltpu.VMEM((rows, width), BF16)],
        compiler_params=small,
        cost_estimate=cost(matmul // 4, weight_bytes // 4),
        name="out",
    )(core, offs, gated, *out_parts)
    ahead_landed = swap_cores(ahead_send)
    first_shapes = [halves[0], struct((rows, 2 * slab + folded), BF16)]
    ahead_0, partner_pack = pl.pallas_call(
        first_kernel,
        grid=(1,),
        in_specs=[smem] + all_of(x_own, x_theirs, ahead_keep, ahead_landed, gated),
        out_specs=all_of(*first_shapes),
        out_shape=first_shapes,
        compiler_params=small,
        name="first",
    )(core, *in_hbm([x_own, x_theirs]), ahead_keep, ahead_landed, gated)
    ahead_in = along_sections(ahead_0, 1)
    packs_near = [to_partner(partner_pack)] + [from_host(packs[m - 1], m) for m in between]
    back_send, back_keep = backward(in_hbm([after(up_0, ahead_0)]), 0)
    back_send, back_keep, ahead_in, packs_near = lax.optimization_barrier(
        (back_send, back_keep, ahead_in, packs_near)
    )
    back_landed = swap_cores(back_send)
    back_0 = pl.pallas_call(
        settle_kernel,
        grid=(1,),
        in_specs=[smem] + all_of(up_own, up_theirs, back_keep, back_landed),
        out_specs=all_of(halves[0])[0],
        out_shape=halves[0],
        compiler_params=small,
        name="settle",
    )(core, *in_hbm([up_own, up_theirs, back_keep]), back_landed)
    back_in = along_sections(back_0, -1)

    packs_beyond = [to_beyond(packs[n // 2 + m - 2], m) for m in between]
    ahead_their = swap_cores(ahead_in)
    ahead_send, ahead_keep = pl.pallas_call(
        on_host(functools.partial(forward_kernel, parts, heads)),
        grid=(heads,),
        in_specs=[smem] * 5
        + all_of(ahead_in, ahead_their, new_own, new_theirs)
        + [row_of(keep, keep.shape[0] - 1)]
        + [hbm] * parts
        + all_of(*out_parts),
        out_specs=all_of(*halves),
        out_shape=kept_halves,
        scratch_shapes=[
            pltpu.VMEM((rows, width), BF16),
            pltpu.VMEM((rows, width), BF16),
            pltpu.VMEM((heads, rows, HEAD_DIM), BF16),
            pltpu.VMEM((rows, width), BF16),
            pltpu.SemaphoreType.DMA((heads * parts,)),
        ]
        + weight_scratch,
        compiler_params=params,
        cost_estimate=cost(2 * matmul, 2 * weight_bytes),
        name="forward",
    )(host_flag, core,
        in_offs,
        offs,
        first_flag,
        *in_hbm([ahead_in]),
        ahead_their,
        *in_hbm([new_own, new_theirs, keep]),
        *in_hbm(in_parts),
        *out_parts,
    )
    ahead_send, ahead_keep, back_in, packs_beyond = lax.optimization_barrier(
        (ahead_send, ahead_keep, back_in, packs_beyond)
    )
    ahead_landed = swap_cores(ahead_send)

    cut_shapes = [halves[0]] + [struct((2 * share, depth), BF16)] * (n - 2)
    up_mine, *cuts = pl.pallas_call(
        functools.partial(cut_kernel, n),
        grid=(1,),
        in_specs=[smem] * 3 + all_of(back_in, new_own, new_theirs),
        out_specs=all_of(*cut_shapes),
        out_shape=cut_shapes,
        compiler_params=small,
        name="cut",
    )(core, offs, last_flag, back_in, *in_hbm([new_own, new_theirs]))
    up_their = swap_cores(up_mine)
    landed = [from_host(cuts[m - 1], m) for m in between]
    landed += [to_beyond(cuts[n // 2 + m - 2], m) for m in between]
    message_inputs = [new_own, new_theirs, ahead_in, ahead_keep, ahead_landed, up_mine, back_0]
    message_shapes = [halves[0], struct((2 * share, depth + width), BF16)]
    ahead_1, message = pl.pallas_call(
        message_kernel,
        grid=(1,),
        in_specs=[smem] * 3 + all_of(*message_inputs),
        out_specs=all_of(*message_shapes),
        out_shape=message_shapes,
        compiler_params=small,
        name="message",
    )(core, offs, first_flag, *in_hbm(message_inputs[:4]), *message_inputs[4:6], *in_hbm([back_0]))
    landed = landed + [to_partner(message)]
    back_send, back_keep = backward([up_mine, up_their], 1)
    back_send, back_keep, landed = lax.optimization_barrier((back_send, back_keep, landed))
    landed = landed[-1:] + landed[:-1]
    last_inputs = [up_mine, *in_hbm([back_keep]), swap_cores(back_send)]
    last_shapes = [halves[0], struct((share, width), BF16)]
    back_1, back_other = pl.pallas_call(
        last_kernel,
        grid=(1,),
        in_specs=all_of(*last_inputs),
        out_specs=all_of(*last_shapes),
        out_shape=last_shapes,
        compiler_params=small,
        name="last",
    )(*last_inputs)
    back_last = to_partner(back_other)

    landed_halves = jnp.stack(
        [landed[0][:, :depth]]
        + [jnp.where(is_host, landed[m], landed[n // 2 + m - 1]) for m in between]
    )
    landed_other = swap_cores(landed_halves)
    grad_inputs = [gated, up_0, up_own, up_near, up_mine, up_their, landed_halves, landed_other]
    grad_inputs += packs_near + packs_beyond
    grad_inputs[0] = after(gated, back_1)
    grad_inputs[8:] = in_hbm(grad_inputs[8:])
    grads = pl.pallas_call(
        functools.partial(grads_kernel, n, (ticks * length * n) ** (-0.5)),
        grid=(1,),
        in_specs=[smem] * 3 + all_of(*grad_inputs),
        out_specs=pl.BlockSpec((slab, depth), lambda *_: (0, 0)),
        out_shape=struct((slab, depth), F32),
        scratch_shapes=[pltpu.VMEM((rows, depth), BF16)],
        compiler_params=small,
        cost_estimate=cost(matmul // 4, weight_bytes // 4),
        name="grads",
    )(host_flag, core, offs, *grad_inputs)

    first_pack, last_cut = lax.optimization_barrier((packs_near[0], landed[0], back_1))[:2]
    finish_inputs = [ahead_0, ahead_1, back_0, first_pack, last_cut]
    finish_shapes = [struct((ticks, share, width), BF16), struct((share, width), BF16)]
    ahead, back_first = pl.pallas_call(
        functools.partial(finish_kernel, slab),
        grid=(1,),
        in_specs=[smem] + all_of(*finish_inputs),
        out_specs=all_of(*finish_shapes),
        out_shape=finish_shapes,
        compiler_params=small,
        name="finish",
    )(host_flag, *finish_inputs)
    back = jnp.stack([back_first, jnp.where(is_host, back_1[0], back_last)])
    return (ahead[None], back[None], grads[None])


def solution(mesh):
    in_specs = (
        P(None, "dp", None),
        P("section", "dp", None),
        P(None, "dp", None),
        P("section", "dp", None),
        P("section", None, "dp", None),
        P("section", "dp", "cores"),
        P("section", "cores", "dp"),
        P("dp", None),
        P("dp", None),
        P("dp", None, None, None),
        P("dp", None, None, None),
    )
    out_specs = (
        P("section", None, ("dp", "cores"), None),
        P("section", None, ("dp", "cores"), None),
        P("section", "cores", "dp"),
    )
    return jax.shard_map(
        per_device, mesh=mesh, in_specs=in_specs, out_specs=out_specs, check_vma=False
    )
```

```python
import functools

import jax
import jax.numpy as jnp
from jax import lax
from jax.experimental import pallas as pl
from jax.experimental.pallas import tpu as pltpu
from jax.sharding import PartitionSpec as P

HEAD_DIM = 128
BLOCK = 24
BLOCKS = 4
EPSILON = 1e-06
SCALING = HEAD_DIM ** (-0.5)
VMEM_BYTES = 34 * 1024 * 1024
SMALL_VMEM_BYTES = 16 * 1024 * 1024

F32 = jnp.float32
BF16 = jnp.bfloat16


def on_host(kernel):
    def guarded(host, *refs):
        pl.when(host[0] != 0)(functools.partial(kernel, *refs))

    return guarded


def dot(a, b):
    return lax.dot_general(a, b, (((1,), (0,)), ((), ())), preferred_element_type=F32)


def dot_nt(a, b):
    return lax.dot_general(a, b, (((1,), (1,)), ((), ())), preferred_element_type=F32)


def dot_tn(a, b):
    return lax.dot_general(a, b, (((0,), (0,)), ((), ())), preferred_element_type=F32)


def row_root(floats):
    return lax.rsqrt(jnp.mean(floats * floats, axis=-1, keepdims=True) + EPSILON)


def sigmoid(x):
    return 1.0 / (1.0 + jnp.exp(-x))


def attend(pre, keep):
    sig = sigmoid(pre)
    active = pre * sig
    gate = active[:, :HEAD_DIM]
    vqk = active[:, HEAD_DIM:].astype(BF16)
    value = vqk[:, :HEAD_DIM]
    query = vqk[:, HEAD_DIM : 2 * HEAD_DIM]
    key = vqk[:, 2 * HEAD_DIM :]
    scores = dot_nt(query, key) * SCALING
    sig_s = sigmoid(scores)
    probs = (scores * sig_s * keep).astype(BF16)
    mixed = dot(probs, value)
    gated = (mixed * row_root(mixed) * gate).astype(BF16)
    return sig, gate, vqk, scores, sig_s, probs, mixed, gated


def project(normed, offs, weights, of_head):
    total = None
    for j, weight in enumerate(weights):
        depth = weight.shape[0]
        columns = pl.ds(pl.multiple_of(offs[j], depth), depth)
        term = dot(normed[:, columns], weight[:, of_head])
        total = term if total is None else total + term
    return total


def columns_of_head(h, size):
    return pl.ds(pl.multiple_of(h * size, size), size)


def weight_copies(sources, targets, sems, h):
    of_head = columns_of_head(h, 4 * HEAD_DIM)
    return [
        pltpu.make_async_copy(
            source.at[:, of_head], target.at[:, of_head], sems.at[h * len(sources) + j]
        )
        for j, (source, target) in enumerate(zip(sources, targets))
    ]


def project_kernel(parts, heads, offs, x_own, x_theirs, stash_own, stash_theirs, keep, *rest):
    sources, rest = rest[:parts], rest[parts:]
    gated_out, saved, rest = rest[0], rest[1:7], rest[7:]
    weights, rest = rest[:parts], rest[parts:]
    held, (normed, sems, out_sems) = rest[:6], rest[6:]
    gate_out, vqk_out, slope_out, mixed_out, probs_out, factor_out = held
    length = x_own.shape[0]
    rows = 2 * length
    head = pl.program_id(0)

    def saved_copies(h):
        copies = []
        for i, (source, target) in enumerate(zip(held, saved)):
            if i < 4:
                at = (slice(None), slice(None), columns_of_head(h, source.shape[2] // heads))
            else:
                at = (slice(None), h)
            copies.append(
                pltpu.make_async_copy(source.at[at], target.at[at], out_sems.at[h * 6 + i])
            )
        return copies

    @pl.when(head == 0)
    def _():
        for h in range(heads):
            for copy in weight_copies(sources, weights, sems, h):
                copy.start()
        blocks = [x_own, x_theirs]
        for t in range(stash_own.shape[0]):
            blocks += [stash_own.at[t], stash_theirs.at[t]]
        for i, block in enumerate(blocks):
            floats = block[...].astype(F32)
            normed[pl.ds(i * length, length), :] = (floats * row_root(floats)).astype(BF16)

    for copy in weight_copies(sources, weights, sems, head):
        copy.wait()
    pre_all = project(normed, offs, weights, columns_of_head(head, 4 * HEAD_DIM))
    for i in range(1 + stash_own.shape[0]):
        pre = pre_all[i * rows : (i + 1) * rows]
        kept = keep[i]
        sig, gate, vqk, scores, sig_s, probs, mixed, gated = attend(pre, kept)
        gated_out[i] = gated
        if i > 0:
            narrow = columns_of_head(head, HEAD_DIM)
            gate_out[i - 1, :, narrow] = gate
            vqk_out[i - 1, :, columns_of_head(head, 3 * HEAD_DIM)] = vqk
            slope_out[i - 1, :, columns_of_head(head, 4 * HEAD_DIM)] = sig * (
                1.0 + pre * (1.0 - sig)
            )
            mixed_out[i - 1, :, narrow] = mixed
            probs_out[i - 1, head] = probs
            factor_out[i - 1, head] = kept * sig_s * (1.0 + scores * (1.0 - sig_s)) * SCALING
    for copy in saved_copies(head):
        copy.start()

    @pl.when(head == heads - 1)
    def _():
        for h in range(heads):
            for copy in saved_copies(h):
                copy.wait()


def split_rows(core, part, send, keep):
    share = send.shape[1]
    cores = part.shape[0] // (2 * share)
    for r in range(2):
        base = r * cores * share
        mine = pl.multiple_of(base + core * share, share)
        other = pl.multiple_of(base + (cores - 1 - core) * share, share)
        send[r] = part[pl.ds(other, share), :]
        keep[r] = part[pl.ds(mine, share), :]


def early_kernel(offs, gated, upstream, *rest):
    weights, (part, grad_gated) = rest[:-2], rest[-2:]
    depth = weights[0].shape[1]
    total = None
    for j, weight in enumerate(weights):
        columns = pl.ds(pl.multiple_of(offs[j], depth), depth)
        part[:, columns] = dot(gated[0], weight[...]).astype(BF16)
        term = dot_nt(upstream[:, columns], weight[...])
        total = term if total is None else total + term
    grad_gated[...] = total


def out_kernel(skip, core, offs, gated, early, *rest):
    weights, (send, keep, part) = rest[:-3], rest[-3:]
    depth = weights[0].shape[1]
    part[...] = early[...]
    for j, weight in enumerate(weights):
        columns = pl.ds(pl.multiple_of(offs[skip + j], depth), depth)
        part[:, columns] = dot(gated[0], weight[...]).astype(BF16)
    split_rows(core[0], part, send, keep)


def assemble(core, fresh, mine, theirs, new_own, new_theirs, whole):
    share = mine.shape[1]
    length = new_own.shape[0]
    cores = length // share
    use_fresh = fresh != 0
    for r, source in enumerate((new_own, new_theirs)):
        for owner, landed in ((core, mine), (cores - 1 - core, theirs)):
            inside = pl.multiple_of(owner * share, share)
            rows = source[pl.ds(inside, share), :]
            at = pl.multiple_of(r * length + owner * share, share)
            whole[pl.ds(at, share), :] = jnp.where(use_fresh, rows, landed[r])


def forward_kernel(parts, heads, core, in_offs, offs, fresh, mine, theirs, new_own, new_theirs, keep, *rest):
    sources, rest = rest[:parts], rest[parts:]
    in_parts, rest = rest[-parts:], rest[:-parts]
    out_parts = rest[:-7]
    send, kept, whole, normed, gated, part, sems = rest[-7:]
    depth = out_parts[0].shape[1]
    head = pl.program_id(0)

    @pl.when(head == 0)
    def _():
        for h in range(heads):
            for copy in weight_copies(sources, in_parts, sems, h):
                copy.start()
        assemble(core[0], fresh[0], mine, theirs, new_own, new_theirs, whole)
        floats = whole[...].astype(F32)
        normed[...] = (floats * row_root(floats)).astype(BF16)

    for copy in weight_copies(sources, in_parts, sems, head):
        copy.wait()
    pre = project(normed, in_offs, in_parts, columns_of_head(head, 4 * HEAD_DIM))
    gated[head] = attend(pre, keep[0])[-1]

    @pl.when(head == heads - 1)
    def _():
        for j in range(len(out_parts)):
            columns = pl.ds(pl.multiple_of(offs[j], depth), depth)
            total = None
            for h in range(heads):
                term = dot(gated[h], out_parts[j][pl.ds(h * HEAD_DIM, HEAD_DIM), :])
                total = term if total is None else total + term
            part[:, columns] = total.astype(BF16)
        split_rows(core[0], part, send, kept)


def backward_kernel(parts, n, skip, tick, split, core, in_offs, offs, *rest):
    n = n - skip
    count = 8 + n + parts
    up_sources, rest = rest[: 1 + split], rest[1 + split :]
    early, rest = (rest[0], rest[1:]) if skip else (None, rest)
    sources, rest = (None,) + rest[:count], rest[count:]
    send, keep = rest[:2]
    held, (grad_normed, scaled, part, begun, up_sems, sems) = (
        rest[2 : 3 + count],
        rest[3 + count :],
    )
    ups, gate, vqk, slope, mixed, probs, factor, x_own, x_theirs = held[:9]
    out_parts, in_parts = held[9 : 9 + n], held[9 + n :]
    wide = 4 * HEAD_DIM
    heads = out_parts[0].shape[0] // HEAD_DIM
    copies = []
    for i, (source, target) in enumerate(zip(sources[: 9 + n], held[: 9 + n])):
        if i == 0:
            continue
        if i < 9:
            source = source.at[tick]
        copies.append(pltpu.make_async_copy(source, target, sems.at[i]))
    up_copies = []
    if not split:
        up_copies.append(pltpu.make_async_copy(up_sources[0], ups, up_sems.at[0]))
    if skip:
        up_copies.append(pltpu.make_async_copy(early, begun, up_sems.at[1]))
    copies = [None] + copies
    by_head = []
    for h in range(heads):
        of_head = slice(h * wide, (h + 1) * wide)
        by_head.append(
            [
                pltpu.make_async_copy(
                    sources[9 + n + j].at[:, of_head],
                    in_parts[j].at[:, of_head],
                    sems.at[9 + n + h * parts + j],
                )
                for j in range(parts)
            ]
        )
    first = list(range(9, 9 + n))
    second = [1, 4, 2, 5, 6, 3]
    for i in (7, 8):
        copies[i].start()
    for copy in up_copies:
        copy.start()
    for i in first + second:
        copies[i].start()
    for of_head in by_head:
        for copy in of_head:
            copy.start()
    if split:
        share = up_sources[0].shape[1]
        cores = ups.shape[0] // (2 * share)
        for half, owner in enumerate((core[0], cores - 1 - core[0])):
            for r in range(2):
                at = pl.multiple_of((r * cores + owner) * share, share)
                ups[pl.ds(at, share), :] = up_sources[half][r]
    roots = []
    for i, source in ((7, x_own), (8, x_theirs)):
        copies[i].wait()
        floats = source[...].astype(F32)
        roots.append(row_root(floats))
        scaled[pl.ds((i - 7) * source.shape[0], source.shape[0]), :] = floats * roots[-1]
    for copy in up_copies:
        copy.wait()
    depth = out_parts[0].shape[1]
    length = x_own.shape[0]
    grad_gated = begun[...] if skip else None
    for j in range(n):
        columns = pl.ds(pl.multiple_of(offs[skip + j], depth), depth)
        copies[first[j]].wait()
        term = dot_nt(ups[:, columns], out_parts[j][...])
        grad_gated = term if grad_gated is None else grad_gated + term
    grad_gated = grad_gated.astype(BF16).astype(F32)
    for i in second:
        copies[i].wait()

    def through_head(h):
        cut = slice(h * HEAD_DIM, (h + 1) * HEAD_DIM)
        up = grad_gated[:, cut]
        mixed_h = mixed[:, cut]
        root = row_root(mixed_h)
        normed = mixed_h * root
        grad_n = up * gate[:, cut]
        grad_gate = up * normed
        grad_mixed = root * (grad_n - normed * jnp.mean(grad_n * normed, axis=-1, keepdims=True))
        low = grad_mixed.astype(BF16)
        base = 3 * h * HEAD_DIM
        value = vqk[:, base : base + HEAD_DIM]
        query = vqk[:, base + HEAD_DIM : base + 2 * HEAD_DIM]
        key = vqk[:, base + 2 * HEAD_DIM : base + 3 * HEAD_DIM]
        grad_scores = (dot_nt(low, value) * factor[h]).astype(BF16)
        grad_value = dot_tn(probs[h], low)
        grad_query = dot(grad_scores, key)
        grad_key = dot_tn(grad_scores, query)
        grad_active = jnp.concatenate([grad_gate, grad_value, grad_query, grad_key], axis=1)
        return (grad_active * slope[:, h * wide : (h + 1) * wide]).astype(BF16)

    grad_pre = through_head(0)
    for h in range(heads):
        for copy in by_head[h]:
            copy.wait()
        following = through_head(h + 1) if h + 1 < heads else None
        for j in range(parts):
            rows_of = in_parts[j].shape[0]
            columns = pl.ds(pl.multiple_of(in_offs[j], rows_of), rows_of)
            term = dot_nt(grad_pre, in_parts[j][:, h * wide : (h + 1) * wide])
            if h == 0:
                grad_normed[:, columns] = term
            else:
                grad_normed[:, columns] += term
        grad_pre = following
    for r, root in enumerate(roots):
        rows = pl.ds(r * length, length)
        scaled_rows = scaled[rows, :]
        grad_n = grad_normed[rows, :]
        mean = jnp.mean(grad_n * scaled_rows, axis=-1, keepdims=True)
        part[rows, :] = (root * (grad_n - scaled_rows * mean)).astype(BF16)
    split_rows(core[0], part, send, keep)


def pack_kernel(n, offs, gated, up_own, up_theirs, whole, *packs):
    depth = packs[0].shape[1] - 2 * gated.shape[2]
    slab = gated.shape[2]
    length = up_own.shape[0]
    whole[:length, :] = up_own[...]
    whole[length:, :] = up_theirs[...]
    for j in range(2, n):
        pack = packs[j - 2]
        columns = pl.ds(pl.multiple_of(offs[j], depth), depth)
        pack[:, :slab] = gated[1]
        pack[:, slab : 2 * slab] = gated[2]
        pack[:length, 2 * slab :] = up_own[:, columns]
        pack[length:, 2 * slab :] = up_theirs[:, columns]


def fold(rows, target, start):
    share, width = rows.shape
    blocks = target.shape[0] // share
    size = width // blocks
    for k in range(blocks):
        target[k * share : (k + 1) * share, start : start + size] = rows[
            :, k * size : (k + 1) * size
        ]


def unfold(folded, start, target):
    share, width = target.shape
    blocks = folded.shape[0] // share
    size = width // blocks
    for k in range(blocks):
        target[:, k * size : (k + 1) * size] = folded[
            k * share : (k + 1) * share, start : start + size
        ]


def finish_kernel(slab, host, ahead_0, ahead_1, back_0, pack, message, ahead, back):
    width = back.shape[1]
    depth = message.shape[1] - width

    @pl.when(host[0] != 0)
    def _():
        ahead[0] = ahead_0[0]
        ahead[1] = ahead_1[0]
        back[...] = back_0[0]

    @pl.when(host[0] == 0)
    def _():
        unfold(pack, 2 * slab, ahead.at[0])
        unfold(message, depth + width // 2, ahead.at[1])
        unfold(message, depth, back)


def settle_kernel(core, own, theirs, keep, landed, total):
    share = keep.shape[1]
    here = pl.ds(pl.multiple_of(core[0] * share, share), share)
    for r, source in enumerate((own, theirs)):
        total[r] = (
            source[here, :].astype(F32) + keep[r].astype(F32) + landed[r].astype(F32)
        ).astype(BF16)


def first_kernel(core, own, theirs, keep, landed, gated, total, pack):
    slab = gated.shape[2]
    settle_kernel(core, own, theirs, keep, landed, total)
    pack[:, :slab] = gated[1]
    pack[:, slab : 2 * slab] = gated[2]
    fold(total[1], pack, 2 * slab)


def message_kernel(
    core, offs, fresh, new_own, new_theirs, passed, keep, landed, up, back, ahead, message
):
    share = keep.shape[1]
    depth = message.shape[1] - up.shape[2]
    here = pl.ds(pl.multiple_of(core[0] * share, share), share)
    columns = pl.ds(pl.multiple_of(offs[1], depth), depth)
    for r, source in enumerate((new_own, new_theirs)):
        residual = jnp.where(fresh[0] != 0, source[here, :], passed[r])
        ahead[r] = (
            residual.astype(F32) + keep[r].astype(F32) + landed[r].astype(F32)
        ).astype(BF16)
        message[r * share : (r + 1) * share, :depth] = up[r, :, columns]
    fold(back[1], message, depth)
    fold(ahead[1], message, depth + up.shape[2] // 2)


def last_kernel(up, keep, landed, back, other):
    for r in range(2):
        back[r] = (
            up[r].astype(F32) + keep[r].astype(F32) + landed[r].astype(F32)
        ).astype(BF16)
    other[...] = back[1]


def cut_kernel(n, core, offs, fresh, landed, new_own, new_theirs, mine, *pieces):
    share = landed.shape[1]
    depth = pieces[-1].shape[1]
    here = pl.ds(pl.multiple_of(core[0] * share, share), share)
    for r, source in enumerate((new_own, new_theirs)):
        mine[r] = jnp.where(fresh[0] != 0, source[here, :], landed[r])
        for j in range(2, n):
            columns = pl.ds(pl.multiple_of(offs[j], depth), depth)
            pieces[j - 2][r * share : (r + 1) * share, :] = mine[r, :, columns]


def grads_kernel(
    n, scaling, host, core, offs, gated, up_0, up_own, up_near, mine, theirs, halves, other, *rest
):
    packs = rest[: n - 1]
    out, whole = rest[n - 1 :]
    slab = gated.shape[2]
    depth = out.shape[1]
    share = mine.shape[1]
    cores = whole.shape[0] // (2 * share)
    at_host = host[0] != 0
    columns = pl.ds(pl.multiple_of(offs[0], depth), depth)

    def product(first, second, third, upstream):
        for half, owner in enumerate((core[0], cores - 1 - core[0])):
            for r in range(2):
                at = pl.multiple_of((r * cores + owner) * share, share)
                whole[pl.ds(at, share), :] = upstream(half, r)
        return dot_tn(first, third) + dot_tn(second, whole[...])

    up_pair = jnp.concatenate([up_near[...], up_own[:, columns]], axis=0)
    total = product(
        jnp.where(at_host, gated[1], packs[0][:, :slab]),
        jnp.where(at_host, gated[2], packs[0][:, slab : 2 * slab]),
        jnp.where(at_host, up_0[:, columns], up_pair),
        lambda half, r: jnp.where(
            at_host,
            (mine, theirs)[half][r, :, columns],
            (halves, other)[half][0, r * share : (r + 1) * share, :],
        ),
    )
    for m in range(1, n // 2):
        near, beyond = m, n // 2 + m - 1
        pack = jnp.where(at_host, packs[near][...], packs[beyond][...])
        total = total + product(
            pack[:, :slab],
            pack[:, slab : 2 * slab],
            pack[:, 2 * slab :],
            lambda half, r: (halves, other)[half][m, r * share : (r + 1) * share, :],
        )
    out[...] = total * scaling


def in_hbm(arrays):
    return [pltpu.with_memory_space_constraint(x, pltpu.HBM) for x in arrays]


def after(value, *earlier):
    return lax.optimization_barrier((value,) + earlier)[0]


def block_keep(live_blocks, block_marks):
    length = BLOCKS * BLOCK
    places = jnp.arange(length, dtype=jnp.int32)
    owners = places // BLOCK
    marked = jnp.repeat(jnp.repeat(block_marks, BLOCK, axis=-2), BLOCK, axis=-1) == 1
    allowed = (owners[:, None] == owners[None, :]) | marked
    causal = places[:, None] >= places[None, :]
    tokens = live_blocks[..., None, None] * BLOCK
    keeping = causal & allowed & (places[:, None] < tokens) & (places[None, :] < tokens)
    return jnp.where(keeping, 1.0 / jnp.maximum(tokens, 1).astype(F32), 0.0)


def per_device(
    arrivals,
    in_flight,
    cotangent,
    grad_flight,
    stashed,
    in_weight,
    out_weight,
    forward_blocks,
    backward_blocks,
    forward_marks,
    backward_marks,
):
    section_no = lax.axis_index("section")
    sections = lax.axis_size("section")
    core_no = lax.axis_index("cores")
    cores = lax.axis_size("cores")
    dp_no = lax.axis_index("dp")
    n = lax.axis_size("dp")
    ticks = arrivals.shape[0]
    length = arrivals.shape[1]
    width = arrivals.shape[2]
    rows = 2 * length
    share = length // cores
    in_shard = in_weight[0]
    out_shard = out_weight[0]
    depth = in_shard.shape[0]
    slab = out_shard.shape[0]
    heads = slab // HEAD_DIM
    wide = 4 * HEAD_DIM

    hosts = [2 * k + 1 if 4 * k < n - 2 else 2 * k for k in range(n // 2)]
    host_table = jnp.array(hosts, jnp.int32)
    is_host = dp_no == host_table[dp_no // 2]

    def from_partner(x):
        return lax.ppermute(x, "dp", [(h ^ 1, h) for h in hosts])

    def to_partner(x):
        return lax.ppermute(x, "dp", [(h, h ^ 1) for h in hosts])

    def from_host(x, m):
        return lax.ppermute(x, "dp", [(hosts[k ^ m], hosts[k]) for k in range(n // 2)])

    def to_beyond(x, m):
        return lax.ppermute(
            x, "dp", [(hosts[k ^ m], hosts[k] ^ 1) for k in range(n // 2)]
        )

    def swap_cores(x):
        return lax.ppermute(x, "cores", [(c, cores - 1 - c) for c in range(cores)])

    def along_sections(x, by):
        pairs = [
            (i * n + h, (i + by) * n + h)
            for i in range(sections)
            if 0 <= i + by < sections
            for h in hosts
        ]
        return lax.ppermute(x, ("section", "dp"), pairs)

    first_section = section_no == 0
    last_section = section_no == sections - 1
    between = range(1, n // 2)

    pieces = max(1, min(2, depth // 256))
    piece = depth // pieces
    in_far = [from_host(in_shard, m) for m in between]
    in_near = [
        from_partner(in_shard[i * piece : (i + 1) * piece]) for i in range(pieces)
    ]
    out_near = from_partner(out_shard)
    in_pass = [from_host(in_near[0], m) for m in between]
    in_far, in_near, rows_in, tables_in = lax.optimization_barrier(
        (
            in_far,
            in_near,
            (arrivals, in_flight, cotangent, grad_flight, stashed),
            (forward_blocks, forward_marks, backward_blocks, backward_marks),
        )
    )
    in_pass += [from_host(in_near[i], m) for i in range(1, pieces) for m in between]
    in_parts = [in_shard] + in_far + in_near + in_pass
    arrivals, in_flight, cotangent, grad_flight, stashed = rows_in
    tables = jnp.concatenate(
        [
            jnp.concatenate([b[..., None], m.reshape(m.shape[:2] + (-1,))], axis=-1)
            for b, m in (tables_in[:2], tables_in[2:])
        ],
        axis=0,
    )
    near_tables = from_partner(tables)
    stash_own = stashed[0]
    stash_theirs = from_partner(stash_own)
    x_own = jnp.where(first_section, arrivals[0], in_flight[0])
    x_theirs = from_partner(x_own)
    up_own = jnp.where(last_section, cotangent[0], grad_flight[0])
    new_own = jnp.where(first_section, arrivals[1], cotangent[1])
    out_own, out_near, near_tables = lax.optimization_barrier((out_shard, out_near, near_tables))
    out_far = [from_host(out_own, m) for m in between]
    out_parts = [out_shard, out_near] + out_far + [from_host(out_near, m) for m in between]
    up_late, new_late, stash_theirs = lax.optimization_barrier((up_own, new_own, stash_theirs))
    up_theirs = from_partner(up_late)
    up_near = to_partner(
        lax.dynamic_slice_in_dim(up_late, (dp_no ^ 1) * depth, depth, axis=1)
    )
    new_theirs = from_partner(new_late)
    far_hosts = [host_table[(dp_no // 2) ^ m] for m in between]
    owners = [dp_no, dp_no ^ 1] + far_hosts + [h ^ 1 for h in far_hosts]
    offs = jnp.stack(owners).astype(jnp.int32) * depth
    in_offs = [dp_no * depth] + [h * depth for h in far_hosts]
    in_offs += [(dp_no ^ 1) * depth + i * piece for i in range(pieces)]
    in_offs += [(h ^ 1) * depth + i * piece for i in range(pieces) for h in far_hosts]
    in_offs = jnp.stack(in_offs).astype(jnp.int32)
    parts = len(in_parts)
    core = jnp.reshape(core_no, (1,)).astype(jnp.int32)
    first_flag = jnp.reshape(first_section, (1,)).astype(jnp.int32)
    host_flag = jnp.reshape(is_host, (1,)).astype(jnp.int32)
    last_flag = jnp.reshape(last_section, (1,)).astype(jnp.int32)

    both_tables = jnp.stack([tables, near_tables], axis=1)
    ahead_at = sections - 1 - section_no
    chosen = jnp.stack(
        [
            lax.dynamic_index_in_dim(both_tables[way], at, axis=1, keepdims=False)
            for way, at in (
                (0, ahead_at),
                (1, section_no),
                (1, section_no + 1),
                (0, ahead_at + 1),
            )
        ]
    )
    kept = block_keep(chosen[..., 0], chosen[..., 1:].reshape(-1, 2, BLOCKS, BLOCKS))
    blank = jnp.zeros_like(kept[:, 0])
    keep = jnp.concatenate(
        [
            jnp.concatenate([kept[:, 0], blank], axis=2),
            jnp.concatenate([blank, kept[:, 1]], axis=2),
        ],
        axis=1,
    )

    smem = pl.BlockSpec(memory_space=pltpu.SMEM)
    hbm = pl.BlockSpec(memory_space=pltpu.HBM)
    vmem = pl.BlockSpec(memory_space=pltpu.VMEM)

    def all_of(*arrays):
        return [pl.BlockSpec(x.shape, lambda *_, d=x.ndim: (0,) * d) for x in arrays]

    def row_of(x, i):
        return pl.BlockSpec((1,) + x.shape[1:], lambda *_: (i,) + (0,) * (x.ndim - 1))

    params = pltpu.CompilerParams(vmem_limit_bytes=VMEM_BYTES)
    small = pltpu.CompilerParams(vmem_limit_bytes=SMALL_VMEM_BYTES)

    def cost(multiply_adds, bytes_accessed):
        return pl.CostEstimate(
            flops=2 * multiply_adds, bytes_accessed=bytes_accessed, transcendentals=0
        )

    def struct(shape, dtype):
        return jax.ShapeDtypeStruct(shape, dtype)

    halves = [struct((2, share, width), BF16)] * 2
    kept_halves = [halves[0], pltpu.HBM(halves[0].shape, BF16)]
    matmul = rows * width * 4 * slab
    weight_bytes = 2 * width * 5 * slab

    by_head = lambda lead, last: pl.BlockSpec(lead + (last,), lambda h: (0,) * len(lead) + (h,))
    saved_shapes = [
        struct((2, rows, slab), F32),
        struct((2, rows, 3 * slab), BF16),
        struct((2, rows, 4 * slab), F32),
        struct((2, rows, slab), F32),
        struct((2, heads, rows, rows), BF16),
        struct((2, heads, rows, rows), F32),
    ]
    weight_scratch = [pltpu.VMEM(x.shape, BF16) for x in in_parts]
    gated, gate, vqk, slope, mixed, probs, factor = pl.pallas_call(
        on_host(functools.partial(project_kernel, parts, heads)),
        grid=(heads,),
        in_specs=[smem] * 2
        + all_of(x_own, x_theirs, stash_own, stash_theirs, keep)
        + [hbm] * parts,
        out_specs=[by_head((3, rows), HEAD_DIM)] + [hbm] * 6,
        out_shape=[struct((3, rows, slab), BF16)]
        + [pltpu.HBM(x.shape, x.dtype) for x in saved_shapes],
        scratch_shapes=weight_scratch
        + [pltpu.VMEM(x.shape, x.dtype) for x in saved_shapes]
        + [
            pltpu.VMEM((3 * rows, width), BF16),
            pltpu.SemaphoreType.DMA((heads * parts,)),
            pltpu.SemaphoreType.DMA((heads * 6,)),
        ],
        compiler_params=params,
        cost_estimate=cost(3 * matmul, 2 * weight_bytes),
        name="project",
    )(host_flag, in_offs, x_own, x_theirs, stash_own, stash_theirs, keep, *in_hbm(in_parts))

    def backward(ups, tick_no, early=()):
        split = len(ups) - 1
        skip = soon if early else 0
        layered = [gate, vqk, slope, mixed, probs, factor, stash_own, stash_theirs]
        plain = list(out_parts[skip:]) + list(in_parts)
        return pl.pallas_call(
            on_host(functools.partial(backward_kernel, parts, n, skip, tick_no, split)),
            grid=(1,),
            in_specs=[smem] * 4
            + [vmem if split else hbm] * len(ups)
            + [hbm] * (len(early) + len(layered) + len(plain)),
            out_specs=all_of(*halves),
            out_shape=kept_halves,
            scratch_shapes=[pltpu.VMEM((rows, width), BF16)]
            + [pltpu.VMEM(x.shape[1:], x.dtype) for x in layered]
            + [pltpu.VMEM(x.shape, x.dtype) for x in plain]
            + [
                pltpu.VMEM((rows, width), F32),
                pltpu.VMEM((rows, width), F32),
                pltpu.VMEM((rows, width), BF16),
                pltpu.VMEM((rows, slab), F32),
                pltpu.SemaphoreType.DMA((2,)),
                pltpu.SemaphoreType.DMA((1 + len(layered) + n + heads * parts,)),
            ],
            compiler_params=params,
            cost_estimate=cost((16 if split else 2) * matmul, 2 * weight_bytes),
            name="backward",
        )(host_flag, core, in_offs, offs, *ups, *in_hbm(early + tuple(layered)), *plain[: n - skip], *in_hbm(in_parts))

    gated, new_theirs, up_near = lax.optimization_barrier((gated, new_theirs, up_near))

    pack_shapes = [struct((rows, width), BF16)]
    pack_shapes += [struct((rows, 2 * slab + depth), BF16)] * (n - 2)
    folded = share * width // rows
    up_0, *packs = pl.pallas_call(
        functools.partial(pack_kernel, n),
        grid=(1,),
        in_specs=[smem] * 1 + all_of(gated, up_own, up_theirs),
        out_specs=all_of(*pack_shapes),
        out_shape=[pltpu.HBM(pack_shapes[0].shape, BF16)] + pack_shapes[1:],
        compiler_params=small,
        name="pack",
    )(offs, gated, up_own, up_theirs)
    soon = n // 2 + 1
    packs, soon_parts = lax.optimization_barrier((packs, out_parts[:soon]))
    early_shapes = [struct((rows, width), BF16), struct((rows, slab), F32)]
    early_part, early_grad = pl.pallas_call(
        early_kernel,
        grid=(1,),
        in_specs=[smem] + [row_of(gated, 0)] + all_of(up_0, *soon_parts),
        out_specs=all_of(*early_shapes),
        out_shape=[early_shapes[0], pltpu.HBM(early_shapes[1].shape, F32)],
        compiler_params=small,
        name="early",
    )(offs, gated, *in_hbm([up_0]), *soon_parts)
    early_part, early_grad, late_parts = lax.optimization_barrier(
        (early_part, early_grad, out_parts[soon:])
    )
    out_parts = soon_parts + late_parts

    ahead_send, ahead_keep = pl.pallas_call(
        functools.partial(out_kernel, soon),
        grid=(1,),
        in_specs=[smem] * 2 + [row_of(gated, 0)] + all_of(early_part, *out_parts[soon:]),
        out_specs=all_of(*halves),
        out_shape=halves,
        scratch_shapes=[pltpu.VMEM((rows, width), BF16)],
        compiler_params=small,
        cost_estimate=cost(matmul // 4, weight_bytes // 4),
        name="out",
    )(core, offs, gated, early_part, *out_parts[soon:])
    ahead_landed = swap_cores(ahead_send)
    first_shapes = [halves[0], struct((rows, 2 * slab + folded), BF16)]
    ahead_0, partner_pack = pl.pallas_call(
        first_kernel,
        grid=(1,),
        in_specs=[smem] + all_of(x_own, x_theirs, ahead_keep, ahead_landed, gated),
        out_specs=all_of(*first_shapes),
        out_shape=first_shapes,
        compiler_params=small,
        name="first",
    )(core, *in_hbm([x_own, x_theirs]), ahead_keep, ahead_landed, gated)
    ahead_in = along_sections(ahead_0, 1)
    packs_near = [to_partner(partner_pack)] + [from_host(packs[m - 1], m) for m in between]
    back_send, back_keep = backward(in_hbm([after(up_0, ahead_0)]), 0, (early_grad,))
    back_send, back_keep, ahead_in, packs_near = lax.optimization_barrier(
        (back_send, back_keep, ahead_in, packs_near)
    )
    back_landed = swap_cores(back_send)
    back_0 = pl.pallas_call(
        settle_kernel,
        grid=(1,),
        in_specs=[smem] + all_of(up_own, up_theirs, back_keep, back_landed),
        out_specs=all_of(halves[0])[0],
        out_shape=halves[0],
        compiler_params=small,
        name="settle",
    )(core, *in_hbm([up_own, up_theirs, back_keep]), back_landed)
    back_in = along_sections(back_0, -1)

    packs_beyond = [to_beyond(packs[n // 2 + m - 2], m) for m in between]
    ahead_their = swap_cores(ahead_in)
    ahead_send, ahead_keep = pl.pallas_call(
        on_host(functools.partial(forward_kernel, parts, heads)),
        grid=(heads,),
        in_specs=[smem] * 5
        + all_of(ahead_in, ahead_their, new_own, new_theirs)
        + [row_of(keep, keep.shape[0] - 1)]
        + [hbm] * parts
        + all_of(*out_parts),
        out_specs=all_of(*halves),
        out_shape=kept_halves,
        scratch_shapes=[
            pltpu.VMEM((rows, width), BF16),
            pltpu.VMEM((rows, width), BF16),
            pltpu.VMEM((heads, rows, HEAD_DIM), BF16),
            pltpu.VMEM((rows, width), BF16),
            pltpu.SemaphoreType.DMA((heads * parts,)),
        ]
        + weight_scratch,
        compiler_params=params,
        cost_estimate=cost(2 * matmul, 2 * weight_bytes),
        name="forward",
    )(host_flag, core,
        in_offs,
        offs,
        first_flag,
        *in_hbm([ahead_in]),
        ahead_their,
        *in_hbm([new_own, new_theirs, keep]),
        *in_hbm(in_parts),
        *out_parts,
    )
    ahead_send, ahead_keep, back_in, packs_beyond = lax.optimization_barrier(
        (ahead_send, ahead_keep, back_in, packs_beyond)
    )
    ahead_landed = swap_cores(ahead_send)

    cut_shapes = [halves[0]] + [struct((2 * share, depth), BF16)] * (n - 2)
    up_mine, *cuts = pl.pallas_call(
        functools.partial(cut_kernel, n),
        grid=(1,),
        in_specs=[smem] * 3 + all_of(back_in, new_own, new_theirs),
        out_specs=all_of(*cut_shapes),
        out_shape=cut_shapes,
        compiler_params=small,
        name="cut",
    )(core, offs, last_flag, back_in, *in_hbm([new_own, new_theirs]))
    up_their = swap_cores(up_mine)
    landed = [from_host(cuts[m - 1], m) for m in between]
    landed += [to_beyond(cuts[n // 2 + m - 2], m) for m in between]
    message_inputs = [new_own, new_theirs, ahead_in, ahead_keep, ahead_landed, up_mine, back_0]
    message_shapes = [halves[0], struct((2 * share, depth + width), BF16)]
    ahead_1, message = pl.pallas_call(
        message_kernel,
        grid=(1,),
        in_specs=[smem] * 3 + all_of(*message_inputs),
        out_specs=all_of(*message_shapes),
        out_shape=message_shapes,
        compiler_params=small,
        name="message",
    )(core, offs, first_flag, *in_hbm(message_inputs[:4]), *message_inputs[4:6], *in_hbm([back_0]))
    landed = landed + [to_partner(message)]
    back_send, back_keep = backward([up_mine, up_their], 1)
    back_send, back_keep, landed = lax.optimization_barrier((back_send, back_keep, landed))
    landed = landed[-1:] + landed[:-1]
    last_inputs = [up_mine, *in_hbm([back_keep]), swap_cores(back_send)]
    last_shapes = [halves[0], struct((share, width), BF16)]
    back_1, back_other = pl.pallas_call(
        last_kernel,
        grid=(1,),
        in_specs=all_of(*last_inputs),
        out_specs=all_of(*last_shapes),
        out_shape=last_shapes,
        compiler_params=small,
        name="last",
    )(*last_inputs)
    back_last = to_partner(back_other)

    landed_halves = jnp.stack(
        [landed[0][:, :depth]]
        + [jnp.where(is_host, landed[m], landed[n // 2 + m - 1]) for m in between]
    )
    landed_other = swap_cores(landed_halves)
    grad_inputs = [gated, up_0, up_own, up_near, up_mine, up_their, landed_halves, landed_other]
    grad_inputs += packs_near + packs_beyond
    grad_inputs[0] = after(gated, back_1)
    grad_inputs[8:] = in_hbm(grad_inputs[8:])
    grads = pl.pallas_call(
        functools.partial(grads_kernel, n, (ticks * length * n) ** (-0.5)),
        grid=(1,),
        in_specs=[smem] * 3 + all_of(*grad_inputs),
        out_specs=pl.BlockSpec((slab, depth), lambda *_: (0, 0)),
        out_shape=struct((slab, depth), F32),
        scratch_shapes=[pltpu.VMEM((rows, depth), BF16)],
        compiler_params=small,
        cost_estimate=cost(matmul // 4, weight_bytes // 4),
        name="grads",
    )(host_flag, core, offs, *grad_inputs)

    first_pack, last_cut = lax.optimization_barrier((packs_near[0], landed[0], back_1))[:2]
    finish_inputs = [ahead_0, ahead_1, back_0, first_pack, last_cut]
    finish_shapes = [struct((ticks, share, width), BF16), struct((share, width), BF16)]
    ahead, back_first = pl.pallas_call(
        functools.partial(finish_kernel, slab),
        grid=(1,),
        in_specs=[smem] + all_of(*finish_inputs),
        out_specs=all_of(*finish_shapes),
        out_shape=finish_shapes,
        compiler_params=small,
        name="finish",
    )(host_flag, *finish_inputs)
    back = jnp.stack([back_first, jnp.where(is_host, back_1[0], back_last)])
    return (ahead[None], back[None], grads[None])


def solution(mesh):
    in_specs = (
        P(None, "dp", None),
        P("section", "dp", None),
        P(None, "dp", None),
        P("section", "dp", None),
        P("section", None, "dp", None),
        P("section", "dp", "cores"),
        P("section", "cores", "dp"),
        P("dp", None),
        P("dp", None),
        P("dp", None, None, None),
        P("dp", None, None, None),
    )
    out_specs = (
        P("section", None, ("dp", "cores"), None),
        P("section", None, ("dp", "cores"), None),
        P("section", "cores", "dp"),
    )
    return jax.shard_map(
        per_device, mesh=mesh, in_specs=in_specs, out_specs=out_specs, check_vma=False
    )
```

```python
import functools

import jax
import jax.numpy as jnp
from jax import lax
from jax.experimental import pallas as pl
from jax.experimental.pallas import tpu as pltpu
from jax.sharding import PartitionSpec as P

HEAD_DIM = 128
BLOCK = 24
BLOCKS = 4
EPSILON = 1e-06
SCALING = HEAD_DIM ** (-0.5)
VMEM_BYTES = 34 * 1024 * 1024
SMALL_VMEM_BYTES = 16 * 1024 * 1024

F32 = jnp.float32
BF16 = jnp.bfloat16


def on_host(kernel):
    def guarded(host, *refs):
        pl.when(host[0] != 0)(functools.partial(kernel, *refs))

    return guarded


def dot(a, b):
    return lax.dot_general(a, b, (((1,), (0,)), ((), ())), preferred_element_type=F32)


def dot_nt(a, b):
    return lax.dot_general(a, b, (((1,), (1,)), ((), ())), preferred_element_type=F32)


def dot_tn(a, b):
    return lax.dot_general(a, b, (((0,), (0,)), ((), ())), preferred_element_type=F32)


def row_root(floats):
    return lax.rsqrt(jnp.mean(floats * floats, axis=-1, keepdims=True) + EPSILON)


def sigmoid(x):
    return 1.0 / (1.0 + jnp.exp(-x))


def attend(pre, keep):
    sig = sigmoid(pre)
    active = pre * sig
    gate = active[:, :HEAD_DIM]
    vqk = active[:, HEAD_DIM:].astype(BF16)
    value = vqk[:, :HEAD_DIM]
    query = vqk[:, HEAD_DIM : 2 * HEAD_DIM]
    key = vqk[:, 2 * HEAD_DIM :]
    scores = dot_nt(query, key) * SCALING
    sig_s = sigmoid(scores)
    probs = (scores * sig_s * keep).astype(BF16)
    mixed = dot(probs, value)
    gated = (mixed * row_root(mixed) * gate).astype(BF16)
    return sig, gate, vqk, scores, sig_s, probs, mixed, gated


def project(normed, offs, weights, of_head):
    total = None
    for j, weight in enumerate(weights):
        depth = weight.shape[0]
        columns = pl.ds(pl.multiple_of(offs[j], depth), depth)
        term = dot(normed[:, columns], weight[:, of_head])
        total = term if total is None else total + term
    return total


def columns_of_head(h, size):
    return pl.ds(pl.multiple_of(h * size, size), size)


def weight_copies(sources, targets, sems, h):
    of_head = columns_of_head(h, 4 * HEAD_DIM)
    return [
        pltpu.make_async_copy(
            source.at[:, of_head], target.at[:, of_head], sems.at[h * len(sources) + j]
        )
        for j, (source, target) in enumerate(zip(sources, targets))
    ]


def project_kernel(parts, heads, offs, x_own, x_theirs, stash_own, stash_theirs, keep, *rest):
    sources, rest = rest[:parts], rest[parts:]
    gated_out, saved, rest = rest[0], rest[1:7], rest[7:]
    weights, rest = rest[:parts], rest[parts:]
    held, (normed, sems, out_sems) = rest[:6], rest[6:]
    gate_out, vqk_out, slope_out, mixed_out, probs_out, factor_out = held
    length = x_own.shape[0]
    rows = 2 * length
    head = pl.program_id(0)

    def saved_copies(h):
        copies = []
        for i, (source, target) in enumerate(zip(held, saved)):
            if i < 4:
                at = (slice(None), slice(None), columns_of_head(h, source.shape[2] // heads))
            else:
                at = (slice(None), h)
            copies.append(
                pltpu.make_async_copy(source.at[at], target.at[at], out_sems.at[h * 6 + i])
            )
        return copies

    @pl.when(head == 0)
    def _():
        for h in range(heads):
            for copy in weight_copies(sources, weights, sems, h):
                copy.start()
        blocks = [x_own, x_theirs]
        for t in range(stash_own.shape[0]):
            blocks += [stash_own.at[t], stash_theirs.at[t]]
        for i, block in enumerate(blocks):
            floats = block[...].astype(F32)
            normed[pl.ds(i * length, length), :] = (floats * row_root(floats)).astype(BF16)

    for copy in weight_copies(sources, weights, sems, head):
        copy.wait()
    pre_all = project(normed, offs, weights, columns_of_head(head, 4 * HEAD_DIM))
    for i in range(1 + stash_own.shape[0]):
        pre = pre_all[i * rows : (i + 1) * rows]
        kept = keep[i]
        sig, gate, vqk, scores, sig_s, probs, mixed, gated = attend(pre, kept)
        gated_out[i] = gated
        if i > 0:
            narrow = columns_of_head(head, HEAD_DIM)
            gate_out[i - 1, :, narrow] = gate
            vqk_out[i - 1, :, columns_of_head(head, 3 * HEAD_DIM)] = vqk
            slope_out[i - 1, :, columns_of_head(head, 4 * HEAD_DIM)] = sig * (
                1.0 + pre * (1.0 - sig)
            )
            mixed_out[i - 1, :, narrow] = mixed
            probs_out[i - 1, head] = probs
            factor_out[i - 1, head] = kept * sig_s * (1.0 + scores * (1.0 - sig_s)) * SCALING
    for copy in saved_copies(head):
        copy.start()

    @pl.when(head == heads - 1)
    def _():
        for h in range(heads):
            for copy in saved_copies(h):
                copy.wait()


def split_rows(core, part, send, keep):
    share = send.shape[1]
    cores = part.shape[0] // (2 * share)
    for r in range(2):
        base = r * cores * share
        mine = pl.multiple_of(base + core * share, share)
        other = pl.multiple_of(base + (cores - 1 - core) * share, share)
        send[r] = part[pl.ds(other, share), :]
        keep[r] = part[pl.ds(mine, share), :]


def early_kernel(offs, gated, upstream, *rest):
    weights, (part, grad_gated) = rest[:-2], rest[-2:]
    depth = weights[0].shape[1]
    total = None
    for j, weight in enumerate(weights):
        columns = pl.ds(pl.multiple_of(offs[j], depth), depth)
        part[:, columns] = dot(gated[0], weight[...]).astype(BF16)
        term = dot_nt(upstream[:, columns], weight[...])
        total = term if total is None else total + term
    grad_gated[...] = total


def out_kernel(skip, core, offs, gated, early, *rest):
    weights, (send, keep, part) = rest[:-3], rest[-3:]
    depth = weights[0].shape[1]
    part[...] = early[...]
    for j, weight in enumerate(weights):
        columns = pl.ds(pl.multiple_of(offs[skip + j], depth), depth)
        part[:, columns] = dot(gated[0], weight[...]).astype(BF16)
    split_rows(core[0], part, send, keep)


def assemble(core, fresh, mine, theirs, new_own, new_theirs, whole):
    share = mine.shape[1]
    length = new_own.shape[0]
    cores = length // share
    use_fresh = fresh != 0
    for r, source in enumerate((new_own, new_theirs)):
        for owner, landed in ((core, mine), (cores - 1 - core, theirs)):
            inside = pl.multiple_of(owner * share, share)
            rows = source[pl.ds(inside, share), :]
            at = pl.multiple_of(r * length + owner * share, share)
            whole[pl.ds(at, share), :] = jnp.where(use_fresh, rows, landed[r])


def forward_kernel(parts, heads, core, in_offs, offs, fresh, mine, theirs, new_own, new_theirs, keep, *rest):
    sources, rest = rest[:parts], rest[parts:]
    in_parts, rest = rest[-parts:], rest[:-parts]
    out_parts = rest[:-7]
    send, kept, whole, normed, gated, part, sems = rest[-7:]
    depth = out_parts[0].shape[1]
    head = pl.program_id(0)

    @pl.when(head == 0)
    def _():
        for h in range(heads):
            for copy in weight_copies(sources, in_parts, sems, h):
                copy.start()
        assemble(core[0], fresh[0], mine, theirs, new_own, new_theirs, whole)
        floats = whole[...].astype(F32)
        normed[...] = (floats * row_root(floats)).astype(BF16)

    for copy in weight_copies(sources, in_parts, sems, head):
        copy.wait()
    pre = project(normed, in_offs, in_parts, columns_of_head(head, 4 * HEAD_DIM))
    gated[head] = attend(pre, keep[0])[-1]

    @pl.when(head == heads - 1)
    def _():
        for j in range(len(out_parts)):
            columns = pl.ds(pl.multiple_of(offs[j], depth), depth)
            total = None
            for h in range(heads):
                term = dot(gated[h], out_parts[j][pl.ds(h * HEAD_DIM, HEAD_DIM), :])
                total = term if total is None else total + term
            part[:, columns] = total.astype(BF16)
        split_rows(core[0], part, send, kept)


def backward_kernel(parts, n, skip, tick, split, core, in_offs, offs, *rest):
    n = n - skip
    count = 8 + n + parts
    up_sources, rest = rest[: 1 + split], rest[1 + split :]
    early, rest = (rest[0], rest[1:]) if skip else (None, rest)
    sources, rest = (None,) + rest[:count], rest[count:]
    send, keep = rest[:2]
    held, (grad_normed, scaled, part, begun, up_sems, sems) = (
        rest[2 : 3 + count],
        rest[3 + count :],
    )
    ups, gate, vqk, slope, mixed, probs, factor, x_own, x_theirs = held[:9]
    out_parts, in_parts = held[9 : 9 + n], held[9 + n :]
    wide = 4 * HEAD_DIM
    heads = out_parts[0].shape[0] // HEAD_DIM
    copies = []
    for i, (source, target) in enumerate(zip(sources[: 9 + n], held[: 9 + n])):
        if i == 0:
            continue
        if i < 9:
            source = source.at[tick]
        copies.append(pltpu.make_async_copy(source, target, sems.at[i]))
    up_copies = []
    if not split:
        up_copies.append(pltpu.make_async_copy(up_sources[0], ups, up_sems.at[0]))
    if skip:
        up_copies.append(pltpu.make_async_copy(early, begun, up_sems.at[1]))
    copies = [None] + copies
    by_head = []
    for h in range(heads):
        of_head = slice(h * wide, (h + 1) * wide)
        by_head.append(
            [
                pltpu.make_async_copy(
                    sources[9 + n + j].at[:, of_head],
                    in_parts[j].at[:, of_head],
                    sems.at[9 + n + h * parts + j],
                )
                for j in range(parts)
            ]
        )
    first = list(range(9, 9 + n))
    second = [1, 4, 2, 5, 6, 3]
    for i in (7, 8):
        copies[i].start()
    for copy in up_copies:
        copy.start()
    for i in first + second:
        copies[i].start()
    for of_head in by_head:
        for copy in of_head:
            copy.start()
    if split:
        share = up_sources[0].shape[1]
        cores = ups.shape[0] // (2 * share)
        for half, owner in enumerate((core[0], cores - 1 - core[0])):
            for r in range(2):
                at = pl.multiple_of((r * cores + owner) * share, share)
                ups[pl.ds(at, share), :] = up_sources[half][r]
    roots = []
    for i, source in ((7, x_own), (8, x_theirs)):
        copies[i].wait()
        floats = source[...].astype(F32)
        roots.append(row_root(floats))
        scaled[pl.ds((i - 7) * source.shape[0], source.shape[0]), :] = floats * roots[-1]
    for copy in up_copies:
        copy.wait()
    depth = out_parts[0].shape[1]
    length = x_own.shape[0]
    grad_gated = begun[...] if skip else None
    for j in range(n):
        columns = pl.ds(pl.multiple_of(offs[skip + j], depth), depth)
        copies[first[j]].wait()
        term = dot_nt(ups[:, columns], out_parts[j][...])
        grad_gated = term if grad_gated is None else grad_gated + term
    grad_gated = grad_gated.astype(BF16).astype(F32)
    for i in second:
        copies[i].wait()

    def through_head(h):
        cut = slice(h * HEAD_DIM, (h + 1) * HEAD_DIM)
        up = grad_gated[:, cut]
        mixed_h = mixed[:, cut]
        root = row_root(mixed_h)
        normed = mixed_h * root
        grad_n = up * gate[:, cut]
        grad_gate = up * normed
        grad_mixed = root * (grad_n - normed * jnp.mean(grad_n * normed, axis=-1, keepdims=True))
        low = grad_mixed.astype(BF16)
        base = 3 * h * HEAD_DIM
        value = vqk[:, base : base + HEAD_DIM]
        query = vqk[:, base + HEAD_DIM : base + 2 * HEAD_DIM]
        key = vqk[:, base + 2 * HEAD_DIM : base + 3 * HEAD_DIM]
        grad_scores = (dot_nt(low, value) * factor[h]).astype(BF16)
        grad_value = dot_tn(probs[h], low)
        grad_query = dot(grad_scores, key)
        grad_key = dot_tn(grad_scores, query)
        grad_active = jnp.concatenate([grad_gate, grad_value, grad_query, grad_key], axis=1)
        return (grad_active * slope[:, h * wide : (h + 1) * wide]).astype(BF16)

    grad_pre = through_head(0)
    for h in range(heads):
        for copy in by_head[h]:
            copy.wait()
        following = through_head(h + 1) if h + 1 < heads else None
        for j in range(parts):
            rows_of = in_parts[j].shape[0]
            columns = pl.ds(pl.multiple_of(in_offs[j], rows_of), rows_of)
            term = dot_nt(grad_pre, in_parts[j][:, h * wide : (h + 1) * wide])
            if h == 0:
                grad_normed[:, columns] = term
            else:
                grad_normed[:, columns] += term
        grad_pre = following
    for r, root in enumerate(roots):
        rows = pl.ds(r * length, length)
        scaled_rows = scaled[rows, :]
        grad_n = grad_normed[rows, :]
        mean = jnp.mean(grad_n * scaled_rows, axis=-1, keepdims=True)
        part[rows, :] = (root * (grad_n - scaled_rows * mean)).astype(BF16)
    split_rows(core[0], part, send, keep)


def pack_kernel(n, offs, gated, up_own, up_theirs, whole, *packs):
    depth = packs[0].shape[1] - 2 * gated.shape[2]
    slab = gated.shape[2]
    length = up_own.shape[0]
    whole[:length, :] = up_own[...]
    whole[length:, :] = up_theirs[...]
    for j in range(2, n):
        pack = packs[j - 2]
        columns = pl.ds(pl.multiple_of(offs[j], depth), depth)
        pack[:, :slab] = gated[1]
        pack[:, slab : 2 * slab] = gated[2]
        pack[:length, 2 * slab :] = up_own[:, columns]
        pack[length:, 2 * slab :] = up_theirs[:, columns]


def fold(rows, target, start):
    share, width = rows.shape
    blocks = target.shape[0] // share
    size = width // blocks
    for k in range(blocks):
        target[k * share : (k + 1) * share, start : start + size] = rows[
            :, k * size : (k + 1) * size
        ]


def unfold(folded, start, target):
    share, width = target.shape
    blocks = folded.shape[0] // share
    size = width // blocks
    for k in range(blocks):
        target[:, k * size : (k + 1) * size] = folded[
            k * share : (k + 1) * share, start : start + size
        ]


def finish_kernel(slab, host, ahead_0, ahead_1, back_0, pack, message, given, ahead, back):
    width = back.shape[1]
    depth = message.shape[1] - width // 2

    @pl.when(host[0] != 0)
    def _():
        ahead[0] = ahead_0[0]
        ahead[1] = ahead_1[0]
        back[...] = back_0[0]

    @pl.when(host[0] == 0)
    def _():
        unfold(pack, 2 * slab, ahead.at[0])
        unfold(message, depth, ahead.at[1])
        back[...] = given[...]


def settle_kernel(core, own, theirs, keep, landed, total):
    share = keep.shape[1]
    here = pl.ds(pl.multiple_of(core[0] * share, share), share)
    for r, source in enumerate((own, theirs)):
        total[r] = (
            source[here, :].astype(F32) + keep[r].astype(F32) + landed[r].astype(F32)
        ).astype(BF16)


def settle_two_kernel(core, own, theirs, keep, landed, total, other):
    settle_kernel(core, own, theirs, keep, landed, total)
    other[...] = total[1]


def first_kernel(core, own, theirs, keep, landed, gated, total, pack):
    slab = gated.shape[2]
    settle_kernel(core, own, theirs, keep, landed, total)
    pack[:, :slab] = gated[1]
    pack[:, slab : 2 * slab] = gated[2]
    fold(total[1], pack, 2 * slab)


def message_kernel(
    core, offs, fresh, new_own, new_theirs, passed, keep, landed, up, ahead, message
):
    share = keep.shape[1]
    depth = message.shape[1] - up.shape[2] // 2
    here = pl.ds(pl.multiple_of(core[0] * share, share), share)
    columns = pl.ds(pl.multiple_of(offs[1], depth), depth)
    for r, source in enumerate((new_own, new_theirs)):
        residual = jnp.where(fresh[0] != 0, source[here, :], passed[r])
        ahead[r] = (
            residual.astype(F32) + keep[r].astype(F32) + landed[r].astype(F32)
        ).astype(BF16)
        message[r * share : (r + 1) * share, :depth] = up[r, :, columns]
    fold(ahead[1], message, depth)


def last_kernel(up, keep, landed, back, other):
    for r in range(2):
        back[r] = (
            up[r].astype(F32) + keep[r].astype(F32) + landed[r].astype(F32)
        ).astype(BF16)
    other[...] = back[1]


def cut_kernel(n, core, offs, fresh, landed, new_own, new_theirs, mine, *pieces):
    share = landed.shape[1]
    depth = pieces[-1].shape[1]
    here = pl.ds(pl.multiple_of(core[0] * share, share), share)
    for r, source in enumerate((new_own, new_theirs)):
        mine[r] = jnp.where(fresh[0] != 0, source[here, :], landed[r])
        for j in range(2, n):
            columns = pl.ds(pl.multiple_of(offs[j], depth), depth)
            pieces[j - 2][r * share : (r + 1) * share, :] = mine[r, :, columns]


def grads_kernel(
    n, scaling, host, core, offs, gated, up_0, up_own, up_near, mine, theirs, halves, other, *rest
):
    packs = rest[: n - 1]
    out, whole = rest[n - 1 :]
    slab = gated.shape[2]
    depth = out.shape[1]
    share = mine.shape[1]
    cores = whole.shape[0] // (2 * share)
    at_host = host[0] != 0
    columns = pl.ds(pl.multiple_of(offs[0], depth), depth)

    def product(first, second, third, upstream):
        for half, owner in enumerate((core[0], cores - 1 - core[0])):
            for r in range(2):
                at = pl.multiple_of((r * cores + owner) * share, share)
                whole[pl.ds(at, share), :] = upstream(half, r)
        return dot_tn(first, third) + dot_tn(second, whole[...])

    up_pair = jnp.concatenate([up_near[...], up_own[:, columns]], axis=0)
    total = product(
        jnp.where(at_host, gated[1], packs[0][:, :slab]),
        jnp.where(at_host, gated[2], packs[0][:, slab : 2 * slab]),
        jnp.where(at_host, up_0[:, columns], up_pair),
        lambda half, r: jnp.where(
            at_host,
            (mine, theirs)[half][r, :, columns],
            (halves, other)[half][0, r * share : (r + 1) * share, :],
        ),
    )
    for m in range(1, n // 2):
        near, beyond = m, n // 2 + m - 1
        pack = jnp.where(at_host, packs[near][...], packs[beyond][...])
        total = total + product(
            pack[:, :slab],
            pack[:, slab : 2 * slab],
            pack[:, 2 * slab :],
            lambda half, r: (halves, other)[half][m, r * share : (r + 1) * share, :],
        )
    out[...] = total * scaling


def in_hbm(arrays):
    return [pltpu.with_memory_space_constraint(x, pltpu.HBM) for x in arrays]


def after(value, *earlier):
    return lax.optimization_barrier((value,) + earlier)[0]


def block_keep(live_blocks, block_marks):
    length = BLOCKS * BLOCK
    places = jnp.arange(length, dtype=jnp.int32)
    owners = places // BLOCK
    marked = jnp.repeat(jnp.repeat(block_marks, BLOCK, axis=-2), BLOCK, axis=-1) == 1
    allowed = (owners[:, None] == owners[None, :]) | marked
    causal = places[:, None] >= places[None, :]
    tokens = live_blocks[..., None, None] * BLOCK
    keeping = causal & allowed & (places[:, None] < tokens) & (places[None, :] < tokens)
    return jnp.where(keeping, 1.0 / jnp.maximum(tokens, 1).astype(F32), 0.0)


def per_device(
    arrivals,
    in_flight,
    cotangent,
    grad_flight,
    stashed,
    in_weight,
    out_weight,
    forward_blocks,
    backward_blocks,
    forward_marks,
    backward_marks,
):
    section_no = lax.axis_index("section")
    sections = lax.axis_size("section")
    core_no = lax.axis_index("cores")
    cores = lax.axis_size("cores")
    dp_no = lax.axis_index("dp")
    n = lax.axis_size("dp")
    ticks = arrivals.shape[0]
    length = arrivals.shape[1]
    width = arrivals.shape[2]
    rows = 2 * length
    share = length // cores
    in_shard = in_weight[0]
    out_shard = out_weight[0]
    depth = in_shard.shape[0]
    slab = out_shard.shape[0]
    heads = slab // HEAD_DIM
    wide = 4 * HEAD_DIM

    hosts = [2 * k + 1 if 4 * k < n - 2 else 2 * k for k in range(n // 2)]
    host_table = jnp.array(hosts, jnp.int32)
    is_host = dp_no == host_table[dp_no // 2]

    def from_partner(x):
        return lax.ppermute(x, "dp", [(h ^ 1, h) for h in hosts])

    def to_partner(x):
        return lax.ppermute(x, "dp", [(h, h ^ 1) for h in hosts])

    def from_host(x, m):
        return lax.ppermute(x, "dp", [(hosts[k ^ m], hosts[k]) for k in range(n // 2)])

    def to_beyond(x, m):
        return lax.ppermute(
            x, "dp", [(hosts[k ^ m], hosts[k] ^ 1) for k in range(n // 2)]
        )

    def swap_cores(x):
        return lax.ppermute(x, "cores", [(c, cores - 1 - c) for c in range(cores)])

    def along_sections(x, by):
        pairs = [
            (i * n + h, (i + by) * n + h)
            for i in range(sections)
            if 0 <= i + by < sections
            for h in hosts
        ]
        return lax.ppermute(x, ("section", "dp"), pairs)

    first_section = section_no == 0
    last_section = section_no == sections - 1
    between = range(1, n // 2)

    pieces = max(1, min(2, depth // 256))
    piece = depth // pieces
    in_far = [from_host(in_shard, m) for m in between]
    in_near = [
        from_partner(in_shard[i * piece : (i + 1) * piece]) for i in range(pieces)
    ]
    out_near = from_partner(out_shard)
    in_pass = [from_host(in_near[0], m) for m in between]
    in_far, in_near, rows_in, tables_in = lax.optimization_barrier(
        (
            in_far,
            in_near,
            (arrivals, in_flight, cotangent, grad_flight, stashed),
            (forward_blocks, forward_marks, backward_blocks, backward_marks),
        )
    )
    in_pass += [from_host(in_near[i], m) for i in range(1, pieces) for m in between]
    in_parts = [in_shard] + in_far + in_near + in_pass
    arrivals, in_flight, cotangent, grad_flight, stashed = rows_in
    tables = jnp.concatenate(
        [
            jnp.concatenate([b[..., None], m.reshape(m.shape[:2] + (-1,))], axis=-1)
            for b, m in (tables_in[:2], tables_in[2:])
        ],
        axis=0,
    )
    near_tables = from_partner(tables)
    stash_own = stashed[0]
    stash_theirs = from_partner(stash_own)
    x_own = jnp.where(first_section, arrivals[0], in_flight[0])
    x_theirs = from_partner(x_own)
    up_own = jnp.where(last_section, cotangent[0], grad_flight[0])
    new_own = jnp.where(first_section, arrivals[1], cotangent[1])
    out_own, out_near, near_tables = lax.optimization_barrier((out_shard, out_near, near_tables))
    out_far = [from_host(out_own, m) for m in between]
    out_parts = [out_shard, out_near] + out_far + [from_host(out_near, m) for m in between]
    up_late, new_late, stash_theirs = lax.optimization_barrier((up_own, new_own, stash_theirs))
    up_theirs = from_partner(up_late)
    up_near = to_partner(
        lax.dynamic_slice_in_dim(up_late, (dp_no ^ 1) * depth, depth, axis=1)
    )
    new_theirs = from_partner(new_late)
    far_hosts = [host_table[(dp_no // 2) ^ m] for m in between]
    owners = [dp_no, dp_no ^ 1] + far_hosts + [h ^ 1 for h in far_hosts]
    offs = jnp.stack(owners).astype(jnp.int32) * depth
    in_offs = [dp_no * depth] + [h * depth for h in far_hosts]
    in_offs += [(dp_no ^ 1) * depth + i * piece for i in range(pieces)]
    in_offs += [(h ^ 1) * depth + i * piece for i in range(pieces) for h in far_hosts]
    in_offs = jnp.stack(in_offs).astype(jnp.int32)
    parts = len(in_parts)
    core = jnp.reshape(core_no, (1,)).astype(jnp.int32)
    first_flag = jnp.reshape(first_section, (1,)).astype(jnp.int32)
    host_flag = jnp.reshape(is_host, (1,)).astype(jnp.int32)
    last_flag = jnp.reshape(last_section, (1,)).astype(jnp.int32)

    both_tables = jnp.stack([tables, near_tables], axis=1)
    ahead_at = sections - 1 - section_no
    chosen = jnp.stack(
        [
            lax.dynamic_index_in_dim(both_tables[way], at, axis=1, keepdims=False)
            for way, at in (
                (0, ahead_at),
                (1, section_no),
                (1, section_no + 1),
                (0, ahead_at + 1),
            )
        ]
    )
    kept = block_keep(chosen[..., 0], chosen[..., 1:].reshape(-1, 2, BLOCKS, BLOCKS))
    blank = jnp.zeros_like(kept[:, 0])
    keep = jnp.concatenate(
        [
            jnp.concatenate([kept[:, 0], blank], axis=2),
            jnp.concatenate([blank, kept[:, 1]], axis=2),
        ],
        axis=1,
    )

    smem = pl.BlockSpec(memory_space=pltpu.SMEM)
    hbm = pl.BlockSpec(memory_space=pltpu.HBM)
    vmem = pl.BlockSpec(memory_space=pltpu.VMEM)

    def all_of(*arrays):
        return [pl.BlockSpec(x.shape, lambda *_, d=x.ndim: (0,) * d) for x in arrays]

    def row_of(x, i):
        return pl.BlockSpec((1,) + x.shape[1:], lambda *_: (i,) + (0,) * (x.ndim - 1))

    params = pltpu.CompilerParams(vmem_limit_bytes=VMEM_BYTES)
    small = pltpu.CompilerParams(vmem_limit_bytes=SMALL_VMEM_BYTES)

    def cost(multiply_adds, bytes_accessed):
        return pl.CostEstimate(
            flops=2 * multiply_adds, bytes_accessed=bytes_accessed, transcendentals=0
        )

    def struct(shape, dtype):
        return jax.ShapeDtypeStruct(shape, dtype)

    halves = [struct((2, share, width), BF16)] * 2
    kept_halves = [halves[0], pltpu.HBM(halves[0].shape, BF16)]
    matmul = rows * width * 4 * slab
    weight_bytes = 2 * width * 5 * slab

    by_head = lambda lead, last: pl.BlockSpec(lead + (last,), lambda h: (0,) * len(lead) + (h,))
    saved_shapes = [
        struct((2, rows, slab), F32),
        struct((2, rows, 3 * slab), BF16),
        struct((2, rows, 4 * slab), F32),
        struct((2, rows, slab), F32),
        struct((2, heads, rows, rows), BF16),
        struct((2, heads, rows, rows), F32),
    ]
    weight_scratch = [pltpu.VMEM(x.shape, BF16) for x in in_parts]
    gated, gate, vqk, slope, mixed, probs, factor = pl.pallas_call(
        on_host(functools.partial(project_kernel, parts, heads)),
        grid=(heads,),
        in_specs=[smem] * 2
        + all_of(x_own, x_theirs, stash_own, stash_theirs, keep)
        + [hbm] * parts,
        out_specs=[by_head((3, rows), HEAD_DIM)] + [hbm] * 6,
        out_shape=[struct((3, rows, slab), BF16)]
        + [pltpu.HBM(x.shape, x.dtype) for x in saved_shapes],
        scratch_shapes=weight_scratch
        + [pltpu.VMEM(x.shape, x.dtype) for x in saved_shapes]
        + [
            pltpu.VMEM((3 * rows, width), BF16),
            pltpu.SemaphoreType.DMA((heads * parts,)),
            pltpu.SemaphoreType.DMA((heads * 6,)),
        ],
        compiler_params=params,
        cost_estimate=cost(3 * matmul, 2 * weight_bytes),
        name="project",
    )(host_flag, in_offs, x_own, x_theirs, stash_own, stash_theirs, keep, *in_hbm(in_parts))

    def backward(ups, tick_no, early=()):
        split = len(ups) - 1
        skip = soon if early else 0
        layered = [gate, vqk, slope, mixed, probs, factor, stash_own, stash_theirs]
        plain = list(out_parts[skip:]) + list(in_parts)
        return pl.pallas_call(
            on_host(functools.partial(backward_kernel, parts, n, skip, tick_no, split)),
            grid=(1,),
            in_specs=[smem] * 4
            + [vmem if split else hbm] * len(ups)
            + [hbm] * (len(early) + len(layered) + len(plain)),
            out_specs=all_of(*halves),
            out_shape=kept_halves,
            scratch_shapes=[pltpu.VMEM((rows, width), BF16)]
            + [pltpu.VMEM(x.shape[1:], x.dtype) for x in layered]
            + [pltpu.VMEM(x.shape, x.dtype) for x in plain]
            + [
                pltpu.VMEM((rows, width), F32),
                pltpu.VMEM((rows, width), F32),
                pltpu.VMEM((rows, width), BF16),
                pltpu.VMEM((rows, slab), F32),
                pltpu.SemaphoreType.DMA((2,)),
                pltpu.SemaphoreType.DMA((1 + len(layered) + n + heads * parts,)),
            ],
            compiler_params=params,
            cost_estimate=cost((16 if split else 2) * matmul, 2 * weight_bytes),
            name="backward",
        )(host_flag, core, in_offs, offs, *ups, *in_hbm(early + tuple(layered)), *plain[: n - skip], *in_hbm(in_parts))

    gated, new_theirs, up_near = lax.optimization_barrier((gated, new_theirs, up_near))

    pack_shapes = [struct((rows, width), BF16)]
    pack_shapes += [struct((rows, 2 * slab + depth), BF16)] * (n - 2)
    folded = share * width // rows
    up_0, *packs = pl.pallas_call(
        functools.partial(pack_kernel, n),
        grid=(1,),
        in_specs=[smem] * 1 + all_of(gated, up_own, up_theirs),
        out_specs=all_of(*pack_shapes),
        out_shape=[pltpu.HBM(pack_shapes[0].shape, BF16)] + pack_shapes[1:],
        compiler_params=small,
        name="pack",
    )(offs, gated, up_own, up_theirs)
    soon = n // 2 + 1
    packs, soon_parts = lax.optimization_barrier((packs, out_parts[:soon]))
    early_shapes = [struct((rows, width), BF16), struct((rows, slab), F32)]
    early_part, early_grad = pl.pallas_call(
        early_kernel,
        grid=(1,),
        in_specs=[smem] + [row_of(gated, 0)] + all_of(up_0, *soon_parts),
        out_specs=all_of(*early_shapes),
        out_shape=[early_shapes[0], pltpu.HBM(early_shapes[1].shape, F32)],
        compiler_params=small,
        name="early",
    )(offs, gated, *in_hbm([up_0]), *soon_parts)
    early_part, early_grad, late_parts = lax.optimization_barrier(
        (early_part, early_grad, out_parts[soon:])
    )
    out_parts = soon_parts + late_parts

    ahead_send, ahead_keep = pl.pallas_call(
        functools.partial(out_kernel, soon),
        grid=(1,),
        in_specs=[smem] * 2 + [row_of(gated, 0)] + all_of(early_part, *out_parts[soon:]),
        out_specs=all_of(*halves),
        out_shape=halves,
        scratch_shapes=[pltpu.VMEM((rows, width), BF16)],
        compiler_params=small,
        cost_estimate=cost(matmul // 4, weight_bytes // 4),
        name="out",
    )(core, offs, gated, early_part, *out_parts[soon:])
    ahead_landed = swap_cores(ahead_send)
    first_shapes = [halves[0], struct((rows, 2 * slab + folded), BF16)]
    ahead_0, partner_pack = pl.pallas_call(
        first_kernel,
        grid=(1,),
        in_specs=[smem] + all_of(x_own, x_theirs, ahead_keep, ahead_landed, gated),
        out_specs=all_of(*first_shapes),
        out_shape=first_shapes,
        compiler_params=small,
        name="first",
    )(core, *in_hbm([x_own, x_theirs]), ahead_keep, ahead_landed, gated)
    ahead_in = along_sections(ahead_0, 1)
    packs_near = [to_partner(partner_pack)] + [from_host(packs[m - 1], m) for m in between]
    back_send, back_keep = backward(in_hbm([after(up_0, ahead_0)]), 0, (early_grad,))
    back_send, back_keep, ahead_in, packs_near = lax.optimization_barrier(
        (back_send, back_keep, ahead_in, packs_near)
    )
    back_landed = swap_cores(back_send)
    settled = [halves[0], struct((share, width), BF16)]
    back_0, back_given = pl.pallas_call(
        settle_two_kernel,
        grid=(1,),
        in_specs=[smem] + all_of(up_own, up_theirs, back_keep, back_landed),
        out_specs=all_of(*settled),
        out_shape=settled,
        compiler_params=small,
        name="settle",
    )(core, *in_hbm([up_own, up_theirs, back_keep]), back_landed)
    back_in = along_sections(back_0, -1)

    packs_beyond = [to_beyond(packs[n // 2 + m - 2], m) for m in between]
    ahead_their = swap_cores(ahead_in)
    ahead_send, ahead_keep = pl.pallas_call(
        on_host(functools.partial(forward_kernel, parts, heads)),
        grid=(heads,),
        in_specs=[smem] * 5
        + all_of(ahead_in, ahead_their, new_own, new_theirs)
        + [row_of(keep, keep.shape[0] - 1)]
        + [hbm] * parts
        + all_of(*out_parts),
        out_specs=all_of(*halves),
        out_shape=kept_halves,
        scratch_shapes=[
            pltpu.VMEM((rows, width), BF16),
            pltpu.VMEM((rows, width), BF16),
            pltpu.VMEM((heads, rows, HEAD_DIM), BF16),
            pltpu.VMEM((rows, width), BF16),
            pltpu.SemaphoreType.DMA((heads * parts,)),
        ]
        + weight_scratch,
        compiler_params=params,
        cost_estimate=cost(2 * matmul, 2 * weight_bytes),
        name="forward",
    )(host_flag, core,
        in_offs,
        offs,
        first_flag,
        *in_hbm([ahead_in]),
        ahead_their,
        *in_hbm([new_own, new_theirs, keep]),
        *in_hbm(in_parts),
        *out_parts,
    )
    ahead_send, ahead_keep, back_in, packs_beyond = lax.optimization_barrier(
        (ahead_send, ahead_keep, back_in, packs_beyond)
    )
    ahead_landed = swap_cores(ahead_send)

    cut_shapes = [halves[0]] + [struct((2 * share, depth), BF16)] * (n - 2)
    up_mine, *cuts = pl.pallas_call(
        functools.partial(cut_kernel, n),
        grid=(1,),
        in_specs=[smem] * 3 + all_of(back_in, new_own, new_theirs),
        out_specs=all_of(*cut_shapes),
        out_shape=cut_shapes,
        compiler_params=small,
        name="cut",
    )(core, offs, last_flag, back_in, *in_hbm([new_own, new_theirs]))
    up_their = swap_cores(up_mine)
    landed = [from_host(cuts[m - 1], m) for m in between]
    landed += [to_beyond(cuts[n // 2 + m - 2], m) for m in between]
    message_inputs = [new_own, new_theirs, ahead_in, ahead_keep, ahead_landed, up_mine]
    message_shapes = [halves[0], struct((2 * share, depth + width // 2), BF16)]
    ahead_1, message = pl.pallas_call(
        message_kernel,
        grid=(1,),
        in_specs=[smem] * 3 + all_of(*message_inputs),
        out_specs=all_of(*message_shapes),
        out_shape=message_shapes,
        compiler_params=small,
        name="message",
    )(core, offs, first_flag, *in_hbm(message_inputs[:4]), *message_inputs[4:])
    landed = landed + [to_partner(message)]
    back_send, back_keep = backward([up_mine, up_their], 1)
    back_given = to_partner(back_given)
    back_given, back_send, back_keep, landed = lax.optimization_barrier(
        (back_given, back_send, back_keep, landed)
    )
    landed = landed[-1:] + landed[:-1]
    last_inputs = [up_mine, *in_hbm([back_keep]), swap_cores(back_send)]
    last_shapes = [halves[0], struct((share, width), BF16)]
    back_1, back_other = pl.pallas_call(
        last_kernel,
        grid=(1,),
        in_specs=all_of(*last_inputs),
        out_specs=all_of(*last_shapes),
        out_shape=last_shapes,
        compiler_params=small,
        name="last",
    )(*last_inputs)
    back_last = to_partner(back_other)

    landed_halves = jnp.stack(
        [landed[0][:, :depth]]
        + [jnp.where(is_host, landed[m], landed[n // 2 + m - 1]) for m in between]
    )
    landed_other = swap_cores(landed_halves)
    grad_inputs = [gated, up_0, up_own, up_near, up_mine, up_their, landed_halves, landed_other]
    grad_inputs += packs_near + packs_beyond
    grad_inputs[0] = after(gated, back_1)
    grad_inputs[8:] = in_hbm(grad_inputs[8:])
    grads = pl.pallas_call(
        functools.partial(grads_kernel, n, (ticks * length * n) ** (-0.5)),
        grid=(1,),
        in_specs=[smem] * 3 + all_of(*grad_inputs),
        out_specs=pl.BlockSpec((slab, depth), lambda *_: (0, 0)),
        out_shape=struct((slab, depth), F32),
        scratch_shapes=[pltpu.VMEM((rows, depth), BF16)],
        compiler_params=small,
        cost_estimate=cost(matmul // 4, weight_bytes // 4),
        name="grads",
    )(host_flag, core, offs, *grad_inputs)

    first_pack, last_cut = lax.optimization_barrier((packs_near[0], landed[0], back_1))[:2]
    finish_inputs = [ahead_0, ahead_1, back_0, first_pack, last_cut, back_given]
    finish_shapes = [struct((ticks, share, width), BF16), struct((share, width), BF16)]
    ahead, back_first = pl.pallas_call(
        functools.partial(finish_kernel, slab),
        grid=(1,),
        in_specs=[smem] + all_of(*finish_inputs),
        out_specs=all_of(*finish_shapes),
        out_shape=finish_shapes,
        compiler_params=small,
        name="finish",
    )(host_flag, *finish_inputs)
    back = jnp.stack([back_first, jnp.where(is_host, back_1[0], back_last)])
    return (ahead[None], back[None], grads[None])


def solution(mesh):
    in_specs = (
        P(None, "dp", None),
        P("section", "dp", None),
        P(None, "dp", None),
        P("section", "dp", None),
        P("section", None, "dp", None),
        P("section", "dp", "cores"),
        P("section", "cores", "dp"),
        P("dp", None),
        P("dp", None),
        P("dp", None, None, None),
        P("dp", None, None, None),
    )
    out_specs = (
        P("section", None, ("dp", "cores"), None),
        P("section", None, ("dp", "cores"), None),
        P("section", "cores", "dp"),
    )
    return jax.shard_map(
        per_device, mesh=mesh, in_specs=in_specs, out_specs=out_specs, check_vma=False
    )
```

```python
import functools

import jax
import jax.numpy as jnp
from jax import lax
from jax.experimental import pallas as pl
from jax.experimental.pallas import tpu as pltpu
from jax.sharding import PartitionSpec as P

HEAD_DIM = 128
BLOCK = 24
BLOCKS = 4
EPSILON = 1e-06
SCALING = HEAD_DIM ** (-0.5)
VMEM_BYTES = 34 * 1024 * 1024
SMALL_VMEM_BYTES = 16 * 1024 * 1024

F32 = jnp.float32
BF16 = jnp.bfloat16


def on_host(kernel):
    def guarded(host, *refs):
        pl.when(host[0] != 0)(functools.partial(kernel, *refs))

    return guarded


def dot(a, b):
    return lax.dot_general(a, b, (((1,), (0,)), ((), ())), preferred_element_type=F32)


def dot_nt(a, b):
    return lax.dot_general(a, b, (((1,), (1,)), ((), ())), preferred_element_type=F32)


def dot_tn(a, b):
    return lax.dot_general(a, b, (((0,), (0,)), ((), ())), preferred_element_type=F32)


def row_root(floats):
    return lax.rsqrt(jnp.mean(floats * floats, axis=-1, keepdims=True) + EPSILON)


def sigmoid(x):
    return 1.0 / (1.0 + jnp.exp(-x))


def attend(pre, keep):
    sig = sigmoid(pre)
    active = pre * sig
    gate = active[:, :HEAD_DIM]
    vqk = active[:, HEAD_DIM:].astype(BF16)
    value = vqk[:, :HEAD_DIM]
    query = vqk[:, HEAD_DIM : 2 * HEAD_DIM]
    key = vqk[:, 2 * HEAD_DIM :]
    scores = dot_nt(query, key) * SCALING
    sig_s = sigmoid(scores)
    probs = (scores * sig_s * keep).astype(BF16)
    mixed = dot(probs, value)
    gated = (mixed * row_root(mixed) * gate).astype(BF16)
    return sig, gate, vqk, scores, sig_s, probs, mixed, gated


def project(normed, offs, weights, of_head):
    total = None
    for j, weight in enumerate(weights):
        depth = weight.shape[0]
        columns = pl.ds(pl.multiple_of(offs[j], depth), depth)
        term = dot(normed[:, columns], weight[:, of_head])
        total = term if total is None else total + term
    return total


def columns_of_head(h, size):
    return pl.ds(pl.multiple_of(h * size, size), size)


def weight_copies(sources, targets, sems, h):
    of_head = columns_of_head(h, 4 * HEAD_DIM)
    return [
        pltpu.make_async_copy(
            source.at[:, of_head], target.at[:, of_head], sems.at[h * len(sources) + j]
        )
        for j, (source, target) in enumerate(zip(sources, targets))
    ]


def project_kernel(parts, heads, offs, x_own, x_theirs, stash_own, stash_theirs, keep, *rest):
    sources, rest = rest[:parts], rest[parts:]
    gated_out, saved, rest = rest[0], rest[1:7], rest[7:]
    weights, rest = rest[:parts], rest[parts:]
    held, (normed, sems, out_sems) = rest[:6], rest[6:]
    gate_out, vqk_out, slope_out, mixed_out, probs_out, factor_out = held
    length = x_own.shape[0]
    rows = 2 * length
    head = pl.program_id(0)

    def saved_copies(h):
        copies = []
        for i, (source, target) in enumerate(zip(held, saved)):
            if i < 4:
                at = (slice(None), slice(None), columns_of_head(h, source.shape[2] // heads))
            else:
                at = (slice(None), h)
            copies.append(
                pltpu.make_async_copy(source.at[at], target.at[at], out_sems.at[h * 6 + i])
            )
        return copies

    @pl.when(head == 0)
    def _():
        for h in range(heads):
            for copy in weight_copies(sources, weights, sems, h):
                copy.start()
        blocks = [x_own, x_theirs]
        for t in range(stash_own.shape[0]):
            blocks += [stash_own.at[t], stash_theirs.at[t]]
        for i, block in enumerate(blocks):
            floats = block[...].astype(F32)
            normed[pl.ds(i * length, length), :] = (floats * row_root(floats)).astype(BF16)

    for copy in weight_copies(sources, weights, sems, head):
        copy.wait()
    pre_all = project(normed, offs, weights, columns_of_head(head, 4 * HEAD_DIM))
    for i in range(1 + stash_own.shape[0]):
        pre = pre_all[i * rows : (i + 1) * rows]
        kept = keep[i]
        sig, gate, vqk, scores, sig_s, probs, mixed, gated = attend(pre, kept)
        gated_out[i] = gated
        if i > 0:
            narrow = columns_of_head(head, HEAD_DIM)
            gate_out[i - 1, :, narrow] = gate
            vqk_out[i - 1, :, columns_of_head(head, 3 * HEAD_DIM)] = vqk
            slope_out[i - 1, :, columns_of_head(head, 4 * HEAD_DIM)] = sig * (
                1.0 + pre * (1.0 - sig)
            )
            mixed_out[i - 1, :, narrow] = mixed
            probs_out[i - 1, head] = probs
            factor_out[i - 1, head] = kept * sig_s * (1.0 + scores * (1.0 - sig_s)) * SCALING
    for copy in saved_copies(head):
        copy.start()

    @pl.when(head == heads - 1)
    def _():
        for h in range(heads):
            for copy in saved_copies(h):
                copy.wait()


def split_rows(core, part, send, keep):
    share = send.shape[1]
    cores = part.shape[0] // (2 * share)
    for r in range(2):
        base = r * cores * share
        mine = pl.multiple_of(base + core * share, share)
        other = pl.multiple_of(base + (cores - 1 - core) * share, share)
        send[r] = part[pl.ds(other, share), :]
        keep[r] = part[pl.ds(mine, share), :]


def early_kernel(offs, gated, upstream, *rest):
    weights, (part, grad_gated) = rest[:-2], rest[-2:]
    depth = weights[0].shape[1]
    total = None
    for j, weight in enumerate(weights):
        columns = pl.ds(pl.multiple_of(offs[j], depth), depth)
        part[:, columns] = dot(gated[0], weight[...]).astype(BF16)
        term = dot_nt(upstream[:, columns], weight[...])
        total = term if total is None else total + term
    grad_gated[...] = total


def out_kernel(skip, core, offs, gated, early, *rest):
    weights, (send, keep, part) = rest[:-3], rest[-3:]
    depth = weights[0].shape[1]
    part[...] = early[...]
    for j, weight in enumerate(weights):
        columns = pl.ds(pl.multiple_of(offs[skip + j], depth), depth)
        part[:, columns] = dot(gated[0], weight[...]).astype(BF16)
    split_rows(core[0], part, send, keep)


def assemble(core, fresh, mine, theirs, new_own, new_theirs, whole):
    share = mine.shape[1]
    length = new_own.shape[0]
    cores = length // share
    use_fresh = fresh != 0
    for r, source in enumerate((new_own, new_theirs)):
        for owner, landed in ((core, mine), (cores - 1 - core, theirs)):
            inside = pl.multiple_of(owner * share, share)
            rows = source[pl.ds(inside, share), :]
            at = pl.multiple_of(r * length + owner * share, share)
            whole[pl.ds(at, share), :] = jnp.where(use_fresh, rows, landed[r])


def forward_kernel(parts, heads, core, in_offs, offs, fresh, mine, theirs, new_own, new_theirs, keep, *rest):
    sources, rest = rest[:parts], rest[parts:]
    in_parts, rest = rest[-parts:], rest[:-parts]
    out_parts = rest[:-7]
    send, kept, whole, normed, gated, part, sems = rest[-7:]
    depth = out_parts[0].shape[1]
    head = pl.program_id(0)

    @pl.when(head == 0)
    def _():
        for h in range(heads):
            for copy in weight_copies(sources, in_parts, sems, h):
                copy.start()
        assemble(core[0], fresh[0], mine, theirs, new_own, new_theirs, whole)
        floats = whole[...].astype(F32)
        normed[...] = (floats * row_root(floats)).astype(BF16)

    for copy in weight_copies(sources, in_parts, sems, head):
        copy.wait()
    pre = project(normed, in_offs, in_parts, columns_of_head(head, 4 * HEAD_DIM))
    gated[head] = attend(pre, keep[0])[-1]

    @pl.when(head == heads - 1)
    def _():
        for j in range(len(out_parts)):
            columns = pl.ds(pl.multiple_of(offs[j], depth), depth)
            total = None
            for h in range(heads):
                term = dot(gated[h], out_parts[j][pl.ds(h * HEAD_DIM, HEAD_DIM), :])
                total = term if total is None else total + term
            part[:, columns] = total.astype(BF16)
        split_rows(core[0], part, send, kept)


def backward_kernel(parts, n, skip, tick, split, core, in_offs, offs, *rest):
    n = n - skip
    count = 8 + n + parts
    up_sources, rest = rest[: 1 + split], rest[1 + split :]
    early, rest = (rest[0], rest[1:]) if skip else (None, rest)
    sources, rest = (None,) + rest[:count], rest[count:]
    send, keep = rest[:2]
    held, (grad_normed, part, begun, up_sems, sems) = (
        rest[2 : 3 + count],
        rest[3 + count :],
    )
    ups, gate, vqk, slope, mixed, probs, factor, x_own, x_theirs = held[:9]
    out_parts, in_parts = held[9 : 9 + n], held[9 + n :]
    wide = 4 * HEAD_DIM
    heads = out_parts[0].shape[0] // HEAD_DIM
    copies = []
    for i, (source, target) in enumerate(zip(sources[: 9 + n], held[: 9 + n])):
        if i == 0:
            continue
        if i < 9:
            source = source.at[tick]
        copies.append(pltpu.make_async_copy(source, target, sems.at[i]))
    up_copies = []
    if not split:
        up_copies.append(pltpu.make_async_copy(up_sources[0], ups, up_sems.at[0]))
    if skip:
        up_copies.append(pltpu.make_async_copy(early, begun, up_sems.at[1]))
    copies = [None] + copies
    by_head = []
    for h in range(heads):
        of_head = slice(h * wide, (h + 1) * wide)
        by_head.append(
            [
                pltpu.make_async_copy(
                    sources[9 + n + j].at[:, of_head],
                    in_parts[j].at[:, of_head],
                    sems.at[9 + n + h * parts + j],
                )
                for j in range(parts)
            ]
        )
    first = list(range(9, 9 + n))
    second = [1, 4, 2, 5, 6, 3]
    for copy in up_copies:
        copy.start()
    for i in first + second:
        copies[i].start()
    for of_head in by_head:
        for copy in of_head:
            copy.start()
    for i in (7, 8):
        copies[i].start()
    if split:
        share = up_sources[0].shape[1]
        cores = ups.shape[0] // (2 * share)
        for half, owner in enumerate((core[0], cores - 1 - core[0])):
            for r in range(2):
                at = pl.multiple_of((r * cores + owner) * share, share)
                ups[pl.ds(at, share), :] = up_sources[half][r]
    for copy in up_copies:
        copy.wait()
    depth = out_parts[0].shape[1]
    length = x_own.shape[0]
    grad_gated = begun[...] if skip else None
    for j in range(n):
        columns = pl.ds(pl.multiple_of(offs[skip + j], depth), depth)
        copies[first[j]].wait()
        term = dot_nt(ups[:, columns], out_parts[j][...])
        grad_gated = term if grad_gated is None else grad_gated + term
    grad_gated = grad_gated.astype(BF16).astype(F32)
    for i in second:
        copies[i].wait()

    def through_head(h):
        cut = slice(h * HEAD_DIM, (h + 1) * HEAD_DIM)
        up = grad_gated[:, cut]
        mixed_h = mixed[:, cut]
        root = row_root(mixed_h)
        normed = mixed_h * root
        grad_n = up * gate[:, cut]
        grad_gate = up * normed
        grad_mixed = root * (grad_n - normed * jnp.mean(grad_n * normed, axis=-1, keepdims=True))
        low = grad_mixed.astype(BF16)
        base = 3 * h * HEAD_DIM
        value = vqk[:, base : base + HEAD_DIM]
        query = vqk[:, base + HEAD_DIM : base + 2 * HEAD_DIM]
        key = vqk[:, base + 2 * HEAD_DIM : base + 3 * HEAD_DIM]
        grad_scores = (dot_nt(low, value) * factor[h]).astype(BF16)
        grad_value = dot_tn(probs[h], low)
        grad_query = dot(grad_scores, key)
        grad_key = dot_tn(grad_scores, query)
        grad_active = jnp.concatenate([grad_gate, grad_value, grad_query, grad_key], axis=1)
        return (grad_active * slope[:, h * wide : (h + 1) * wide]).astype(BF16)

    grad_pre = through_head(0)
    for h in range(heads):
        for copy in by_head[h]:
            copy.wait()
        following = through_head(h + 1) if h + 1 < heads else None
        for j in range(parts):
            rows_of = in_parts[j].shape[0]
            columns = pl.ds(pl.multiple_of(in_offs[j], rows_of), rows_of)
            term = dot_nt(grad_pre, in_parts[j][:, h * wide : (h + 1) * wide])
            if h == 0:
                grad_normed[:, columns] = term
            else:
                grad_normed[:, columns] += term
        grad_pre = following
    for r, source in enumerate((x_own, x_theirs)):
        copies[7 + r].wait()
        rows = pl.ds(r * length, length)
        floats = source[...].astype(F32)
        root = row_root(floats)
        scaled = floats * root
        grad_n = grad_normed[rows, :]
        mean = jnp.mean(grad_n * scaled, axis=-1, keepdims=True)
        part[rows, :] = (root * (grad_n - scaled * mean)).astype(BF16)
    split_rows(core[0], part, send, keep)


def pack_kernel(n, offs, gated, up_own, up_theirs, whole, *packs):
    depth = packs[0].shape[1] - 2 * gated.shape[2]
    slab = gated.shape[2]
    length = up_own.shape[0]
    whole[:length, :] = up_own[...]
    whole[length:, :] = up_theirs[...]
    for j in range(2, n):
        pack = packs[j - 2]
        columns = pl.ds(pl.multiple_of(offs[j], depth), depth)
        pack[:, :slab] = gated[1]
        pack[:, slab : 2 * slab] = gated[2]
        pack[:length, 2 * slab :] = up_own[:, columns]
        pack[length:, 2 * slab :] = up_theirs[:, columns]


def fold(rows, target, start):
    share, width = rows.shape
    blocks = target.shape[0] // share
    size = width // blocks
    for k in range(blocks):
        target[k * share : (k + 1) * share, start : start + size] = rows[
            :, k * size : (k + 1) * size
        ]


def unfold(folded, start, target):
    share, width = target.shape
    blocks = folded.shape[0] // share
    size = width // blocks
    for k in range(blocks):
        target[:, k * size : (k + 1) * size] = folded[
            k * share : (k + 1) * share, start : start + size
        ]


def finish_kernel(slab, host, ahead_0, ahead_1, back_0, pack, message, given, ahead, back):
    width = back.shape[1]
    depth = message.shape[1] - width // 2

    @pl.when(host[0] != 0)
    def _():
        ahead[0] = ahead_0[0]
        ahead[1] = ahead_1[0]
        back[...] = back_0[0]

    @pl.when(host[0] == 0)
    def _():
        unfold(pack, 2 * slab, ahead.at[0])
        unfold(message, depth, ahead.at[1])
        back[...] = given[...]


def settle_kernel(core, own, theirs, keep, landed, total):
    share = keep.shape[1]
    here = pl.ds(pl.multiple_of(core[0] * share, share), share)
    for r, source in enumerate((own, theirs)):
        total[r] = (
            source[here, :].astype(F32) + keep[r].astype(F32) + landed[r].astype(F32)
        ).astype(BF16)


def first_kernel(core, own, theirs, keep, landed, gated, total, pack):
    slab = gated.shape[2]
    settle_kernel(core, own, theirs, keep, landed, total)
    pack[:, :slab] = gated[1]
    pack[:, slab : 2 * slab] = gated[2]
    fold(total[1], pack, 2 * slab)


def message_kernel(
    core, offs, fresh, new_own, new_theirs, passed, keep, landed, up, ahead, message
):
    share = keep.shape[1]
    depth = message.shape[1] - up.shape[2] // 2
    here = pl.ds(pl.multiple_of(core[0] * share, share), share)
    columns = pl.ds(pl.multiple_of(offs[1], depth), depth)
    for r, source in enumerate((new_own, new_theirs)):
        residual = jnp.where(fresh[0] != 0, source[here, :], passed[r])
        ahead[r] = (
            residual.astype(F32) + keep[r].astype(F32) + landed[r].astype(F32)
        ).astype(BF16)
        message[r * share : (r + 1) * share, :depth] = up[r, :, columns]
    fold(ahead[1], message, depth)


def last_kernel(up, keep, landed, back, other):
    for r in range(2):
        back[r] = (
            up[r].astype(F32) + keep[r].astype(F32) + landed[r].astype(F32)
        ).astype(BF16)
    other[...] = back[1]


def cut_kernel(n, core, offs, fresh, landed, new_own, new_theirs, mine, *pieces):
    share = landed.shape[1]
    depth = pieces[-1].shape[1]
    here = pl.ds(pl.multiple_of(core[0] * share, share), share)
    for r, source in enumerate((new_own, new_theirs)):
        mine[r] = jnp.where(fresh[0] != 0, source[here, :], landed[r])
        for j in range(2, n):
            columns = pl.ds(pl.multiple_of(offs[j], depth), depth)
            pieces[j - 2][r * share : (r + 1) * share, :] = mine[r, :, columns]


def grads_kernel(
    n, scaling, host, core, offs, gated, up_0, up_own, up_near, mine, theirs, halves, other, *rest
):
    packs = rest[: n - 1]
    out, whole = rest[n - 1 :]
    slab = gated.shape[2]
    depth = out.shape[1]
    share = mine.shape[1]
    cores = whole.shape[0] // (2 * share)
    at_host = host[0] != 0
    columns = pl.ds(pl.multiple_of(offs[0], depth), depth)

    def product(first, second, third, upstream):
        for half, owner in enumerate((core[0], cores - 1 - core[0])):
            for r in range(2):
                at = pl.multiple_of((r * cores + owner) * share, share)
                whole[pl.ds(at, share), :] = upstream(half, r)
        return dot_tn(first, third) + dot_tn(second, whole[...])

    up_pair = jnp.concatenate([up_near[...], up_own[:, columns]], axis=0)
    total = product(
        jnp.where(at_host, gated[1], packs[0][:, :slab]),
        jnp.where(at_host, gated[2], packs[0][:, slab : 2 * slab]),
        jnp.where(at_host, up_0[:, columns], up_pair),
        lambda half, r: jnp.where(
            at_host,
            (mine, theirs)[half][r, :, columns],
            (halves, other)[half][0, r * share : (r + 1) * share, :],
        ),
    )
    for m in range(1, n // 2):
        near, beyond = m, n // 2 + m - 1
        pack = jnp.where(at_host, packs[near][...], packs[beyond][...])
        total = total + product(
            pack[:, :slab],
            pack[:, slab : 2 * slab],
            pack[:, 2 * slab :],
            lambda half, r: (halves, other)[half][m, r * share : (r + 1) * share, :],
        )
    out[...] = total * scaling


def in_hbm(arrays):
    return [pltpu.with_memory_space_constraint(x, pltpu.HBM) for x in arrays]


def after(value, *earlier):
    return lax.optimization_barrier((value,) + earlier)[0]


def block_keep(live_blocks, block_marks):
    length = BLOCKS * BLOCK
    places = jnp.arange(length, dtype=jnp.int32)
    owners = places // BLOCK
    marked = jnp.repeat(jnp.repeat(block_marks, BLOCK, axis=-2), BLOCK, axis=-1) == 1
    allowed = (owners[:, None] == owners[None, :]) | marked
    causal = places[:, None] >= places[None, :]
    tokens = live_blocks[..., None, None] * BLOCK
    keeping = causal & allowed & (places[:, None] < tokens) & (places[None, :] < tokens)
    return jnp.where(keeping, 1.0 / jnp.maximum(tokens, 1).astype(F32), 0.0)


def per_device(
    arrivals,
    in_flight,
    cotangent,
    grad_flight,
    stashed,
    in_weight,
    out_weight,
    forward_blocks,
    backward_blocks,
    forward_marks,
    backward_marks,
):
    section_no = lax.axis_index("section")
    sections = lax.axis_size("section")
    core_no = lax.axis_index("cores")
    cores = lax.axis_size("cores")
    dp_no = lax.axis_index("dp")
    n = lax.axis_size("dp")
    ticks = arrivals.shape[0]
    length = arrivals.shape[1]
    width = arrivals.shape[2]
    rows = 2 * length
    share = length // cores
    in_shard = in_weight[0]
    out_shard = out_weight[0]
    depth = in_shard.shape[0]
    slab = out_shard.shape[0]
    heads = slab // HEAD_DIM
    wide = 4 * HEAD_DIM

    hosts = [2 * k + 1 if 4 * k < n - 2 else 2 * k for k in range(n // 2)]
    host_table = jnp.array(hosts, jnp.int32)
    is_host = dp_no == host_table[dp_no // 2]

    def from_partner(x):
        return lax.ppermute(x, "dp", [(h ^ 1, h) for h in hosts])

    def to_partner(x):
        return lax.ppermute(x, "dp", [(h, h ^ 1) for h in hosts])

    def from_host(x, m):
        return lax.ppermute(x, "dp", [(hosts[k ^ m], hosts[k]) for k in range(n // 2)])

    def to_beyond(x, m):
        return lax.ppermute(
            x, "dp", [(hosts[k ^ m], hosts[k] ^ 1) for k in range(n // 2)]
        )

    def swap_cores(x):
        return lax.ppermute(x, "cores", [(c, cores - 1 - c) for c in range(cores)])

    def along_sections(x, by):
        pairs = [
            (i * n + h, (i + by) * n + h)
            for i in range(sections)
            if 0 <= i + by < sections
            for h in hosts
        ]
        return lax.ppermute(x, ("section", "dp"), pairs)

    first_section = section_no == 0
    last_section = section_no == sections - 1
    between = range(1, n // 2)

    pieces = max(1, min(2, depth // 256))
    piece = depth // pieces
    in_far = [from_host(in_shard, m) for m in between]
    in_near = [
        from_partner(in_shard[i * piece : (i + 1) * piece]) for i in range(pieces)
    ]
    out_near = from_partner(out_shard)
    in_pass = [from_host(in_near[0], m) for m in between]
    in_far, in_near, rows_in, tables_in = lax.optimization_barrier(
        (
            in_far,
            in_near,
            (arrivals, in_flight, cotangent, grad_flight, stashed),
            (forward_blocks, forward_marks, backward_blocks, backward_marks),
        )
    )
    in_pass += [from_host(in_near[i], m) for i in range(1, pieces) for m in between]
    in_parts = [in_shard] + in_far + in_near + in_pass
    arrivals, in_flight, cotangent, grad_flight, stashed = rows_in
    tables = jnp.concatenate(
        [
            jnp.concatenate([b[..., None], m.reshape(m.shape[:2] + (-1,))], axis=-1)
            for b, m in (tables_in[:2], tables_in[2:])
        ],
        axis=0,
    )
    near_tables = from_partner(tables)
    stash_own = stashed[0]
    stash_theirs = from_partner(stash_own)
    x_own = jnp.where(first_section, arrivals[0], in_flight[0])
    x_theirs = from_partner(x_own)
    up_own = jnp.where(last_section, cotangent[0], grad_flight[0])
    new_own = jnp.where(first_section, arrivals[1], cotangent[1])
    out_own, out_near, near_tables = lax.optimization_barrier((out_shard, out_near, near_tables))
    out_far = [from_host(out_own, m) for m in between]
    out_parts = [out_shard, out_near] + out_far + [from_host(out_near, m) for m in between]
    up_late, new_late, stash_theirs = lax.optimization_barrier((up_own, new_own, stash_theirs))
    up_theirs = from_partner(up_late)
    up_near = to_partner(
        lax.dynamic_slice_in_dim(up_late, (dp_no ^ 1) * depth, depth, axis=1)
    )
    new_theirs = from_partner(new_late)
    far_hosts = [host_table[(dp_no // 2) ^ m] for m in between]
    owners = [dp_no, dp_no ^ 1] + far_hosts + [h ^ 1 for h in far_hosts]
    offs = jnp.stack(owners).astype(jnp.int32) * depth
    in_offs = [dp_no * depth] + [h * depth for h in far_hosts]
    in_offs += [(dp_no ^ 1) * depth + i * piece for i in range(pieces)]
    in_offs += [(h ^ 1) * depth + i * piece for i in range(pieces) for h in far_hosts]
    in_offs = jnp.stack(in_offs).astype(jnp.int32)
    parts = len(in_parts)
    core = jnp.reshape(core_no, (1,)).astype(jnp.int32)
    first_flag = jnp.reshape(first_section, (1,)).astype(jnp.int32)
    host_flag = jnp.reshape(is_host, (1,)).astype(jnp.int32)
    last_flag = jnp.reshape(last_section, (1,)).astype(jnp.int32)

    both_tables = jnp.stack([tables, near_tables], axis=1)
    ahead_at = sections - 1 - section_no
    chosen = jnp.stack(
        [
            lax.dynamic_index_in_dim(both_tables[way], at, axis=1, keepdims=False)
            for way, at in (
                (0, ahead_at),
                (1, section_no),
                (1, section_no + 1),
                (0, ahead_at + 1),
            )
        ]
    )
    kept = block_keep(chosen[..., 0], chosen[..., 1:].reshape(-1, 2, BLOCKS, BLOCKS))
    blank = jnp.zeros_like(kept[:, 0])
    keep = jnp.concatenate(
        [
            jnp.concatenate([kept[:, 0], blank], axis=2),
            jnp.concatenate([blank, kept[:, 1]], axis=2),
        ],
        axis=1,
    )

    smem = pl.BlockSpec(memory_space=pltpu.SMEM)
    hbm = pl.BlockSpec(memory_space=pltpu.HBM)
    vmem = pl.BlockSpec(memory_space=pltpu.VMEM)

    def all_of(*arrays):
        return [pl.BlockSpec(x.shape, lambda *_, d=x.ndim: (0,) * d) for x in arrays]

    def row_of(x, i):
        return pl.BlockSpec((1,) + x.shape[1:], lambda *_: (i,) + (0,) * (x.ndim - 1))

    params = pltpu.CompilerParams(vmem_limit_bytes=VMEM_BYTES)
    small = pltpu.CompilerParams(vmem_limit_bytes=SMALL_VMEM_BYTES)

    def cost(multiply_adds, bytes_accessed):
        return pl.CostEstimate(
            flops=2 * multiply_adds, bytes_accessed=bytes_accessed, transcendentals=0
        )

    def struct(shape, dtype):
        return jax.ShapeDtypeStruct(shape, dtype)

    halves = [struct((2, share, width), BF16)] * 2
    kept_halves = [halves[0], pltpu.HBM(halves[0].shape, BF16)]
    matmul = rows * width * 4 * slab
    weight_bytes = 2 * width * 5 * slab

    by_head = lambda lead, last: pl.BlockSpec(lead + (last,), lambda h: (0,) * len(lead) + (h,))
    saved_shapes = [
        struct((2, rows, slab), F32),
        struct((2, rows, 3 * slab), BF16),
        struct((2, rows, 4 * slab), F32),
        struct((2, rows, slab), F32),
        struct((2, heads, rows, rows), BF16),
        struct((2, heads, rows, rows), F32),
    ]
    weight_scratch = [pltpu.VMEM(x.shape, BF16) for x in in_parts]
    gated, gate, vqk, slope, mixed, probs, factor = pl.pallas_call(
        on_host(functools.partial(project_kernel, parts, heads)),
        grid=(heads,),
        in_specs=[smem] * 2
        + all_of(x_own, x_theirs, stash_own, stash_theirs, keep)
        + [hbm] * parts,
        out_specs=[by_head((3, rows), HEAD_DIM)] + [hbm] * 6,
        out_shape=[struct((3, rows, slab), BF16)]
        + [pltpu.HBM(x.shape, x.dtype) for x in saved_shapes],
        scratch_shapes=weight_scratch
        + [pltpu.VMEM(x.shape, x.dtype) for x in saved_shapes]
        + [
            pltpu.VMEM((3 * rows, width), BF16),
            pltpu.SemaphoreType.DMA((heads * parts,)),
            pltpu.SemaphoreType.DMA((heads * 6,)),
        ],
        compiler_params=params,
        cost_estimate=cost(3 * matmul, 2 * weight_bytes),
        name="project",
    )(host_flag, in_offs, x_own, x_theirs, stash_own, stash_theirs, keep, *in_hbm(in_parts))

    def backward(ups, tick_no, early=()):
        split = len(ups) - 1
        skip = soon if early else 0
        layered = [gate, vqk, slope, mixed, probs, factor, stash_own, stash_theirs]
        plain = list(out_parts[skip:]) + list(in_parts)
        return pl.pallas_call(
            on_host(functools.partial(backward_kernel, parts, n, skip, tick_no, split)),
            grid=(1,),
            in_specs=[smem] * 4
            + [vmem if split else hbm] * len(ups)
            + [hbm] * (len(early) + len(layered) + len(plain)),
            out_specs=all_of(*halves),
            out_shape=kept_halves,
            scratch_shapes=[pltpu.VMEM((rows, width), BF16)]
            + [pltpu.VMEM(x.shape[1:], x.dtype) for x in layered]
            + [pltpu.VMEM(x.shape, x.dtype) for x in plain]
            + [
                pltpu.VMEM((rows, width), F32),
                pltpu.VMEM((rows, width), BF16),
                pltpu.VMEM((rows, slab), F32),
                pltpu.SemaphoreType.DMA((2,)),
                pltpu.SemaphoreType.DMA((1 + len(layered) + n + heads * parts,)),
            ],
            compiler_params=params,
            cost_estimate=cost((16 if split else 2) * matmul, 2 * weight_bytes),
            name="backward",
        )(host_flag, core, in_offs, offs, *ups, *in_hbm(early + tuple(layered)), *plain[: n - skip], *in_hbm(in_parts))

    gated, new_theirs, up_near = lax.optimization_barrier((gated, new_theirs, up_near))

    pack_shapes = [struct((rows, width), BF16)]
    pack_shapes += [struct((rows, 2 * slab + depth), BF16)] * (n - 2)
    folded = share * width // rows
    up_0, *packs = pl.pallas_call(
        functools.partial(pack_kernel, n),
        grid=(1,),
        in_specs=[smem] * 1 + all_of(gated, up_own, up_theirs),
        out_specs=all_of(*pack_shapes),
        out_shape=[pltpu.HBM(pack_shapes[0].shape, BF16)] + pack_shapes[1:],
        compiler_params=small,
        name="pack",
    )(offs, gated, up_own, up_theirs)
    soon = n // 2 + 1
    packs, soon_parts = lax.optimization_barrier((packs, out_parts[:soon]))
    early_shapes = [struct((rows, width), BF16), struct((rows, slab), F32)]
    early_part, early_grad = pl.pallas_call(
        early_kernel,
        grid=(1,),
        in_specs=[smem] + [row_of(gated, 0)] + all_of(up_0, *soon_parts),
        out_specs=all_of(*early_shapes),
        out_shape=[early_shapes[0], pltpu.HBM(early_shapes[1].shape, F32)],
        compiler_params=small,
        name="early",
    )(offs, gated, *in_hbm([up_0]), *soon_parts)
    early_part, early_grad, late_parts = lax.optimization_barrier(
        (early_part, early_grad, out_parts[soon:])
    )
    out_parts = soon_parts + late_parts

    ahead_send, ahead_keep = pl.pallas_call(
        functools.partial(out_kernel, soon),
        grid=(1,),
        in_specs=[smem] * 2 + [row_of(gated, 0)] + all_of(early_part, *out_parts[soon:]),
        out_specs=all_of(*halves),
        out_shape=halves,
        scratch_shapes=[pltpu.VMEM((rows, width), BF16)],
        compiler_params=small,
        cost_estimate=cost(matmul // 4, weight_bytes // 4),
        name="out",
    )(core, offs, gated, early_part, *out_parts[soon:])
    ahead_landed = swap_cores(ahead_send)
    first_shapes = [halves[0], struct((rows, 2 * slab + folded), BF16)]
    ahead_0, partner_pack = pl.pallas_call(
        first_kernel,
        grid=(1,),
        in_specs=[smem] + all_of(x_own, x_theirs, ahead_keep, ahead_landed, gated),
        out_specs=all_of(*first_shapes),
        out_shape=first_shapes,
        compiler_params=small,
        name="first",
    )(core, *in_hbm([x_own, x_theirs]), ahead_keep, ahead_landed, gated)
    ahead_in = along_sections(ahead_0, 1)
    packs_near = [to_partner(partner_pack)] + [from_host(packs[m - 1], m) for m in between]
    back_send, back_keep = backward(in_hbm([after(up_0, ahead_0)]), 0, (early_grad,))
    back_send, back_keep, ahead_in, packs_near = lax.optimization_barrier(
        (back_send, back_keep, ahead_in, packs_near)
    )
    back_landed = swap_cores(back_send)
    back_0 = pl.pallas_call(
        settle_kernel,
        grid=(1,),
        in_specs=[smem] + all_of(up_own, up_theirs, back_keep, back_landed),
        out_specs=all_of(halves[0])[0],
        out_shape=halves[0],
        compiler_params=small,
        name="settle",
    )(core, *in_hbm([up_own, up_theirs, back_keep]), back_landed)
    back_in = along_sections(back_0, -1)

    packs_beyond = [to_beyond(packs[n // 2 + m - 2], m) for m in between]
    ahead_their = swap_cores(ahead_in)
    ahead_send, ahead_keep = pl.pallas_call(
        on_host(functools.partial(forward_kernel, parts, heads)),
        grid=(heads,),
        in_specs=[smem] * 5
        + all_of(ahead_in, ahead_their, new_own, new_theirs)
        + [row_of(keep, keep.shape[0] - 1)]
        + [hbm] * parts
        + all_of(*out_parts),
        out_specs=all_of(*halves),
        out_shape=kept_halves,
        scratch_shapes=[
            pltpu.VMEM((rows, width), BF16),
            pltpu.VMEM((rows, width), BF16),
            pltpu.VMEM((heads, rows, HEAD_DIM), BF16),
            pltpu.VMEM((rows, width), BF16),
            pltpu.SemaphoreType.DMA((heads * parts,)),
        ]
        + weight_scratch,
        compiler_params=params,
        cost_estimate=cost(2 * matmul, 2 * weight_bytes),
        name="forward",
    )(host_flag, core,
        in_offs,
        offs,
        first_flag,
        *in_hbm([ahead_in]),
        ahead_their,
        *in_hbm([new_own, new_theirs, keep]),
        *in_hbm(in_parts),
        *out_parts,
    )
    ahead_send, ahead_keep, back_in, packs_beyond = lax.optimization_barrier(
        (ahead_send, ahead_keep, back_in, packs_beyond)
    )
    ahead_landed = swap_cores(ahead_send)

    cut_shapes = [halves[0]] + [struct((2 * share, depth), BF16)] * (n - 2)
    up_mine, *cuts = pl.pallas_call(
        functools.partial(cut_kernel, n),
        grid=(1,),
        in_specs=[smem] * 3 + all_of(back_in, new_own, new_theirs),
        out_specs=all_of(*cut_shapes),
        out_shape=cut_shapes,
        compiler_params=small,
        name="cut",
    )(core, offs, last_flag, back_in, *in_hbm([new_own, new_theirs]))
    up_their = swap_cores(up_mine)
    landed = [from_host(cuts[m - 1], m) for m in between]
    landed += [to_beyond(cuts[n // 2 + m - 2], m) for m in between]
    message_inputs = [new_own, new_theirs, ahead_in, ahead_keep, ahead_landed, up_mine]
    message_shapes = [halves[0], struct((2 * share, depth + width // 2), BF16)]
    ahead_1, message = pl.pallas_call(
        message_kernel,
        grid=(1,),
        in_specs=[smem] * 3 + all_of(*message_inputs),
        out_specs=all_of(*message_shapes),
        out_shape=message_shapes,
        compiler_params=small,
        name="message",
    )(core, offs, first_flag, *in_hbm(message_inputs[:4]), *message_inputs[4:])
    landed = landed + [to_partner(message)]
    back_send, back_keep = backward([up_mine, up_their], 1)
    back_given = to_partner(back_0[1])
    back_given, back_send, back_keep, landed = lax.optimization_barrier(
        (back_given, back_send, back_keep, landed)
    )
    landed = landed[-1:] + landed[:-1]
    last_inputs = [up_mine, *in_hbm([back_keep]), swap_cores(back_send)]
    last_shapes = [halves[0], struct((share, width), BF16)]
    back_1, back_other = pl.pallas_call(
        last_kernel,
        grid=(1,),
        in_specs=all_of(*last_inputs),
        out_specs=all_of(*last_shapes),
        out_shape=last_shapes,
        compiler_params=small,
        name="last",
    )(*last_inputs)
    back_last = to_partner(back_other)

    landed_halves = jnp.stack(
        [landed[0][:, :depth]]
        + [jnp.where(is_host, landed[m], landed[n // 2 + m - 1]) for m in between]
    )
    landed_other = swap_cores(landed_halves)
    grad_inputs = [gated, up_0, up_own, up_near, up_mine, up_their, landed_halves, landed_other]
    grad_inputs += packs_near + packs_beyond
    grad_inputs[0] = after(gated, back_1)
    grad_inputs[8:] = in_hbm(grad_inputs[8:])
    grads = pl.pallas_call(
        functools.partial(grads_kernel, n, (ticks * length * n) ** (-0.5)),
        grid=(1,),
        in_specs=[smem] * 3 + all_of(*grad_inputs),
        out_specs=pl.BlockSpec((slab, depth), lambda *_: (0, 0)),
        out_shape=struct((slab, depth), F32),
        scratch_shapes=[pltpu.VMEM((rows, depth), BF16)],
        compiler_params=small,
        cost_estimate=cost(matmul // 4, weight_bytes // 4),
        name="grads",
    )(host_flag, core, offs, *grad_inputs)

    first_pack, last_cut = lax.optimization_barrier((packs_near[0], landed[0], back_1))[:2]
    finish_inputs = [ahead_0, ahead_1, back_0, first_pack, last_cut, back_given]
    finish_shapes = [struct((ticks, share, width), BF16), struct((share, width), BF16)]
    ahead, back_first = pl.pallas_call(
        functools.partial(finish_kernel, slab),
        grid=(1,),
        in_specs=[smem] + all_of(*finish_inputs),
        out_specs=all_of(*finish_shapes),
        out_shape=finish_shapes,
        compiler_params=small,
        name="finish",
    )(host_flag, *finish_inputs)
    back = jnp.stack([back_first, jnp.where(is_host, back_1[0], back_last)])
    return (ahead[None], back[None], grads[None])


def solution(mesh):
    in_specs = (
        P(None, "dp", None),
        P("section", "dp", None),
        P(None, "dp", None),
        P("section", "dp", None),
        P("section", None, "dp", None),
        P("section", "dp", "cores"),
        P("section", "cores", "dp"),
        P("dp", None),
        P("dp", None),
        P("dp", None, None, None),
        P("dp", None, None, None),
    )
    out_specs = (
        P("section", None, ("dp", "cores"), None),
        P("section", None, ("dp", "cores"), None),
        P("section", "cores", "dp"),
    )
    return jax.shard_map(
        per_device, mesh=mesh, in_specs=in_specs, out_specs=out_specs, check_vma=False
    )
```

```python
import functools

import jax
import jax.numpy as jnp
from jax import lax
from jax.experimental import pallas as pl
from jax.experimental.pallas import tpu as pltpu
from jax.sharding import PartitionSpec as P

HEAD_DIM = 128
BLOCK = 24
BLOCKS = 4
EPSILON = 1e-06
SCALING = HEAD_DIM ** (-0.5)
VMEM_BYTES = 34 * 1024 * 1024
SMALL_VMEM_BYTES = 16 * 1024 * 1024

F32 = jnp.float32
BF16 = jnp.bfloat16


def on_host(kernel):
    def guarded(host, *refs):
        pl.when(host[0] != 0)(functools.partial(kernel, *refs))

    return guarded


def dot(a, b):
    return lax.dot_general(a, b, (((1,), (0,)), ((), ())), preferred_element_type=F32)


def dot_nt(a, b):
    return lax.dot_general(a, b, (((1,), (1,)), ((), ())), preferred_element_type=F32)


def dot_tn(a, b):
    return lax.dot_general(a, b, (((0,), (0,)), ((), ())), preferred_element_type=F32)


def row_root(floats):
    return lax.rsqrt(jnp.mean(floats * floats, axis=-1, keepdims=True) + EPSILON)


def sigmoid(x):
    return 1.0 / (1.0 + jnp.exp(-x))


def attend(pre, keep):
    sig = sigmoid(pre)
    active = pre * sig
    gate = active[:, :HEAD_DIM]
    vqk = active[:, HEAD_DIM:].astype(BF16)
    value = vqk[:, :HEAD_DIM]
    query = vqk[:, HEAD_DIM : 2 * HEAD_DIM]
    key = vqk[:, 2 * HEAD_DIM :]
    scores = dot_nt(query, key) * SCALING
    sig_s = sigmoid(scores)
    probs = (scores * sig_s * keep).astype(BF16)
    mixed = dot(probs, value)
    gated = (mixed * row_root(mixed) * gate).astype(BF16)
    return sig, gate, vqk, scores, sig_s, probs, mixed, gated


def project(normed, offs, weights, of_head):
    total = None
    for j, weight in enumerate(weights):
        depth = weight.shape[0]
        columns = pl.ds(pl.multiple_of(offs[j], depth), depth)
        term = dot(normed[:, columns], weight[:, of_head])
        total = term if total is None else total + term
    return total


def columns_of_head(h, size):
    return pl.ds(pl.multiple_of(h * size, size), size)


def weight_copies(sources, targets, sems, h):
    of_head = columns_of_head(h, 4 * HEAD_DIM)
    return [
        pltpu.make_async_copy(
            source.at[:, of_head], target.at[:, of_head], sems.at[h * len(sources) + j]
        )
        for j, (source, target) in enumerate(zip(sources, targets))
    ]


def project_kernel(parts, heads, offs, x_own, x_theirs, stash_own, stash_theirs, keep, *rest):
    sources, rest = rest[:parts], rest[parts:]
    gated_out, saved, rest = rest[0], rest[1:7], rest[7:]
    weights, rest = rest[:parts], rest[parts:]
    held, (normed, sems, out_sems) = rest[:6], rest[6:]
    gate_out, vqk_out, slope_out, mixed_out, probs_out, factor_out = held
    length = x_own.shape[0]
    rows = 2 * length
    head = pl.program_id(0)

    def saved_copies(h):
        copies = []
        for i, (source, target) in enumerate(zip(held, saved)):
            if i < 4:
                at = (slice(None), slice(None), columns_of_head(h, source.shape[2] // heads))
            else:
                at = (slice(None), h)
            copies.append(
                pltpu.make_async_copy(source.at[at], target.at[at], out_sems.at[h * 6 + i])
            )
        return copies

    @pl.when(head == 0)
    def _():
        for h in range(heads):
            for copy in weight_copies(sources, weights, sems, h):
                copy.start()
        blocks = [x_own, x_theirs]
        for t in range(stash_own.shape[0]):
            blocks += [stash_own.at[t], stash_theirs.at[t]]
        for i, block in enumerate(blocks):
            floats = block[...].astype(F32)
            normed[pl.ds(i * length, length), :] = (floats * row_root(floats)).astype(BF16)

    for copy in weight_copies(sources, weights, sems, head):
        copy.wait()
    pre_all = project(normed, offs, weights, columns_of_head(head, 4 * HEAD_DIM))
    for i in range(1 + stash_own.shape[0]):
        pre = pre_all[i * rows : (i + 1) * rows]
        kept = keep[i]
        sig, gate, vqk, scores, sig_s, probs, mixed, gated = attend(pre, kept)
        gated_out[i] = gated
        if i > 0:
            narrow = columns_of_head(head, HEAD_DIM)
            gate_out[i - 1, :, narrow] = gate
            vqk_out[i - 1, :, columns_of_head(head, 3 * HEAD_DIM)] = vqk
            slope_out[i - 1, :, columns_of_head(head, 4 * HEAD_DIM)] = sig * (
                1.0 + pre * (1.0 - sig)
            )
            mixed_out[i - 1, :, narrow] = mixed
            probs_out[i - 1, head] = probs
            factor_out[i - 1, head] = kept * sig_s * (1.0 + scores * (1.0 - sig_s)) * SCALING
    for copy in saved_copies(head):
        copy.start()

    @pl.when(head == heads - 1)
    def _():
        for h in range(heads):
            for copy in saved_copies(h):
                copy.wait()


def split_rows(core, part, send, keep):
    share = send.shape[1]
    cores = part.shape[0] // (2 * share)
    for r in range(2):
        base = r * cores * share
        mine = pl.multiple_of(base + core * share, share)
        other = pl.multiple_of(base + (cores - 1 - core) * share, share)
        send[r] = part[pl.ds(other, share), :]
        keep[r] = part[pl.ds(mine, share), :]


def early_kernel(offs, gated, upstream, *rest):
    weights, (part, grad_gated) = rest[:-2], rest[-2:]
    depth = weights[0].shape[1]
    total = None
    for j, weight in enumerate(weights):
        columns = pl.ds(pl.multiple_of(offs[j], depth), depth)
        part[:, columns] = dot(gated[0], weight[...]).astype(BF16)
        term = dot_nt(upstream[:, columns], weight[...])
        total = term if total is None else total + term
    grad_gated[...] = total


def out_kernel(skip, core, offs, gated, early, *rest):
    weights, (send, keep, part) = rest[:-3], rest[-3:]
    depth = weights[0].shape[1]
    part[...] = early[...]
    for j, weight in enumerate(weights):
        columns = pl.ds(pl.multiple_of(offs[skip + j], depth), depth)
        part[:, columns] = dot(gated[0], weight[...]).astype(BF16)
    split_rows(core[0], part, send, keep)


def assemble(core, fresh, mine, theirs, new_own, new_theirs, whole):
    share = mine.shape[1]
    length = new_own.shape[0]
    cores = length // share
    use_fresh = fresh != 0
    for r, source in enumerate((new_own, new_theirs)):
        for owner, landed in ((core, mine), (cores - 1 - core, theirs)):
            inside = pl.multiple_of(owner * share, share)
            rows = source[pl.ds(inside, share), :]
            at = pl.multiple_of(r * length + owner * share, share)
            whole[pl.ds(at, share), :] = jnp.where(use_fresh, rows, landed[r])


def forward_kernel(parts, heads, core, in_offs, offs, fresh, mine, theirs, new_own, new_theirs, keep, *rest):
    sources, rest = rest[:parts], rest[parts:]
    in_parts, rest = rest[-parts:], rest[:-parts]
    out_parts = rest[:-7]
    send, kept, whole, normed, gated, part, sems = rest[-7:]
    depth = out_parts[0].shape[1]
    head = pl.program_id(0)

    @pl.when(head == 0)
    def _():
        for h in range(heads):
            for copy in weight_copies(sources, in_parts, sems, h):
                copy.start()
        assemble(core[0], fresh[0], mine, theirs, new_own, new_theirs, whole)
        floats = whole[...].astype(F32)
        normed[...] = (floats * row_root(floats)).astype(BF16)

    for copy in weight_copies(sources, in_parts, sems, head):
        copy.wait()
    pre = project(normed, in_offs, in_parts, columns_of_head(head, 4 * HEAD_DIM))
    gated[head] = attend(pre, keep[0])[-1]

    @pl.when(head == heads - 1)
    def _():
        for j in range(len(out_parts)):
            columns = pl.ds(pl.multiple_of(offs[j], depth), depth)
            total = None
            for h in range(heads):
                term = dot(gated[h], out_parts[j][pl.ds(h * HEAD_DIM, HEAD_DIM), :])
                total = term if total is None else total + term
            part[:, columns] = total.astype(BF16)
        split_rows(core[0], part, send, kept)


def backward_kernel(parts, n, skip, tick, split, core, in_offs, offs, *rest):
    n = n - skip
    count = 8 + n + parts
    up_sources, rest = rest[: 1 + split], rest[1 + split :]
    early, rest = (rest[0], rest[1:]) if skip else (None, rest)
    sources, rest = (None,) + rest[:count], rest[count:]
    send, keep = rest[:2]
    held, (grad_normed, scaled, part, begun, up_sems, sems) = (
        rest[2 : 3 + count],
        rest[3 + count :],
    )
    ups, gate, vqk, slope, mixed, probs, factor, x_own, x_theirs = held[:9]
    out_parts, in_parts = held[9 : 9 + n], held[9 + n :]
    wide = 4 * HEAD_DIM
    heads = out_parts[0].shape[0] // HEAD_DIM
    copies = []
    for i, (source, target) in enumerate(zip(sources[: 9 + n], held[: 9 + n])):
        if i == 0:
            continue
        if i < 9:
            source = source.at[tick]
        copies.append(pltpu.make_async_copy(source, target, sems.at[i]))
    up_copies = []
    if not split:
        up_copies.append(pltpu.make_async_copy(up_sources[0], ups, up_sems.at[0]))
    if skip:
        up_copies.append(pltpu.make_async_copy(early, begun, up_sems.at[1]))
    copies = [None] + copies
    by_head = []
    for h in range(heads):
        of_head = slice(h * wide, (h + 1) * wide)
        by_head.append(
            [
                pltpu.make_async_copy(
                    sources[9 + n + j].at[:, of_head],
                    in_parts[j].at[:, of_head],
                    sems.at[9 + n + h * parts + j],
                )
                for j in range(parts)
            ]
        )
    first = list(range(9, 9 + n))
    second = [1, 4, 2, 5, 6, 3]
    for i in (7, 8):
        copies[i].start()
    for copy in up_copies:
        copy.start()
    for i in first + second:
        copies[i].start()
    for of_head in by_head:
        for copy in of_head:
            copy.start()
    if split:
        share = up_sources[0].shape[1]
        cores = ups.shape[0] // (2 * share)
        for half, owner in enumerate((core[0], cores - 1 - core[0])):
            for r in range(2):
                at = pl.multiple_of((r * cores + owner) * share, share)
                ups[pl.ds(at, share), :] = up_sources[half][r]
    roots = []
    for i, source in ((7, x_own), (8, x_theirs)):
        copies[i].wait()
        floats = source[...].astype(F32)
        roots.append(row_root(floats))
        scaled[pl.ds((i - 7) * source.shape[0], source.shape[0]), :] = floats * roots[-1]
    for copy in up_copies:
        copy.wait()
    depth = out_parts[0].shape[1]
    length = x_own.shape[0]
    grad_gated = begun[...] if skip else None
    for j in range(n):
        columns = pl.ds(pl.multiple_of(offs[skip + j], depth), depth)
        copies[first[j]].wait()
        term = dot_nt(ups[:, columns], out_parts[j][...])
        grad_gated = term if grad_gated is None else grad_gated + term
    grad_gated = grad_gated.astype(BF16).astype(F32)
    for i in second:
        copies[i].wait()

    def through_head(h):
        cut = slice(h * HEAD_DIM, (h + 1) * HEAD_DIM)
        up = grad_gated[:, cut]
        mixed_h = mixed[:, cut]
        root = row_root(mixed_h)
        normed = mixed_h * root
        grad_n = up * gate[:, cut]
        grad_gate = up * normed
        grad_mixed = root * (grad_n - normed * jnp.mean(grad_n * normed, axis=-1, keepdims=True))
        low = grad_mixed.astype(BF16)
        base = 3 * h * HEAD_DIM
        value = vqk[:, base : base + HEAD_DIM]
        query = vqk[:, base + HEAD_DIM : base + 2 * HEAD_DIM]
        key = vqk[:, base + 2 * HEAD_DIM : base + 3 * HEAD_DIM]
        grad_scores = (dot_nt(low, value) * factor[h]).astype(BF16)
        grad_value = dot_tn(probs[h], low)
        grad_query = dot(grad_scores, key)
        grad_key = dot_tn(grad_scores, query)
        grad_active = jnp.concatenate([grad_gate, grad_value, grad_query, grad_key], axis=1)
        return (grad_active * slope[:, h * wide : (h + 1) * wide]).astype(BF16)

    grad_pre = through_head(0)
    for h in range(heads):
        for copy in by_head[h]:
            copy.wait()
        following = through_head(h + 1) if h + 1 < heads else None
        for j in range(parts):
            rows_of = in_parts[j].shape[0]
            columns = pl.ds(pl.multiple_of(in_offs[j], rows_of), rows_of)
            term = dot_nt(grad_pre, in_parts[j][:, h * wide : (h + 1) * wide])
            if h == 0:
                grad_normed[:, columns] = term
            else:
                grad_normed[:, columns] += term
        grad_pre = following
    for r, root in enumerate(roots):
        rows = pl.ds(r * length, length)
        scaled_rows = scaled[rows, :]
        grad_n = grad_normed[rows, :]
        mean = jnp.mean(grad_n * scaled_rows, axis=-1, keepdims=True)
        part[rows, :] = (root * (grad_n - scaled_rows * mean)).astype(BF16)
    split_rows(core[0], part, send, keep)


def pack_kernel(n, offs, gated, up_own, up_theirs, whole, *packs):
    depth = packs[0].shape[1] - 2 * gated.shape[2]
    slab = gated.shape[2]
    length = up_own.shape[0]
    whole[:length, :] = up_own[...]
    whole[length:, :] = up_theirs[...]
    for j in range(2, n):
        pack = packs[j - 2]
        columns = pl.ds(pl.multiple_of(offs[j], depth), depth)
        pack[:, :slab] = gated[1]
        pack[:, slab : 2 * slab] = gated[2]
        pack[:length, 2 * slab :] = up_own[:, columns]
        pack[length:, 2 * slab :] = up_theirs[:, columns]


def fold(rows, target, start):
    share, width = rows.shape
    blocks = target.shape[0] // share
    size = width // blocks
    for k in range(blocks):
        target[k * share : (k + 1) * share, start : start + size] = rows[
            :, k * size : (k + 1) * size
        ]


def unfold(folded, start, target):
    share, width = target.shape
    blocks = folded.shape[0] // share
    size = width // blocks
    for k in range(blocks):
        target[:, k * size : (k + 1) * size] = folded[
            k * share : (k + 1) * share, start : start + size
        ]


def finish_kernel(host, ahead_0, ahead_1, back_0, message, given, ahead, back):
    width = back.shape[1]
    depth = message.shape[1] - width // 2

    @pl.when(host[0] != 0)
    def _():
        ahead[0] = ahead_0[0]
        ahead[1] = ahead_1[0]
        back[...] = back_0[0]

    @pl.when(host[0] == 0)
    def _():
        ahead[0] = given[0]
        unfold(message, depth, ahead.at[1])
        back[...] = given[1]


def settle_kernel(core, own, theirs, keep, landed, total):
    share = keep.shape[1]
    here = pl.ds(pl.multiple_of(core[0] * share, share), share)
    for r, source in enumerate((own, theirs)):
        total[r] = (
            source[here, :].astype(F32) + keep[r].astype(F32) + landed[r].astype(F32)
        ).astype(BF16)


def settle_two_kernel(core, own, theirs, keep, landed, earlier, total, pair):
    settle_kernel(core, own, theirs, keep, landed, total)
    pair[0] = earlier[1]
    pair[1] = total[1]


def first_kernel(core, own, theirs, keep, landed, gated, total, pack):
    slab = gated.shape[2]
    settle_kernel(core, own, theirs, keep, landed, total)
    pack[:, :slab] = gated[1]
    pack[:, slab : 2 * slab] = gated[2]


def message_kernel(
    core, offs, fresh, new_own, new_theirs, passed, keep, landed, up, ahead, message
):
    share = keep.shape[1]
    depth = message.shape[1] - up.shape[2] // 2
    here = pl.ds(pl.multiple_of(core[0] * share, share), share)
    columns = pl.ds(pl.multiple_of(offs[1], depth), depth)
    for r, source in enumerate((new_own, new_theirs)):
        residual = jnp.where(fresh[0] != 0, source[here, :], passed[r])
        ahead[r] = (
            residual.astype(F32) + keep[r].astype(F32) + landed[r].astype(F32)
        ).astype(BF16)
        message[r * share : (r + 1) * share, :depth] = up[r, :, columns]
    fold(ahead[1], message, depth)


def last_kernel(up, keep, landed, back, other):
    for r in range(2):
        back[r] = (
            up[r].astype(F32) + keep[r].astype(F32) + landed[r].astype(F32)
        ).astype(BF16)
    other[...] = back[1]


def cut_kernel(n, core, offs, fresh, landed, new_own, new_theirs, mine, *pieces):
    share = landed.shape[1]
    depth = pieces[-1].shape[1]
    here = pl.ds(pl.multiple_of(core[0] * share, share), share)
    for r, source in enumerate((new_own, new_theirs)):
        mine[r] = jnp.where(fresh[0] != 0, source[here, :], landed[r])
        for j in range(2, n):
            columns = pl.ds(pl.multiple_of(offs[j], depth), depth)
            pieces[j - 2][r * share : (r + 1) * share, :] = mine[r, :, columns]


def grads_kernel(
    n, scaling, host, core, offs, gated, up_0, up_own, up_near, mine, theirs, halves, other, *rest
):
    packs = rest[: n - 1]
    out, whole = rest[n - 1 :]
    slab = gated.shape[2]
    depth = out.shape[1]
    share = mine.shape[1]
    cores = whole.shape[0] // (2 * share)
    at_host = host[0] != 0
    columns = pl.ds(pl.multiple_of(offs[0], depth), depth)

    def product(first, second, third, upstream):
        for half, owner in enumerate((core[0], cores - 1 - core[0])):
            for r in range(2):
                at = pl.multiple_of((r * cores + owner) * share, share)
                whole[pl.ds(at, share), :] = upstream(half, r)
        return dot_tn(first, third) + dot_tn(second, whole[...])

    up_pair = jnp.concatenate([up_near[...], up_own[:, columns]], axis=0)
    total = product(
        jnp.where(at_host, gated[1], packs[0][:, :slab]),
        jnp.where(at_host, gated[2], packs[0][:, slab : 2 * slab]),
        jnp.where(at_host, up_0[:, columns], up_pair),
        lambda half, r: jnp.where(
            at_host,
            (mine, theirs)[half][r, :, columns],
            (halves, other)[half][0, r * share : (r + 1) * share, :],
        ),
    )
    for m in range(1, n // 2):
        near, beyond = m, n // 2 + m - 1
        pack = jnp.where(at_host, packs[near][...], packs[beyond][...])
        total = total + product(
            pack[:, :slab],
            pack[:, slab : 2 * slab],
            pack[:, 2 * slab :],
            lambda half, r: (halves, other)[half][m, r * share : (r + 1) * share, :],
        )
    out[...] = total * scaling


def in_hbm(arrays):
    return [pltpu.with_memory_space_constraint(x, pltpu.HBM) for x in arrays]


def after(value, *earlier):
    return lax.optimization_barrier((value,) + earlier)[0]


def block_keep(live_blocks, block_marks):
    length = BLOCKS * BLOCK
    places = jnp.arange(length, dtype=jnp.int32)
    owners = places // BLOCK
    marked = jnp.repeat(jnp.repeat(block_marks, BLOCK, axis=-2), BLOCK, axis=-1) == 1
    allowed = (owners[:, None] == owners[None, :]) | marked
    causal = places[:, None] >= places[None, :]
    tokens = live_blocks[..., None, None] * BLOCK
    keeping = causal & allowed & (places[:, None] < tokens) & (places[None, :] < tokens)
    return jnp.where(keeping, 1.0 / jnp.maximum(tokens, 1).astype(F32), 0.0)


def per_device(
    arrivals,
    in_flight,
    cotangent,
    grad_flight,
    stashed,
    in_weight,
    out_weight,
    forward_blocks,
    backward_blocks,
    forward_marks,
    backward_marks,
):
    section_no = lax.axis_index("section")
    sections = lax.axis_size("section")
    core_no = lax.axis_index("cores")
    cores = lax.axis_size("cores")
    dp_no = lax.axis_index("dp")
    n = lax.axis_size("dp")
    ticks = arrivals.shape[0]
    length = arrivals.shape[1]
    width = arrivals.shape[2]
    rows = 2 * length
    share = length // cores
    in_shard = in_weight[0]
    out_shard = out_weight[0]
    depth = in_shard.shape[0]
    slab = out_shard.shape[0]
    heads = slab // HEAD_DIM
    wide = 4 * HEAD_DIM

    hosts = [2 * k + 1 if 4 * k < n - 2 else 2 * k for k in range(n // 2)]
    host_table = jnp.array(hosts, jnp.int32)
    is_host = dp_no == host_table[dp_no // 2]

    def from_partner(x):
        return lax.ppermute(x, "dp", [(h ^ 1, h) for h in hosts])

    def to_partner(x):
        return lax.ppermute(x, "dp", [(h, h ^ 1) for h in hosts])

    def from_host(x, m):
        return lax.ppermute(x, "dp", [(hosts[k ^ m], hosts[k]) for k in range(n // 2)])

    def to_beyond(x, m):
        return lax.ppermute(
            x, "dp", [(hosts[k ^ m], hosts[k] ^ 1) for k in range(n // 2)]
        )

    def swap_cores(x):
        return lax.ppermute(x, "cores", [(c, cores - 1 - c) for c in range(cores)])

    def along_sections(x, by):
        pairs = [
            (i * n + h, (i + by) * n + h)
            for i in range(sections)
            if 0 <= i + by < sections
            for h in hosts
        ]
        return lax.ppermute(x, ("section", "dp"), pairs)

    first_section = section_no == 0
    last_section = section_no == sections - 1
    between = range(1, n // 2)

    pieces = max(1, min(2, depth // 256))
    piece = depth // pieces
    in_far = [from_host(in_shard, m) for m in between]
    in_near = [
        from_partner(in_shard[i * piece : (i + 1) * piece]) for i in range(pieces)
    ]
    out_near = from_partner(out_shard)
    in_pass = [from_host(in_near[0], m) for m in between]
    in_far, in_near, rows_in, tables_in = lax.optimization_barrier(
        (
            in_far,
            in_near,
            (arrivals, in_flight, cotangent, grad_flight, stashed),
            (forward_blocks, forward_marks, backward_blocks, backward_marks),
        )
    )
    in_pass += [from_host(in_near[i], m) for i in range(1, pieces) for m in between]
    in_parts = [in_shard] + in_far + in_near + in_pass
    arrivals, in_flight, cotangent, grad_flight, stashed = rows_in
    tables = jnp.concatenate(
        [
            jnp.concatenate([b[..., None], m.reshape(m.shape[:2] + (-1,))], axis=-1)
            for b, m in (tables_in[:2], tables_in[2:])
        ],
        axis=0,
    )
    near_tables = from_partner(tables)
    stash_own = stashed[0]
    stash_theirs = from_partner(stash_own)
    x_own = jnp.where(first_section, arrivals[0], in_flight[0])
    x_theirs = from_partner(x_own)
    up_own = jnp.where(last_section, cotangent[0], grad_flight[0])
    new_own = jnp.where(first_section, arrivals[1], cotangent[1])
    out_own, out_near, near_tables = lax.optimization_barrier((out_shard, out_near, near_tables))
    out_far = [from_host(out_own, m) for m in between]
    out_parts = [out_shard, out_near] + out_far + [from_host(out_near, m) for m in between]
    up_late, new_late, stash_theirs = lax.optimization_barrier((up_own, new_own, stash_theirs))
    up_theirs = from_partner(up_late)
    up_near = to_partner(
        lax.dynamic_slice_in_dim(up_late, (dp_no ^ 1) * depth, depth, axis=1)
    )
    new_theirs = from_partner(new_late)
    far_hosts = [host_table[(dp_no // 2) ^ m] for m in between]
    owners = [dp_no, dp_no ^ 1] + far_hosts + [h ^ 1 for h in far_hosts]
    offs = jnp.stack(owners).astype(jnp.int32) * depth
    in_offs = [dp_no * depth] + [h * depth for h in far_hosts]
    in_offs += [(dp_no ^ 1) * depth + i * piece for i in range(pieces)]
    in_offs += [(h ^ 1) * depth + i * piece for i in range(pieces) for h in far_hosts]
    in_offs = jnp.stack(in_offs).astype(jnp.int32)
    parts = len(in_parts)
    core = jnp.reshape(core_no, (1,)).astype(jnp.int32)
    first_flag = jnp.reshape(first_section, (1,)).astype(jnp.int32)
    host_flag = jnp.reshape(is_host, (1,)).astype(jnp.int32)
    last_flag = jnp.reshape(last_section, (1,)).astype(jnp.int32)

    both_tables = jnp.stack([tables, near_tables], axis=1)
    ahead_at = sections - 1 - section_no
    chosen = jnp.stack(
        [
            lax.dynamic_index_in_dim(both_tables[way], at, axis=1, keepdims=False)
            for way, at in (
                (0, ahead_at),
                (1, section_no),
                (1, section_no + 1),
                (0, ahead_at + 1),
            )
        ]
    )
    kept = block_keep(chosen[..., 0], chosen[..., 1:].reshape(-1, 2, BLOCKS, BLOCKS))
    blank = jnp.zeros_like(kept[:, 0])
    keep = jnp.concatenate(
        [
            jnp.concatenate([kept[:, 0], blank], axis=2),
            jnp.concatenate([blank, kept[:, 1]], axis=2),
        ],
        axis=1,
    )

    smem = pl.BlockSpec(memory_space=pltpu.SMEM)
    hbm = pl.BlockSpec(memory_space=pltpu.HBM)
    vmem = pl.BlockSpec(memory_space=pltpu.VMEM)

    def all_of(*arrays):
        return [pl.BlockSpec(x.shape, lambda *_, d=x.ndim: (0,) * d) for x in arrays]

    def row_of(x, i):
        return pl.BlockSpec((1,) + x.shape[1:], lambda *_: (i,) + (0,) * (x.ndim - 1))

    params = pltpu.CompilerParams(vmem_limit_bytes=VMEM_BYTES)
    small = pltpu.CompilerParams(vmem_limit_bytes=SMALL_VMEM_BYTES)

    def cost(multiply_adds, bytes_accessed):
        return pl.CostEstimate(
            flops=2 * multiply_adds, bytes_accessed=bytes_accessed, transcendentals=0
        )

    def struct(shape, dtype):
        return jax.ShapeDtypeStruct(shape, dtype)

    halves = [struct((2, share, width), BF16)] * 2
    kept_halves = [halves[0], pltpu.HBM(halves[0].shape, BF16)]
    matmul = rows * width * 4 * slab
    weight_bytes = 2 * width * 5 * slab

    by_head = lambda lead, last: pl.BlockSpec(lead + (last,), lambda h: (0,) * len(lead) + (h,))
    saved_shapes = [
        struct((2, rows, slab), F32),
        struct((2, rows, 3 * slab), BF16),
        struct((2, rows, 4 * slab), F32),
        struct((2, rows, slab), F32),
        struct((2, heads, rows, rows), BF16),
        struct((2, heads, rows, rows), F32),
    ]
    weight_scratch = [pltpu.VMEM(x.shape, BF16) for x in in_parts]
    gated, gate, vqk, slope, mixed, probs, factor = pl.pallas_call(
        on_host(functools.partial(project_kernel, parts, heads)),
        grid=(heads,),
        in_specs=[smem] * 2
        + all_of(x_own, x_theirs, stash_own, stash_theirs, keep)
        + [hbm] * parts,
        out_specs=[by_head((3, rows), HEAD_DIM)] + [hbm] * 6,
        out_shape=[struct((3, rows, slab), BF16)]
        + [pltpu.HBM(x.shape, x.dtype) for x in saved_shapes],
        scratch_shapes=weight_scratch
        + [pltpu.VMEM(x.shape, x.dtype) for x in saved_shapes]
        + [
            pltpu.VMEM((3 * rows, width), BF16),
            pltpu.SemaphoreType.DMA((heads * parts,)),
            pltpu.SemaphoreType.DMA((heads * 6,)),
        ],
        compiler_params=params,
        cost_estimate=cost(3 * matmul, 2 * weight_bytes),
        name="project",
    )(host_flag, in_offs, x_own, x_theirs, stash_own, stash_theirs, keep, *in_hbm(in_parts))

    def backward(ups, tick_no, early=()):
        split = len(ups) - 1
        skip = soon if early else 0
        layered = [gate, vqk, slope, mixed, probs, factor, stash_own, stash_theirs]
        plain = list(out_parts[skip:]) + list(in_parts)
        return pl.pallas_call(
            on_host(functools.partial(backward_kernel, parts, n, skip, tick_no, split)),
            grid=(1,),
            in_specs=[smem] * 4
            + [vmem if split else hbm] * len(ups)
            + [hbm] * (len(early) + len(layered) + len(plain)),
            out_specs=all_of(*halves),
            out_shape=kept_halves,
            scratch_shapes=[pltpu.VMEM((rows, width), BF16)]
            + [pltpu.VMEM(x.shape[1:], x.dtype) for x in layered]
            + [pltpu.VMEM(x.shape, x.dtype) for x in plain]
            + [
                pltpu.VMEM((rows, width), F32),
                pltpu.VMEM((rows, width), F32),
                pltpu.VMEM((rows, width), BF16),
                pltpu.VMEM((rows, slab), F32),
                pltpu.SemaphoreType.DMA((2,)),
                pltpu.SemaphoreType.DMA((1 + len(layered) + n + heads * parts,)),
            ],
            compiler_params=params,
            cost_estimate=cost((16 if split else 2) * matmul, 2 * weight_bytes),
            name="backward",
        )(host_flag, core, in_offs, offs, *ups, *in_hbm(early + tuple(layered)), *plain[: n - skip], *in_hbm(in_parts))

    gated, new_theirs, up_near = lax.optimization_barrier((gated, new_theirs, up_near))

    pack_shapes = [struct((rows, width), BF16)]
    pack_shapes += [struct((rows, 2 * slab + depth), BF16)] * (n - 2)
    folded = share * width // rows
    up_0, *packs = pl.pallas_call(
        functools.partial(pack_kernel, n),
        grid=(1,),
        in_specs=[smem] * 1 + all_of(gated, up_own, up_theirs),
        out_specs=all_of(*pack_shapes),
        out_shape=[pltpu.HBM(pack_shapes[0].shape, BF16)] + pack_shapes[1:],
        compiler_params=small,
        name="pack",
    )(offs, gated, up_own, up_theirs)
    soon = n // 2 + 1
    packs, soon_parts = lax.optimization_barrier((packs, out_parts[:soon]))
    early_shapes = [struct((rows, width), BF16), struct((rows, slab), F32)]
    early_part, early_grad = pl.pallas_call(
        early_kernel,
        grid=(1,),
        in_specs=[smem] + [row_of(gated, 0)] + all_of(up_0, *soon_parts),
        out_specs=all_of(*early_shapes),
        out_shape=[early_shapes[0], pltpu.HBM(early_shapes[1].shape, F32)],
        compiler_params=small,
        name="early",
    )(offs, gated, *in_hbm([up_0]), *soon_parts)
    early_part, early_grad, late_parts = lax.optimization_barrier(
        (early_part, early_grad, out_parts[soon:])
    )
    out_parts = soon_parts + late_parts

    ahead_send, ahead_keep = pl.pallas_call(
        functools.partial(out_kernel, soon),
        grid=(1,),
        in_specs=[smem] * 2 + [row_of(gated, 0)] + all_of(early_part, *out_parts[soon:]),
        out_specs=all_of(*halves),
        out_shape=halves,
        scratch_shapes=[pltpu.VMEM((rows, width), BF16)],
        compiler_params=small,
        cost_estimate=cost(matmul // 4, weight_bytes // 4),
        name="out",
    )(core, offs, gated, early_part, *out_parts[soon:])
    ahead_landed = swap_cores(ahead_send)
    first_shapes = [halves[0], struct((rows, 2 * slab), BF16)]
    ahead_0, partner_pack = pl.pallas_call(
        first_kernel,
        grid=(1,),
        in_specs=[smem] + all_of(x_own, x_theirs, ahead_keep, ahead_landed, gated),
        out_specs=all_of(*first_shapes),
        out_shape=first_shapes,
        compiler_params=small,
        name="first",
    )(core, *in_hbm([x_own, x_theirs]), ahead_keep, ahead_landed, gated)
    ahead_in = along_sections(ahead_0, 1)
    packs_near = [to_partner(partner_pack)] + [from_host(packs[m - 1], m) for m in between]
    back_send, back_keep = backward(in_hbm([after(up_0, ahead_0)]), 0, (early_grad,))
    back_send, back_keep, ahead_in, packs_near = lax.optimization_barrier(
        (back_send, back_keep, ahead_in, packs_near)
    )
    back_landed = swap_cores(back_send)
    settled = list(halves)
    back_0, back_given = pl.pallas_call(
        settle_two_kernel,
        grid=(1,),
        in_specs=[smem] + all_of(up_own, up_theirs, back_keep, back_landed, ahead_0),
        out_specs=all_of(*settled),
        out_shape=settled,
        compiler_params=small,
        name="settle",
    )(core, *in_hbm([up_own, up_theirs, back_keep]), back_landed, *in_hbm([ahead_0]))
    back_in = along_sections(back_0, -1)

    packs_beyond = [to_beyond(packs[n // 2 + m - 2], m) for m in between]
    ahead_their = swap_cores(ahead_in)
    ahead_send, ahead_keep = pl.pallas_call(
        on_host(functools.partial(forward_kernel, parts, heads)),
        grid=(heads,),
        in_specs=[smem] * 5
        + all_of(ahead_in, ahead_their, new_own, new_theirs)
        + [row_of(keep, keep.shape[0] - 1)]
        + [hbm] * parts
        + all_of(*out_parts),
        out_specs=all_of(*halves),
        out_shape=kept_halves,
        scratch_shapes=[
            pltpu.VMEM((rows, width), BF16),
            pltpu.VMEM((rows, width), BF16),
            pltpu.VMEM((heads, rows, HEAD_DIM), BF16),
            pltpu.VMEM((rows, width), BF16),
            pltpu.SemaphoreType.DMA((heads * parts,)),
        ]
        + weight_scratch,
        compiler_params=params,
        cost_estimate=cost(2 * matmul, 2 * weight_bytes),
        name="forward",
    )(host_flag, core,
        in_offs,
        offs,
        first_flag,
        *in_hbm([ahead_in]),
        ahead_their,
        *in_hbm([new_own, new_theirs, keep]),
        *in_hbm(in_parts),
        *out_parts,
    )
    ahead_send, ahead_keep, back_in, packs_beyond = lax.optimization_barrier(
        (ahead_send, ahead_keep, back_in, packs_beyond)
    )
    ahead_landed = swap_cores(ahead_send)

    cut_shapes = [halves[0]] + [struct((2 * share, depth), BF16)] * (n - 2)
    up_mine, *cuts = pl.pallas_call(
        functools.partial(cut_kernel, n),
        grid=(1,),
        in_specs=[smem] * 3 + all_of(back_in, new_own, new_theirs),
        out_specs=all_of(*cut_shapes),
        out_shape=cut_shapes,
        compiler_params=small,
        name="cut",
    )(core, offs, last_flag, back_in, *in_hbm([new_own, new_theirs]))
    up_their = swap_cores(up_mine)
    landed = [from_host(cuts[m - 1], m) for m in between]
    landed += [to_beyond(cuts[n // 2 + m - 2], m) for m in between]
    message_inputs = [new_own, new_theirs, ahead_in, ahead_keep, ahead_landed, up_mine]
    message_shapes = [halves[0], struct((2 * share, depth + width // 2), BF16)]
    ahead_1, message = pl.pallas_call(
        message_kernel,
        grid=(1,),
        in_specs=[smem] * 3 + all_of(*message_inputs),
        out_specs=all_of(*message_shapes),
        out_shape=message_shapes,
        compiler_params=small,
        name="message",
    )(core, offs, first_flag, *in_hbm(message_inputs[:4]), *message_inputs[4:])
    landed = landed + [to_partner(message)]
    back_send, back_keep = backward([up_mine, up_their], 1)
    back_given = to_partner(back_given)
    back_given, back_send, back_keep, landed = lax.optimization_barrier(
        (back_given, back_send, back_keep, landed)
    )
    landed = landed[-1:] + landed[:-1]
    last_inputs = [up_mine, *in_hbm([back_keep]), swap_cores(back_send)]
    last_shapes = [halves[0], struct((share, width), BF16)]
    back_1, back_other = pl.pallas_call(
        last_kernel,
        grid=(1,),
        in_specs=all_of(*last_inputs),
        out_specs=all_of(*last_shapes),
        out_shape=last_shapes,
        compiler_params=small,
        name="last",
    )(*last_inputs)
    back_last = to_partner(back_other)

    landed_halves = jnp.stack(
        [landed[0][:, :depth]]
        + [jnp.where(is_host, landed[m], landed[n // 2 + m - 1]) for m in between]
    )
    landed_other = swap_cores(landed_halves)
    grad_inputs = [gated, up_0, up_own, up_near, up_mine, up_their, landed_halves, landed_other]
    grad_inputs += packs_near + packs_beyond
    grad_inputs[0] = after(gated, back_1)
    grad_inputs[8:] = in_hbm(grad_inputs[8:])
    grads = pl.pallas_call(
        functools.partial(grads_kernel, n, (ticks * length * n) ** (-0.5)),
        grid=(1,),
        in_specs=[smem] * 3 + all_of(*grad_inputs),
        out_specs=pl.BlockSpec((slab, depth), lambda *_: (0, 0)),
        out_shape=struct((slab, depth), F32),
        scratch_shapes=[pltpu.VMEM((rows, depth), BF16)],
        compiler_params=small,
        cost_estimate=cost(matmul // 4, weight_bytes // 4),
        name="grads",
    )(host_flag, core, offs, *grad_inputs)

    last_cut = after(landed[0], back_1)
    finish_inputs = [ahead_0, ahead_1, back_0, last_cut, back_given]
    finish_shapes = [struct((ticks, share, width), BF16), struct((share, width), BF16)]
    ahead, back_first = pl.pallas_call(
        finish_kernel,
        grid=(1,),
        in_specs=[smem] + all_of(*finish_inputs),
        out_specs=all_of(*finish_shapes),
        out_shape=finish_shapes,
        compiler_params=small,
        name="finish",
    )(host_flag, *finish_inputs)
    back = jnp.stack([back_first, jnp.where(is_host, back_1[0], back_last)])
    return (ahead[None], back[None], grads[None])


def solution(mesh):
    in_specs = (
        P(None, "dp", None),
        P("section", "dp", None),
        P(None, "dp", None),
        P("section", "dp", None),
        P("section", None, "dp", None),
        P("section", "dp", "cores"),
        P("section", "cores", "dp"),
        P("dp", None),
        P("dp", None),
        P("dp", None, None, None),
        P("dp", None, None, None),
    )
    out_specs = (
        P("section", None, ("dp", "cores"), None),
        P("section", None, ("dp", "cores"), None),
        P("section", "cores", "dp"),
    )
    return jax.shard_map(
        per_device, mesh=mesh, in_specs=in_specs, out_specs=out_specs, check_vma=False
    )
```
